32 devices in a mesh: groups: 2 (over y), dom: 4 (over x, core), col: 4 (over z).
Axes of the slice: x: 2, y: 2, z: 4, core: 2. Of those that a mesh axis runs over, the one named last changes fastest.
Arguments:
- sigma_next: bfloat16 [8, 2048, 2048], P(('groups', 'dom'), 'col'), parts along dimension 0, as said below
- separator: bfloat16 [8, 2048, 2048], P(('groups', 'dom'), 'col'), parts along dimension 0, as said below
- inverse_pivot: bfloat16 [8, 2048, 2048], P(('groups', 'dom'), 'col'), parts along dimension 0
- coupling_rate: float32 [8], P(('groups', 'dom')), parts along dimension 0, may hold values from 0.15 to 0.45
- lengths: int32 [8], P(('groups', 'dom')), parts along dimension 0, may hold values from 1 to 4, 10 in all
- step_index: int32 [8], P(('groups', 'dom')), parts along dimension 0, may hold values from 0 to 3
- node_class: int32 [4096], P('groups'), parts along dimension 0, may hold values from 0 to 3
Outputs:
- covariance: bfloat16 [8, 2048, 2048], P(('groups', 'dom'), 'col'), parts along dimension 0
- variances: float32 [8, 2048], P(('groups', 'dom'), 'col'), parts along dimension 0
The draws below stay inside these ranges and needn't reach their ends.
There are 2 independent parts, one for each index of `groups`. The reference program is written for one: setup_inputs(seed, part) draws one part's arguments, and reference() takes and returns one part's arrays. A program takes and returns all parts, laid end to end along the dimension named above; each array names one. Nothing has to cross between parts.
Inputs may be any that keep to these rules, and one draw needn't show every extreme that they name: Every block of sigma_next is exactly symmetric. Every block of separator is exactly symmetric.
All inputs are finite; a program needn't handle non-finite values. No bound on the sum of `lengths` on one device may be relied on, other than what follows from the above.
Results may differ from the reference program's by a relative error of at most 0.0027.
Values may be sent and summed in bfloat16 or wider, within the bound.
No kernel may reach another device: no remote copies, remote signals or barrier semaphores. Data moves between devices by JAX's collectives and lax.ppermute only.
A program may use at most 192 MiB of HBM per device.

```python
import math
import jax
import jax.numpy as jnp
import numpy as np

GX = 64
GY = 32
MOSTLEN = 4
NODES = 2048
N_DOM = 4


def symmetric_block(noise, diag_draw, spread):
    mirrored = (noise + jnp.swapaxes(noise, 1, 2)) * 0.70710678
    rows_idx = jnp.arange(NODES)[:, None]
    cols_idx = jnp.arange(NODES)[None, :]
    on_diag = (rows_idx == cols_idx)[None, :, :]
    return jnp.where(on_diag, diag_draw, spread * mirrored)


def draw_sigma_next(key, part):
    key = jax.random.fold_in(key, 11)
    first, second = jax.random.split(key)
    shape = (N_DOM, NODES, NODES)
    noise = jax.random.normal(first, shape, jnp.float32)
    diag_draw = jax.random.uniform(second, (N_DOM, NODES, 1), jnp.float32, 1.0, 2.5)
    return symmetric_block(noise, diag_draw, 0.5 / math.sqrt(NODES)).astype(jnp.bfloat16)


def draw_separator(key, part):
    key = jax.random.fold_in(key, 23)
    first, second = jax.random.split(key)
    shape = (N_DOM, NODES, NODES)
    noise = jax.random.normal(first, shape, jnp.float32)
    diag_draw = jax.random.uniform(second, (N_DOM, NODES, 1), jnp.float32, 1.0, 2.5)
    return symmetric_block(noise, diag_draw, 0.5 / math.sqrt(NODES)).astype(jnp.bfloat16)


def draw_inverse_pivot(key, part):
    key = jax.random.fold_in(key, 37)
    first, second = jax.random.split(key)
    shape = (N_DOM, NODES, NODES)
    noise = jax.random.normal(first, shape, jnp.float32)
    diag_draw = jax.random.uniform(second, (N_DOM, NODES, 1), jnp.float32, 0.6, 1.6)
    return symmetric_block(noise, diag_draw, 0.5 / math.sqrt(NODES)).astype(jnp.bfloat16)


def draw_step_index(key, part):
    key = jax.random.fold_in(key, 53)
    first, second = jax.random.split(key)
    steps_drawn = jax.random.randint(first, (N_DOM,), 0, MOSTLEN, jnp.int32)
    zero_at = jax.random.randint(second, (), 0, N_DOM, jnp.int32)
    top_at = (zero_at + 1) % N_DOM
    places = jnp.arange(N_DOM, dtype=jnp.int32)
    steps_drawn = jnp.where(places == top_at, MOSTLEN - 1, steps_drawn)
    steps_drawn = jnp.where(places == zero_at, 0, steps_drawn)
    return steps_drawn.astype(jnp.int32)


def place_ends(drawn, key, least, top_value):
    extent = drawn.shape
    spot = [jax.random.randint(jax.random.fold_in(key, axis), (), 0, extent[axis]) for axis in range(len(extent))]
    drawn = drawn.at[tuple(spot)].set(least)
    longest = extent.index(max(extent))
    spot[longest] = (spot[longest] + 1) % extent[longest]
    return drawn.at[tuple(spot)].set(top_value)


def steps_of(own_key, extent, cuts, smallest, top_value):
    level = 1.0
    for axis_at, parts in cuts:
        heights = jax.random.uniform(jax.random.fold_in(jax.random.fold_in(own_key, 6), axis_at), (parts,), jnp.float32, smallest / len(cuts), top_value / len(cuts))
        level = level * jnp.repeat(jnp.exp(heights), extent[axis_at] // parts).reshape((-1,) + (1,) * (len(extent) - 1 - axis_at))
    return level


def split_up(count, total, bound, skew):
    loads = [(1 << 20) // math.isqrt(standing ** skew) + 1 for standing in range(2, count + 1)]
    rest, given = total - bound - (count - 1), [1] * (count - 1)
    while rest > 0:
        free = [i for i in range(count - 1) if given[i] < bound]
        pool, remaining = sum([loads[i] for i in free]), rest
        for i in free:
            more = min(bound - given[i], max(1, remaining * loads[i] // pool), rest)
            given[i] = given[i] + more
            rest = rest - more
    return np.array([bound] + given)


def uneven(stream_key, number_of, total, most, skew):
    if number_of == 2:
        one = jax.random.randint(stream_key, (), max(1, total - most), min(most, total - 1) + 1)
        return jnp.stack([one, total - one])
    sizes = jnp.asarray(split_up(number_of, total, most, skew), jnp.int32)
    couples = (number_of - 1) // 2
    giver, taker = sizes[1:1 + 2 * couples:2], sizes[2:2 + 2 * couples:2]
    slack = jnp.minimum(giver - 1, most - taker)
    shifted = jax.random.randint(jax.random.fold_in(stream_key, 1), (couples,), 0, 1 << 20) % (slack + 1)
    sizes = sizes.at[1:1 + 2 * couples:2].set(giver - shifted).at[2:2 + 2 * couples:2].set(taker + shifted)
    return sizes[jax.random.permutation(jax.random.fold_in(stream_key, 2), number_of)]


def setup_inputs(seed: int = 0, part: int = 0) -> dict:
    splits = jax.random.split(jax.random.key(seed), 8)
    own_keys = jax.random.split(jax.random.fold_in(splits[7], part), 8)
    return {
        "sigma_next": draw_sigma_next(jax.random.fold_in(jax.random.fold_in(splits[7], part), 71), part),
        "separator": draw_separator(jax.random.fold_in(jax.random.fold_in(splits[7], part), 71), part),
        "inverse_pivot": draw_inverse_pivot(jax.random.fold_in(jax.random.fold_in(splits[7], part), 71), part),
        "coupling_rate": jnp.clip(jnp.exp(math.log(0.45) - 1.0986122 * jax.random.uniform(own_keys[3], (N_DOM,), jnp.float32) ** steps_of(own_keys[3], (N_DOM,), ((0, 4),), -0.2, 0.2)), 0.15, 0.45),
        "lengths": uneven(own_keys[4], N_DOM, 2 * N_DOM + 2, MOSTLEN, 2).astype(jnp.int32),
        "step_index": draw_step_index(jax.random.fold_in(jax.random.fold_in(splits[7], part), 71), part),
        "node_class": place_ends(jax.random.randint(own_keys[6], (NODES,), 0, 4), jax.random.fold_in(own_keys[6], 1), 0, 3).astype(jnp.int32),
    }


def class_weights(node_class):
    picks = (node_class[:, None] == jnp.arange(4)[None, :]).astype(jnp.float32)
    across_weight = picks @ jnp.array([0.25, 0.375, 0.125, 0.5], jnp.float32)
    along_weight = picks @ jnp.array([0.25, 0.125, 0.375, 0.0], jnp.float32)
    return across_weight, along_weight


def couple(panel, node_class, rate):
    across_weight, along_weight = class_weights(node_class)
    count = panel.shape[0]
    grid = panel.reshape(count, GY, GX)
    padded = jnp.pad(grid, ((0, 0), (1, 1), (1, 1)))
    across = (padded[:, 1:-1, :-2] + padded[:, 1:-1, 2:]).reshape(count, GY * GX)
    along = (padded[:, :-2, 1:-1] + padded[:, 2:, 1:-1]).reshape(count, GY * GX)
    return rate * (panel + across_weight * across + along_weight * along)


def reference(sigma_next, separator, inverse_pivot, coupling_rate, lengths, step_index, node_class):
    cov_list = []
    var_list = []
    for part_id in range(N_DOM):
        if part_id + 1 < N_DOM:
            upper = separator[part_id + 1]
        else:
            upper = jnp.zeros_like(separator[0])
        prior = jnp.where(step_index[part_id] == 0, upper, sigma_next[part_id])
        pivot = inverse_pivot[part_id].astype(jnp.float32)
        coupled = couple(pivot, node_class, coupling_rate[part_id]).astype(jnp.bfloat16)
        half = jnp.dot(coupled, prior, preferred_element_type=jnp.float32).astype(jnp.bfloat16)
        full = pivot + jnp.dot(half, coupled.T, preferred_element_type=jnp.float32)
        active = step_index[part_id] < lengths[part_id]
        old = sigma_next[part_id]
        cov_list.append(jnp.where(active, full.astype(jnp.bfloat16), old))
        var_list.append(jnp.where(active, jnp.diagonal(full), jnp.diagonal(old).astype(jnp.float32)))
    return jnp.stack(cov_list), jnp.stack(var_list)
```

```python
import functools

import jax
import jax.numpy as jnp
from jax import lax
from jax.experimental import pallas as pl
from jax.experimental.pallas import tpu as pltpu
from jax.sharding import PartitionSpec as P

GX = 64
GY = 32
BF16 = jnp.bfloat16
F32 = jnp.float32
MIB = 1 << 20


def passed_along(value, axis, steps):
    count = lax.axis_size(axis)
    initial, last = (max(0, -steps), min(count, count - steps))
    return lax.ppermute(value, axis, [(source, source + steps) for source in range(initial, last)])


def couple_kernel(rate_ref, class_ref, pivot_ref, out_ref, weight_ref):
    nodes = pivot_ref.shape[1]

    @pl.when(pl.program_id(0) == 0)
    def _():
        kind = class_ref[...]
        across = jnp.where(
            kind == 0, 0.25, jnp.where(kind == 1, 0.375, jnp.where(kind == 2, 0.125, 0.5))
        ).astype(F32)
        along = jnp.where(
            kind == 0, 0.25, jnp.where(kind == 1, 0.125, jnp.where(kind == 2, 0.375, 0.0))
        ).astype(F32)
        node = lax.broadcasted_iota(jnp.int32, (1, nodes), 1)
        column = node % GX
        parts = (
            jnp.where(column > 0, across, 0.0),
            jnp.where(column < GX - 1, across, 0.0),
            jnp.where(node >= GX, along, 0.0),
            jnp.where(node < nodes - GX, along, 0.0),
        )
        for which, part in enumerate(parts):
            weight_ref[which] = jnp.broadcast_to(part, (16, nodes))

    rate = rate_ref[0]

    def group(step, carry):
        rows = pl.ds(pl.multiple_of(step * 16, 16), 16)
        value = pivot_ref[rows, :].astype(F32)
        total = (
            value
            + weight_ref[0] * pltpu.roll(value, 1, 1)
            + weight_ref[1] * pltpu.roll(value, nodes - 1, 1)
            + weight_ref[2] * pltpu.roll(value, GX, 1)
            + weight_ref[3] * pltpu.roll(value, nodes - GX, 1)
        )
        out_ref[rows, :] = (rate * total).astype(BF16)
        return carry

    lax.fori_loop(0, pivot_ref.shape[0] // 16, group, 0)


def couple(pivot, node_class, rate):
    rows, nodes = pivot.shape
    chunk = min(rows, 128)
    return pl.pallas_call(
        couple_kernel,
        out_shape=jax.ShapeDtypeStruct((rows, nodes), BF16),
        grid=(rows // chunk,),
        in_specs=[
            pl.BlockSpec(memory_space=pltpu.SMEM),
            pl.BlockSpec((1, nodes), lambda i: (0, 0)),
            pl.BlockSpec((chunk, nodes), lambda i: (i, 0)),
        ],
        out_specs=pl.BlockSpec((chunk, nodes), lambda i: (i, 0)),
        scratch_shapes=[pltpu.VMEM((4, 16, nodes), F32)],
        compiler_params=pltpu.CompilerParams(vmem_limit_bytes=16 * MIB),
        cost_estimate=pl.CostEstimate(
            flops=10 * rows * nodes, bytes_accessed=4 * rows * nodes, transcendentals=0
        ),
        name="couple",
    )(rate, node_class.reshape(1, nodes), pivot)


def turned(block, odd):
    return block + odd * (3 - 2 * block)


def route(source, target, doms):
    pairs = []
    for dom in range(doms):
        odd = dom % 2
        pairs.append((dom * 4 + turned(source, odd), dom * 4 + turned(target, odd)))
    return pairs


def moved(value, source, target):
    return lax.ppermute(value, ("dom", "col"), route(source, target, lax.axis_size("dom")))


def prior_kernel(place_ref, step_ref, shifted_ref, sigma_ref, row_ref, far_ref, near_ref, last_ref):
    odd = place_ref[0]
    width = last_ref.shape[1]

    def fill(source):
        row_ref[...] = source[...]
        for block in (0, 2, 3):
            start = pl.multiple_of(turned(block, odd) * width, 128)
            value = source[:, pl.ds(start, width)]
            at = {0: 0, 2: 1, 3: 2}[block]
            far_ref[:, at * width : (at + 1) * width] = value
            if block >= 2:
                near_ref[:, (block - 2) * width : (block - 1) * width] = value
            if block == 3:
                last_ref[...] = value

    @pl.when(step_ref[0] == 0)
    def _():
        fill(shifted_ref)

    @pl.when(step_ref[0] != 0)
    def _():
        fill(sigma_ref)


def prior_parts(place, step, shifted, sigma):
    rows, nodes = sigma.shape
    chunk = 128
    width = nodes // 4
    out = lambda blocks: jax.ShapeDtypeStruct((rows, blocks * width), BF16)
    spec = lambda blocks: pl.BlockSpec((chunk, blocks * width), lambda i, place, step: (i, 0))
    return pl.pallas_call(
        prior_kernel,
        out_shape=(out(4), out(3), out(2), out(1)),
        grid_spec=pltpu.PrefetchScalarGridSpec(
            num_scalar_prefetch=2,
            grid=(rows // chunk,),
            in_specs=[
                pl.BlockSpec(
                    (chunk, nodes), lambda i, place, step: (jnp.where(step[0] == 0, i, 0), 0)
                ),
                pl.BlockSpec(
                    (chunk, nodes), lambda i, place, step: (jnp.where(step[0] == 0, 0, i), 0)
                ),
            ],
            out_specs=(spec(4), spec(3), spec(2), spec(1)),
        ),
        compiler_params=pltpu.CompilerParams(vmem_limit_bytes=16 * MIB),
        cost_estimate=pl.CostEstimate(
            flops=0, bytes_accessed=7 * rows * nodes, transcendentals=0
        ),
        name="prior_parts",
    )(place, step, shifted, sigma)


def assemble(prior_ref, odd, row_ref, far_ref, near_ref, last_ref):
    width = last_ref.shape[1]

    def put(value, row, column):
        rows = pl.ds(pl.multiple_of(turned(row, odd) * width, 128), width)
        columns = pl.ds(pl.multiple_of(turned(column, odd) * width, 128), width)
        prior_ref[rows, columns] = value

    prior_ref[pl.ds(pl.multiple_of(turned(1, odd) * width, 128), width), :] = row_ref[...]
    for block in (0, 2, 3):
        columns = pl.ds(pl.multiple_of(turned(block, odd) * width, 128), width)
        put(row_ref[:, columns].T, block, 1)
    for at, block in enumerate((0, 2, 3)):
        value = far_ref[:, at * width : (at + 1) * width]
        put(value, 0, block)
        if block:
            put(value.T, block, 0)
    put(near_ref[:, :width], 2, 2)
    value = near_ref[:, width:]
    put(value, 2, 3)
    put(value.T, 3, 2)
    put(last_ref[...], 3, 3)


def half_kernel(count, place_ref, row_ref, far_ref, near_ref, last_ref, *refs):
    coupled_refs, half_refs, prior_ref = refs[:count], refs[count : 2 * count], refs[2 * count]

    @pl.when(place_ref[1] == 1)
    def _():
        assemble(prior_ref, place_ref[0], row_ref, far_ref, near_ref, last_ref)

        def columns_of(step, carry):
            columns = pl.ds(pl.multiple_of(step * 256, 256), 256)
            for coupled_ref, half_ref in zip(coupled_refs, half_refs):
                half_ref[:, columns] = jnp.dot(
                    coupled_ref[...], prior_ref[:, columns], preferred_element_type=F32
                ).astype(BF16)
            return carry

        lax.fori_loop(0, prior_ref.shape[0] // 256, columns_of, 0)


def halves(place, parts, coupled):
    rows, nodes = coupled[0].shape
    count = len(coupled)
    vmem = pl.BlockSpec(memory_space=pltpu.VMEM)
    return pl.pallas_call(
        functools.partial(half_kernel, count),
        out_shape=tuple(jax.ShapeDtypeStruct((rows, nodes), BF16) for _ in coupled),
        in_specs=[pl.BlockSpec(memory_space=pltpu.SMEM)] + [vmem] * (4 + count),
        out_specs=tuple(vmem for _ in coupled),
        scratch_shapes=[pltpu.VMEM((nodes, nodes), BF16)],
        compiler_params=pltpu.CompilerParams(vmem_limit_bytes=40 * MIB),
        cost_estimate=pl.CostEstimate(
            flops=2 * count * rows * nodes * nodes,
            bytes_accessed=(5 + 4 * count) * rows * nodes,
            transcendentals=0,
        ),
        name="halves",
    )(place, *parts, *coupled)


def product_kernel(place_ref, half_ref, c0, c1, c2, c3, out_ref):
    @pl.when(place_ref[1] == 1)
    def _():
        width = out_ref.shape[1] // 4
        for block, coupled_ref in enumerate((c0, c1, c2, c3)):
            start = turned(block, place_ref[0]) * width

            def columns_of(step, carry):
                value = lax.dot_general(
                    half_ref[...],
                    coupled_ref[pl.ds(pl.multiple_of(step * 256, 256), 256), :],
                    (((1,), (1,)), ((), ())),
                    preferred_element_type=F32,
                )
                columns = pl.ds(pl.multiple_of(start + step * 256, 256), 256)
                out_ref[:, columns] = value.astype(BF16)
                return carry

            lax.fori_loop(0, width // 256, columns_of, 0)


def product(place, half, coupled):
    rows, nodes = half.shape
    vmem = pl.BlockSpec(memory_space=pltpu.VMEM)
    return pl.pallas_call(
        product_kernel,
        out_shape=jax.ShapeDtypeStruct((rows, nodes), BF16),
        in_specs=[pl.BlockSpec(memory_space=pltpu.SMEM)] + [vmem] * 5,
        out_specs=vmem,
        compiler_params=pltpu.CompilerParams(vmem_limit_bytes=40 * MIB),
        cost_estimate=pl.CostEstimate(
            flops=2 * rows * nodes * nodes, bytes_accessed=12 * rows * nodes, transcendentals=0
        ),
        name="product",
    )(place, half, *coupled)


def final_kernel(place_ref, active_ref, pivot_ref, q0, q1, q2, q3, sigma_ref, out_ref, var_ref):
    rows, nodes = pivot_ref.shape
    place = place_ref[1]
    start = pl.multiple_of(place_ref[2] * (nodes // 4) + pl.program_id(0) * rows, 128)
    square = (rows, rows)
    on_diagonal = lax.broadcasted_iota(jnp.int32, square, 0) == lax.broadcasted_iota(
        jnp.int32, square, 1
    )

    def diagonal(value):
        return jnp.sum(jnp.where(on_diagonal, value, 0.0), axis=0, keepdims=True)

    for which, product_ref in enumerate((q0, q1, q2, q3)):

        @pl.when((active_ref[0] != 0) & (place == which))
        def _():
            out_ref[...] = (pivot_ref[...].astype(F32) + product_ref[...].astype(F32)).astype(BF16)
            columns = pl.ds(start, rows)
            var_ref[...] = diagonal(
                pivot_ref[:, columns].astype(F32) + product_ref[:, columns].astype(F32)
            )

    @pl.when(active_ref[0] == 0)
    def _():
        out_ref[...] = sigma_ref[...]
        var_ref[...] = diagonal(sigma_ref[:, pl.ds(start, rows)].astype(F32))


def final(place, active, pivot, products, sigma):
    rows, nodes = pivot.shape
    chunk = 128

    def picked(which):
        return pl.BlockSpec(
            (chunk, nodes), lambda i, place, active: (jnp.where(place[1] == which, i, 0), 0)
        )

    return pl.pallas_call(
        final_kernel,
        out_shape=(
            jax.ShapeDtypeStruct((rows, nodes), BF16),
            jax.ShapeDtypeStruct((1, rows), F32),
        ),
        grid_spec=pltpu.PrefetchScalarGridSpec(
            num_scalar_prefetch=2,
            grid=(rows // chunk,),
            in_specs=[pl.BlockSpec((chunk, nodes), lambda i, place, active: (i, 0))]
            + [picked(which) for which in range(4)]
            + [
                pl.BlockSpec(
                    (chunk, nodes), lambda i, place, active: (jnp.where(active[0] == 0, i, 0), 0)
                )
            ],
            out_specs=(
                pl.BlockSpec((chunk, nodes), lambda i, place, active: (i, 0)),
                pl.BlockSpec((1, chunk), lambda i, place, active: (0, i)),
            ),
        ),
        compiler_params=pltpu.CompilerParams(vmem_limit_bytes=16 * MIB),
        cost_estimate=pl.CostEstimate(
            flops=2 * rows * nodes, bytes_accessed=8 * rows * nodes, transcendentals=0
        ),
        name="final",
    )(place, active, pivot, *products, sigma)


def owned(sigma_next, separator, inverse_pivot, coupling_rate, lengths, step_index, node_class):
    sigma, pivot = sigma_next[0], inverse_pivot[0]
    odd = lax.axis_index("dom") % 2
    col = lax.axis_index("col")
    place = jnp.stack([odd, turned(col, odd), col]).astype(jnp.int32)
    active = (step_index < lengths).astype(jnp.int32)

    shifted = passed_along(separator, "dom", -1)[0]
    coupled = couple(pivot, node_class, coupling_rate)
    c2 = moved(coupled, 2, 1)
    c0 = moved(coupled, 0, 1)
    row, far, near, last = prior_parts(place, step_index, shifted, sigma)
    parts = (row, moved(far, 0, 1), moved(near, 2, 1), moved(last, 3, 1))
    c3 = moved(coupled, 3, 1)
    panels = (c0, coupled, c2, c3)
    h0, h1, h2 = halves(place, parts, panels[:3])
    (h3,) = halves(place, parts, panels[3:])
    q3 = product(place, h3, panels)
    r3 = moved(q3, 1, 3)
    q2 = product(place, h2, panels)
    r2 = moved(q2, 1, 2)
    q0 = product(place, h0, panels)
    r0 = moved(q0, 1, 0)
    q1 = product(place, h1, panels)
    covariance, variances = final(place, active, pivot, (r0, q1, r2, r3), sigma)
    return (covariance[None], variances)


def gathered(sigma_next, separator, inverse_pivot, coupling_rate, lengths, step_index, node_class):
    shifted = passed_along(separator, "dom", -1)
    prior = jnp.where(step_index[0] == 0, shifted[0], sigma_next[0])
    pivot = inverse_pivot[0].astype(F32)
    coupled = couple(inverse_pivot[0], node_class, coupling_rate)
    rows = coupled.shape[0]
    half = jnp.dot(
        coupled,
        lax.all_gather(prior, "col", axis=0, tiled=True),
        preferred_element_type=F32,
    ).astype(BF16)
    product = lax.dot_general(
        half,
        lax.all_gather(coupled, "col", axis=0, tiled=True),
        (((1,), (1,)), ((), ())),
        preferred_element_type=F32,
    )
    full = pivot + product
    active = step_index[0] < lengths[0]
    old = sigma_next[0]
    covariance = jnp.where(active, full.astype(BF16), old)
    first_col = lax.axis_index("col") * rows
    new_block = lax.dynamic_slice_in_dim(full, first_col, rows, 1)
    old_block = lax.dynamic_slice_in_dim(old, first_col, rows, 1)
    variances = jnp.where(active, jnp.diagonal(new_block), jnp.diagonal(old_block).astype(F32))
    return (covariance[None], variances[None])


def solution(mesh):
    local = owned if mesh.shape["col"] == 4 and mesh.shape["dom"] % 2 == 0 else gathered
    return jax.shard_map(
        local,
        mesh=mesh,
        in_specs=(
            P(("groups", "dom"), "col", None),
            P(("groups", "dom"), "col", None),
            P(("groups", "dom"), "col", None),
            P(("groups", "dom")),
            P(("groups", "dom")),
            P(("groups", "dom")),
            P("groups"),
        ),
        out_specs=(P(("groups", "dom"), "col", None), P(("groups", "dom"), "col")),
        check_vma=False,
    )
```

```python
import functools

import jax
import jax.numpy as jnp
from jax import lax
from jax.experimental import pallas as pl
from jax.experimental.pallas import tpu as pltpu
from jax.sharding import PartitionSpec as P

GX = 64
GY = 32
BF16 = jnp.bfloat16
F32 = jnp.float32
MIB = 1 << 20


def passed_along(value, axis, steps):
    count = lax.axis_size(axis)
    initial, last = (max(0, -steps), min(count, count - steps))
    return lax.ppermute(value, axis, [(source, source + steps) for source in range(initial, last)])


LIGHT = pl.CostEstimate(flops=1 << 20, bytes_accessed=1 << 16, transcendentals=0)


def couple_kernel(rate_ref, class_ref, pivot_ref, out_ref, weight_ref):
    nodes = pivot_ref.shape[1]

    @pl.when(pl.program_id(0) == 0)
    def _():
        kind = class_ref[...]
        across = jnp.where(
            kind == 0, 0.25, jnp.where(kind == 1, 0.375, jnp.where(kind == 2, 0.125, 0.5))
        ).astype(F32)
        along = jnp.where(
            kind == 0, 0.25, jnp.where(kind == 1, 0.125, jnp.where(kind == 2, 0.375, 0.0))
        ).astype(F32)
        node = lax.broadcasted_iota(jnp.int32, (1, nodes), 1)
        column = node % GX
        parts = (
            jnp.where(column > 0, across, 0.0),
            jnp.where(column < GX - 1, across, 0.0),
            jnp.where(node >= GX, along, 0.0),
            jnp.where(node < nodes - GX, along, 0.0),
        )
        for which, part in enumerate(parts):
            weight_ref[which] = jnp.broadcast_to(part, (16, nodes))

    rate = rate_ref[0]

    def group(step, carry):
        rows = pl.ds(pl.multiple_of(step * 16, 16), 16)
        value = pivot_ref[rows, :].astype(F32)
        total = (
            value
            + weight_ref[0] * pltpu.roll(value, 1, 1)
            + weight_ref[1] * pltpu.roll(value, nodes - 1, 1)
            + weight_ref[2] * pltpu.roll(value, GX, 1)
            + weight_ref[3] * pltpu.roll(value, nodes - GX, 1)
        )
        out_ref[rows, :] = (rate * total).astype(BF16)
        return carry

    lax.fori_loop(0, pivot_ref.shape[0] // 16, group, 0)


def couple(pivot, node_class, rate):
    rows, nodes = pivot.shape
    chunk = min(rows, 128)
    return pl.pallas_call(
        couple_kernel,
        out_shape=jax.ShapeDtypeStruct((rows, nodes), BF16),
        grid=(rows // chunk,),
        in_specs=[
            pl.BlockSpec(memory_space=pltpu.SMEM),
            pl.BlockSpec((1, nodes), lambda i: (0, 0)),
            pl.BlockSpec((chunk, nodes), lambda i: (i, 0)),
        ],
        out_specs=pl.BlockSpec((chunk, nodes), lambda i: (i, 0)),
        scratch_shapes=[pltpu.VMEM((4, 16, nodes), F32)],
        compiler_params=pltpu.CompilerParams(vmem_limit_bytes=8 * MIB),
        cost_estimate=LIGHT,
        name="couple",
    )(rate, node_class.reshape(1, nodes), pivot)


def turned(block, odd):
    return block + odd * (3 - 2 * block)


def route(source, target, doms):
    pairs = []
    for dom in range(doms):
        odd = dom % 2
        pairs.append((dom * 4 + turned(source, odd), dom * 4 + turned(target, odd)))
    return pairs


def moved(value, source, target):
    return lax.ppermute(value, ("dom", "col"), route(source, target, lax.axis_size("dom")))


def couple_here(place, pivot, node_class, rate):
    rows, nodes = pivot.shape
    chunk = 128

    def kernel(place_ref, *refs):
        @pl.when(place_ref[1] == 1)
        def _():
            couple_kernel(*refs)

    return pl.pallas_call(
        kernel,
        out_shape=jax.ShapeDtypeStruct((rows, nodes), BF16),
        grid_spec=pltpu.PrefetchScalarGridSpec(
            num_scalar_prefetch=1,
            grid=(rows // chunk,),
            in_specs=[
                pl.BlockSpec(memory_space=pltpu.SMEM),
                pl.BlockSpec((1, nodes), lambda i, place: (0, 0)),
                pl.BlockSpec((chunk, nodes), lambda i, place: (i, 0)),
            ],
            out_specs=pl.BlockSpec((chunk, nodes), lambda i, place: (i, 0)),
            scratch_shapes=[pltpu.VMEM((4, 16, nodes), F32)],
        ),
        compiler_params=pltpu.CompilerParams(vmem_limit_bytes=8 * MIB),
        cost_estimate=LIGHT,
        name="couple_here",
    )(place, rate, node_class.reshape(1, nodes), pivot)


def turn_kernel(place_ref, coupled_ref, *refs):
    @pl.when(place_ref[1] == 1)
    def _():
        refs[-1][...] = coupled_ref[...].T


def turn(place, panel, coupled, across):
    rows, nodes = coupled.shape
    chunk = 128
    ratio = rows // chunk
    return pl.pallas_call(
        turn_kernel,
        out_shape=jax.ShapeDtypeStruct((nodes, nodes), BF16),
        grid_spec=pltpu.PrefetchScalarGridSpec(
            num_scalar_prefetch=1,
            grid=(ratio,),
            in_specs=[pl.BlockSpec((chunk, nodes), lambda i, place: (i, 0))]
            + ([] if across is None else [pl.BlockSpec(memory_space=pl.ANY)]),
            out_specs=pl.BlockSpec(
                (nodes, chunk), lambda i, place: (0, turned(panel, place[0]) * ratio + i)
            ),
        ),
        input_output_aliases={} if across is None else {2: 0},
        compiler_params=pltpu.CompilerParams(vmem_limit_bytes=8 * MIB),
        cost_estimate=LIGHT,
        name="turn",
    )(place, coupled, *(() if across is None else (across,)))


def multiply_kernel(place_ref, left_ref, right_ref, out_ref):
    @pl.when(place_ref[1] == 1)
    def _():
        out_ref[...] = jnp.dot(
            left_ref[...], right_ref[...], preferred_element_type=F32
        ).astype(BF16)


def multiply(place, left, right, first=lambda odd: 0, count=4):
    rows, nodes = left.shape
    width = nodes // 4
    return pl.pallas_call(
        multiply_kernel,
        out_shape=jax.ShapeDtypeStruct((rows, count * width), BF16),
        grid_spec=pltpu.PrefetchScalarGridSpec(
            num_scalar_prefetch=1,
            grid=(count,),
            in_specs=[
                pl.BlockSpec((rows, nodes), lambda n, place: (0, 0)),
                pl.BlockSpec((nodes, width), lambda n, place: (0, first(place[0]) + n)),
            ],
            out_specs=pl.BlockSpec((rows, width), lambda n, place: (0, n)),
        ),
        compiler_params=pltpu.CompilerParams(vmem_limit_bytes=16 * MIB),
        cost_estimate=LIGHT,
        name="multiply",
    )(place, left, right)


def prior_kernel(step_ref, shifted_ref, sigma_ref, out_ref):
    @pl.when(step_ref[0] == 0)
    def _():
        out_ref[...] = shifted_ref[...]

    @pl.when(step_ref[0] != 0)
    def _():
        out_ref[...] = sigma_ref[...]


def near_kernel(place_ref, step_ref, shifted_ref, sigma_ref, near_ref, last_ref):
    width = last_ref.shape[1]
    prior_kernel(step_ref, shifted_ref, sigma_ref, near_ref)
    start = pl.multiple_of((1 - place_ref[0]) * width, 128)
    last_ref[...] = near_ref[:, pl.ds(start, width)]


def far_kernel(place_ref, step_ref, shifted_ref, sigma_ref, near_ref, other_ref, far_ref):
    width = near_ref.shape[1] // 2
    prior_kernel(step_ref, shifted_ref, sigma_ref, other_ref)
    start = pl.multiple_of(place_ref[0] * width, 128)
    far_ref[:, :width] = other_ref[:, pl.ds(start, width)]
    far_ref[:, width:] = near_ref[...]


def prior_half(kernel, side, sent, place, step, shifted, sigma, *more):
    rows, nodes = sigma.shape
    chunk = 128
    width = nodes // 4
    half = lambda column: pl.BlockSpec((chunk, 2 * width), column)
    return pl.pallas_call(
        kernel,
        out_shape=(
            jax.ShapeDtypeStruct((rows, 2 * width), BF16),
            jax.ShapeDtypeStruct((rows, sent * width), BF16),
        ),
        grid_spec=pltpu.PrefetchScalarGridSpec(
            num_scalar_prefetch=2,
            grid=(rows // chunk,),
            in_specs=[
                half(lambda i, place, step: (jnp.where(step[0] == 0, i, 0), 0)),
                half(lambda i, place, step: (jnp.where(step[0] == 0, 0, i), side(place[0]))),
            ]
            + [half(lambda i, place, step: (i, 0))] * len(more),
            out_specs=(
                half(lambda i, place, step: (i, 0)),
                pl.BlockSpec((chunk, sent * width), lambda i, place, step: (i, 0)),
            ),
        ),
        compiler_params=pltpu.CompilerParams(vmem_limit_bytes=12 * MIB),
        cost_estimate=LIGHT,
        name="prior_half",
    )(place, step, shifted, sigma, *more)


def assemble_kernel(place_ref, near_own, other_own, near_two, last_three, far_zero, out_ref):
    @pl.when(place_ref[1] == 1)
    def _():
        odd = place_ref[0]
        width = last_three.shape[1]

        def at(block):
            return pl.ds(pl.multiple_of(block * width, 128), width)

        near = 2 * (1 - odd)
        half = pl.ds(pl.multiple_of(near * width, 128), 2 * width)
        row = [turned(block, odd) for block in range(4)]
        other = pl.ds(pl.multiple_of(2 * odd * width, 128), 2 * width)
        out_ref[at(row[1]), half] = near_own[...]
        out_ref[at(row[1]), other] = other_own[...]
        out_ref[at(row[2]), half] = near_two[...]
        out_ref[at(row[0]), at(row[0])] = far_zero[:, :width]
        out_ref[at(row[0]), half] = far_zero[:, width:]
        out_ref[at(row[3]), at(row[3])] = last_three[...]
        for step in range(2):
            out_ref[at(near + step), at(row[1])] = near_own[:, step * width : (1 + step) * width].T
            out_ref[at(near + step), at(row[0])] = far_zero[:, (1 + step) * width : (2 + step) * width].T
        out_ref[at(row[0]), at(row[1])] = other_own[:, at(odd)].T
        out_ref[at(row[3]), at(row[2])] = near_two[:, at(1 - odd)].T


def assemble(place, *parts):
    nodes = 2 * parts[0].shape[1]
    vmem = pl.BlockSpec(memory_space=pltpu.VMEM)
    return pl.pallas_call(
        assemble_kernel,
        out_shape=jax.ShapeDtypeStruct((nodes, nodes), BF16),
        in_specs=[pl.BlockSpec(memory_space=pltpu.SMEM)] + [vmem] * 5,
        out_specs=vmem,
        compiler_params=pltpu.CompilerParams(vmem_limit_bytes=20 * MIB),
        cost_estimate=LIGHT,
        name="assemble",
    )(place, *parts)


def final_kernel(
    place_ref, active_ref, pivot_ref, q0, q0_last, q1, q2, q2_last, q3_near, q3_other, sigma_ref, out_ref, var_ref
):
    rows, nodes = pivot_ref.shape
    width = nodes // 4
    odd, place = place_ref[0], place_ref[1]
    here = pl.multiple_of(pl.program_id(0) * rows, 128)
    square = (rows, rows)
    on_diagonal = lax.broadcasted_iota(jnp.int32, square, 0) == lax.broadcasted_iota(
        jnp.int32, square, 1
    )

    def at(block, count=1):
        return pl.ds(pl.multiple_of(block * width, 128), count * width)

    def own(block):
        return pl.ds(pl.multiple_of(block * width + here, 128), rows)

    def diagonal(value):
        return jnp.sum(jnp.where(on_diagonal, value, 0.0), axis=0, keepdims=True)

    def add(columns, product):
        out_ref[:, columns] = (pivot_ref[:, columns].astype(F32) + product.astype(F32)).astype(BF16)

    def trace(product):
        var_ref[...] = diagonal(
            pivot_ref[:, own(place_ref[2])].astype(F32) + product.astype(F32)
        )

    active = active_ref[0] != 0

    @pl.when(active & (place == 0))
    def _():
        add(at(odd, 3), q0[...])
        add(at(3 - 3 * odd), q0_last[...])
        trace(q0[:, own(2 * odd)])

    @pl.when(active & (place == 1))
    def _():
        add(slice(None), q1[...])
        trace(q1[:, own(place_ref[2])])

    @pl.when(active & (place == 2))
    def _():
        add(at(odd, 3), q2[...])
        add(at(3 - 3 * odd), q2_last[...])
        trace(q2[:, own(2 - 2 * odd)])

    @pl.when(active & (place == 3))
    def _():
        add(at(2 - 2 * odd, 2), q3_near[...])
        add(at(2 * odd, 2), q3_other[...])
        trace(q3_near[:, own(1 - odd)])

    @pl.when(active_ref[0] == 0)
    def _():
        out_ref[...] = sigma_ref[...]
        var_ref[...] = diagonal(sigma_ref[:, own(place_ref[2])].astype(F32))


def final(place, active, pivot, products, sigma):
    rows, nodes = pivot.shape
    chunk = 128
    width = nodes // 4

    def picked(which, blocks):
        return pl.BlockSpec(
            (chunk, blocks * width), lambda i, place, active: (jnp.where(place[1] == which, i, 0), 0)
        )

    return pl.pallas_call(
        final_kernel,
        out_shape=(
            jax.ShapeDtypeStruct((rows, nodes), BF16),
            jax.ShapeDtypeStruct((1, rows), F32),
        ),
        grid_spec=pltpu.PrefetchScalarGridSpec(
            num_scalar_prefetch=2,
            grid=(rows // chunk,),
            in_specs=[
                pl.BlockSpec((chunk, nodes), lambda i, place, active: (i, 0)),
                picked(0, 3),
                picked(0, 1),
                picked(1, 4),
                picked(2, 3),
                picked(2, 1),
                picked(3, 2),
                picked(3, 2),
                pl.BlockSpec(
                    (chunk, nodes), lambda i, place, active: (jnp.where(active[0] == 0, i, 0), 0)
                ),
            ],
            out_specs=(
                pl.BlockSpec((chunk, nodes), lambda i, place, active: (i, 0)),
                pl.BlockSpec((1, chunk), lambda i, place, active: (0, i)),
            ),
        ),
        compiler_params=pltpu.CompilerParams(vmem_limit_bytes=16 * MIB),
        cost_estimate=LIGHT,
        name="final",
    )(place, active, pivot, *products, sigma)


def owned(sigma_next, separator, inverse_pivot, coupling_rate, lengths, step_index, node_class):
    sigma, pivot = sigma_next[0], inverse_pivot[0]
    odd = lax.axis_index("dom") % 2
    col = lax.axis_index("col")
    place = jnp.stack([odd, turned(col, odd), col]).astype(jnp.int32)
    active = (step_index < lengths).astype(jnp.int32)
    width = pivot.shape[1] // 4

    half = 2 * width

    p2 = moved(pivot, 2, 1)
    p0 = moved(pivot, 0, 1)
    near = lax.dynamic_slice_in_dim(separator[0], odd * half, half, 1)
    other = lax.dynamic_slice_in_dim(separator[0], (1 - odd) * half, half, 1)
    near = passed_along(near, "dom", -1)
    other = passed_along(other, "dom", -1)
    c1 = couple(pivot, node_class, coupling_rate)
    across = turn(place, 1, c1, None)

    near = lax.optimization_barrier((near, across))[0]
    near, last = prior_half(near_kernel, lambda odd: 1 - odd, 1, place, step_index, near, sigma)
    near_two, last_three = moved(near, 2, 1), moved(last, 3, 1)
    other, far = prior_half(far_kernel, lambda odd: odd, 3, place, step_index, other, sigma, near)
    far_zero = moved(far, 0, 1)
    c2 = couple_here(place, p2, node_class, coupling_rate)
    across = turn(place, 2, c2, across)
    c0 = couple_here(place, p0, node_class, coupling_rate)
    across = turn(place, 0, c0, across)
    c3 = lax.optimization_barrier((c1, last_three, near_two, far_zero, across))[0]
    c3 = moved(c3, 3, 1)
    prior = assemble(place, near, other, near_two, last_three, far_zero)
    h2 = multiply(place, c2, prior)
    most = lambda odd: odd
    rest = lambda odd: 3 - 3 * odd
    q2 = moved(multiply(place, h2, across, most, 3), 1, 2)
    h0 = multiply(place, c0, prior)
    q0 = moved(multiply(place, h0, across, most, 3), 1, 0)
    h1 = multiply(place, c1, prior)

    across = turn(place, 3, c3, across)
    h3 = multiply(place, c3, prior)
    q3_near = moved(multiply(place, h3, across, lambda odd: 2 - 2 * odd, 2), 1, 3)
    q3_other = moved(multiply(place, h3, across, lambda odd: 2 * odd, 2), 1, 3)
    q2_last = moved(multiply(place, h2, across, rest, 1), 1, 2)
    q0_last = moved(multiply(place, h0, across, rest, 1), 1, 0)
    q1 = multiply(place, h1, across)
    products = (q0, q0_last, q1, q2, q2_last, q3_near, q3_other)
    covariance, variances = final(place, active, pivot, products, sigma)
    return (covariance[None], variances)


def gathered(sigma_next, separator, inverse_pivot, coupling_rate, lengths, step_index, node_class):
    shifted = passed_along(separator, "dom", -1)
    prior = jnp.where(step_index[0] == 0, shifted[0], sigma_next[0])
    pivot = inverse_pivot[0].astype(F32)
    coupled = couple(inverse_pivot[0], node_class, coupling_rate)
    rows = coupled.shape[0]
    half = jnp.dot(
        coupled,
        lax.all_gather(prior, "col", axis=0, tiled=True),
        preferred_element_type=F32,
    ).astype(BF16)
    product = lax.dot_general(
        half,
        lax.all_gather(coupled, "col", axis=0, tiled=True),
        (((1,), (1,)), ((), ())),
        preferred_element_type=F32,
    )
    full = pivot + product
    active = step_index[0] < lengths[0]
    old = sigma_next[0]
    covariance = jnp.where(active, full.astype(BF16), old)
    first_col = lax.axis_index("col") * rows
    new_block = lax.dynamic_slice_in_dim(full, first_col, rows, 1)
    old_block = lax.dynamic_slice_in_dim(old, first_col, rows, 1)
    variances = jnp.where(active, jnp.diagonal(new_block), jnp.diagonal(old_block).astype(F32))
    return (covariance[None], variances[None])


def solution(mesh):
    local = owned if mesh.shape["col"] == 4 and mesh.shape["dom"] % 2 == 0 else gathered
    return jax.shard_map(
        local,
        mesh=mesh,
        in_specs=(
            P(("groups", "dom"), "col", None),
            P(("groups", "dom"), "col", None),
            P(("groups", "dom"), "col", None),
            P(("groups", "dom")),
            P(("groups", "dom")),
            P(("groups", "dom")),
            P("groups"),
        ),
        out_specs=(P(("groups", "dom"), "col", None), P(("groups", "dom"), "col")),
        check_vma=False,
    )
```

```python
import functools

import jax
import jax.numpy as jnp
from jax import lax
from jax.experimental import pallas as pl
from jax.experimental.pallas import tpu as pltpu
from jax.sharding import PartitionSpec as P

GX = 64
GY = 32
BF16 = jnp.bfloat16
F32 = jnp.float32
MIB = 1 << 20


def passed_along(value, axis, steps):
    count = lax.axis_size(axis)
    initial, last = (max(0, -steps), min(count, count - steps))
    return lax.ppermute(value, axis, [(source, source + steps) for source in range(initial, last)])


LIGHT = pl.CostEstimate(flops=1 << 20, bytes_accessed=1 << 16, transcendentals=0)


def couple_kernel(rate_ref, class_ref, pivot_ref, out_ref, weight_ref):
    nodes = pivot_ref.shape[1]

    @pl.when(pl.program_id(0) == 0)
    def _():
        kind = class_ref[...]
        across = jnp.where(
            kind == 0, 0.25, jnp.where(kind == 1, 0.375, jnp.where(kind == 2, 0.125, 0.5))
        ).astype(F32)
        along = jnp.where(
            kind == 0, 0.25, jnp.where(kind == 1, 0.125, jnp.where(kind == 2, 0.375, 0.0))
        ).astype(F32)
        node = lax.broadcasted_iota(jnp.int32, (1, nodes), 1)
        column = node % GX
        parts = (
            jnp.where(column > 0, across, 0.0),
            jnp.where(column < GX - 1, across, 0.0),
            jnp.where(node >= GX, along, 0.0),
            jnp.where(node < nodes - GX, along, 0.0),
        )
        for which, part in enumerate(parts):
            weight_ref[which] = jnp.broadcast_to(part, (16, nodes))

    rate = rate_ref[0]

    def group(step, carry):
        rows = pl.ds(pl.multiple_of(step * 16, 16), 16)
        value = pivot_ref[rows, :].astype(F32)
        total = (
            value
            + weight_ref[0] * pltpu.roll(value, 1, 1)
            + weight_ref[1] * pltpu.roll(value, nodes - 1, 1)
            + weight_ref[2] * pltpu.roll(value, GX, 1)
            + weight_ref[3] * pltpu.roll(value, nodes - GX, 1)
        )
        out_ref[rows, :] = (rate * total).astype(BF16)
        return carry

    lax.fori_loop(0, pivot_ref.shape[0] // 16, group, 0)


def couple(pivot, node_class, rate):
    rows, nodes = pivot.shape
    chunk = min(rows, 128)
    return pl.pallas_call(
        couple_kernel,
        out_shape=jax.ShapeDtypeStruct((rows, nodes), BF16),
        grid=(rows // chunk,),
        in_specs=[
            pl.BlockSpec(memory_space=pltpu.SMEM),
            pl.BlockSpec((1, nodes), lambda i: (0, 0)),
            pl.BlockSpec((chunk, nodes), lambda i: (i, 0)),
        ],
        out_specs=pl.BlockSpec((chunk, nodes), lambda i: (i, 0)),
        scratch_shapes=[pltpu.VMEM((4, 16, nodes), F32)],
        compiler_params=pltpu.CompilerParams(vmem_limit_bytes=8 * MIB),
        cost_estimate=LIGHT,
        name="couple",
    )(rate, node_class.reshape(1, nodes), pivot)


def turned(block, odd):
    return block + odd * (3 - 2 * block)


def route(source, target, doms):
    pairs = []
    for dom in range(doms):
        odd = dom % 2
        pairs.append((dom * 4 + turned(source, odd), dom * 4 + turned(target, odd)))
    return pairs


def moved(value, source, target):
    return lax.ppermute(value, ("dom", "col"), route(source, target, lax.axis_size("dom")))


def couple_here(place, pivot, node_class, rate):
    rows, nodes = pivot.shape
    chunk = 128

    def kernel(place_ref, *refs):
        @pl.when(place_ref[1] == 1)
        def _():
            couple_kernel(*refs)

    return pl.pallas_call(
        kernel,
        out_shape=jax.ShapeDtypeStruct((rows, nodes), BF16),
        grid_spec=pltpu.PrefetchScalarGridSpec(
            num_scalar_prefetch=1,
            grid=(rows // chunk,),
            in_specs=[
                pl.BlockSpec(memory_space=pltpu.SMEM),
                pl.BlockSpec((1, nodes), lambda i, place: (0, 0)),
                pl.BlockSpec((chunk, nodes), lambda i, place: (i, 0)),
            ],
            out_specs=pl.BlockSpec((chunk, nodes), lambda i, place: (i, 0)),
            scratch_shapes=[pltpu.VMEM((4, 16, nodes), F32)],
        ),
        compiler_params=pltpu.CompilerParams(vmem_limit_bytes=8 * MIB),
        cost_estimate=LIGHT,
        name="couple_here",
    )(place, rate, node_class.reshape(1, nodes), pivot)


def turn_kernel(place_ref, coupled_ref, *refs):
    @pl.when(place_ref[1] == 1)
    def _():
        refs[-1][...] = coupled_ref[...].T


def turn(place, panel, coupled, across):
    rows, nodes = coupled.shape
    chunk = 128
    ratio = rows // chunk
    return pl.pallas_call(
        turn_kernel,
        out_shape=jax.ShapeDtypeStruct((nodes, nodes), BF16),
        grid_spec=pltpu.PrefetchScalarGridSpec(
            num_scalar_prefetch=1,
            grid=(ratio,),
            in_specs=[pl.BlockSpec((chunk, nodes), lambda i, place: (i, 0))]
            + ([] if across is None else [pl.BlockSpec(memory_space=pl.ANY)]),
            out_specs=pl.BlockSpec(
                (nodes, chunk), lambda i, place: (0, turned(panel, place[0]) * ratio + i)
            ),
        ),
        input_output_aliases={} if across is None else {2: 0},
        compiler_params=pltpu.CompilerParams(vmem_limit_bytes=8 * MIB),
        cost_estimate=LIGHT,
        name="turn",
    )(place, coupled, *(() if across is None else (across,)))


def multiply_kernel(place_ref, left_ref, right_ref, out_ref):
    @pl.when(place_ref[1] == 1)
    def _():
        out_ref[...] = jnp.dot(
            left_ref[...], right_ref[...], preferred_element_type=F32
        ).astype(BF16)


def multiply(place, left, right, first=lambda odd: 0, count=4):
    rows, nodes = left.shape
    width = nodes // 4
    return pl.pallas_call(
        multiply_kernel,
        out_shape=jax.ShapeDtypeStruct((rows, count * width), BF16),
        grid_spec=pltpu.PrefetchScalarGridSpec(
            num_scalar_prefetch=1,
            grid=(count,),
            in_specs=[
                pl.BlockSpec((rows, nodes), lambda n, place: (0, 0)),
                pl.BlockSpec((nodes, width), lambda n, place: (0, first(place[0]) + n)),
            ],
            out_specs=pl.BlockSpec((rows, width), lambda n, place: (0, n)),
        ),
        compiler_params=pltpu.CompilerParams(vmem_limit_bytes=16 * MIB),
        cost_estimate=LIGHT,
        name="multiply",
    )(place, left, right)


def prior_kernel(step_ref, shifted_ref, sigma_ref, out_ref):
    @pl.when(step_ref[0] == 0)
    def _():
        out_ref[...] = shifted_ref[...]

    @pl.when(step_ref[0] != 0)
    def _():
        out_ref[...] = sigma_ref[...]


def parts_kernel(place_ref, step_ref, shifted_ref, sigma_ref, row_ref, far_ref, near_ref, last_ref):
    odd = place_ref[0]
    width = last_ref.shape[1]

    def at(block, count=1):
        return pl.ds(pl.multiple_of(block * width, 128), count * width)

    prior_kernel(step_ref, shifted_ref, sigma_ref, row_ref)
    near = row_ref[:, at(2 - 2 * odd, 2)]
    near_ref[...] = near
    far_ref[:, width:] = near
    far_ref[:, :width] = row_ref[:, at(3 * odd)]
    last_ref[...] = row_ref[:, at(3 - 3 * odd)]


def prior_parts(place, step, shifted, sigma):
    rows, nodes = sigma.shape
    chunk = 128
    width = nodes // 4
    out = lambda blocks: jax.ShapeDtypeStruct((rows, blocks * width), BF16)
    spec = lambda blocks: pl.BlockSpec((chunk, blocks * width), lambda i, place, step: (i, 0))
    return pl.pallas_call(
        parts_kernel,
        out_shape=(out(4), out(3), out(2), out(1)),
        grid_spec=pltpu.PrefetchScalarGridSpec(
            num_scalar_prefetch=2,
            grid=(rows // chunk,),
            in_specs=[
                pl.BlockSpec(
                    (chunk, nodes), lambda i, place, step: (jnp.where(step[0] == 0, i, 0), 0)
                ),
                pl.BlockSpec(
                    (chunk, nodes), lambda i, place, step: (jnp.where(step[0] == 0, 0, i), 0)
                ),
            ],
            out_specs=(spec(4), spec(3), spec(2), spec(1)),
        ),
        compiler_params=pltpu.CompilerParams(vmem_limit_bytes=12 * MIB),
        cost_estimate=LIGHT,
        name="prior_parts",
    )(place, step, shifted, sigma)


def assemble_kernel(place_ref, own, near_two, last_three, far_zero, out_ref):
    @pl.when(place_ref[1] == 1)
    def _():
        odd = place_ref[0]
        width = last_three.shape[1]

        def at(block):
            return pl.ds(pl.multiple_of(block * width, 128), width)

        near = 2 * (1 - odd)
        half = pl.ds(pl.multiple_of(near * width, 128), 2 * width)
        row = [turned(block, odd) for block in range(4)]
        out_ref[at(row[1]), :] = own[...]
        out_ref[at(row[2]), half] = near_two[...]
        out_ref[at(row[0]), at(row[0])] = far_zero[:, :width]
        out_ref[at(row[0]), half] = far_zero[:, width:]
        out_ref[at(row[3]), at(row[3])] = last_three[...]
        for step in range(2):
            out_ref[at(near + step), at(row[1])] = own[:, at(near + step)].T
            piece = slice((1 + step) * width, (2 + step) * width)
            out_ref[at(near + step), at(row[0])] = far_zero[:, piece].T
        out_ref[at(row[0]), at(row[1])] = own[:, at(row[0])].T
        out_ref[at(row[3]), at(row[2])] = near_two[:, at(1 - odd)].T


def assemble(place, *parts):
    nodes = parts[0].shape[1]
    vmem = pl.BlockSpec(memory_space=pltpu.VMEM)
    return pl.pallas_call(
        assemble_kernel,
        out_shape=jax.ShapeDtypeStruct((nodes, nodes), BF16),
        in_specs=[pl.BlockSpec(memory_space=pltpu.SMEM)] + [vmem] * 4,
        out_specs=vmem,
        compiler_params=pltpu.CompilerParams(vmem_limit_bytes=20 * MIB),
        cost_estimate=LIGHT,
        name="assemble",
    )(place, *parts)


def final_kernel(
    place_ref, active_ref, pivot_ref, q0, q0_last, q1, q2, q2_last, q3_near, q3_other, sigma_ref, out_ref, var_ref
):
    rows, nodes = pivot_ref.shape
    width = nodes // 4
    odd, place = place_ref[0], place_ref[1]
    here = pl.multiple_of(pl.program_id(0) * rows, 128)
    square = (rows, rows)
    on_diagonal = lax.broadcasted_iota(jnp.int32, square, 0) == lax.broadcasted_iota(
        jnp.int32, square, 1
    )

    def at(block, count=1):
        return pl.ds(pl.multiple_of(block * width, 128), count * width)

    def own(block):
        return pl.ds(pl.multiple_of(block * width + here, 128), rows)

    def diagonal(value):
        return jnp.sum(jnp.where(on_diagonal, value, 0.0), axis=0, keepdims=True)

    def add(columns, product):
        out_ref[:, columns] = (pivot_ref[:, columns].astype(F32) + product.astype(F32)).astype(BF16)

    def trace(product):
        var_ref[...] = diagonal(
            pivot_ref[:, own(place_ref[2])].astype(F32) + product.astype(F32)
        )

    active = active_ref[0] != 0

    @pl.when(active & (place == 0))
    def _():
        add(at(odd, 3), q0[...])
        add(at(3 - 3 * odd), q0_last[...])
        trace(q0[:, own(2 * odd)])

    @pl.when(active & (place == 1))
    def _():
        add(slice(None), q1[...])
        trace(q1[:, own(place_ref[2])])

    @pl.when(active & (place == 2))
    def _():
        add(at(odd, 3), q2[...])
        add(at(3 - 3 * odd), q2_last[:, pl.ds(here, rows)].T)
        trace(q2[:, own(2 - 2 * odd)])

    @pl.when(active & (place == 3))
    def _():
        add(at(2 - 2 * odd, 2), q3_near[...])
        add(at(2 * odd, 2), q3_other[...])
        trace(q3_near[:, own(1 - odd)])

    @pl.when(active_ref[0] == 0)
    def _():
        out_ref[...] = sigma_ref[...]
        var_ref[...] = diagonal(sigma_ref[:, own(place_ref[2])].astype(F32))


def final(place, active, pivot, products, sigma):
    rows, nodes = pivot.shape
    chunk = 128
    width = nodes // 4

    def picked(which, blocks):
        return pl.BlockSpec(
            (chunk, blocks * width), lambda i, place, active: (jnp.where(place[1] == which, i, 0), 0)
        )

    return pl.pallas_call(
        final_kernel,
        out_shape=(
            jax.ShapeDtypeStruct((rows, nodes), BF16),
            jax.ShapeDtypeStruct((1, rows), F32),
        ),
        grid_spec=pltpu.PrefetchScalarGridSpec(
            num_scalar_prefetch=2,
            grid=(rows // chunk,),
            in_specs=[
                pl.BlockSpec((chunk, nodes), lambda i, place, active: (i, 0)),
                picked(0, 3),
                picked(0, 1),
                picked(1, 4),
                picked(2, 3),
                pl.BlockSpec((rows, width), lambda i, place, active: (0, 0)),
                picked(3, 2),
                picked(3, 2),
                pl.BlockSpec(
                    (chunk, nodes), lambda i, place, active: (jnp.where(active[0] == 0, i, 0), 0)
                ),
            ],
            out_specs=(
                pl.BlockSpec((chunk, nodes), lambda i, place, active: (i, 0)),
                pl.BlockSpec((1, chunk), lambda i, place, active: (0, i)),
            ),
        ),
        compiler_params=pltpu.CompilerParams(vmem_limit_bytes=16 * MIB),
        cost_estimate=LIGHT,
        name="final",
    )(place, active, pivot, *products, sigma)


def owned(sigma_next, separator, inverse_pivot, coupling_rate, lengths, step_index, node_class):
    sigma, pivot = sigma_next[0], inverse_pivot[0]
    odd = lax.axis_index("dom") % 2
    col = lax.axis_index("col")
    place = jnp.stack([odd, turned(col, odd), col]).astype(jnp.int32)
    active = (step_index < lengths).astype(jnp.int32)
    width = pivot.shape[1] // 4


    shifted = passed_along(separator, "dom", -1)[0]
    p2 = moved(pivot, 2, 1)
    p0 = moved(pivot, 0, 1)
    c1 = couple(pivot, node_class, coupling_rate)
    across = turn(place, 1, c1, None)

    shifted = lax.optimization_barrier((shifted, p2, p0, across))[0]
    row, far, near, last = prior_parts(place, step_index, shifted, sigma)
    far_zero, near_two, last_three = moved(far, 0, 1), moved(near, 2, 1), moved(last, 3, 1)

    p2 = lax.optimization_barrier((p2, last))[0]
    c2 = couple_here(place, p2, node_class, coupling_rate)
    across = turn(place, 2, c2, across)
    c0 = couple_here(place, p0, node_class, coupling_rate)
    across = turn(place, 0, c0, across)
    c3 = lax.optimization_barrier((c1, last_three, near_two, far_zero, across))[0]
    c3 = moved(c3, 3, 1)
    prior = assemble(place, row, near_two, last_three, far_zero)
    most = lambda odd: odd
    rest = lambda odd: 3 - 3 * odd
    h2 = multiply(place, c2, prior)
    q2 = multiply(place, h2, across, most, 3)
    h0 = multiply(place, lax.optimization_barrier((c0, q2))[0], prior)
    q2 = moved(q2, 1, 2)
    q0 = moved(multiply(place, h0, across, most, 3), 1, 0)

    across = turn(place, 3, c3, across)
    h3 = multiply(place, c3, prior)
    q3_near = moved(multiply(place, h3, across, lambda odd: 2 - 2 * odd, 2), 1, 3)
    q3_other = multiply(place, h3, across, lambda odd: 2 * odd, 2)
    q0_last = multiply(place, h0, across, rest, 1)
    h1 = multiply(place, lax.optimization_barrier((c1, q2, q3_other, q0_last))[0], prior)
    q3_other, q0_last = moved(q3_other, 1, 3), moved(q0_last, 1, 0)
    q1 = multiply(place, h1, across)
    q2_last = lax.optimization_barrier((q3_near, q0, q1))[0]
    q2_last = moved(lax.dynamic_slice_in_dim(q2_last, odd * width, width, 1), 3, 2)
    products = (q0, q0_last, q1, q2, q2_last, q3_near, q3_other)
    covariance, variances = final(place, active, pivot, products, sigma)
    return (covariance[None], variances)


def gathered(sigma_next, separator, inverse_pivot, coupling_rate, lengths, step_index, node_class):
    shifted = passed_along(separator, "dom", -1)
    prior = jnp.where(step_index[0] == 0, shifted[0], sigma_next[0])
    pivot = inverse_pivot[0].astype(F32)
    coupled = couple(inverse_pivot[0], node_class, coupling_rate)
    rows = coupled.shape[0]
    half = jnp.dot(
        coupled,
        lax.all_gather(prior, "col", axis=0, tiled=True),
        preferred_element_type=F32,
    ).astype(BF16)
    product = lax.dot_general(
        half,
        lax.all_gather(coupled, "col", axis=0, tiled=True),
        (((1,), (1,)), ((), ())),
        preferred_element_type=F32,
    )
    full = pivot + product
    active = step_index[0] < lengths[0]
    old = sigma_next[0]
    covariance = jnp.where(active, full.astype(BF16), old)
    first_col = lax.axis_index("col") * rows
    new_block = lax.dynamic_slice_in_dim(full, first_col, rows, 1)
    old_block = lax.dynamic_slice_in_dim(old, first_col, rows, 1)
    variances = jnp.where(active, jnp.diagonal(new_block), jnp.diagonal(old_block).astype(F32))
    return (covariance[None], variances[None])


def solution(mesh):
    local = owned if mesh.shape["col"] == 4 and mesh.shape["dom"] % 2 == 0 else gathered
    return jax.shard_map(
        local,
        mesh=mesh,
        in_specs=(
            P(("groups", "dom"), "col", None),
            P(("groups", "dom"), "col", None),
            P(("groups", "dom"), "col", None),
            P(("groups", "dom")),
            P(("groups", "dom")),
            P(("groups", "dom")),
            P("groups"),
        ),
        out_specs=(P(("groups", "dom"), "col", None), P(("groups", "dom"), "col")),
        check_vma=False,
    )
```

```python
import functools

import jax
import jax.numpy as jnp
from jax import lax
from jax.experimental import pallas as pl
from jax.experimental.pallas import tpu as pltpu
from jax.sharding import PartitionSpec as P

GX = 64
GY = 32
BF16 = jnp.bfloat16
F32 = jnp.float32
MIB = 1 << 20


def passed_along(value, axis, steps):
    count = lax.axis_size(axis)
    initial, last = (max(0, -steps), min(count, count - steps))
    return lax.ppermute(value, axis, [(source, source + steps) for source in range(initial, last)])


LIGHT = pl.CostEstimate(flops=1 << 20, bytes_accessed=1 << 16, transcendentals=0)


def couple_kernel(rate_ref, class_ref, pivot_ref, out_ref, weight_ref):
    nodes = pivot_ref.shape[1]

    @pl.when(pl.program_id(0) == 0)
    def _():
        kind = class_ref[...]
        across = jnp.where(
            kind == 0, 0.25, jnp.where(kind == 1, 0.375, jnp.where(kind == 2, 0.125, 0.5))
        ).astype(F32)
        along = jnp.where(
            kind == 0, 0.25, jnp.where(kind == 1, 0.125, jnp.where(kind == 2, 0.375, 0.0))
        ).astype(F32)
        node = lax.broadcasted_iota(jnp.int32, (1, nodes), 1)
        column = node % GX
        parts = (
            jnp.where(column > 0, across, 0.0),
            jnp.where(column < GX - 1, across, 0.0),
            jnp.where(node >= GX, along, 0.0),
            jnp.where(node < nodes - GX, along, 0.0),
        )
        for which, part in enumerate(parts):
            weight_ref[which] = jnp.broadcast_to(part, (16, nodes))

    rate = rate_ref[0]

    def group(step, carry):
        rows = pl.ds(pl.multiple_of(step * 16, 16), 16)
        value = pivot_ref[rows, :].astype(F32)
        total = (
            value
            + weight_ref[0] * pltpu.roll(value, 1, 1)
            + weight_ref[1] * pltpu.roll(value, nodes - 1, 1)
            + weight_ref[2] * pltpu.roll(value, GX, 1)
            + weight_ref[3] * pltpu.roll(value, nodes - GX, 1)
        )
        out_ref[rows, :] = (rate * total).astype(BF16)
        return carry

    lax.fori_loop(0, pivot_ref.shape[0] // 16, group, 0)


def couple(pivot, node_class, rate):
    rows, nodes = pivot.shape
    chunk = min(rows, 128)
    return pl.pallas_call(
        couple_kernel,
        out_shape=jax.ShapeDtypeStruct((rows, nodes), BF16),
        grid=(rows // chunk,),
        in_specs=[
            pl.BlockSpec(memory_space=pltpu.SMEM),
            pl.BlockSpec((1, nodes), lambda i: (0, 0)),
            pl.BlockSpec((chunk, nodes), lambda i: (i, 0)),
        ],
        out_specs=pl.BlockSpec((chunk, nodes), lambda i: (i, 0)),
        scratch_shapes=[pltpu.VMEM((4, 16, nodes), F32)],
        compiler_params=pltpu.CompilerParams(vmem_limit_bytes=6 * MIB),
        cost_estimate=LIGHT,
        name="couple",
    )(rate, node_class.reshape(1, nodes), pivot)


def turned(block, odd):
    return block + odd * (3 - 2 * block)


def route(source, target, doms):
    pairs = []
    for dom in range(doms):
        odd = dom % 2
        pairs.append((dom * 4 + turned(source, odd), dom * 4 + turned(target, odd)))
    return pairs


def moved(value, source, target):
    return lax.ppermute(value, ("dom", "col"), route(source, target, lax.axis_size("dom")))


def couple_here(place, pivot, node_class, rate):
    rows, nodes = pivot.shape
    chunk = 128

    def kernel(place_ref, *refs):
        @pl.when(place_ref[1] == 1)
        def _():
            couple_kernel(*refs)

    return pl.pallas_call(
        kernel,
        out_shape=jax.ShapeDtypeStruct((rows, nodes), BF16),
        grid_spec=pltpu.PrefetchScalarGridSpec(
            num_scalar_prefetch=1,
            grid=(rows // chunk,),
            in_specs=[
                pl.BlockSpec(memory_space=pltpu.SMEM),
                pl.BlockSpec((1, nodes), lambda i, place: (0, 0)),
                pl.BlockSpec((chunk, nodes), lambda i, place: (i, 0)),
            ],
            out_specs=pl.BlockSpec((chunk, nodes), lambda i, place: (i, 0)),
            scratch_shapes=[pltpu.VMEM((4, 16, nodes), F32)],
        ),
        compiler_params=pltpu.CompilerParams(vmem_limit_bytes=8 * MIB),
        cost_estimate=LIGHT,
        name="couple_here",
    )(place, rate, node_class.reshape(1, nodes), pivot)


def turn_kernel(place_ref, coupled_ref, *refs):
    @pl.when(place_ref[1] == 1)
    def _():
        refs[-1][...] = coupled_ref[...].T


def turn(place, panel, part, coupled, across):
    rows, nodes = coupled.shape
    chunk = 128
    steps = rows // chunk
    ratio = nodes // 4 // chunk
    return pl.pallas_call(
        turn_kernel,
        out_shape=jax.ShapeDtypeStruct((nodes, nodes), BF16),
        grid_spec=pltpu.PrefetchScalarGridSpec(
            num_scalar_prefetch=1,
            grid=(steps,),
            in_specs=[pl.BlockSpec((chunk, nodes), lambda i, place: (i, 0))]
            + ([] if across is None else [pl.BlockSpec(memory_space=pl.ANY)]),
            out_specs=pl.BlockSpec(
                (nodes, chunk),
                lambda i, place: (0, turned(panel, place[0]) * ratio + part * steps + i),
            ),
        ),
        input_output_aliases={} if across is None else {2: 0},
        compiler_params=pltpu.CompilerParams(vmem_limit_bytes=4 * MIB),
        cost_estimate=LIGHT,
        name="turn",
    )(place, coupled, *(() if across is None else (across,)))


def multiply_kernel(first, count, lefts, place_ref, *refs):
    left_refs, right_ref, out_ref = refs[:lefts], refs[lefts], refs[-1]
    width = right_ref.shape[0] // 4

    @pl.when(place_ref[1] == 1)
    def _():
        def block(step, carry):
            source = pl.multiple_of((first(place_ref[0]) + step) * width, 128)
            target = pl.multiple_of(step * width, 128)
            row = 0
            for left_ref in left_refs:
                rows = left_ref.shape[0]
                out_ref[row : row + rows, pl.ds(target, width)] = jnp.dot(
                    left_ref[...], right_ref[:, pl.ds(source, width)], preferred_element_type=F32
                ).astype(BF16)
                row += rows
            return carry

        lax.fori_loop(0, count, block, 0)


def multiply(place, lefts, right, first=lambda odd: 0, count=4):
    rows = sum(left.shape[0] for left in lefts)
    width = right.shape[0] // 4
    vmem = pl.BlockSpec(memory_space=pltpu.VMEM)
    return pl.pallas_call(
        functools.partial(multiply_kernel, first, count, len(lefts)),
        out_shape=jax.ShapeDtypeStruct((rows, count * width), BF16),
        in_specs=[pl.BlockSpec(memory_space=pltpu.SMEM)] + [vmem] * (len(lefts) + 1),
        out_specs=vmem,
        compiler_params=pltpu.CompilerParams(vmem_limit_bytes=6 * MIB),
        cost_estimate=LIGHT,
        name="multiply",
    )(place, *lefts, right)


def zero_kernel(place_ref, left_ref, right_ref, two_ref, out_ref):
    odd = place_ref[0]
    width = right_ref.shape[0] // 4
    multiply_kernel(lambda odd: 2 * odd, 2, 1, place_ref, left_ref, right_ref, out_ref)

    @pl.when(place_ref[1] == 1)
    def _():
        out_ref[:, 2 * width :] = two_ref[:, pl.ds(pl.multiple_of(2 * odd * width, 128), width)]


def product_zero(place, half, across, two):
    rows = half.shape[0]
    width = across.shape[0] // 4
    vmem = pl.BlockSpec(memory_space=pltpu.VMEM)
    return pl.pallas_call(
        zero_kernel,
        out_shape=jax.ShapeDtypeStruct((rows, 3 * width), BF16),
        in_specs=[pl.BlockSpec(memory_space=pltpu.SMEM)] + [vmem] * 3,
        out_specs=vmem,
        compiler_params=pltpu.CompilerParams(vmem_limit_bytes=6 * MIB),
        cost_estimate=LIGHT,
        name="product_zero",
    )(place, half, across, two)


def prior_kernel(step_ref, shifted_ref, sigma_ref, out_ref):
    @pl.when(step_ref[0] == 0)
    def _():
        out_ref[...] = shifted_ref[...]

    @pl.when(step_ref[0] != 0)
    def _():
        out_ref[...] = sigma_ref[...]


def parts_kernel(place_ref, step_ref, shifted_ref, sigma_ref, row_ref, far_ref, near_ref, last_ref):
    odd = place_ref[0]
    width = last_ref.shape[1]

    def at(block, count=1):
        return pl.ds(pl.multiple_of(block * width, 128), count * width)

    prior_kernel(step_ref, shifted_ref, sigma_ref, row_ref)
    near = row_ref[:, at(2 - 2 * odd, 2)]
    near_ref[...] = near
    far_ref[:, width:] = near
    far_ref[:, :width] = row_ref[:, at(3 * odd)]
    last_ref[...] = row_ref[:, at(3 - 3 * odd)]


def prior_parts(place, step, shifted, sigma):
    rows, nodes = sigma.shape
    chunk = 128
    width = nodes // 4
    out = lambda blocks: jax.ShapeDtypeStruct((rows, blocks * width), BF16)
    spec = lambda blocks: pl.BlockSpec((chunk, blocks * width), lambda i, place, step: (i, 0))
    return pl.pallas_call(
        parts_kernel,
        out_shape=(out(4), out(3), out(2), out(1)),
        grid_spec=pltpu.PrefetchScalarGridSpec(
            num_scalar_prefetch=2,
            grid=(rows // chunk,),
            in_specs=[
                pl.BlockSpec(
                    (chunk, nodes), lambda i, place, step: (jnp.where(step[0] == 0, i, 0), 0)
                ),
                pl.BlockSpec(
                    (chunk, nodes), lambda i, place, step: (jnp.where(step[0] == 0, 0, i), 0)
                ),
            ],
            out_specs=(spec(4), spec(3), spec(2), spec(1)),
        ),
        compiler_params=pltpu.CompilerParams(vmem_limit_bytes=8 * MIB),
        cost_estimate=LIGHT,
        name="prior_parts",
    )(place, step, shifted, sigma)


def assemble_kernel(place_ref, own, near_two, last_three, far_zero, out_ref):
    @pl.when(place_ref[1] == 1)
    def _():
        odd = place_ref[0]
        width = last_three.shape[1]

        def at(block):
            return pl.ds(pl.multiple_of(block * width, 128), width)

        near = 2 * (1 - odd)
        half = pl.ds(pl.multiple_of(near * width, 128), 2 * width)
        row = [turned(block, odd) for block in range(4)]
        out_ref[at(row[1]), :] = own[...]
        out_ref[at(row[2]), half] = near_two[...]
        out_ref[at(row[0]), at(row[0])] = far_zero[:, :width]
        out_ref[at(row[0]), half] = far_zero[:, width:]
        out_ref[at(row[3]), at(row[3])] = last_three[...]
        for step in range(2):
            out_ref[at(near + step), at(row[1])] = own[:, at(near + step)].T
            piece = slice((1 + step) * width, (2 + step) * width)
            out_ref[at(near + step), at(row[0])] = far_zero[:, piece].T
        out_ref[at(row[0]), at(row[1])] = own[:, at(row[0])].T
        out_ref[at(row[3]), at(row[2])] = near_two[:, at(1 - odd)].T


def assemble(place, *parts):
    nodes = parts[0].shape[1]
    vmem = pl.BlockSpec(memory_space=pltpu.VMEM)
    return pl.pallas_call(
        assemble_kernel,
        out_shape=jax.ShapeDtypeStruct((nodes, nodes), BF16),
        in_specs=[pl.BlockSpec(memory_space=pltpu.SMEM)] + [vmem] * 4,
        out_specs=vmem,
        compiler_params=pltpu.CompilerParams(vmem_limit_bytes=6 * MIB),
        cost_estimate=LIGHT,
        name="assemble",
    )(place, *parts)


def final_kernel(
    place_ref, active_ref, pivot_ref, sigma_ref,
    q0, q0_two, q0_last, q2, q2_last, q3_near, q3_other,
    q01, q11, q21, q31,
    out_ref, var_ref,
):
    rows, nodes = pivot_ref.shape
    width = nodes // 4
    odd, place = place_ref[0], place_ref[1]
    here = pl.multiple_of(pl.program_id(0) * rows, 128)
    square = (rows, rows)
    on_diagonal = lax.broadcasted_iota(jnp.int32, square, 0) == lax.broadcasted_iota(
        jnp.int32, square, 1
    )

    def at(block, count=1):
        return pl.ds(pl.multiple_of(block * width, 128), count * width)

    def own(block):
        return pl.ds(pl.multiple_of(block * width + here, 128), rows)

    def diagonal(value):
        return jnp.sum(jnp.where(on_diagonal, value, 0.0), axis=0, keepdims=True)

    def add(columns, product):
        out_ref[:, columns] = (pivot_ref[:, columns].astype(F32) + product.astype(F32)).astype(BF16)

    def trace(product):
        var_ref[...] = diagonal(
            pivot_ref[:, own(place_ref[2])].astype(F32) + product.astype(F32)
        )

    active = active_ref[0] != 0

    @pl.when(active & (place == 0))
    def _():
        add(at(2 * odd, 2), q0[...])
        add(at(turned(3, odd)), q0_last[:, pl.ds(here, rows)].T)
        add(at(turned(2, odd)), q0_two[:, pl.ds(here, rows)].T)
        trace(q0[:, own(odd)])

    @pl.when(active & (place == 1))
    def _():
        add(at(turned(0, odd)), q01[...].T)
        add(at(turned(1, odd)), q11[...])
        add(at(turned(2, odd)), q21[...].T)
        add(at(turned(3, odd)), q31[...].T)
        trace(q11[:, pl.ds(here, rows)])

    @pl.when(active & (place == 2))
    def _():
        add(at(odd, 3), q2[...])
        add(at(turned(3, odd)), q2_last[:, pl.ds(here, rows)].T)
        trace(q2[:, own(2 - 2 * odd)])

    @pl.when(active & (place == 3))
    def _():
        add(at(2 - 2 * odd, 2), q3_near[...])
        add(at(2 * odd, 2), q3_other[...])
        trace(q3_near[:, own(1 - odd)])

    @pl.when(active_ref[0] == 0)
    def _():
        out_ref[...] = sigma_ref[...]
        var_ref[...] = diagonal(sigma_ref[:, own(place_ref[2])].astype(F32))


def final(place, active, pivot, sigma, received, kept):
    rows, nodes = pivot.shape
    chunk = 128
    width = nodes // 4

    def picked(which, blocks):
        return pl.BlockSpec(
            (chunk, blocks * width), lambda i, place, active: (jnp.where(place[1] == which, i, 0), 0)
        )

    def turned_block(start):
        return pl.BlockSpec(
            (rows, chunk),
            lambda i, place, active: (
                0,
                jnp.where(place[1] == 1, start(place[0]) * (width // chunk) + i, 0),
            ),
        )

    whole = pl.BlockSpec((rows, width), lambda i, place, active: (0, 0))
    return pl.pallas_call(
        final_kernel,
        out_shape=(
            jax.ShapeDtypeStruct((rows, nodes), BF16),
            jax.ShapeDtypeStruct((1, rows), F32),
        ),
        grid_spec=pltpu.PrefetchScalarGridSpec(
            num_scalar_prefetch=2,
            grid=(rows // chunk,),
            in_specs=[
                pl.BlockSpec((chunk, nodes), lambda i, place, active: (i, 0)),
                pl.BlockSpec(
                    (chunk, nodes), lambda i, place, active: (jnp.where(active[0] == 0, i, 0), 0)
                ),
                picked(0, 2),
                pl.BlockSpec((rows, width), lambda i, place, active: (0, 2)),
                whole,
                picked(2, 3),
                whole,
                picked(3, 2),
                picked(3, 2),
                turned_block(lambda odd: 1 - odd),
                picked(1, 1),
                turned_block(lambda odd: 1),
                turned_block(lambda odd: 1 - odd),
            ],
            out_specs=(
                pl.BlockSpec((chunk, nodes), lambda i, place, active: (i, 0)),
                pl.BlockSpec((1, chunk), lambda i, place, active: (0, i)),
            ),
        ),
        compiler_params=pltpu.CompilerParams(vmem_limit_bytes=12 * MIB),
        cost_estimate=LIGHT,
        name="final",
    )(place, active, pivot, sigma, *received, *kept)


def owned(sigma_next, separator, inverse_pivot, coupling_rate, lengths, step_index, node_class):
    sigma, pivot = sigma_next[0], inverse_pivot[0]
    odd = lax.axis_index("dom") % 2
    col = lax.axis_index("col")
    place = jnp.stack([odd, turned(col, odd), col]).astype(jnp.int32)
    active = (step_index < lengths).astype(jnp.int32)
    rows, width = pivot.shape[0], pivot.shape[1] // 4
    after = lambda value, *others: lax.optimization_barrier((value, *others))[0]

    shifted = passed_along(separator, "dom", -1)[0]
    p2 = moved(pivot, 2, 1)
    p0 = moved(pivot, 0, 1)
    c1 = couple(pivot, node_class, coupling_rate)
    c3a = moved(c1[: rows // 2], 3, 1)
    across = turn(place, 1, 0, c1, None)

    row, far, near, last = prior_parts(place, step_index, after(shifted, across), sigma)
    far_zero, near_two, last_three = moved(far, 0, 1), moved(near, 2, 1), moved(after(last, p2, p0), 3, 1)

    c2 = couple_here(place, after(p2, last), node_class, coupling_rate)
    across = turn(place, 2, 0, c2, across)
    c0 = couple_here(place, after(p0, c3a, across), node_class, coupling_rate)
    across = turn(place, 0, 0, c0, across)
    c3b = moved(after(c1[rows // 2 :], last_three, across), 3, 1)
    prior = assemble(place, row, near_two, last_three, far_zero)

    h2 = multiply(place, [c2], prior)
    q2_own = multiply(place, [h2], across, lambda odd: odd, 3)
    q2 = moved(q2_own, 1, 2)
    h0 = multiply(place, [after(c0, q2_own)], prior)
    q0_own = product_zero(place, h0, across, q2_own)
    q0 = moved(q0_own, 1, 0)

    across = turn(place, 3, 0, c3a, across)
    across = turn(place, 3, 1, c3b, across)
    h3 = multiply(place, [c3a, c3b], prior)
    q3_near = moved(multiply(place, [h3], across, lambda odd: 2 - 2 * odd, 2), 1, 3)
    q3_own = multiply(place, [h3], across, lambda odd: 2 * odd, 2)
    q3_other = moved(q3_own, 1, 3)
    q0_last = moved(lax.dynamic_slice_in_dim(q3_own, odd * width, width, 1), 1, 0)
    h1 = multiply(place, [after(c1, q2, q3_own)], prior)
    q11 = multiply(place, [h1], across, lambda odd: 1 + odd, 1)
    q2_last = after(q3_near, q0, q11)
    q2_last = moved(lax.dynamic_slice_in_dim(q2_last, odd * width, width, 1), 3, 2)
    received = (q0, q0, q0_last, q2, q2_last, q3_near, q3_other)
    kept = (q0_own, q11, q2_own, q3_own)
    covariance, variances = final(place, active, pivot, sigma, received, kept)
    return (covariance[None], variances)


def gathered(sigma_next, separator, inverse_pivot, coupling_rate, lengths, step_index, node_class):
    shifted = passed_along(separator, "dom", -1)
    prior = jnp.where(step_index[0] == 0, shifted[0], sigma_next[0])
    pivot = inverse_pivot[0].astype(F32)
    coupled = couple(inverse_pivot[0], node_class, coupling_rate)
    rows = coupled.shape[0]
    half = jnp.dot(
        coupled,
        lax.all_gather(prior, "col", axis=0, tiled=True),
        preferred_element_type=F32,
    ).astype(BF16)
    product = lax.dot_general(
        half,
        lax.all_gather(coupled, "col", axis=0, tiled=True),
        (((1,), (1,)), ((), ())),
        preferred_element_type=F32,
    )
    full = pivot + product
    active = step_index[0] < lengths[0]
    old = sigma_next[0]
    covariance = jnp.where(active, full.astype(BF16), old)
    first_col = lax.axis_index("col") * rows
    new_block = lax.dynamic_slice_in_dim(full, first_col, rows, 1)
    old_block = lax.dynamic_slice_in_dim(old, first_col, rows, 1)
    variances = jnp.where(active, jnp.diagonal(new_block), jnp.diagonal(old_block).astype(F32))
    return (covariance[None], variances[None])


def solution(mesh):
    local = owned if mesh.shape["col"] == 4 and mesh.shape["dom"] % 2 == 0 else gathered
    return jax.shard_map(
        local,
        mesh=mesh,
        in_specs=(
            P(("groups", "dom"), "col", None),
            P(("groups", "dom"), "col", None),
            P(("groups", "dom"), "col", None),
            P(("groups", "dom")),
            P(("groups", "dom")),
            P(("groups", "dom")),
            P("groups"),
        ),
        out_specs=(P(("groups", "dom"), "col", None), P(("groups", "dom"), "col")),
        check_vma=False,
    )
```

```python
import functools

import jax
import jax.numpy as jnp
from jax import lax
from jax.experimental import pallas as pl
from jax.experimental.pallas import tpu as pltpu
from jax.sharding import PartitionSpec as P

GX = 64
GY = 32
BF16 = jnp.bfloat16
F32 = jnp.float32
MIB = 1 << 20


def passed_along(value, axis, steps):
    count = lax.axis_size(axis)
    initial, last = (max(0, -steps), min(count, count - steps))
    return lax.ppermute(value, axis, [(source, source + steps) for source in range(initial, last)])


LIGHT = pl.CostEstimate(flops=1 << 20, bytes_accessed=1 << 16, transcendentals=0)


def couple_kernel(rate_ref, class_ref, pivot_ref, out_ref, weight_ref):
    nodes = pivot_ref.shape[1]

    @pl.when(pl.program_id(0) == 0)
    def _():
        kind = class_ref[...]
        across = jnp.where(
            kind == 0, 0.25, jnp.where(kind == 1, 0.375, jnp.where(kind == 2, 0.125, 0.5))
        ).astype(F32)
        along = jnp.where(
            kind == 0, 0.25, jnp.where(kind == 1, 0.125, jnp.where(kind == 2, 0.375, 0.0))
        ).astype(F32)
        node = lax.broadcasted_iota(jnp.int32, (1, nodes), 1)
        column = node % GX
        parts = (
            jnp.where(column > 0, across, 0.0),
            jnp.where(column < GX - 1, across, 0.0),
            jnp.where(node >= GX, along, 0.0),
            jnp.where(node < nodes - GX, along, 0.0),
        )
        for which, part in enumerate(parts):
            weight_ref[which] = jnp.broadcast_to(part, (16, nodes))

    rate = rate_ref[0]

    def group(step, carry):
        rows = pl.ds(pl.multiple_of(step * 16, 16), 16)
        value = pivot_ref[rows, :].astype(F32)
        total = (
            value
            + weight_ref[0] * pltpu.roll(value, 1, 1)
            + weight_ref[1] * pltpu.roll(value, nodes - 1, 1)
            + weight_ref[2] * pltpu.roll(value, GX, 1)
            + weight_ref[3] * pltpu.roll(value, nodes - GX, 1)
        )
        out_ref[rows, :] = (rate * total).astype(BF16)
        return carry

    lax.fori_loop(0, pivot_ref.shape[0] // 16, group, 0)


def couple(pivot, node_class, rate, part=0, parts=1):
    rows, nodes = pivot.shape[0] // parts, pivot.shape[1]
    chunk = min(rows, 128)
    steps = rows // chunk
    return pl.pallas_call(
        couple_kernel,
        out_shape=jax.ShapeDtypeStruct((rows, nodes), BF16),
        grid=(steps,),
        in_specs=[
            pl.BlockSpec(memory_space=pltpu.SMEM),
            pl.BlockSpec((1, nodes), lambda i: (0, 0)),
            pl.BlockSpec((chunk, nodes), lambda i: (part * steps + i, 0)),
        ],
        out_specs=pl.BlockSpec((chunk, nodes), lambda i: (i, 0)),
        scratch_shapes=[pltpu.VMEM((4, 16, nodes), F32)],
        compiler_params=pltpu.CompilerParams(vmem_limit_bytes=6 * MIB),
        cost_estimate=LIGHT,
        name="couple",
    )(rate, node_class.reshape(1, nodes), pivot)


def turned(block, odd):
    return block + odd * (3 - 2 * block)


def route(source, target, doms):
    pairs = []
    for dom in range(doms):
        odd = dom % 2
        pairs.append((dom * 4 + turned(source, odd), dom * 4 + turned(target, odd)))
    return pairs


def moved(value, source, target):
    return lax.ppermute(value, ("dom", "col"), route(source, target, lax.axis_size("dom")))


def couple_here(place, pivot, node_class, rate):
    rows, nodes = pivot.shape
    chunk = 128

    def kernel(place_ref, *refs):
        @pl.when(place_ref[1] == 1)
        def _():
            couple_kernel(*refs)

    return pl.pallas_call(
        kernel,
        out_shape=jax.ShapeDtypeStruct((rows, nodes), BF16),
        grid_spec=pltpu.PrefetchScalarGridSpec(
            num_scalar_prefetch=1,
            grid=(rows // chunk,),
            in_specs=[
                pl.BlockSpec(memory_space=pltpu.SMEM),
                pl.BlockSpec((1, nodes), lambda i, place: (0, 0)),
                pl.BlockSpec((chunk, nodes), lambda i, place: (i, 0)),
            ],
            out_specs=pl.BlockSpec((chunk, nodes), lambda i, place: (i, 0)),
            scratch_shapes=[pltpu.VMEM((4, 16, nodes), F32)],
        ),
        compiler_params=pltpu.CompilerParams(vmem_limit_bytes=8 * MIB),
        cost_estimate=LIGHT,
        name="couple_here",
    )(place, rate, node_class.reshape(1, nodes), pivot)


def turn_kernel(place_ref, coupled_ref, *refs):
    @pl.when(place_ref[1] == 1)
    def _():
        refs[-1][...] = coupled_ref[...].T


def turn(place, panel, part, coupled, across):
    rows, nodes = coupled.shape
    chunk = 128
    steps = rows // chunk
    ratio = nodes // 4 // chunk
    return pl.pallas_call(
        turn_kernel,
        out_shape=jax.ShapeDtypeStruct((nodes, nodes), BF16),
        grid_spec=pltpu.PrefetchScalarGridSpec(
            num_scalar_prefetch=1,
            grid=(steps,),
            in_specs=[pl.BlockSpec((chunk, nodes), lambda i, place: (i, 0))]
            + ([] if across is None else [pl.BlockSpec(memory_space=pl.ANY)]),
            out_specs=pl.BlockSpec(
                (nodes, chunk),
                lambda i, place: (0, turned(panel, place[0]) * ratio + part * steps + i),
            ),
        ),
        input_output_aliases={} if across is None else {2: 0},
        compiler_params=pltpu.CompilerParams(vmem_limit_bytes=4 * MIB),
        cost_estimate=LIGHT,
        name="turn",
    )(place, coupled, *(() if across is None else (across,)))


def multiply_kernel(first, count, lefts, place_ref, *refs):
    left_refs, right_ref, out_ref = refs[:lefts], refs[lefts], refs[-1]
    width = right_ref.shape[0] // 4

    @pl.when(place_ref[1] == 1)
    def _():
        def block(step, carry):
            source = pl.multiple_of((first(place_ref[0]) + step) * width, 128)
            target = pl.multiple_of(step * width, 128)
            row = 0
            for left_ref in left_refs:
                rows = left_ref.shape[0]
                out_ref[row : row + rows, pl.ds(target, width)] = jnp.dot(
                    left_ref[...], right_ref[:, pl.ds(source, width)], preferred_element_type=F32
                ).astype(BF16)
                row += rows
            return carry

        lax.fori_loop(0, count, block, 0)


def multiply(place, lefts, right, first=lambda odd: 0, count=4):
    rows = sum(left.shape[0] for left in lefts)
    width = right.shape[0] // 4
    vmem = pl.BlockSpec(memory_space=pltpu.VMEM)
    return pl.pallas_call(
        functools.partial(multiply_kernel, first, count, len(lefts)),
        out_shape=jax.ShapeDtypeStruct((rows, count * width), BF16),
        in_specs=[pl.BlockSpec(memory_space=pltpu.SMEM)] + [vmem] * (len(lefts) + 1),
        out_specs=vmem,
        compiler_params=pltpu.CompilerParams(vmem_limit_bytes=6 * MIB),
        cost_estimate=LIGHT,
        name="multiply",
    )(place, *lefts, right)


def two_kernel(place_ref, left_ref, right_ref, zero_ref, out_ref):
    odd = place_ref[0]
    width = right_ref.shape[0] // 4
    multiply_kernel(lambda odd: 1, 2, 1, place_ref, left_ref, right_ref, out_ref)

    @pl.when(place_ref[1] == 1)
    def _():
        out_ref[:, 2 * width :] = zero_ref[:, pl.ds(pl.multiple_of((2 - 2 * odd) * width, 128), width)]


def product_two(place, half, across, zero):
    rows = half.shape[0]
    width = across.shape[0] // 4
    vmem = pl.BlockSpec(memory_space=pltpu.VMEM)
    return pl.pallas_call(
        two_kernel,
        out_shape=jax.ShapeDtypeStruct((rows, 3 * width), BF16),
        in_specs=[pl.BlockSpec(memory_space=pltpu.SMEM)] + [vmem] * 3,
        out_specs=vmem,
        compiler_params=pltpu.CompilerParams(vmem_limit_bytes=6 * MIB),
        cost_estimate=LIGHT,
        name="product_two",
    )(place, half, across, zero)


def prior_kernel(step_ref, shifted_ref, sigma_ref, out_ref):
    @pl.when(step_ref[0] == 0)
    def _():
        out_ref[...] = shifted_ref[...]

    @pl.when(step_ref[0] != 0)
    def _():
        out_ref[...] = sigma_ref[...]


def parts_kernel(place_ref, step_ref, shifted_ref, sigma_ref, row_ref, far_ref, near_ref, last_ref):
    odd = place_ref[0]
    width = last_ref.shape[1]

    def at(block, count=1):
        return pl.ds(pl.multiple_of(block * width, 128), count * width)

    prior_kernel(step_ref, shifted_ref, sigma_ref, row_ref)
    near = row_ref[:, at(2 - 2 * odd, 2)]
    near_ref[...] = near
    far_ref[:, width:] = near
    far_ref[:, :width] = row_ref[:, at(3 * odd)]
    last_ref[...] = row_ref[:, at(3 - 3 * odd)]


def prior_parts(place, step, shifted, sigma):
    rows, nodes = sigma.shape
    chunk = 128
    width = nodes // 4
    out = lambda blocks: jax.ShapeDtypeStruct((rows, blocks * width), BF16)
    spec = lambda blocks: pl.BlockSpec((chunk, blocks * width), lambda i, place, step: (i, 0))
    return pl.pallas_call(
        parts_kernel,
        out_shape=(out(4), out(3), out(2), out(1)),
        grid_spec=pltpu.PrefetchScalarGridSpec(
            num_scalar_prefetch=2,
            grid=(rows // chunk,),
            in_specs=[
                pl.BlockSpec(
                    (chunk, nodes), lambda i, place, step: (jnp.where(step[0] == 0, i, 0), 0)
                ),
                pl.BlockSpec(
                    (chunk, nodes), lambda i, place, step: (jnp.where(step[0] == 0, 0, i), 0)
                ),
            ],
            out_specs=(spec(4), spec(3), spec(2), spec(1)),
        ),
        compiler_params=pltpu.CompilerParams(vmem_limit_bytes=8 * MIB),
        cost_estimate=LIGHT,
        name="prior_parts",
    )(place, step, shifted, sigma)


def assemble_kernel(place_ref, own, near_two, last_three, far_zero, out_ref):
    @pl.when(place_ref[1] == 1)
    def _():
        odd = place_ref[0]
        width = last_three.shape[1]

        def at(block):
            return pl.ds(pl.multiple_of(block * width, 128), width)

        near = 2 * (1 - odd)
        half = pl.ds(pl.multiple_of(near * width, 128), 2 * width)
        row = [turned(block, odd) for block in range(4)]
        out_ref[at(row[1]), :] = own[...]
        out_ref[at(row[2]), half] = near_two[...]
        out_ref[at(row[0]), at(row[0])] = far_zero[:, :width]
        out_ref[at(row[0]), half] = far_zero[:, width:]
        out_ref[at(row[3]), at(row[3])] = last_three[...]
        for step in range(2):
            out_ref[at(near + step), at(row[1])] = own[:, at(near + step)].T
            piece = slice((1 + step) * width, (2 + step) * width)
            out_ref[at(near + step), at(row[0])] = far_zero[:, piece].T
        out_ref[at(row[0]), at(row[1])] = own[:, at(row[0])].T
        out_ref[at(row[3]), at(row[2])] = near_two[:, at(1 - odd)].T


def assemble(place, *parts):
    nodes = parts[0].shape[1]
    vmem = pl.BlockSpec(memory_space=pltpu.VMEM)
    return pl.pallas_call(
        assemble_kernel,
        out_shape=jax.ShapeDtypeStruct((nodes, nodes), BF16),
        in_specs=[pl.BlockSpec(memory_space=pltpu.SMEM)] + [vmem] * 4,
        out_specs=vmem,
        compiler_params=pltpu.CompilerParams(vmem_limit_bytes=6 * MIB),
        cost_estimate=LIGHT,
        name="assemble",
    )(place, *parts)


def final_kernel(
    place_ref, active_ref, pivot_ref, sigma_ref,
    q0, q0_last, q2, q2_zero, q2_last, q3_two, q3_other, q3_last,
    q01, q11, q21, q31,
    out_ref, var_ref,
):
    rows, nodes = pivot_ref.shape
    width = nodes // 4
    odd, place = place_ref[0], place_ref[1]
    here = pl.multiple_of(pl.program_id(0) * rows, 128)
    square = (rows, rows)
    on_diagonal = lax.broadcasted_iota(jnp.int32, square, 0) == lax.broadcasted_iota(
        jnp.int32, square, 1
    )

    def at(block, count=1):
        return pl.ds(pl.multiple_of(block * width, 128), count * width)

    def own(block):
        return pl.ds(pl.multiple_of(block * width + here, 128), rows)

    def diagonal(value):
        return jnp.sum(jnp.where(on_diagonal, value, 0.0), axis=0, keepdims=True)

    def add(columns, product):
        out_ref[:, columns] = (pivot_ref[:, columns].astype(F32) + product.astype(F32)).astype(BF16)

    def trace(product):
        var_ref[...] = diagonal(
            pivot_ref[:, own(place_ref[2])].astype(F32) + product.astype(F32)
        )

    active = active_ref[0] != 0

    @pl.when(active & (place == 0))
    def _():
        add(at(odd, 3), q0[...])
        add(at(turned(3, odd)), q0_last[:, pl.ds(here, rows)].T)
        trace(q0[:, own(2 * odd)])

    @pl.when(active & (place == 1))
    def _():
        add(at(turned(0, odd)), q01[...].T)
        add(at(turned(1, odd)), q11[...])
        add(at(turned(2, odd)), q21[...].T)
        add(at(turned(3, odd)), q31[...].T)
        trace(q11[:, pl.ds(here, rows)])

    @pl.when(active & (place == 2))
    def _():
        add(at(turned(0, odd)), q2_zero[:, pl.ds(here, rows)].T)
        add(at(1, 2), q2[...])
        add(at(turned(3, odd)), q2_last[:, pl.ds(here, rows)].T)
        trace(q2[:, own(1 - odd)])

    @pl.when(active & (place == 3))
    def _():
        add(at(2 * odd, 2), q3_other[...])
        add(at(turned(2, odd)), q3_two[...])
        add(at(turned(3, odd)), q3_last[...])
        trace(q3_last[:, pl.ds(here, rows)])

    @pl.when(active_ref[0] == 0)
    def _():
        out_ref[...] = sigma_ref[...]
        var_ref[...] = diagonal(sigma_ref[:, own(place_ref[2])].astype(F32))


def final(place, active, pivot, sigma, received, kept):
    rows, nodes = pivot.shape
    chunk = 128
    width = nodes // 4

    def picked(which, blocks):
        return pl.BlockSpec(
            (chunk, blocks * width), lambda i, place, active: (jnp.where(place[1] == which, i, 0), 0)
        )

    def turned_block(start):
        return pl.BlockSpec(
            (rows, chunk),
            lambda i, place, active: (
                0,
                jnp.where(place[1] == 1, start(place[0]) * (width // chunk) + i, 0),
            ),
        )

    whole = lambda block: pl.BlockSpec((rows, width), lambda i, place, active: (0, block))
    return pl.pallas_call(
        final_kernel,
        out_shape=(
            jax.ShapeDtypeStruct((rows, nodes), BF16),
            jax.ShapeDtypeStruct((1, rows), F32),
        ),
        grid_spec=pltpu.PrefetchScalarGridSpec(
            num_scalar_prefetch=2,
            grid=(rows // chunk,),
            in_specs=[
                pl.BlockSpec((chunk, nodes), lambda i, place, active: (i, 0)),
                pl.BlockSpec(
                    (chunk, nodes), lambda i, place, active: (jnp.where(active[0] == 0, i, 0), 0)
                ),
                picked(0, 3),
                whole(0),
                picked(2, 2),
                whole(2),
                whole(0),
                picked(3, 1),
                picked(3, 2),
                picked(3, 1),
                turned_block(lambda odd: 1),
                picked(1, 1),
                turned_block(lambda odd: odd),
                turned_block(lambda odd: 1 - odd),
            ],
            out_specs=(
                pl.BlockSpec((chunk, nodes), lambda i, place, active: (i, 0)),
                pl.BlockSpec((1, chunk), lambda i, place, active: (0, i)),
            ),
        ),
        compiler_params=pltpu.CompilerParams(vmem_limit_bytes=12 * MIB),
        cost_estimate=LIGHT,
        name="final",
    )(place, active, pivot, sigma, *received, *kept)


def owned(sigma_next, separator, inverse_pivot, coupling_rate, lengths, step_index, node_class):
    sigma, pivot = sigma_next[0], inverse_pivot[0]
    odd = lax.axis_index("dom") % 2
    col = lax.axis_index("col")
    place = jnp.stack([odd, turned(col, odd), col]).astype(jnp.int32)
    active = (step_index < lengths).astype(jnp.int32)
    rows, width = pivot.shape[0], pivot.shape[1] // 4
    after = lambda value, *others: lax.optimization_barrier((value, *others))[0]

    shifted = passed_along(separator, "dom", -1)[0]
    p2 = moved(pivot, 2, 1)
    p0 = moved(pivot, 0, 1)
    c1 = [couple(pivot, node_class, coupling_rate, part, 2) for part in range(2)]
    across = turn(place, 1, 0, c1[0], None)
    across = turn(place, 1, 1, c1[1], across)

    row, far, near, last = prior_parts(place, step_index, after(shifted, across), sigma)
    far_zero, near_two, last_three = moved(far, 0, 1), moved(near, 2, 1), moved(last, 3, 1)

    c2 = couple_here(place, after(p2, last), node_class, coupling_rate)
    across = turn(place, 2, 0, c2, across)
    c0 = couple_here(place, after(p0, across), node_class, coupling_rate)
    across = turn(place, 0, 0, c0, across)
    c3 = [
        moved(after(c1[0], last_three, near_two, across), 3, 1),
        moved(after(c1[1], far_zero), 3, 1),
    ]
    prior = assemble(place, row, near_two, last_three, far_zero)

    h0 = multiply(place, [c0], prior)
    q0_own = multiply(place, [h0], across, lambda odd: odd, 3)
    q0 = moved(q0_own, 1, 0)
    h2 = multiply(place, [after(c2, q0_own)], prior)
    q2_own = product_two(place, h2, across, q0_own)
    q2 = moved(q2_own, 1, 2)

    h3 = multiply(place, c3, prior)
    q3_two = moved(multiply(place, [h3], across, lambda odd: 2 - odd, 1), 1, 3)
    q3_own = multiply(place, [h3], across, lambda odd: 2 * odd, 2)
    q3_other = moved(q3_own, 1, 3)
    q30 = lax.dynamic_slice_in_dim(q3_own, odd * width, width, 1)
    q0_last = moved(q30, 1, 0)
    across = turn(place, 3, 0, c3[0], after(across, q30))
    across = turn(place, 3, 1, c3[1], across)
    q33 = multiply(place, [h3], across, lambda odd: 3 - 3 * odd, 1)
    q3_last = moved(q33, 1, 3)
    q2_last = moved(after(q3_two, q0, q33), 3, 2)
    h1 = multiply(place, [after(c1[0], q33), c1[1]], prior)
    q11 = multiply(place, [h1], across, lambda odd: 1 + odd, 1)
    received = (q0, q0_last, q2, q2, q2_last, q3_two, q3_other, q3_last)
    kept = (q0_own, q11, q2_own, q3_own)
    covariance, variances = final(place, active, pivot, sigma, received, kept)
    return (covariance[None], variances)


def gathered(sigma_next, separator, inverse_pivot, coupling_rate, lengths, step_index, node_class):
    shifted = passed_along(separator, "dom", -1)
    prior = jnp.where(step_index[0] == 0, shifted[0], sigma_next[0])
    pivot = inverse_pivot[0].astype(F32)
    coupled = couple(inverse_pivot[0], node_class, coupling_rate)
    rows = coupled.shape[0]
    half = jnp.dot(
        coupled,
        lax.all_gather(prior, "col", axis=0, tiled=True),
        preferred_element_type=F32,
    ).astype(BF16)
    product = lax.dot_general(
        half,
        lax.all_gather(coupled, "col", axis=0, tiled=True),
        (((1,), (1,)), ((), ())),
        preferred_element_type=F32,
    )
    full = pivot + product
    active = step_index[0] < lengths[0]
    old = sigma_next[0]
    covariance = jnp.where(active, full.astype(BF16), old)
    first_col = lax.axis_index("col") * rows
    new_block = lax.dynamic_slice_in_dim(full, first_col, rows, 1)
    old_block = lax.dynamic_slice_in_dim(old, first_col, rows, 1)
    variances = jnp.where(active, jnp.diagonal(new_block), jnp.diagonal(old_block).astype(F32))
    return (covariance[None], variances[None])


def solution(mesh):
    local = owned if mesh.shape["col"] == 4 and mesh.shape["dom"] % 2 == 0 else gathered
    return jax.shard_map(
        local,
        mesh=mesh,
        in_specs=(
            P(("groups", "dom"), "col", None),
            P(("groups", "dom"), "col", None),
            P(("groups", "dom"), "col", None),
            P(("groups", "dom")),
            P(("groups", "dom")),
            P(("groups", "dom")),
            P("groups"),
        ),
        out_specs=(P(("groups", "dom"), "col", None), P(("groups", "dom"), "col")),
        check_vma=False,
    )
```

```python
import functools

import jax
import jax.numpy as jnp
from jax import lax
from jax.experimental import pallas as pl
from jax.experimental.pallas import tpu as pltpu
from jax.sharding import PartitionSpec as P

GX = 64
GY = 32
BF16 = jnp.bfloat16
F32 = jnp.float32
MIB = 1 << 20


def passed_along(value, axis, steps):
    count = lax.axis_size(axis)
    initial, last = (max(0, -steps), min(count, count - steps))
    return lax.ppermute(value, axis, [(source, source + steps) for source in range(initial, last)])


LIGHT = pl.CostEstimate(flops=1 << 20, bytes_accessed=1 << 16, transcendentals=0)


def couple_kernel(rate_ref, class_ref, pivot_ref, out_ref, weight_ref):
    nodes = pivot_ref.shape[1]

    @pl.when(pl.program_id(0) == 0)
    def _():
        kind = class_ref[...]
        across = jnp.where(
            kind == 0, 0.25, jnp.where(kind == 1, 0.375, jnp.where(kind == 2, 0.125, 0.5))
        ).astype(F32)
        along = jnp.where(
            kind == 0, 0.25, jnp.where(kind == 1, 0.125, jnp.where(kind == 2, 0.375, 0.0))
        ).astype(F32)
        node = lax.broadcasted_iota(jnp.int32, (1, nodes), 1)
        column = node % GX
        parts = (
            jnp.where(column > 0, across, 0.0),
            jnp.where(column < GX - 1, across, 0.0),
            jnp.where(node >= GX, along, 0.0),
            jnp.where(node < nodes - GX, along, 0.0),
        )
        for which, part in enumerate(parts):
            weight_ref[which] = jnp.broadcast_to(part, (16, nodes))

    rate = rate_ref[0]

    def group(step, carry):
        rows = pl.ds(pl.multiple_of(step * 16, 16), 16)
        value = pivot_ref[rows, :].astype(F32)
        total = (
            value
            + weight_ref[0] * pltpu.roll(value, 1, 1)
            + weight_ref[1] * pltpu.roll(value, nodes - 1, 1)
            + weight_ref[2] * pltpu.roll(value, GX, 1)
            + weight_ref[3] * pltpu.roll(value, nodes - GX, 1)
        )
        out_ref[rows, :] = (rate * total).astype(BF16)
        return carry

    lax.fori_loop(0, pivot_ref.shape[0] // 16, group, 0)


def couple(pivot, node_class, rate, part=0, parts=1):
    rows, nodes = pivot.shape[0] // parts, pivot.shape[1]
    chunk = min(rows, 128)
    steps = rows // chunk
    return pl.pallas_call(
        couple_kernel,
        out_shape=jax.ShapeDtypeStruct((rows, nodes), BF16),
        grid=(steps,),
        in_specs=[
            pl.BlockSpec(memory_space=pltpu.SMEM),
            pl.BlockSpec((1, nodes), lambda i: (0, 0)),
            pl.BlockSpec((chunk, nodes), lambda i: (part * steps + i, 0)),
        ],
        out_specs=pl.BlockSpec((chunk, nodes), lambda i: (i, 0)),
        scratch_shapes=[pltpu.VMEM((4, 16, nodes), F32)],
        compiler_params=pltpu.CompilerParams(vmem_limit_bytes=6 * MIB),
        cost_estimate=LIGHT,
        name="couple",
    )(rate, node_class.reshape(1, nodes), pivot)


def turned(block, odd):
    return block + odd * (3 - 2 * block)


def route(source, target, doms):
    pairs = []
    for dom in range(doms):
        odd = dom % 2
        pairs.append((dom * 4 + turned(source, odd), dom * 4 + turned(target, odd)))
    return pairs


def moved(value, source, target):
    return lax.ppermute(value, ("dom", "col"), route(source, target, lax.axis_size("dom")))


def couple_here(place, pivot, node_class, rate):
    rows, nodes = pivot.shape
    chunk = 128

    def kernel(place_ref, *refs):
        @pl.when(place_ref[1] == 1)
        def _():
            couple_kernel(*refs)

    return pl.pallas_call(
        kernel,
        out_shape=jax.ShapeDtypeStruct((rows, nodes), BF16),
        grid_spec=pltpu.PrefetchScalarGridSpec(
            num_scalar_prefetch=1,
            grid=(rows // chunk,),
            in_specs=[
                pl.BlockSpec(memory_space=pltpu.SMEM),
                pl.BlockSpec((1, nodes), lambda i, place: (0, 0)),
                pl.BlockSpec((chunk, nodes), lambda i, place: (i, 0)),
            ],
            out_specs=pl.BlockSpec((chunk, nodes), lambda i, place: (i, 0)),
            scratch_shapes=[pltpu.VMEM((4, 16, nodes), F32)],
        ),
        compiler_params=pltpu.CompilerParams(vmem_limit_bytes=8 * MIB),
        cost_estimate=LIGHT,
        name="couple_here",
    )(place, rate, node_class.reshape(1, nodes), pivot)


def turn_kernel(place_ref, coupled_ref, *refs):
    @pl.when(place_ref[1] == 1)
    def _():
        refs[-1][...] = coupled_ref[...].T


def turn(place, panel, part, coupled, across):
    rows, nodes = coupled.shape
    chunk = 128
    steps = rows // chunk
    ratio = nodes // 4 // chunk
    return pl.pallas_call(
        turn_kernel,
        out_shape=jax.ShapeDtypeStruct((nodes, nodes), BF16),
        grid_spec=pltpu.PrefetchScalarGridSpec(
            num_scalar_prefetch=1,
            grid=(steps,),
            in_specs=[pl.BlockSpec((chunk, nodes), lambda i, place: (i, 0))]
            + ([] if across is None else [pl.BlockSpec(memory_space=pl.ANY)]),
            out_specs=pl.BlockSpec(
                (nodes, chunk),
                lambda i, place: (0, turned(panel, place[0]) * ratio + part * steps + i),
            ),
        ),
        input_output_aliases={} if across is None else {2: 0},
        compiler_params=pltpu.CompilerParams(vmem_limit_bytes=4 * MIB),
        cost_estimate=LIGHT,
        name="turn",
    )(place, coupled, *(() if across is None else (across,)))


def multiply_kernel(first, count, lefts, place_ref, *refs):
    left_refs, right_ref, out_ref = refs[:lefts], refs[lefts], refs[-1]
    width = right_ref.shape[0] // 4

    @pl.when(place_ref[1] == 1)
    def _():
        def block(step, carry):
            source = pl.multiple_of((first(place_ref[0]) + step) * width, 128)
            target = pl.multiple_of(step * width, 128)
            row = 0
            for left_ref in left_refs:
                rows = left_ref.shape[0]
                out_ref[row : row + rows, pl.ds(target, width)] = jnp.dot(
                    left_ref[...], right_ref[:, pl.ds(source, width)], preferred_element_type=F32
                ).astype(BF16)
                row += rows
            return carry

        lax.fori_loop(0, count, block, 0)


def multiply(place, lefts, right, first=lambda odd: 0, count=4):
    rows = sum(left.shape[0] for left in lefts)
    width = right.shape[0] // 4
    vmem = pl.BlockSpec(memory_space=pltpu.VMEM)
    return pl.pallas_call(
        functools.partial(multiply_kernel, first, count, len(lefts)),
        out_shape=jax.ShapeDtypeStruct((rows, count * width), BF16),
        in_specs=[pl.BlockSpec(memory_space=pltpu.SMEM)] + [vmem] * (len(lefts) + 1),
        out_specs=vmem,
        compiler_params=pltpu.CompilerParams(vmem_limit_bytes=6 * MIB),
        cost_estimate=LIGHT,
        name="multiply",
    )(place, *lefts, right)


def two_kernel(place_ref, left_ref, right_ref, zero_ref, out_ref):
    odd = place_ref[0]
    width = right_ref.shape[0] // 4
    multiply_kernel(lambda odd: 1, 2, 1, place_ref, left_ref, right_ref, out_ref)

    @pl.when(place_ref[1] == 1)
    def _():
        out_ref[:, 2 * width :] = zero_ref[:, pl.ds(pl.multiple_of((2 - 2 * odd) * width, 128), width)]


def product_two(place, half, across, zero):
    rows = half.shape[0]
    width = across.shape[0] // 4
    vmem = pl.BlockSpec(memory_space=pltpu.VMEM)
    return pl.pallas_call(
        two_kernel,
        out_shape=jax.ShapeDtypeStruct((rows, 3 * width), BF16),
        in_specs=[pl.BlockSpec(memory_space=pltpu.SMEM)] + [vmem] * 3,
        out_specs=vmem,
        compiler_params=pltpu.CompilerParams(vmem_limit_bytes=6 * MIB),
        cost_estimate=LIGHT,
        name="product_two",
    )(place, half, across, zero)


def three_kernel(place_ref, left_ref, right_ref, out_ref, zero_ref):
    width = zero_ref.shape[1]
    multiply_kernel(lambda odd: 2 * odd, 2, 1, place_ref, left_ref, right_ref, out_ref)

    @pl.when(place_ref[1] == 1)
    def _():
        zero_ref[...] = out_ref[:, pl.ds(pl.multiple_of(place_ref[0] * width, 128), width)]


def product_three(place, half, across):
    rows = half.shape[0]
    width = across.shape[0] // 4
    vmem = pl.BlockSpec(memory_space=pltpu.VMEM)
    return pl.pallas_call(
        three_kernel,
        out_shape=(
            jax.ShapeDtypeStruct((rows, 2 * width), BF16),
            jax.ShapeDtypeStruct((rows, width), BF16),
        ),
        in_specs=[pl.BlockSpec(memory_space=pltpu.SMEM)] + [vmem] * 2,
        out_specs=(vmem, vmem),
        compiler_params=pltpu.CompilerParams(vmem_limit_bytes=6 * MIB),
        cost_estimate=LIGHT,
        name="product_three",
    )(place, half, across)


def prior_kernel(place_ref, shifted_ref, sigma_ref, out_ref):
    @pl.when(place_ref[3] == 0)
    def _():
        out_ref[...] = shifted_ref[...]

    @pl.when(place_ref[3] != 0)
    def _():
        out_ref[...] = sigma_ref[...]


def parts_kernel(place_ref, shifted_ref, sigma_ref, row_ref, far_ref, near_ref, last_ref):
    odd = place_ref[0]
    width = last_ref.shape[1]

    def at(block, count=1):
        return pl.ds(pl.multiple_of(block * width, 128), count * width)

    prior_kernel(place_ref, shifted_ref, sigma_ref, row_ref)
    near = row_ref[:, at(2 - 2 * odd, 2)]
    near_ref[...] = near
    far_ref[:, width:] = near
    far_ref[:, :width] = row_ref[:, at(3 * odd)]
    last_ref[...] = row_ref[:, at(3 - 3 * odd)]


def prior_parts(place, shifted, sigma):
    rows, nodes = sigma.shape
    chunk = 128
    width = nodes // 4
    out = lambda blocks: jax.ShapeDtypeStruct((rows, blocks * width), BF16)
    spec = lambda blocks: pl.BlockSpec((chunk, blocks * width), lambda i, place: (i, 0))
    return pl.pallas_call(
        parts_kernel,
        out_shape=(out(4), out(3), out(2), out(1)),
        grid_spec=pltpu.PrefetchScalarGridSpec(
            num_scalar_prefetch=1,
            grid=(rows // chunk,),
            in_specs=[
                pl.BlockSpec(
                    (chunk, nodes), lambda i, place: (jnp.where(place[3] == 0, i, 0), 0)
                ),
                pl.BlockSpec(
                    (chunk, nodes), lambda i, place: (jnp.where(place[3] == 0, 0, i), 0)
                ),
            ],
            out_specs=(spec(4), spec(3), spec(2), spec(1)),
        ),
        compiler_params=pltpu.CompilerParams(vmem_limit_bytes=8 * MIB),
        cost_estimate=LIGHT,
        name="prior_parts",
    )(place, shifted, sigma)


def assemble_kernel(place_ref, own, near_two, last_three, far_zero, out_ref):
    @pl.when(place_ref[1] == 1)
    def _():
        odd = place_ref[0]
        width = last_three.shape[1]

        def at(block):
            return pl.ds(pl.multiple_of(block * width, 128), width)

        near = 2 * (1 - odd)
        half = pl.ds(pl.multiple_of(near * width, 128), 2 * width)
        row = [turned(block, odd) for block in range(4)]
        out_ref[at(row[1]), :] = own[...]
        out_ref[at(row[2]), half] = near_two[...]
        out_ref[at(row[0]), at(row[0])] = far_zero[:, :width]
        out_ref[at(row[0]), half] = far_zero[:, width:]
        out_ref[at(row[3]), at(row[3])] = last_three[...]
        for step in range(2):
            out_ref[at(near + step), at(row[1])] = own[:, at(near + step)].T
            piece = slice((1 + step) * width, (2 + step) * width)
            out_ref[at(near + step), at(row[0])] = far_zero[:, piece].T
        out_ref[at(row[0]), at(row[1])] = own[:, at(row[0])].T
        out_ref[at(row[3]), at(row[2])] = near_two[:, at(1 - odd)].T


def assemble(place, *parts):
    nodes = parts[0].shape[1]
    vmem = pl.BlockSpec(memory_space=pltpu.VMEM)
    return pl.pallas_call(
        assemble_kernel,
        out_shape=jax.ShapeDtypeStruct((nodes, nodes), BF16),
        in_specs=[pl.BlockSpec(memory_space=pltpu.SMEM)] + [vmem] * 4,
        out_specs=vmem,
        compiler_params=pltpu.CompilerParams(vmem_limit_bytes=6 * MIB),
        cost_estimate=LIGHT,
        name="assemble",
    )(place, *parts)


def final_kernel(
    place_ref, pivot_ref, sigma_ref,
    q0, q0_last, q2, q2_zero, q2_last, q3_two, q3_other, q3_last,
    q01, q11, q21, q31,
    out_ref, var_ref,
):
    rows, nodes = pivot_ref.shape
    width = nodes // 4
    odd, place = place_ref[0], place_ref[1]
    here = pl.multiple_of(pl.program_id(0) * rows, 128)
    square = (rows, rows)
    on_diagonal = lax.broadcasted_iota(jnp.int32, square, 0) == lax.broadcasted_iota(
        jnp.int32, square, 1
    )

    def at(block, count=1):
        return pl.ds(pl.multiple_of(block * width, 128), count * width)

    def own(block):
        return pl.ds(pl.multiple_of(block * width + here, 128), rows)

    def diagonal(value):
        return jnp.sum(jnp.where(on_diagonal, value, 0.0), axis=0, keepdims=True)

    def add(columns, product):
        out_ref[:, columns] = (pivot_ref[:, columns].astype(F32) + product.astype(F32)).astype(BF16)

    def trace(product):
        var_ref[...] = diagonal(
            pivot_ref[:, own(place_ref[2])].astype(F32) + product.astype(F32)
        )

    active = place_ref[4] != 0

    @pl.when(active & (place == 0))
    def _():
        add(at(odd, 3), q0[...])
        add(at(turned(3, odd)), q0_last[:, pl.ds(here, rows)].T)
        trace(q0[:, own(2 * odd)])

    @pl.when(active & (place == 1))
    def _():
        add(at(turned(0, odd)), q01[...].T)
        add(at(turned(1, odd)), q11[...])
        add(at(turned(2, odd)), q21[...].T)
        add(at(turned(3, odd)), q31[...].T)
        trace(q11[:, pl.ds(here, rows)])

    @pl.when(active & (place == 2))
    def _():
        add(at(turned(0, odd)), q2_zero[:, pl.ds(here, rows)].T)
        add(at(1, 2), q2[...])
        add(at(turned(3, odd)), q2_last[:, pl.ds(here, rows)].T)
        trace(q2[:, own(1 - odd)])

    @pl.when(active & (place == 3))
    def _():
        add(at(2 * odd, 2), q3_other[...])
        add(at(turned(2, odd)), q3_two[...])
        add(at(turned(3, odd)), q3_last[...])
        trace(q3_last[:, pl.ds(here, rows)])

    @pl.when(place_ref[4] == 0)
    def _():
        out_ref[...] = sigma_ref[...]
        var_ref[...] = diagonal(sigma_ref[:, own(place_ref[2])].astype(F32))


def final(place, pivot, sigma, received, kept):
    rows, nodes = pivot.shape
    chunk = 128
    width = nodes // 4

    def picked(which, blocks):
        return pl.BlockSpec(
            (chunk, blocks * width), lambda i, place: (jnp.where(place[1] == which, i, 0), 0)
        )

    def turned_block(start):
        return pl.BlockSpec(
            (rows, chunk),
            lambda i, place: (
                0,
                jnp.where(place[1] == 1, start(place[0]) * (width // chunk) + i, 0),
            ),
        )

    whole = lambda block: pl.BlockSpec((rows, width), lambda i, place: (0, block))
    return pl.pallas_call(
        final_kernel,
        out_shape=(
            jax.ShapeDtypeStruct((rows, nodes), BF16),
            jax.ShapeDtypeStruct((1, rows), F32),
        ),
        grid_spec=pltpu.PrefetchScalarGridSpec(
            num_scalar_prefetch=1,
            grid=(rows // chunk,),
            in_specs=[
                pl.BlockSpec((chunk, nodes), lambda i, place: (i, 0)),
                pl.BlockSpec(
                    (chunk, nodes), lambda i, place: (jnp.where(place[4] == 0, i, 0), 0)
                ),
                picked(0, 3),
                whole(0),
                picked(2, 2),
                whole(2),
                whole(0),
                picked(3, 1),
                picked(3, 2),
                picked(3, 1),
                turned_block(lambda odd: 1),
                picked(1, 1),
                turned_block(lambda odd: odd),
                turned_block(lambda odd: 1 - odd),
            ],
            out_specs=(
                pl.BlockSpec((chunk, nodes), lambda i, place: (i, 0)),
                pl.BlockSpec((1, chunk), lambda i, place: (0, i)),
            ),
        ),
        compiler_params=pltpu.CompilerParams(vmem_limit_bytes=12 * MIB),
        cost_estimate=LIGHT,
        name="final",
    )(place, pivot, sigma, *received, *kept)


def owned(sigma_next, separator, inverse_pivot, coupling_rate, lengths, step_index, node_class):
    sigma, pivot = sigma_next[0], inverse_pivot[0]
    odd = lax.axis_index("dom") % 2
    col = lax.axis_index("col")
    step = step_index[0]
    place = jnp.stack([odd, turned(col, odd), col, step, step < lengths[0]]).astype(jnp.int32)
    after = lambda value, *others: lax.optimization_barrier((value, *others))[0]

    shifted = passed_along(separator, "dom", -1)[0]
    p2 = moved(pivot, 2, 1)
    p0 = moved(pivot, 0, 1)
    c1 = [couple(pivot, node_class, coupling_rate, part, 2) for part in range(2)]
    across = turn(place, 1, 0, c1[0], None)
    across = turn(place, 1, 1, c1[1], across)

    row, far, near, last = prior_parts(place, after(shifted, across), sigma)
    far_zero, near_two, last_three = moved(far, 0, 1), moved(near, 2, 1), moved(last, 3, 1)

    c2 = couple_here(place, after(p2, last), node_class, coupling_rate)
    across = turn(place, 2, 0, c2, across)
    c0 = couple_here(place, after(p0, across), node_class, coupling_rate)
    across = turn(place, 0, 0, c0, across)
    c3 = [
        moved(after(c1[0], last_three, near_two, across), 3, 1),
        moved(after(c1[1], far_zero), 3, 1),
    ]
    prior = assemble(place, row, near_two, last_three, far_zero)

    h0 = multiply(place, [c0], prior)
    q0_own = multiply(place, [h0], across, lambda odd: odd, 3)
    q0 = moved(q0_own, 1, 0)
    h2 = multiply(place, [after(c2, q0_own)], prior)
    q2_own = product_two(place, h2, across, q0_own)
    q2 = moved(q2_own, 1, 2)

    h3 = multiply(place, c3, prior)
    q3_two = moved(multiply(place, [h3], across, lambda odd: 2 - odd, 1), 1, 3)
    q3_own, q30 = product_three(place, h3, across)
    q3_other = moved(q3_own, 1, 3)
    q0_last = moved(q30, 1, 0)
    across = turn(place, 3, 0, c3[0], after(across, q30))
    across = turn(place, 3, 1, c3[1], across)
    q33 = multiply(place, [h3], across, lambda odd: 3 - 3 * odd, 1)
    q3_last = moved(q33, 1, 3)
    q2_last = moved(after(q3_two, q0, q33), 3, 2)
    h1 = multiply(place, [after(c1[0], q33), c1[1]], prior)
    q11 = multiply(place, [h1], across, lambda odd: 1 + odd, 1)
    received = (q0, q0_last, q2, q2, q2_last, q3_two, q3_other, q3_last)
    kept = (q0_own, q11, q2_own, q3_own)
    covariance, variances = final(place, pivot, sigma, received, kept)
    return (covariance[None], variances)


def gathered(sigma_next, separator, inverse_pivot, coupling_rate, lengths, step_index, node_class):
    shifted = passed_along(separator, "dom", -1)
    prior = jnp.where(step_index[0] == 0, shifted[0], sigma_next[0])
    pivot = inverse_pivot[0].astype(F32)
    coupled = couple(inverse_pivot[0], node_class, coupling_rate)
    rows = coupled.shape[0]
    half = jnp.dot(
        coupled,
        lax.all_gather(prior, "col", axis=0, tiled=True),
        preferred_element_type=F32,
    ).astype(BF16)
    product = lax.dot_general(
        half,
        lax.all_gather(coupled, "col", axis=0, tiled=True),
        (((1,), (1,)), ((), ())),
        preferred_element_type=F32,
    )
    full = pivot + product
    active = step_index[0] < lengths[0]
    old = sigma_next[0]
    covariance = jnp.where(active, full.astype(BF16), old)
    first_col = lax.axis_index("col") * rows
    new_block = lax.dynamic_slice_in_dim(full, first_col, rows, 1)
    old_block = lax.dynamic_slice_in_dim(old, first_col, rows, 1)
    variances = jnp.where(active, jnp.diagonal(new_block), jnp.diagonal(old_block).astype(F32))
    return (covariance[None], variances[None])


def solution(mesh):
    local = owned if mesh.shape["col"] == 4 and mesh.shape["dom"] % 2 == 0 else gathered
    return jax.shard_map(
        local,
        mesh=mesh,
        in_specs=(
            P(("groups", "dom"), "col", None),
            P(("groups", "dom"), "col", None),
            P(("groups", "dom"), "col", None),
            P(("groups", "dom")),
            P(("groups", "dom")),
            P(("groups", "dom")),
            P("groups"),
        ),
        out_specs=(P(("groups", "dom"), "col", None), P(("groups", "dom"), "col")),
        check_vma=False,
    )
```

```python
import functools

import jax
import jax.numpy as jnp
from jax import lax
from jax.experimental import pallas as pl
from jax.experimental.pallas import tpu as pltpu
from jax.sharding import PartitionSpec as P

GX = 64
GY = 32
BF16 = jnp.bfloat16
F32 = jnp.float32
MIB = 1 << 20


def passed_along(value, axis, steps):
    count = lax.axis_size(axis)
    initial, last = (max(0, -steps), min(count, count - steps))
    return lax.ppermute(value, axis, [(source, source + steps) for source in range(initial, last)])


LIGHT = pl.CostEstimate(flops=1 << 20, bytes_accessed=1 << 16, transcendentals=0)


def couple_kernel(rate_ref, class_ref, pivot_ref, out_ref, weight_ref):
    nodes = pivot_ref.shape[1]

    @pl.when(pl.program_id(0) == 0)
    def _():
        kind = class_ref[...]
        across = jnp.where(
            kind == 0, 0.25, jnp.where(kind == 1, 0.375, jnp.where(kind == 2, 0.125, 0.5))
        ).astype(F32)
        along = jnp.where(
            kind == 0, 0.25, jnp.where(kind == 1, 0.125, jnp.where(kind == 2, 0.375, 0.0))
        ).astype(F32)
        node = lax.broadcasted_iota(jnp.int32, (1, nodes), 1)
        column = node % GX
        parts = (
            jnp.where(column > 0, across, 0.0),
            jnp.where(column < GX - 1, across, 0.0),
            jnp.where(node >= GX, along, 0.0),
            jnp.where(node < nodes - GX, along, 0.0),
        )
        for which, part in enumerate(parts):
            weight_ref[which] = jnp.broadcast_to(part, (16, nodes))

    rate = rate_ref[0]

    def group(step, carry):
        rows = pl.ds(pl.multiple_of(step * 16, 16), 16)
        value = pivot_ref[rows, :].astype(F32)
        total = (
            value
            + weight_ref[0] * pltpu.roll(value, 1, 1)
            + weight_ref[1] * pltpu.roll(value, nodes - 1, 1)
            + weight_ref[2] * pltpu.roll(value, GX, 1)
            + weight_ref[3] * pltpu.roll(value, nodes - GX, 1)
        )
        out_ref[rows, :] = (rate * total).astype(BF16)
        return carry

    lax.fori_loop(0, pivot_ref.shape[0] // 16, group, 0)


def couple(pivot, node_class, rate, part=0, parts=1):
    rows, nodes = pivot.shape[0] // parts, pivot.shape[1]
    chunk = min(rows, 128)
    steps = rows // chunk
    return pl.pallas_call(
        couple_kernel,
        out_shape=jax.ShapeDtypeStruct((rows, nodes), BF16),
        grid=(steps,),
        in_specs=[
            pl.BlockSpec(memory_space=pltpu.SMEM),
            pl.BlockSpec((1, nodes), lambda i: (0, 0)),
            pl.BlockSpec((chunk, nodes), lambda i: (part * steps + i, 0)),
        ],
        out_specs=pl.BlockSpec((chunk, nodes), lambda i: (i, 0)),
        scratch_shapes=[pltpu.VMEM((4, 16, nodes), F32)],
        compiler_params=pltpu.CompilerParams(vmem_limit_bytes=6 * MIB),
        cost_estimate=LIGHT,
        name="couple",
    )(rate, node_class.reshape(1, nodes), pivot)


def turned(block, odd):
    return block + odd * (3 - 2 * block)


def route(source, target, doms):
    pairs = []
    for dom in range(doms):
        odd = dom % 2
        pairs.append((dom * 4 + turned(source, odd), dom * 4 + turned(target, odd)))
    return pairs


def moved(value, source, target):
    return lax.ppermute(value, ("dom", "col"), route(source, target, lax.axis_size("dom")))


def couple_here(place, pivot, node_class, rate):
    rows, nodes = pivot.shape
    chunk = 128

    def kernel(place_ref, *refs):
        @pl.when(place_ref[1] == 1)
        def _():
            couple_kernel(*refs)

    return pl.pallas_call(
        kernel,
        out_shape=jax.ShapeDtypeStruct((rows, nodes), BF16),
        grid_spec=pltpu.PrefetchScalarGridSpec(
            num_scalar_prefetch=1,
            grid=(rows // chunk,),
            in_specs=[
                pl.BlockSpec(memory_space=pltpu.SMEM),
                pl.BlockSpec((1, nodes), lambda i, place: (0, 0)),
                pl.BlockSpec((chunk, nodes), lambda i, place: (i, 0)),
            ],
            out_specs=pl.BlockSpec((chunk, nodes), lambda i, place: (i, 0)),
            scratch_shapes=[pltpu.VMEM((4, 16, nodes), F32)],
        ),
        compiler_params=pltpu.CompilerParams(vmem_limit_bytes=8 * MIB),
        cost_estimate=LIGHT,
        name="couple_here",
    )(place, rate, node_class.reshape(1, nodes), pivot)


def turn_kernel(place_ref, coupled_ref, *refs):
    @pl.when(place_ref[1] == 1)
    def _():
        refs[-1][...] = coupled_ref[...].T


def turn(place, panel, part, coupled, across):
    rows, nodes = coupled.shape
    chunk = 128
    steps = rows // chunk
    ratio = nodes // 4 // chunk
    return pl.pallas_call(
        turn_kernel,
        out_shape=jax.ShapeDtypeStruct((nodes, nodes), BF16),
        grid_spec=pltpu.PrefetchScalarGridSpec(
            num_scalar_prefetch=1,
            grid=(steps,),
            in_specs=[pl.BlockSpec((chunk, nodes), lambda i, place: (i, 0))]
            + ([] if across is None else [pl.BlockSpec(memory_space=pl.ANY)]),
            out_specs=pl.BlockSpec(
                (nodes, chunk),
                lambda i, place: (0, turned(panel, place[0]) * ratio + part * steps + i),
            ),
        ),
        input_output_aliases={} if across is None else {2: 0},
        compiler_params=pltpu.CompilerParams(vmem_limit_bytes=4 * MIB),
        cost_estimate=LIGHT,
        name="turn",
    )(place, coupled, *(() if across is None else (across,)))


def multiply_kernel(first, count, lefts, place_ref, *refs):
    left_refs, right_ref, out_ref = refs[:lefts], refs[lefts], refs[-1]
    width = right_ref.shape[0] // 4

    @pl.when(place_ref[1] == 1)
    def _():
        def block(step, carry):
            source = pl.multiple_of((first(place_ref[0]) + step) * width, 128)
            target = pl.multiple_of(step * width, 128)
            row = 0
            for left_ref in left_refs:
                rows = left_ref.shape[0]
                out_ref[row : row + rows, pl.ds(target, width)] = jnp.dot(
                    left_ref[...], right_ref[:, pl.ds(source, width)], preferred_element_type=F32
                ).astype(BF16)
                row += rows
            return carry

        lax.fori_loop(0, count, block, 0)


def multiply(place, lefts, right, first=lambda odd: 0, count=4):
    rows = sum(left.shape[0] for left in lefts)
    width = right.shape[0] // 4
    vmem = pl.BlockSpec(memory_space=pltpu.VMEM)
    return pl.pallas_call(
        functools.partial(multiply_kernel, first, count, len(lefts)),
        out_shape=jax.ShapeDtypeStruct((rows, count * width), BF16),
        in_specs=[pl.BlockSpec(memory_space=pltpu.SMEM)] + [vmem] * (len(lefts) + 1),
        out_specs=vmem,
        compiler_params=pltpu.CompilerParams(vmem_limit_bytes=6 * MIB),
        cost_estimate=LIGHT,
        name="multiply",
    )(place, *lefts, right)


def two_kernel(place_ref, left_ref, right_ref, zero_ref, out_ref):
    odd = place_ref[0]
    width = right_ref.shape[0] // 4
    multiply_kernel(lambda odd: 1, 2, 1, place_ref, left_ref, right_ref, out_ref)

    @pl.when(place_ref[1] == 1)
    def _():
        out_ref[:, 2 * width :] = zero_ref[:, pl.ds(pl.multiple_of((2 - 2 * odd) * width, 128), width)]


def product_two(place, half, across, zero):
    rows = half.shape[0]
    width = across.shape[0] // 4
    vmem = pl.BlockSpec(memory_space=pltpu.VMEM)
    return pl.pallas_call(
        two_kernel,
        out_shape=jax.ShapeDtypeStruct((rows, 3 * width), BF16),
        in_specs=[pl.BlockSpec(memory_space=pltpu.SMEM)] + [vmem] * 3,
        out_specs=vmem,
        compiler_params=pltpu.CompilerParams(vmem_limit_bytes=6 * MIB),
        cost_estimate=LIGHT,
        name="product_two",
    )(place, half, across, zero)


def ends_kernel(place_ref, left_ref, right_ref, zero_ref, two_ref):
    for block, out_ref in ((0, zero_ref), (2, two_ref)):
        first = lambda odd: turned(block, odd)
        multiply_kernel(first, 1, 1, place_ref, left_ref, right_ref, out_ref)


def product_ends(place, half, across):
    rows = half.shape[0]
    width = across.shape[0] // 4
    vmem = pl.BlockSpec(memory_space=pltpu.VMEM)
    return pl.pallas_call(
        ends_kernel,
        out_shape=(jax.ShapeDtypeStruct((rows, width), BF16),) * 2,
        in_specs=[pl.BlockSpec(memory_space=pltpu.SMEM)] + [vmem] * 2,
        out_specs=(vmem, vmem),
        compiler_params=pltpu.CompilerParams(vmem_limit_bytes=6 * MIB),
        cost_estimate=LIGHT,
        name="product_ends",
    )(place, half, across)


def other_kernel(place_ref, left_ref, right_ref, zero_ref, out_ref):
    odd = place_ref[0]
    width = zero_ref.shape[1]

    @pl.when(place_ref[1] == 1)
    def _():
        out_ref[:, pl.ds(pl.multiple_of(odd * width, 128), width)] = zero_ref[...]
        source = pl.multiple_of((1 + odd) * width, 128)
        target = pl.multiple_of((1 - odd) * width, 128)
        out_ref[:, pl.ds(target, width)] = jnp.dot(
            left_ref[...], right_ref[:, pl.ds(source, width)], preferred_element_type=F32
        ).astype(BF16)


def product_other(place, half, across, zero):
    rows = half.shape[0]
    width = across.shape[0] // 4
    vmem = pl.BlockSpec(memory_space=pltpu.VMEM)
    return pl.pallas_call(
        other_kernel,
        out_shape=jax.ShapeDtypeStruct((rows, 2 * width), BF16),
        in_specs=[pl.BlockSpec(memory_space=pltpu.SMEM)] + [vmem] * 3,
        out_specs=vmem,
        compiler_params=pltpu.CompilerParams(vmem_limit_bytes=6 * MIB),
        cost_estimate=LIGHT,
        name="product_other",
    )(place, half, across, zero)


def prior_kernel(place_ref, shifted_ref, sigma_ref, out_ref):
    @pl.when(place_ref[3] == 0)
    def _():
        out_ref[...] = shifted_ref[...]

    @pl.when(place_ref[3] != 0)
    def _():
        out_ref[...] = sigma_ref[...]


def parts_kernel(place_ref, shifted_ref, sigma_ref, row_ref, two_ref, zero_ref, last_ref):
    odd = place_ref[0]
    width = last_ref.shape[1]

    def at(block, count=1):
        return pl.ds(pl.multiple_of(block * width, 128), count * width)

    prior_kernel(place_ref, shifted_ref, sigma_ref, row_ref)
    first, last = row_ref[:, at(3 * odd)], row_ref[:, at(3 - 3 * odd)]
    two_ref[:, :width] = first
    two_ref[:, width:] = row_ref[:, at(2 - 2 * odd, 2)]
    zero_ref[:, :width] = first
    zero_ref[:, width:] = last
    last_ref[...] = last


def prior_parts(place, shifted, sigma):
    rows, nodes = sigma.shape
    chunk = 128
    width = nodes // 4
    out = lambda blocks: jax.ShapeDtypeStruct((rows, blocks * width), BF16)
    spec = lambda blocks: pl.BlockSpec((chunk, blocks * width), lambda i, place: (i, 0))
    return pl.pallas_call(
        parts_kernel,
        out_shape=(out(4), out(3), out(2), out(1)),
        grid_spec=pltpu.PrefetchScalarGridSpec(
            num_scalar_prefetch=1,
            grid=(rows // chunk,),
            in_specs=[
                pl.BlockSpec(
                    (chunk, nodes), lambda i, place: (jnp.where(place[3] == 0, i, 0), 0)
                ),
                pl.BlockSpec(
                    (chunk, nodes), lambda i, place: (jnp.where(place[3] == 0, 0, i), 0)
                ),
            ],
            out_specs=(spec(4), spec(3), spec(2), spec(1)),
        ),
        compiler_params=pltpu.CompilerParams(vmem_limit_bytes=8 * MIB),
        cost_estimate=LIGHT,
        name="prior_parts",
    )(place, shifted, sigma)


def assemble_kernel(place_ref, own, two, zero, three, out_ref):
    @pl.when(place_ref[1] == 1)
    def _():
        odd = place_ref[0]
        width = three.shape[1]

        def at(block, count=1):
            return pl.ds(pl.multiple_of(block * width, 128), count * width)

        near = 2 * (1 - odd)
        row = [turned(block, odd) for block in range(4)]
        out_ref[at(row[1]), :] = own[...]
        out_ref[at(row[2]), at(row[0])] = two[:, :width]
        out_ref[at(row[2]), at(near, 2)] = two[:, width:]
        out_ref[at(row[0]), at(row[0])] = zero[:, :width]
        out_ref[at(row[0]), at(row[3])] = zero[:, width:]
        out_ref[at(row[3]), at(row[3])] = three[...]
        for block in (0, 2, 3):
            out_ref[at(row[block]), at(row[1])] = own[:, at(row[block])].T
        out_ref[at(row[0]), at(row[2])] = two[:, :width].T
        out_ref[at(row[3]), at(row[2])] = two[:, at(2 - odd)].T
        out_ref[at(row[3]), at(row[0])] = zero[:, width:].T


def assemble(place, *parts):
    nodes = parts[0].shape[1]
    vmem = pl.BlockSpec(memory_space=pltpu.VMEM)
    return pl.pallas_call(
        assemble_kernel,
        out_shape=jax.ShapeDtypeStruct((nodes, nodes), BF16),
        in_specs=[pl.BlockSpec(memory_space=pltpu.SMEM)] + [vmem] * 4,
        out_specs=vmem,
        compiler_params=pltpu.CompilerParams(vmem_limit_bytes=6 * MIB),
        cost_estimate=LIGHT,
        name="assemble",
    )(place, *parts)


def finish_kernel(place_ref, pivot_ref, *refs):
    sigma_ref, q0, q2, q2_zero, q3_two, q3_other, q01, q11, q21, out_ref, var_ref = refs
    rows, nodes = pivot_ref.shape
    width = nodes // 4
    odd, place = place_ref[0], place_ref[1]
    here = pl.multiple_of(pl.program_id(0) * rows, 128)
    diagonal = diagonal_of(rows)

    def at(block, count=1):
        return pl.ds(pl.multiple_of(block * width, 128), count * width)

    def own(block):
        return pl.ds(pl.multiple_of(block * width + here, 128), rows)

    def add(columns, product):
        out_ref[:, columns] = (pivot_ref[:, columns].astype(F32) + product.astype(F32)).astype(BF16)

    def trace(product):
        var_ref[...] = diagonal(pivot_ref[:, own(place_ref[2])].astype(F32) + product.astype(F32))

    active = place_ref[4] != 0

    @pl.when(active & (place == 0))
    def _():
        add(at(odd, 3), q0[...])
        trace(q0[:, own(2 * odd)])

    @pl.when(active & (place == 1))
    def _():
        add(at(turned(0, odd)), q01[...].T)
        add(at(turned(1, odd)), q11[...])
        add(at(turned(2, odd)), q21[...].T)
        trace(q11[:, pl.ds(here, rows)])

    @pl.when(active & (place == 2))
    def _():
        add(at(turned(0, odd)), q2_zero[:, pl.ds(here, rows)].T)
        add(at(1, 2), q2[...])
        trace(q2[:, own(1 - odd)])

    @pl.when(active & (place == 3))
    def _():
        add(at(2 * odd, 2), q3_other[...])
        add(at(turned(2, odd)), q3_two[...])

    @pl.when(jnp.logical_not(active))
    def _():
        out_ref[...] = sigma_ref[...]
        var_ref[...] = diagonal(sigma_ref[:, own(place_ref[2])].astype(F32))


def diagonal_of(rows):
    square = (rows, rows)
    on_diagonal = lax.broadcasted_iota(jnp.int32, square, 0) == lax.broadcasted_iota(
        jnp.int32, square, 1
    )
    return lambda value: jnp.sum(jnp.where(on_diagonal, value, 0.0), axis=0, keepdims=True)


def last_kernel(place_ref, pivot_ref, *refs):
    q0_last, q2_last, q3_last, q31, old_ref, old_var_ref, out_ref, var_ref = refs
    rows = pivot_ref.shape[0]
    place = place_ref[1]
    here = pl.ds(pl.multiple_of(pl.program_id(0) * rows, 128), rows)
    active = place_ref[4] != 0

    def add(product):
        out_ref[...] = (pivot_ref[...].astype(F32) + product.astype(F32)).astype(BF16)

    out_ref[...] = old_ref[...]
    var_ref[...] = old_var_ref[...]

    @pl.when(active & (place == 0))
    def _():
        add(q0_last[:, here].T)

    @pl.when(active & (place == 1))
    def _():
        add(q31[...].T)

    @pl.when(active & (place == 2))
    def _():
        add(q2_last[:, here].T)

    @pl.when(active & (place == 3))
    def _():
        add(q3_last[...])
        var_ref[...] = diagonal_of(rows)(
            pivot_ref[:, here].astype(F32) + q3_last[:, here].astype(F32)
        )


def finish(place, pivot, sigma, products):
    rows, nodes = pivot.shape
    chunk = 128
    width = nodes // 4

    def picked(which, blocks):
        return pl.BlockSpec(
            (chunk, blocks * width), lambda i, place: (jnp.where(place[1] == which, i, 0), 0)
        )

    def turned_block(start):
        return pl.BlockSpec(
            (rows, chunk),
            lambda i, place: (
                0,
                jnp.where(place[1] == 1, start(place[0]) * (width // chunk) + i, 0),
            ),
        )

    return pl.pallas_call(
        finish_kernel,
        out_shape=(
            jax.ShapeDtypeStruct((rows, nodes), BF16),
            jax.ShapeDtypeStruct((1, rows), F32),
        ),
        grid_spec=pltpu.PrefetchScalarGridSpec(
            num_scalar_prefetch=1,
            grid=(rows // chunk,),
            in_specs=[
                pl.BlockSpec((chunk, nodes), lambda i, place: (i, 0)),
                pl.BlockSpec((chunk, nodes), lambda i, place: (jnp.where(place[4] == 0, i, 0), 0)),
                picked(0, 3),
                picked(2, 2),
                pl.BlockSpec((rows, width), lambda i, place: (0, 2)),
                picked(3, 1),
                picked(3, 2),
                turned_block(lambda odd: 1),
                picked(1, 1),
                turned_block(lambda odd: odd),
            ],
            out_specs=(
                pl.BlockSpec((chunk, nodes), lambda i, place: (i, 0)),
                pl.BlockSpec((1, chunk), lambda i, place: (0, i)),
            ),
        ),
        compiler_params=pltpu.CompilerParams(vmem_limit_bytes=12 * MIB),
        cost_estimate=LIGHT,
        name="finish",
    )(place, pivot, sigma, *products)


def finish_last(place, pivot, products, covariance, variances):
    rows, nodes = pivot.shape
    chunk = 128
    width = nodes // 4
    column = lambda place: 3 - 3 * place[0]
    whole = pl.BlockSpec((rows, width), lambda i, place: (0, 0))
    block = pl.BlockSpec((chunk, width), lambda i, place: (i, column(place)))
    variance = pl.BlockSpec((1, chunk), lambda i, place: (0, i))
    return pl.pallas_call(
        last_kernel,
        out_shape=(
            jax.ShapeDtypeStruct((rows, nodes), BF16),
            jax.ShapeDtypeStruct((1, rows), F32),
        ),
        grid_spec=pltpu.PrefetchScalarGridSpec(
            num_scalar_prefetch=1,
            grid=(rows // chunk,),
            in_specs=[
                block,
                whole,
                whole,
                pl.BlockSpec((chunk, width), lambda i, place: (i, 0)),
                pl.BlockSpec(
                    (rows, chunk), lambda i, place: (0, (1 - place[0]) * (width // chunk) + i)
                ),
                block,
                variance,
            ],
            out_specs=(block, variance),
        ),
        input_output_aliases={6: 0, 7: 1},
        compiler_params=pltpu.CompilerParams(vmem_limit_bytes=12 * MIB),
        cost_estimate=LIGHT,
        name="finish_last",
    )(place, pivot, *products, covariance, variances)


def owned(sigma_next, separator, inverse_pivot, coupling_rate, lengths, step_index, node_class):
    sigma, pivot = sigma_next[0], inverse_pivot[0]
    odd = lax.axis_index("dom") % 2
    col = lax.axis_index("col")
    step = step_index[0]
    place = jnp.stack([odd, turned(col, odd), col, step, step < lengths[0]]).astype(jnp.int32)
    after = lambda value, *others: lax.optimization_barrier((value, *others))[0]

    shifted = passed_along(separator, "dom", -1)[0]
    p0 = moved(pivot, 0, 1)
    p2 = moved(pivot, 2, 1)
    c1 = [couple(pivot, node_class, coupling_rate, part, 2) for part in range(2)]
    across = turn(place, 1, 0, c1[0], None)
    across = turn(place, 1, 1, c1[1], across)

    row, two, zero, last = prior_parts(place, after(shifted, across), sigma)
    zero, two, three = moved(zero, 0, 1), moved(two, 2, 1), moved(last, 3, 1)

    c0 = couple_here(place, after(p0, last), node_class, coupling_rate)
    across = turn(place, 0, 0, c0, across)
    c2 = couple_here(place, after(p2, across), node_class, coupling_rate)
    across = turn(place, 2, 0, c2, across)
    c3 = [
        moved(after(c1[0], three, zero, across), 3, 1),
        moved(after(c1[1], two), 3, 1),
    ]
    prior = assemble(place, row, two, zero, three)

    h0 = multiply(place, [c0], prior)
    q0_own = multiply(place, [h0], across, lambda odd: odd, 3)
    q0 = moved(q0_own, 1, 0)
    h2 = multiply(place, [after(c2, q0_own)], prior)
    q2_own = product_two(place, h2, across, q0_own)
    q2 = moved(q2_own, 1, 2)

    h3 = multiply(place, c3, prior)
    q30, q32 = product_ends(place, h3, across)
    q0_last, q3_two = moved(q30, 1, 0), moved(q32, 1, 3)
    q3_own = product_other(place, h3, across, q30)
    q3_other = moved(q3_own, 1, 3)
    across = turn(place, 3, 0, c3[0], after(across, q3_own, q0_last))
    across = turn(place, 3, 1, c3[1], after(across, q3_two))
    q33 = multiply(place, [h3], across, lambda odd: 3 - 3 * odd, 1)
    q3_last = moved(q33, 1, 3)
    h1 = multiply(place, [after(c1[0], q33), c1[1]], prior)
    q11 = multiply(place, [h1], across, lambda odd: 1 + odd, 1)
    q2_last = moved(after(q3_two, q0, q33), 3, 2)
    products = (q0, q2, q2, q3_two, q3_other, q0_own, q11, q2_own)
    covariance, variances = finish(place, pivot, sigma, products)
    products = (q0_last, q2_last, q3_last, q3_own)
    covariance, variances = finish_last(place, pivot, products, covariance, variances)
    return (covariance[None], variances)


def gathered(sigma_next, separator, inverse_pivot, coupling_rate, lengths, step_index, node_class):
    shifted = passed_along(separator, "dom", -1)
    prior = jnp.where(step_index[0] == 0, shifted[0], sigma_next[0])
    pivot = inverse_pivot[0].astype(F32)
    coupled = couple(inverse_pivot[0], node_class, coupling_rate)
    rows = coupled.shape[0]
    half = jnp.dot(
        coupled,
        lax.all_gather(prior, "col", axis=0, tiled=True),
        preferred_element_type=F32,
    ).astype(BF16)
    product = lax.dot_general(
        half,
        lax.all_gather(coupled, "col", axis=0, tiled=True),
        (((1,), (1,)), ((), ())),
        preferred_element_type=F32,
    )
    full = pivot + product
    active = step_index[0] < lengths[0]
    old = sigma_next[0]
    covariance = jnp.where(active, full.astype(BF16), old)
    first_col = lax.axis_index("col") * rows
    new_block = lax.dynamic_slice_in_dim(full, first_col, rows, 1)
    old_block = lax.dynamic_slice_in_dim(old, first_col, rows, 1)
    variances = jnp.where(active, jnp.diagonal(new_block), jnp.diagonal(old_block).astype(F32))
    return (covariance[None], variances[None])


def solution(mesh):
    local = owned if mesh.shape["col"] == 4 and mesh.shape["dom"] % 2 == 0 else gathered
    return jax.shard_map(
        local,
        mesh=mesh,
        in_specs=(
            P(("groups", "dom"), "col", None),
            P(("groups", "dom"), "col", None),
            P(("groups", "dom"), "col", None),
            P(("groups", "dom")),
            P(("groups", "dom")),
            P(("groups", "dom")),
            P("groups"),
        ),
        out_specs=(P(("groups", "dom"), "col", None), P(("groups", "dom"), "col")),
        check_vma=False,
    )
```

```python
import functools

import jax
import jax.numpy as jnp
from jax import lax
from jax.experimental import pallas as pl
from jax.experimental.pallas import tpu as pltpu
from jax.sharding import PartitionSpec as P

GX = 64
GY = 32
BF16 = jnp.bfloat16
F32 = jnp.float32
MIB = 1 << 20


def passed_along(value, axis, steps):
    count = lax.axis_size(axis)
    initial, last = (max(0, -steps), min(count, count - steps))
    return lax.ppermute(value, axis, [(source, source + steps) for source in range(initial, last)])


LIGHT = pl.CostEstimate(flops=1 << 20, bytes_accessed=1 << 16, transcendentals=0)


def couple_kernel(rate_ref, class_ref, pivot_ref, out_ref, weight_ref):
    nodes = pivot_ref.shape[1]

    @pl.when(pl.program_id(0) == 0)
    def _():
        kind = class_ref[...]
        across = jnp.where(
            kind == 0, 0.25, jnp.where(kind == 1, 0.375, jnp.where(kind == 2, 0.125, 0.5))
        ).astype(F32)
        along = jnp.where(
            kind == 0, 0.25, jnp.where(kind == 1, 0.125, jnp.where(kind == 2, 0.375, 0.0))
        ).astype(F32)
        node = lax.broadcasted_iota(jnp.int32, (1, nodes), 1)
        column = node % GX
        parts = (
            jnp.where(column > 0, across, 0.0),
            jnp.where(column < GX - 1, across, 0.0),
            jnp.where(node >= GX, along, 0.0),
            jnp.where(node < nodes - GX, along, 0.0),
        )
        for which, part in enumerate(parts):
            weight_ref[which] = jnp.broadcast_to(part, (16, nodes))

    rate = rate_ref[0]

    def group(step, carry):
        rows = pl.ds(pl.multiple_of(step * 16, 16), 16)
        value = pivot_ref[rows, :].astype(F32)
        total = (
            value
            + weight_ref[0] * pltpu.roll(value, 1, 1)
            + weight_ref[1] * pltpu.roll(value, nodes - 1, 1)
            + weight_ref[2] * pltpu.roll(value, GX, 1)
            + weight_ref[3] * pltpu.roll(value, nodes - GX, 1)
        )
        out_ref[rows, :] = (rate * total).astype(BF16)
        return carry

    lax.fori_loop(0, pivot_ref.shape[0] // 16, group, 0)


def couple(pivot, node_class, rate, part=0, parts=1):
    rows, nodes = pivot.shape[0] // parts, pivot.shape[1]
    chunk = min(rows, 128)
    steps = rows // chunk
    return pl.pallas_call(
        couple_kernel,
        out_shape=jax.ShapeDtypeStruct((rows, nodes), BF16),
        grid=(steps,),
        in_specs=[
            pl.BlockSpec(memory_space=pltpu.SMEM),
            pl.BlockSpec((1, nodes), lambda i: (0, 0)),
            pl.BlockSpec((chunk, nodes), lambda i: (part * steps + i, 0)),
        ],
        out_specs=pl.BlockSpec((chunk, nodes), lambda i: (i, 0)),
        scratch_shapes=[pltpu.VMEM((4, 16, nodes), F32)],
        compiler_params=pltpu.CompilerParams(vmem_limit_bytes=6 * MIB),
        cost_estimate=LIGHT,
        name="couple",
    )(rate, node_class.reshape(1, nodes), pivot)


def turned(block, odd):
    return block + odd * (3 - 2 * block)


def route(source, target, doms):
    pairs = []
    for dom in range(doms):
        odd = dom % 2
        pairs.append((dom * 4 + turned(source, odd), dom * 4 + turned(target, odd)))
    return pairs


def moved(value, source, target):
    return lax.ppermute(value, ("dom", "col"), route(source, target, lax.axis_size("dom")))


def couple_here(place, pivot, node_class, rate):
    rows, nodes = pivot.shape
    chunk = 128

    def kernel(place_ref, *refs):
        @pl.when(place_ref[1] == 1)
        def _():
            couple_kernel(*refs)

    return pl.pallas_call(
        kernel,
        out_shape=jax.ShapeDtypeStruct((rows, nodes), BF16),
        grid_spec=pltpu.PrefetchScalarGridSpec(
            num_scalar_prefetch=1,
            grid=(rows // chunk,),
            in_specs=[
                pl.BlockSpec(memory_space=pltpu.SMEM),
                pl.BlockSpec((1, nodes), lambda i, place: (0, 0)),
                pl.BlockSpec((chunk, nodes), lambda i, place: (i, 0)),
            ],
            out_specs=pl.BlockSpec((chunk, nodes), lambda i, place: (i, 0)),
            scratch_shapes=[pltpu.VMEM((4, 16, nodes), F32)],
        ),
        compiler_params=pltpu.CompilerParams(vmem_limit_bytes=8 * MIB),
        cost_estimate=LIGHT,
        name="couple_here",
    )(place, rate, node_class.reshape(1, nodes), pivot)


def turn_kernel(place_ref, coupled_ref, *refs):
    @pl.when(place_ref[1] == 1)
    def _():
        refs[-1][...] = coupled_ref[...].T


def turn(place, panel, coupled, across):
    rows, nodes = coupled.shape
    chunk = 128
    steps = rows // chunk
    return pl.pallas_call(
        turn_kernel,
        out_shape=jax.ShapeDtypeStruct((nodes, nodes), BF16),
        grid_spec=pltpu.PrefetchScalarGridSpec(
            num_scalar_prefetch=1,
            grid=(steps,),
            in_specs=[pl.BlockSpec((chunk, nodes), lambda i, place: (i, 0))]
            + ([] if across is None else [pl.BlockSpec(memory_space=pl.ANY)]),
            out_specs=pl.BlockSpec(
                (nodes, chunk), lambda i, place: (0, turned(panel, place[0]) * steps + i)
            ),
        ),
        input_output_aliases={} if across is None else {2: 0},
        compiler_params=pltpu.CompilerParams(vmem_limit_bytes=4 * MIB),
        cost_estimate=LIGHT,
        name="turn",
    )(place, coupled, *(() if across is None else (across,)))


def multiply_kernel(first, count, lefts, place_ref, *refs):
    left_refs, right_ref, out_ref = refs[:lefts], refs[lefts], refs[-1]
    width = right_ref.shape[0] // 4

    @pl.when(place_ref[1] == 1)
    def _():
        def block(step, carry):
            source = pl.multiple_of((first(place_ref[0]) + step) * width, 128)
            target = pl.multiple_of(step * width, 128)
            row = 0
            for left_ref in left_refs:
                rows = left_ref.shape[0]
                out_ref[row : row + rows, pl.ds(target, width)] = jnp.dot(
                    left_ref[...], right_ref[:, pl.ds(source, width)], preferred_element_type=F32
                ).astype(BF16)
                row += rows
            return carry

        lax.fori_loop(0, count, block, 0)


def multiply(place, lefts, right, first=lambda odd: 0, count=4):
    rows = sum(left.shape[0] for left in lefts)
    width = right.shape[0] // 4
    vmem = pl.BlockSpec(memory_space=pltpu.VMEM)
    return pl.pallas_call(
        functools.partial(multiply_kernel, first, count, len(lefts)),
        out_shape=jax.ShapeDtypeStruct((rows, count * width), BF16),
        in_specs=[pl.BlockSpec(memory_space=pltpu.SMEM)] + [vmem] * (len(lefts) + 1),
        out_specs=vmem,
        compiler_params=pltpu.CompilerParams(vmem_limit_bytes=6 * MIB),
        cost_estimate=LIGHT,
        name="multiply",
    )(place, *lefts, right)


def two_kernel(place_ref, left_ref, right_ref, zero_ref, out_ref):
    odd = place_ref[0]
    width = right_ref.shape[0] // 4
    multiply_kernel(lambda odd: 1, 2, 1, place_ref, left_ref, right_ref, out_ref)

    @pl.when(place_ref[1] == 1)
    def _():
        out_ref[:, 2 * width :] = zero_ref[:, pl.ds(pl.multiple_of((2 - 2 * odd) * width, 128), width)]


def product_two(place, half, across, zero):
    rows = half.shape[0]
    width = across.shape[0] // 4
    vmem = pl.BlockSpec(memory_space=pltpu.VMEM)
    return pl.pallas_call(
        two_kernel,
        out_shape=jax.ShapeDtypeStruct((rows, 3 * width), BF16),
        in_specs=[pl.BlockSpec(memory_space=pltpu.SMEM)] + [vmem] * 3,
        out_specs=vmem,
        compiler_params=pltpu.CompilerParams(vmem_limit_bytes=6 * MIB),
        cost_estimate=LIGHT,
        name="product_two",
    )(place, half, across, zero)


def ends_kernel(place_ref, left_ref, right_ref, zero_ref, two_ref):
    for block, out_ref in ((0, zero_ref), (2, two_ref)):
        first = lambda odd: turned(block, odd)
        multiply_kernel(first, 1, 1, place_ref, left_ref, right_ref, out_ref)


def product_ends(place, half, across):
    rows = half.shape[0]
    width = across.shape[0] // 4
    vmem = pl.BlockSpec(memory_space=pltpu.VMEM)
    return pl.pallas_call(
        ends_kernel,
        out_shape=(jax.ShapeDtypeStruct((rows, width), BF16),) * 2,
        in_specs=[pl.BlockSpec(memory_space=pltpu.SMEM)] + [vmem] * 2,
        out_specs=(vmem, vmem),
        compiler_params=pltpu.CompilerParams(vmem_limit_bytes=6 * MIB),
        cost_estimate=LIGHT,
        name="product_ends",
    )(place, half, across)


def other_kernel(place_ref, left_ref, right_ref, zero_ref, out_ref):
    odd = place_ref[0]
    width = zero_ref.shape[1]

    @pl.when(place_ref[1] == 1)
    def _():
        out_ref[:, pl.ds(pl.multiple_of(odd * width, 128), width)] = zero_ref[...]
        source = pl.multiple_of((1 + odd) * width, 128)
        target = pl.multiple_of((1 - odd) * width, 128)
        out_ref[:, pl.ds(target, width)] = jnp.dot(
            left_ref[...], right_ref[:, pl.ds(source, width)], preferred_element_type=F32
        ).astype(BF16)


def product_other(place, half, across, zero):
    rows = half.shape[0]
    width = across.shape[0] // 4
    vmem = pl.BlockSpec(memory_space=pltpu.VMEM)
    return pl.pallas_call(
        other_kernel,
        out_shape=jax.ShapeDtypeStruct((rows, 2 * width), BF16),
        in_specs=[pl.BlockSpec(memory_space=pltpu.SMEM)] + [vmem] * 3,
        out_specs=vmem,
        compiler_params=pltpu.CompilerParams(vmem_limit_bytes=6 * MIB),
        cost_estimate=LIGHT,
        name="product_other",
    )(place, half, across, zero)


def prior_kernel(place_ref, shifted_ref, sigma_ref, out_ref):
    @pl.when(place_ref[3] == 0)
    def _():
        out_ref[...] = shifted_ref[...]

    @pl.when(place_ref[3] != 0)
    def _():
        out_ref[...] = sigma_ref[...]


def parts_kernel(place_ref, shifted_ref, sigma_ref, row_ref, two_ref, zero_ref, last_ref):
    odd = place_ref[0]
    width = last_ref.shape[1]

    def at(block, count=1):
        return pl.ds(pl.multiple_of(block * width, 128), count * width)

    prior_kernel(place_ref, shifted_ref, sigma_ref, row_ref)
    first, last = row_ref[:, at(3 * odd)], row_ref[:, at(3 - 3 * odd)]
    two_ref[:, :width] = first
    two_ref[:, width:] = row_ref[:, at(2 - 2 * odd, 2)]
    zero_ref[:, :width] = first
    zero_ref[:, width:] = last
    last_ref[...] = last


def prior_parts(place, shifted, sigma):
    rows, nodes = sigma.shape
    chunk = 128
    width = nodes // 4
    out = lambda blocks: jax.ShapeDtypeStruct((rows, blocks * width), BF16)
    spec = lambda blocks: pl.BlockSpec((chunk, blocks * width), lambda i, place: (i, 0))
    return pl.pallas_call(
        parts_kernel,
        out_shape=(out(4), out(3), out(2), out(1)),
        grid_spec=pltpu.PrefetchScalarGridSpec(
            num_scalar_prefetch=1,
            grid=(rows // chunk,),
            in_specs=[
                pl.BlockSpec(
                    (chunk, nodes), lambda i, place: (jnp.where(place[3] == 0, i, 0), 0)
                ),
                pl.BlockSpec(
                    (chunk, nodes), lambda i, place: (jnp.where(place[3] == 0, 0, i), 0)
                ),
            ],
            out_specs=(spec(4), spec(3), spec(2), spec(1)),
        ),
        compiler_params=pltpu.CompilerParams(vmem_limit_bytes=8 * MIB),
        cost_estimate=LIGHT,
        name="prior_parts",
    )(place, shifted, sigma)


def assemble_kernel(place_ref, own, two, zero, three, out_ref):
    @pl.when(place_ref[1] == 1)
    def _():
        odd = place_ref[0]
        width = three.shape[1]

        def at(block, count=1):
            return pl.ds(pl.multiple_of(block * width, 128), count * width)

        near = 2 * (1 - odd)
        row = [turned(block, odd) for block in range(4)]
        out_ref[at(row[1]), :] = own[...]
        out_ref[at(row[2]), at(row[0])] = two[:, :width]
        out_ref[at(row[2]), at(near, 2)] = two[:, width:]
        out_ref[at(row[0]), at(row[0])] = zero[:, :width]
        out_ref[at(row[0]), at(row[3])] = zero[:, width:]
        out_ref[at(row[3]), at(row[3])] = three[...]
        for block in (0, 2, 3):
            out_ref[at(row[block]), at(row[1])] = own[:, at(row[block])].T
        out_ref[at(row[0]), at(row[2])] = two[:, :width].T
        out_ref[at(row[3]), at(row[2])] = two[:, at(2 - odd)].T
        out_ref[at(row[3]), at(row[0])] = zero[:, width:].T


def assemble(place, *parts):
    nodes = parts[0].shape[1]
    vmem = pl.BlockSpec(memory_space=pltpu.VMEM)
    return pl.pallas_call(
        assemble_kernel,
        out_shape=jax.ShapeDtypeStruct((nodes, nodes), BF16),
        in_specs=[pl.BlockSpec(memory_space=pltpu.SMEM)] + [vmem] * 4,
        out_specs=vmem,
        compiler_params=pltpu.CompilerParams(vmem_limit_bytes=6 * MIB),
        cost_estimate=LIGHT,
        name="assemble",
    )(place, *parts)


def tick(place, value):
    def kernel(place_ref, value_ref, out_ref):
        for which in range(place.shape[0]):
            out_ref[which] = place_ref[which]

    scalars = pl.BlockSpec(memory_space=pltpu.SMEM)
    return pl.pallas_call(
        kernel,
        out_shape=jax.ShapeDtypeStruct(place.shape, place.dtype),
        in_specs=[scalars, pl.BlockSpec(memory_space=pl.ANY)],
        out_specs=scalars,
        cost_estimate=LIGHT,
        name="tick",
    )(place, value)


def final_kernel(
    place_ref, pivot_ref, sigma_ref,
    q0, q0_last, q2, q2_zero, q2_last, q3_two, q3_other, q3_last,
    q01, q11, q21, q31,
    out_ref, var_ref,
):
    rows, nodes = pivot_ref.shape
    width = nodes // 4
    odd, place = place_ref[0], place_ref[1]
    here = pl.multiple_of(pl.program_id(0) * rows, 128)
    square = (rows, rows)
    on_diagonal = lax.broadcasted_iota(jnp.int32, square, 0) == lax.broadcasted_iota(
        jnp.int32, square, 1
    )

    def at(block, count=1):
        return pl.ds(pl.multiple_of(block * width, 128), count * width)

    def own(block):
        return pl.ds(pl.multiple_of(block * width + here, 128), rows)

    def diagonal(value):
        return jnp.sum(jnp.where(on_diagonal, value, 0.0), axis=0, keepdims=True)

    def add(columns, product):
        out_ref[:, columns] = (pivot_ref[:, columns].astype(F32) + product.astype(F32)).astype(BF16)

    def trace(product):
        var_ref[...] = diagonal(
            pivot_ref[:, own(place_ref[2])].astype(F32) + product.astype(F32)
        )

    active = place_ref[4] != 0

    @pl.when(active & (place == 0))
    def _():
        add(at(odd, 3), q0[...])
        add(at(turned(3, odd)), q0_last[:, pl.ds(here, rows)].T)
        trace(q0[:, own(2 * odd)])

    @pl.when(active & (place == 1))
    def _():
        add(at(turned(0, odd)), q01[...].T)
        add(at(turned(1, odd)), q11[...])
        add(at(turned(2, odd)), q21[...].T)
        add(at(turned(3, odd)), q31[...].T)
        trace(q11[:, pl.ds(here, rows)])

    @pl.when(active & (place == 2))
    def _():
        add(at(turned(0, odd)), q2_zero[:, pl.ds(here, rows)].T)
        add(at(1, 2), q2[...])
        add(at(turned(3, odd)), q2_last[:, pl.ds(here, rows)].T)
        trace(q2[:, own(1 - odd)])

    @pl.when(active & (place == 3))
    def _():
        add(at(2 * odd, 2), q3_other[...])
        add(at(turned(2, odd)), q3_two[...])
        add(at(turned(3, odd)), q3_last[...])
        trace(q3_last[:, pl.ds(here, rows)])

    @pl.when(place_ref[4] == 0)
    def _():
        out_ref[...] = sigma_ref[...]
        var_ref[...] = diagonal(sigma_ref[:, own(place_ref[2])].astype(F32))


def final(place, pivot, sigma, received, kept):
    rows, nodes = pivot.shape
    chunk = 128
    width = nodes // 4

    def picked(which, blocks):
        return pl.BlockSpec(
            (chunk, blocks * width), lambda i, place: (jnp.where(place[1] == which, i, 0), 0)
        )

    def turned_block(start):
        return pl.BlockSpec(
            (rows, chunk),
            lambda i, place: (
                0,
                jnp.where(place[1] == 1, start(place[0]) * (width // chunk) + i, 0),
            ),
        )

    whole = lambda block: pl.BlockSpec((rows, width), lambda i, place: (0, block))
    return pl.pallas_call(
        final_kernel,
        out_shape=(
            jax.ShapeDtypeStruct((rows, nodes), BF16),
            jax.ShapeDtypeStruct((1, rows), F32),
        ),
        grid_spec=pltpu.PrefetchScalarGridSpec(
            num_scalar_prefetch=1,
            grid=(rows // chunk,),
            in_specs=[
                pl.BlockSpec((chunk, nodes), lambda i, place: (i, 0)),
                pl.BlockSpec(
                    (chunk, nodes), lambda i, place: (jnp.where(place[4] == 0, i, 0), 0)
                ),
                picked(0, 3),
                whole(0),
                picked(2, 2),
                whole(2),
                whole(0),
                picked(3, 1),
                picked(3, 2),
                picked(3, 1),
                turned_block(lambda odd: 1),
                picked(1, 1),
                turned_block(lambda odd: odd),
                turned_block(lambda odd: 1 - odd),
            ],
            out_specs=(
                pl.BlockSpec((chunk, nodes), lambda i, place: (i, 0)),
                pl.BlockSpec((1, chunk), lambda i, place: (0, i)),
            ),
        ),
        compiler_params=pltpu.CompilerParams(vmem_limit_bytes=12 * MIB),
        cost_estimate=LIGHT,
        name="final",
    )(place, pivot, sigma, *received, *kept)


def owned(sigma_next, separator, inverse_pivot, coupling_rate, lengths, step_index, node_class):
    sigma, pivot = sigma_next[0], inverse_pivot[0]
    odd = lax.axis_index("dom") % 2
    col = lax.axis_index("col")
    step = step_index[0]
    place = jnp.stack([odd, turned(col, odd), col, step, step < lengths[0]]).astype(jnp.int32)
    after = lambda value, *others: lax.optimization_barrier((value, *others))[0]

    shifted = passed_along(separator, "dom", -1)[0]
    p0 = moved(pivot, 0, 1)
    p2 = moved(pivot, 2, 1)
    c1 = couple(pivot, node_class, coupling_rate)
    across = turn(place, 1, c1, None)

    row, two, zero, last = prior_parts(place, after(shifted, across), sigma)
    zero, two, three = moved(zero, 0, 1), moved(two, 2, 1), moved(last, 3, 1)

    c0 = couple_here(place, after(p0, last), node_class, coupling_rate)
    across = turn(place, 0, c0, across)
    c2 = couple_here(place, after(p2, across), node_class, coupling_rate)
    across = turn(place, 2, c2, across)
    c3 = moved(after(c1, three, zero, two, across), 3, 1)
    prior = assemble(place, row, two, zero, three)

    h0 = multiply(place, [c0], prior)
    q0_own = multiply(place, [h0], across, lambda odd: odd, 3)
    q0 = moved(q0_own, 1, 0)
    h2 = multiply(place, [after(c2, q0_own)], prior)
    q2_own = product_two(place, h2, across, q0_own)
    q2 = moved(q2_own, 1, 2)

    h3 = multiply(place, [c3], prior)
    q30, q32 = product_ends(place, h3, across)
    q0_last, q3_two = moved(q30, 1, 0), moved(q32, 1, 3)
    q3_own = product_other(place, h3, across, q30)
    q3_other = moved(q3_own, 1, 3)
    across = turn(place, 3, c3, after(across, q3_own))
    q33 = multiply(place, [h3], across, lambda odd: 3 - 3 * odd, 1)
    q3_last = moved(q33, 1, 3)
    place_then = tick(tick(place, q0_last), q3_two)
    q2_last = moved(after(q3_two, q0, q33, place_then), 3, 2)
    h1 = multiply(place, [after(c1, q33)], prior)
    q11 = multiply(place, [h1], across, lambda odd: 1 + odd, 1)
    received = (q0, q0_last, q2, q2, q2_last, q3_two, q3_other, q3_last)
    kept = (q0_own, q11, q2_own, q3_own)
    covariance, variances = final(place_then, pivot, sigma, received, kept)
    return (covariance[None], variances)


def gathered(sigma_next, separator, inverse_pivot, coupling_rate, lengths, step_index, node_class):
    shifted = passed_along(separator, "dom", -1)
    prior = jnp.where(step_index[0] == 0, shifted[0], sigma_next[0])
    pivot = inverse_pivot[0].astype(F32)
    coupled = couple(inverse_pivot[0], node_class, coupling_rate)
    rows = coupled.shape[0]
    half = jnp.dot(
        coupled,
        lax.all_gather(prior, "col", axis=0, tiled=True),
        preferred_element_type=F32,
    ).astype(BF16)
    product = lax.dot_general(
        half,
        lax.all_gather(coupled, "col", axis=0, tiled=True),
        (((1,), (1,)), ((), ())),
        preferred_element_type=F32,
    )
    full = pivot + product
    active = step_index[0] < lengths[0]
    old = sigma_next[0]
    covariance = jnp.where(active, full.astype(BF16), old)
    first_col = lax.axis_index("col") * rows
    new_block = lax.dynamic_slice_in_dim(full, first_col, rows, 1)
    old_block = lax.dynamic_slice_in_dim(old, first_col, rows, 1)
    variances = jnp.where(active, jnp.diagonal(new_block), jnp.diagonal(old_block).astype(F32))
    return (covariance[None], variances[None])


def solution(mesh):
    local = owned if mesh.shape["col"] == 4 and mesh.shape["dom"] % 2 == 0 else gathered
    return jax.shard_map(
        local,
        mesh=mesh,
        in_specs=(
            P(("groups", "dom"), "col", None),
            P(("groups", "dom"), "col", None),
            P(("groups", "dom"), "col", None),
            P(("groups", "dom")),
            P(("groups", "dom")),
            P(("groups", "dom")),
            P("groups"),
        ),
        out_specs=(P(("groups", "dom"), "col", None), P(("groups", "dom"), "col")),
        check_vma=False,
    )
```

```python
import functools

import jax
import jax.numpy as jnp
from jax import lax
from jax.experimental import pallas as pl
from jax.experimental.pallas import tpu as pltpu
from jax.sharding import PartitionSpec as P

GX = 64
GY = 32
BF16 = jnp.bfloat16
F32 = jnp.float32
MIB = 1 << 20


def passed_along(value, axis, steps):
    count = lax.axis_size(axis)
    initial, last = (max(0, -steps), min(count, count - steps))
    return lax.ppermute(value, axis, [(source, source + steps) for source in range(initial, last)])


LIGHT = pl.CostEstimate(flops=1 << 20, bytes_accessed=1 << 16, transcendentals=0)
HEAVY = pl.CostEstimate(flops=8000000000, bytes_accessed=1 << 16, transcendentals=0)


def couple_kernel(rate_ref, class_ref, pivot_ref, out_ref, weight_ref):
    nodes = pivot_ref.shape[1]

    @pl.when(pl.program_id(0) == 0)
    def _():
        kind = class_ref[...]
        across = jnp.where(
            kind == 0, 0.25, jnp.where(kind == 1, 0.375, jnp.where(kind == 2, 0.125, 0.5))
        ).astype(F32)
        along = jnp.where(
            kind == 0, 0.25, jnp.where(kind == 1, 0.125, jnp.where(kind == 2, 0.375, 0.0))
        ).astype(F32)
        node = lax.broadcasted_iota(jnp.int32, (1, nodes), 1)
        column = node % GX
        parts = (
            jnp.where(column > 0, across, 0.0),
            jnp.where(column < GX - 1, across, 0.0),
            jnp.where(node >= GX, along, 0.0),
            jnp.where(node < nodes - GX, along, 0.0),
        )
        for which, part in enumerate(parts):
            weight_ref[which] = jnp.broadcast_to(part, (16, nodes))

    rate = rate_ref[0]

    def group(step, carry):
        rows = pl.ds(pl.multiple_of(step * 16, 16), 16)
        value = pivot_ref[rows, :].astype(F32)
        total = (
            value
            + weight_ref[0] * pltpu.roll(value, 1, 1)
            + weight_ref[1] * pltpu.roll(value, nodes - 1, 1)
            + weight_ref[2] * pltpu.roll(value, GX, 1)
            + weight_ref[3] * pltpu.roll(value, nodes - GX, 1)
        )
        out_ref[rows, :] = (rate * total).astype(BF16)
        return carry

    lax.fori_loop(0, pivot_ref.shape[0] // 16, group, 0)


def couple(pivot, node_class, rate, part=0, parts=1):
    rows, nodes = pivot.shape[0] // parts, pivot.shape[1]
    chunk = min(rows, 128)
    steps = rows // chunk
    return pl.pallas_call(
        couple_kernel,
        out_shape=jax.ShapeDtypeStruct((rows, nodes), BF16),
        grid=(steps,),
        in_specs=[
            pl.BlockSpec(memory_space=pltpu.SMEM),
            pl.BlockSpec((1, nodes), lambda i: (0, 0)),
            pl.BlockSpec((chunk, nodes), lambda i: (part * steps + i, 0)),
        ],
        out_specs=pl.BlockSpec((chunk, nodes), lambda i: (i, 0)),
        scratch_shapes=[pltpu.VMEM((4, 16, nodes), F32)],
        compiler_params=pltpu.CompilerParams(vmem_limit_bytes=6 * MIB),
        cost_estimate=LIGHT,
        name="couple",
    )(rate, node_class.reshape(1, nodes), pivot)


def turned(block, odd):
    return block + odd * (3 - 2 * block)


def route(source, target, doms):
    pairs = []
    for dom in range(doms):
        odd = dom % 2
        pairs.append((dom * 4 + turned(source, odd), dom * 4 + turned(target, odd)))
    return pairs


def moved(value, source, target):
    return lax.ppermute(value, ("dom", "col"), route(source, target, lax.axis_size("dom")))


def couple_here(place, pivot, node_class, rate):
    rows, nodes = pivot.shape
    chunk = 128

    def kernel(place_ref, *refs):
        @pl.when(place_ref[1] == 1)
        def _():
            couple_kernel(*refs)

    return pl.pallas_call(
        kernel,
        out_shape=jax.ShapeDtypeStruct((rows, nodes), BF16),
        grid_spec=pltpu.PrefetchScalarGridSpec(
            num_scalar_prefetch=1,
            grid=(rows // chunk,),
            in_specs=[
                pl.BlockSpec(memory_space=pltpu.SMEM),
                pl.BlockSpec((1, nodes), lambda i, place: (0, 0)),
                pl.BlockSpec((chunk, nodes), lambda i, place: (i, 0)),
            ],
            out_specs=pl.BlockSpec((chunk, nodes), lambda i, place: (i, 0)),
            scratch_shapes=[pltpu.VMEM((4, 16, nodes), F32)],
        ),
        compiler_params=pltpu.CompilerParams(vmem_limit_bytes=8 * MIB),
        cost_estimate=LIGHT,
        name="couple_here",
    )(place, rate, node_class.reshape(1, nodes), pivot)


def turn_kernel(place_ref, coupled_ref, *refs):
    @pl.when(place_ref[1] == 1)
    def _():
        refs[-1][...] = coupled_ref[...].T


def turn(place, panel, part, coupled, across):
    rows, nodes = coupled.shape
    chunk = 128
    steps = rows // chunk
    ratio = nodes // 4 // chunk
    return pl.pallas_call(
        turn_kernel,
        out_shape=jax.ShapeDtypeStruct((nodes, nodes), BF16),
        grid_spec=pltpu.PrefetchScalarGridSpec(
            num_scalar_prefetch=1,
            grid=(steps,),
            in_specs=[pl.BlockSpec((chunk, nodes), lambda i, place: (i, 0))]
            + ([] if across is None else [pl.BlockSpec(memory_space=pl.ANY)]),
            out_specs=pl.BlockSpec(
                (nodes, chunk),
                lambda i, place: (0, turned(panel, place[0]) * ratio + part * steps + i),
            ),
        ),
        input_output_aliases={} if across is None else {2: 0},
        compiler_params=pltpu.CompilerParams(vmem_limit_bytes=4 * MIB),
        cost_estimate=LIGHT,
        name="turn",
    )(place, coupled, *(() if across is None else (across,)))


def multiply_kernel(first, count, lefts, place_ref, *refs):
    left_refs, right_ref, out_ref = refs[:lefts], refs[lefts], refs[-1]
    width = right_ref.shape[0] // 4

    @pl.when(place_ref[1] == 1)
    def _():
        def block(step, carry):
            source = pl.multiple_of((first(place_ref[0]) + step) * width, 128)
            target = pl.multiple_of(step * width, 128)
            row = 0
            for left_ref in left_refs:
                rows = left_ref.shape[0]
                out_ref[row : row + rows, pl.ds(target, width)] = jnp.dot(
                    left_ref[...], right_ref[:, pl.ds(source, width)], preferred_element_type=F32
                ).astype(BF16)
                row += rows
            return carry

        lax.fori_loop(0, count, block, 0)


def multiply(place, lefts, right, first=lambda odd: 0, count=4):
    rows = sum(left.shape[0] for left in lefts)
    width = right.shape[0] // 4
    vmem = pl.BlockSpec(memory_space=pltpu.VMEM)
    return pl.pallas_call(
        functools.partial(multiply_kernel, first, count, len(lefts)),
        out_shape=jax.ShapeDtypeStruct((rows, count * width), BF16),
        in_specs=[pl.BlockSpec(memory_space=pltpu.SMEM)] + [vmem] * (len(lefts) + 1),
        out_specs=vmem,
        compiler_params=pltpu.CompilerParams(vmem_limit_bytes=6 * MIB),
        cost_estimate=LIGHT,
        name="multiply",
    )(place, *lefts, right)


def two_kernel(place_ref, left_ref, right_ref, zero_ref, out_ref):
    odd = place_ref[0]
    width = right_ref.shape[0] // 4
    multiply_kernel(lambda odd: 1, 2, 1, place_ref, left_ref, right_ref, out_ref)

    @pl.when(place_ref[1] == 1)
    def _():
        out_ref[:, 2 * width :] = zero_ref[:, pl.ds(pl.multiple_of((2 - 2 * odd) * width, 128), width)]


def product_two(place, half, across, zero):
    rows = half.shape[0]
    width = across.shape[0] // 4
    vmem = pl.BlockSpec(memory_space=pltpu.VMEM)
    return pl.pallas_call(
        two_kernel,
        out_shape=jax.ShapeDtypeStruct((rows, 3 * width), BF16),
        in_specs=[pl.BlockSpec(memory_space=pltpu.SMEM)] + [vmem] * 3,
        out_specs=vmem,
        compiler_params=pltpu.CompilerParams(vmem_limit_bytes=6 * MIB),
        cost_estimate=LIGHT,
        name="product_two",
    )(place, half, across, zero)


def ends_kernel(place_ref, left_ref, right_ref, zero_ref, two_ref):
    for block, out_ref in ((0, zero_ref), (2, two_ref)):
        first = lambda odd: turned(block, odd)
        multiply_kernel(first, 1, 1, place_ref, left_ref, right_ref, out_ref)


def product_ends(place, half, across):
    rows = half.shape[0]
    width = across.shape[0] // 4
    vmem = pl.BlockSpec(memory_space=pltpu.VMEM)
    return pl.pallas_call(
        ends_kernel,
        out_shape=(jax.ShapeDtypeStruct((rows, width), BF16),) * 2,
        in_specs=[pl.BlockSpec(memory_space=pltpu.SMEM)] + [vmem] * 2,
        out_specs=(vmem, vmem),
        compiler_params=pltpu.CompilerParams(vmem_limit_bytes=6 * MIB),
        cost_estimate=LIGHT,
        name="product_ends",
    )(place, half, across)


def rest_kernel(place_ref, left_ref, right_ref, zero_ref, out_ref):
    odd = place_ref[0]
    width = zero_ref.shape[1]

    @pl.when(place_ref[1] == 1)
    def _():
        out_ref[:, pl.ds(pl.multiple_of(odd * width, 128), width)] = zero_ref[...]
        for source, target in ((1 + odd, 1 - odd), (3 - 3 * odd, 2)):
            source = pl.multiple_of(source * width, 128)
            target = pl.multiple_of(target * width, 128)
            out_ref[:, pl.ds(target, width)] = jnp.dot(
                left_ref[...], right_ref[:, pl.ds(source, width)], preferred_element_type=F32
            ).astype(BF16)


def product_rest(place, half, across, zero):
    rows = half.shape[0]
    width = across.shape[0] // 4
    vmem = pl.BlockSpec(memory_space=pltpu.VMEM)
    return pl.pallas_call(
        rest_kernel,
        out_shape=jax.ShapeDtypeStruct((rows, 3 * width), BF16),
        in_specs=[pl.BlockSpec(memory_space=pltpu.SMEM)] + [vmem] * 3,
        out_specs=vmem,
        compiler_params=pltpu.CompilerParams(vmem_limit_bytes=6 * MIB),
        cost_estimate=LIGHT,
        name="product_rest",
    )(place, half, across, zero)


def prior_kernel(place_ref, shifted_ref, sigma_ref, out_ref):
    @pl.when(place_ref[3] == 0)
    def _():
        out_ref[...] = shifted_ref[...]

    @pl.when(place_ref[3] != 0)
    def _():
        out_ref[...] = sigma_ref[...]


def parts_kernel(place_ref, shifted_ref, sigma_ref, row_ref, far_ref, near_ref, last_ref):
    odd = place_ref[0]
    width = last_ref.shape[1]

    def at(block, count=1):
        return pl.ds(pl.multiple_of(block * width, 128), count * width)

    prior_kernel(place_ref, shifted_ref, sigma_ref, row_ref)
    near = row_ref[:, at(2 - 2 * odd, 2)]
    near_ref[...] = near
    far_ref[:, width:] = near
    far_ref[:, :width] = row_ref[:, at(3 * odd)]
    last_ref[...] = row_ref[:, at(3 - 3 * odd)]


def prior_parts(place, shifted, sigma):
    rows, nodes = sigma.shape
    chunk = 128
    width = nodes // 4
    out = lambda blocks: jax.ShapeDtypeStruct((rows, blocks * width), BF16)
    spec = lambda blocks: pl.BlockSpec((chunk, blocks * width), lambda i, place: (i, 0))
    return pl.pallas_call(
        parts_kernel,
        out_shape=(out(4), out(3), out(2), out(1)),
        grid_spec=pltpu.PrefetchScalarGridSpec(
            num_scalar_prefetch=1,
            grid=(rows // chunk,),
            in_specs=[
                pl.BlockSpec(
                    (chunk, nodes), lambda i, place: (jnp.where(place[3] == 0, i, 0), 0)
                ),
                pl.BlockSpec(
                    (chunk, nodes), lambda i, place: (jnp.where(place[3] == 0, 0, i), 0)
                ),
            ],
            out_specs=(spec(4), spec(3), spec(2), spec(1)),
        ),
        compiler_params=pltpu.CompilerParams(vmem_limit_bytes=8 * MIB),
        cost_estimate=LIGHT,
        name="prior_parts",
    )(place, shifted, sigma)


def assemble_kernel(place_ref, own, near_two, last_three, far_zero, out_ref):
    @pl.when(place_ref[1] == 1)
    def _():
        odd = place_ref[0]
        width = last_three.shape[1]

        def at(block):
            return pl.ds(pl.multiple_of(block * width, 128), width)

        near = 2 * (1 - odd)
        half = pl.ds(pl.multiple_of(near * width, 128), 2 * width)
        row = [turned(block, odd) for block in range(4)]
        out_ref[at(row[1]), :] = own[...]
        out_ref[at(row[2]), half] = near_two[...]
        out_ref[at(row[0]), at(row[0])] = far_zero[:, :width]
        out_ref[at(row[0]), half] = far_zero[:, width:]
        out_ref[at(row[3]), at(row[3])] = last_three[...]
        for step in range(2):
            out_ref[at(near + step), at(row[1])] = own[:, at(near + step)].T
            piece = slice((1 + step) * width, (2 + step) * width)
            out_ref[at(near + step), at(row[0])] = far_zero[:, piece].T
        out_ref[at(row[0]), at(row[1])] = own[:, at(row[0])].T
        out_ref[at(row[3]), at(row[2])] = near_two[:, at(1 - odd)].T


def assemble(place, *parts):
    nodes = parts[0].shape[1]
    vmem = pl.BlockSpec(memory_space=pltpu.VMEM)
    return pl.pallas_call(
        assemble_kernel,
        out_shape=jax.ShapeDtypeStruct((nodes, nodes), BF16),
        in_specs=[pl.BlockSpec(memory_space=pltpu.SMEM)] + [vmem] * 4,
        out_specs=vmem,
        compiler_params=pltpu.CompilerParams(vmem_limit_bytes=6 * MIB),
        cost_estimate=LIGHT,
        name="assemble",
    )(place, *parts)


def tick(place, *values, cost=HEAVY):
    def kernel(place_ref, *refs):
        for which in range(place.shape[0]):
            refs[-1][which] = place_ref[which]

    scalars = pl.BlockSpec(memory_space=pltpu.SMEM)
    return pl.pallas_call(
        kernel,
        out_shape=jax.ShapeDtypeStruct(place.shape, place.dtype),
        in_specs=[scalars] + [pl.BlockSpec(memory_space=pl.ANY)] * len(values),
        out_specs=scalars,
        compiler_params=pltpu.CompilerParams(vmem_limit_bytes=MIB),
        cost_estimate=cost,
        name="tick",
    )(place, *values)


def final_kernel(
    place_ref, pivot_ref, sigma_ref,
    q0, q0_last, q2, q2_zero, q2_last, q3_two, q3,
    q01, q11, q21, q31,
    out_ref, var_ref,
):
    rows, nodes = pivot_ref.shape
    width = nodes // 4
    odd, place = place_ref[0], place_ref[1]
    here = pl.multiple_of(pl.program_id(0) * rows, 128)
    square = (rows, rows)
    on_diagonal = lax.broadcasted_iota(jnp.int32, square, 0) == lax.broadcasted_iota(
        jnp.int32, square, 1
    )

    def at(block, count=1):
        return pl.ds(pl.multiple_of(block * width, 128), count * width)

    def own(block):
        return pl.ds(pl.multiple_of(block * width + here, 128), rows)

    def diagonal(value):
        return jnp.sum(jnp.where(on_diagonal, value, 0.0), axis=0, keepdims=True)

    def add(columns, product):
        out_ref[:, columns] = (pivot_ref[:, columns].astype(F32) + product.astype(F32)).astype(BF16)

    def trace(product):
        var_ref[...] = diagonal(
            pivot_ref[:, own(place_ref[2])].astype(F32) + product.astype(F32)
        )

    active = place_ref[4] != 0

    @pl.when(active & (place == 0))
    def _():
        add(at(odd, 3), q0[...])
        add(at(turned(3, odd)), q0_last[:, pl.ds(here, rows)].T)
        trace(q0[:, own(2 * odd)])

    @pl.when(active & (place == 1))
    def _():
        add(at(turned(0, odd)), q01[...].T)
        add(at(turned(1, odd)), q11[...])
        add(at(turned(2, odd)), q21[...].T)
        add(at(turned(3, odd)), q31[...].T)
        trace(q11[:, pl.ds(here, rows)])

    @pl.when(active & (place == 2))
    def _():
        add(at(turned(0, odd)), q2_zero[:, pl.ds(here, rows)].T)
        add(at(1, 2), q2[...])
        add(at(turned(3, odd)), q2_last[:, pl.ds(here, rows)].T)
        trace(q2[:, own(1 - odd)])

    @pl.when(active & (place == 3))
    def _():
        add(at(2 * odd, 2), q3[:, : 2 * width])
        add(at(turned(2, odd)), q3_two[...])
        add(at(turned(3, odd)), q3[:, 2 * width :])
        trace(q3[:, own(2)])

    @pl.when(place_ref[4] == 0)
    def _():
        out_ref[...] = sigma_ref[...]
        var_ref[...] = diagonal(sigma_ref[:, own(place_ref[2])].astype(F32))


def final(place, pivot, sigma, received, kept):
    rows, nodes = pivot.shape
    chunk = 128
    width = nodes // 4

    def picked(which, blocks):
        return pl.BlockSpec(
            (chunk, blocks * width), lambda i, place: (jnp.where(place[1] == which, i, 0), 0)
        )

    def turned_block(start):
        return pl.BlockSpec(
            (rows, chunk),
            lambda i, place: (
                0,
                jnp.where(place[1] == 1, start(place[0]) * (width // chunk) + i, 0),
            ),
        )

    whole = lambda block: pl.BlockSpec((rows, width), lambda i, place: (0, block))
    return pl.pallas_call(
        final_kernel,
        out_shape=(
            jax.ShapeDtypeStruct((rows, nodes), BF16),
            jax.ShapeDtypeStruct((1, rows), F32),
        ),
        grid_spec=pltpu.PrefetchScalarGridSpec(
            num_scalar_prefetch=1,
            grid=(rows // chunk,),
            in_specs=[
                pl.BlockSpec((chunk, nodes), lambda i, place: (i, 0)),
                pl.BlockSpec(
                    (chunk, nodes), lambda i, place: (jnp.where(place[4] == 0, i, 0), 0)
                ),
                picked(0, 3),
                whole(0),
                picked(2, 2),
                whole(2),
                whole(0),
                picked(3, 1),
                picked(3, 3),
                turned_block(lambda odd: 1),
                picked(1, 1),
                turned_block(lambda odd: odd),
                turned_block(lambda odd: 1 - odd),
            ],
            out_specs=(
                pl.BlockSpec((chunk, nodes), lambda i, place: (i, 0)),
                pl.BlockSpec((1, chunk), lambda i, place: (0, i)),
            ),
        ),
        compiler_params=pltpu.CompilerParams(vmem_limit_bytes=12 * MIB),
        cost_estimate=LIGHT,
        name="final",
    )(place, pivot, sigma, *received, *kept)


def owned(sigma_next, separator, inverse_pivot, coupling_rate, lengths, step_index, node_class):
    sigma, pivot = sigma_next[0], inverse_pivot[0]
    odd = lax.axis_index("dom") % 2
    col = lax.axis_index("col")
    step = step_index[0]
    place = jnp.stack([odd, turned(col, odd), col, step, step < lengths[0]]).astype(jnp.int32)
    after = lambda value, *others: lax.optimization_barrier((value, *others))[0]

    shifted = passed_along(separator, "dom", -1)[0]
    p2 = moved(pivot, 2, 1)
    p0 = moved(pivot, 0, 1)
    c1 = [couple(pivot, node_class, coupling_rate, part, 2) for part in range(2)]
    across = turn(place, 1, 0, c1[0], None)
    across = turn(place, 1, 1, c1[1], across)

    row, far, near, last = prior_parts(place, after(shifted, across), sigma)
    far_zero, near_two, last_three = moved(far, 0, 1), moved(near, 2, 1), moved(last, 3, 1)

    c2 = couple_here(place, after(p2, last), node_class, coupling_rate)
    across = turn(place, 2, 0, c2, across)
    c0 = couple_here(place, after(p0, across), node_class, coupling_rate)
    across = turn(place, 0, 0, c0, across)
    c3 = [
        moved(after(c1[0], last_three, near_two, across), 3, 1),
        moved(after(c1[1], far_zero), 3, 1),
    ]
    prior = assemble(place, row, near_two, last_three, far_zero)

    h0 = multiply(place, [c0], prior)
    q0_own = multiply(place, [h0], across, lambda odd: odd, 3)
    q0 = moved(q0_own, 1, 0)
    h2 = multiply(place, [after(c2, q0_own)], prior)
    q2_own = product_two(place, h2, across, q0_own)
    q2 = moved(q2_own, 1, 2)

    h3 = multiply(place, c3, prior)
    q30, q32 = product_ends(place, h3, across)
    q0_last, q3_two = moved(q30, 1, 0), moved(q32, 1, 3)
    across = turn(place, 3, 0, c3[0], after(across, q30))
    across = turn(place, 3, 1, c3[1], across)
    q3_own = product_rest(place, h3, across, q30)
    q3 = moved(q3_own, 1, 3)
    q2_last = moved(q3_two, 3, 2)
    h1 = multiply(place, [after(c1[0], q3_own), c1[1]], prior)
    q11 = multiply(place, [h1], across, lambda odd: 1 + odd, 1)
    received = (q0, q0_last, q2, q2, q2_last, q3_two, q3)
    kept = (q0_own, q11, q2_own, q3_own)
    place = tick(place, q0, cost=LIGHT)
    place = tick(tick(place, q0_last, q2), q2_last)
    covariance, variances = final(place, pivot, sigma, received, kept)
    return (covariance[None], variances)


def gathered(sigma_next, separator, inverse_pivot, coupling_rate, lengths, step_index, node_class):
    shifted = passed_along(separator, "dom", -1)
    prior = jnp.where(step_index[0] == 0, shifted[0], sigma_next[0])
    pivot = inverse_pivot[0].astype(F32)
    coupled = couple(inverse_pivot[0], node_class, coupling_rate)
    rows = coupled.shape[0]
    half = jnp.dot(
        coupled,
        lax.all_gather(prior, "col", axis=0, tiled=True),
        preferred_element_type=F32,
    ).astype(BF16)
    product = lax.dot_general(
        half,
        lax.all_gather(coupled, "col", axis=0, tiled=True),
        (((1,), (1,)), ((), ())),
        preferred_element_type=F32,
    )
    full = pivot + product
    active = step_index[0] < lengths[0]
    old = sigma_next[0]
    covariance = jnp.where(active, full.astype(BF16), old)
    first_col = lax.axis_index("col") * rows
    new_block = lax.dynamic_slice_in_dim(full, first_col, rows, 1)
    old_block = lax.dynamic_slice_in_dim(old, first_col, rows, 1)
    variances = jnp.where(active, jnp.diagonal(new_block), jnp.diagonal(old_block).astype(F32))
    return (covariance[None], variances[None])


def solution(mesh):
    local = owned if mesh.shape["col"] == 4 and mesh.shape["dom"] % 2 == 0 else gathered
    return jax.shard_map(
        local,
        mesh=mesh,
        in_specs=(
            P(("groups", "dom"), "col", None),
            P(("groups", "dom"), "col", None),
            P(("groups", "dom"), "col", None),
            P(("groups", "dom")),
            P(("groups", "dom")),
            P(("groups", "dom")),
            P("groups"),
        ),
        out_specs=(P(("groups", "dom"), "col", None), P(("groups", "dom"), "col")),
        check_vma=False,
    )
```

```python
import functools

import jax
import jax.numpy as jnp
from jax import lax
from jax.experimental import pallas as pl
from jax.experimental.pallas import tpu as pltpu
from jax.sharding import PartitionSpec as P

GX = 64
GY = 32
BF16 = jnp.bfloat16
F32 = jnp.float32
MIB = 1 << 20


def passed_along(value, axis, steps):
    count = lax.axis_size(axis)
    initial, last = (max(0, -steps), min(count, count - steps))
    return lax.ppermute(value, axis, [(source, source + steps) for source in range(initial, last)])


LIGHT = pl.CostEstimate(flops=1 << 20, bytes_accessed=1 << 16, transcendentals=0)
HEAVY = pl.CostEstimate(flops=14000000000, bytes_accessed=1 << 16, transcendentals=0)


def couple_kernel(rate_ref, class_ref, pivot_ref, out_ref, weight_ref):
    nodes = pivot_ref.shape[1]

    @pl.when(pl.program_id(0) == 0)
    def _():
        kind = class_ref[...]
        across = jnp.where(
            kind == 0, 0.25, jnp.where(kind == 1, 0.375, jnp.where(kind == 2, 0.125, 0.5))
        ).astype(F32)
        along = jnp.where(
            kind == 0, 0.25, jnp.where(kind == 1, 0.125, jnp.where(kind == 2, 0.375, 0.0))
        ).astype(F32)
        node = lax.broadcasted_iota(jnp.int32, (1, nodes), 1)
        column = node % GX
        parts = (
            jnp.where(column > 0, across, 0.0),
            jnp.where(column < GX - 1, across, 0.0),
            jnp.where(node >= GX, along, 0.0),
            jnp.where(node < nodes - GX, along, 0.0),
        )
        for which, part in enumerate(parts):
            weight_ref[which] = jnp.broadcast_to(part, (16, nodes))

    rate = rate_ref[0]

    def group(step, carry):
        rows = pl.ds(pl.multiple_of(step * 16, 16), 16)
        value = pivot_ref[rows, :].astype(F32)
        total = (
            value
            + weight_ref[0] * pltpu.roll(value, 1, 1)
            + weight_ref[1] * pltpu.roll(value, nodes - 1, 1)
            + weight_ref[2] * pltpu.roll(value, GX, 1)
            + weight_ref[3] * pltpu.roll(value, nodes - GX, 1)
        )
        out_ref[rows, :] = (rate * total).astype(BF16)
        return carry

    lax.fori_loop(0, pivot_ref.shape[0] // 16, group, 0)


def couple(pivot, node_class, rate, part=0, parts=1):
    rows, nodes = pivot.shape[0] // parts, pivot.shape[1]
    chunk = min(rows, 128)
    steps = rows // chunk
    return pl.pallas_call(
        couple_kernel,
        out_shape=jax.ShapeDtypeStruct((rows, nodes), BF16),
        grid=(steps,),
        in_specs=[
            pl.BlockSpec(memory_space=pltpu.SMEM),
            pl.BlockSpec((1, nodes), lambda i: (0, 0)),
            pl.BlockSpec((chunk, nodes), lambda i: (part * steps + i, 0)),
        ],
        out_specs=pl.BlockSpec((chunk, nodes), lambda i: (i, 0)),
        scratch_shapes=[pltpu.VMEM((4, 16, nodes), F32)],
        compiler_params=pltpu.CompilerParams(vmem_limit_bytes=6 * MIB),
        cost_estimate=LIGHT,
        name="couple",
    )(rate, node_class.reshape(1, nodes), pivot)


def turned(block, odd):
    return block + odd * (3 - 2 * block)


def route(source, target, doms):
    pairs = []
    for dom in range(doms):
        odd = dom % 2
        pairs.append((dom * 4 + turned(source, odd), dom * 4 + turned(target, odd)))
    return pairs


def moved(value, source, target):
    return lax.ppermute(value, ("dom", "col"), route(source, target, lax.axis_size("dom")))


def couple_here(place, pivot, node_class, rate):
    rows, nodes = pivot.shape
    chunk = 128

    def kernel(place_ref, *refs):
        @pl.when(place_ref[1] == 1)
        def _():
            couple_kernel(*refs)

    return pl.pallas_call(
        kernel,
        out_shape=jax.ShapeDtypeStruct((rows, nodes), BF16),
        grid_spec=pltpu.PrefetchScalarGridSpec(
            num_scalar_prefetch=1,
            grid=(rows // chunk,),
            in_specs=[
                pl.BlockSpec(memory_space=pltpu.SMEM),
                pl.BlockSpec((1, nodes), lambda i, place: (0, 0)),
                pl.BlockSpec((chunk, nodes), lambda i, place: (i, 0)),
            ],
            out_specs=pl.BlockSpec((chunk, nodes), lambda i, place: (i, 0)),
            scratch_shapes=[pltpu.VMEM((4, 16, nodes), F32)],
        ),
        compiler_params=pltpu.CompilerParams(vmem_limit_bytes=8 * MIB),
        cost_estimate=LIGHT,
        name="couple_here",
    )(place, rate, node_class.reshape(1, nodes), pivot)


def turn_kernel(place_ref, coupled_ref, *refs):
    @pl.when(place_ref[1] == 1)
    def _():
        refs[-1][...] = coupled_ref[...].T


def turn(place, panel, part, coupled, across):
    rows, nodes = coupled.shape
    chunk = 128
    steps = rows // chunk
    ratio = nodes // 4 // chunk
    return pl.pallas_call(
        turn_kernel,
        out_shape=jax.ShapeDtypeStruct((nodes, nodes), BF16),
        grid_spec=pltpu.PrefetchScalarGridSpec(
            num_scalar_prefetch=1,
            grid=(steps,),
            in_specs=[pl.BlockSpec((chunk, nodes), lambda i, place: (i, 0))]
            + ([] if across is None else [pl.BlockSpec(memory_space=pl.ANY)]),
            out_specs=pl.BlockSpec(
                (nodes, chunk),
                lambda i, place: (0, turned(panel, place[0]) * ratio + part * steps + i),
            ),
        ),
        input_output_aliases={} if across is None else {2: 0},
        compiler_params=pltpu.CompilerParams(vmem_limit_bytes=4 * MIB),
        cost_estimate=LIGHT,
        name="turn",
    )(place, coupled, *(() if across is None else (across,)))


def multiply_kernel(first, count, lefts, place_ref, *refs):
    left_refs, right_ref, out_ref = refs[:lefts], refs[lefts], refs[-1]
    width = right_ref.shape[0] // 4

    @pl.when(place_ref[1] == 1)
    def _():
        def block(step, carry):
            source = pl.multiple_of((first(place_ref[0]) + step) * width, 128)
            target = pl.multiple_of(step * width, 128)
            row = 0
            for left_ref in left_refs:
                rows = left_ref.shape[0]
                out_ref[row : row + rows, pl.ds(target, width)] = jnp.dot(
                    left_ref[...], right_ref[:, pl.ds(source, width)], preferred_element_type=F32
                ).astype(BF16)
                row += rows
            return carry

        lax.fori_loop(0, count, block, 0)


def multiply(place, lefts, right, first=lambda odd: 0, count=4):
    rows = sum(left.shape[0] for left in lefts)
    width = right.shape[0] // 4
    vmem = pl.BlockSpec(memory_space=pltpu.VMEM)
    return pl.pallas_call(
        functools.partial(multiply_kernel, first, count, len(lefts)),
        out_shape=jax.ShapeDtypeStruct((rows, count * width), BF16),
        in_specs=[pl.BlockSpec(memory_space=pltpu.SMEM)] + [vmem] * (len(lefts) + 1),
        out_specs=vmem,
        compiler_params=pltpu.CompilerParams(vmem_limit_bytes=6 * MIB),
        cost_estimate=LIGHT,
        name="multiply",
    )(place, *lefts, right)


def two_kernel(place_ref, left_ref, right_ref, zero_ref, out_ref):
    odd = place_ref[0]
    width = right_ref.shape[0] // 4
    multiply_kernel(lambda odd: 1, 2, 1, place_ref, left_ref, right_ref, out_ref)

    @pl.when(place_ref[1] == 1)
    def _():
        out_ref[:, 2 * width :] = zero_ref[:, pl.ds(pl.multiple_of((2 - 2 * odd) * width, 128), width)]


def product_two(place, half, across, zero):
    rows = half.shape[0]
    width = across.shape[0] // 4
    vmem = pl.BlockSpec(memory_space=pltpu.VMEM)
    return pl.pallas_call(
        two_kernel,
        out_shape=jax.ShapeDtypeStruct((rows, 3 * width), BF16),
        in_specs=[pl.BlockSpec(memory_space=pltpu.SMEM)] + [vmem] * 3,
        out_specs=vmem,
        compiler_params=pltpu.CompilerParams(vmem_limit_bytes=6 * MIB),
        cost_estimate=LIGHT,
        name="product_two",
    )(place, half, across, zero)


def ends_kernel(place_ref, left_ref, right_ref, zero_ref, two_ref):
    for block, out_ref in ((0, zero_ref), (2, two_ref)):
        first = lambda odd: turned(block, odd)
        multiply_kernel(first, 1, 1, place_ref, left_ref, right_ref, out_ref)


def product_ends(place, half, across):
    rows = half.shape[0]
    width = across.shape[0] // 4
    vmem = pl.BlockSpec(memory_space=pltpu.VMEM)
    return pl.pallas_call(
        ends_kernel,
        out_shape=(jax.ShapeDtypeStruct((rows, width), BF16),) * 2,
        in_specs=[pl.BlockSpec(memory_space=pltpu.SMEM)] + [vmem] * 2,
        out_specs=(vmem, vmem),
        compiler_params=pltpu.CompilerParams(vmem_limit_bytes=6 * MIB),
        cost_estimate=LIGHT,
        name="product_ends",
    )(place, half, across)


def rest_kernel(place_ref, left_ref, right_ref, zero_ref, out_ref):
    odd = place_ref[0]
    width = zero_ref.shape[1]

    @pl.when(place_ref[1] == 1)
    def _():
        out_ref[:, pl.ds(pl.multiple_of(odd * width, 128), width)] = zero_ref[...]
        for source, target in ((1 + odd, 1 - odd), (3 - 3 * odd, 2)):
            source = pl.multiple_of(source * width, 128)
            target = pl.multiple_of(target * width, 128)
            out_ref[:, pl.ds(target, width)] = jnp.dot(
                left_ref[...], right_ref[:, pl.ds(source, width)], preferred_element_type=F32
            ).astype(BF16)


def product_rest(place, half, across, zero):
    rows = half.shape[0]
    width = across.shape[0] // 4
    vmem = pl.BlockSpec(memory_space=pltpu.VMEM)
    return pl.pallas_call(
        rest_kernel,
        out_shape=jax.ShapeDtypeStruct((rows, 3 * width), BF16),
        in_specs=[pl.BlockSpec(memory_space=pltpu.SMEM)] + [vmem] * 3,
        out_specs=vmem,
        compiler_params=pltpu.CompilerParams(vmem_limit_bytes=6 * MIB),
        cost_estimate=LIGHT,
        name="product_rest",
    )(place, half, across, zero)


def prior_kernel(place_ref, shifted_ref, sigma_ref, out_ref):
    @pl.when(place_ref[3] == 0)
    def _():
        out_ref[...] = shifted_ref[...]

    @pl.when(place_ref[3] != 0)
    def _():
        out_ref[...] = sigma_ref[...]


def parts_kernel(place_ref, shifted_ref, sigma_ref, row_ref, far_ref, near_ref, last_ref):
    odd = place_ref[0]
    width = last_ref.shape[1]

    def at(block, count=1):
        return pl.ds(pl.multiple_of(block * width, 128), count * width)

    prior_kernel(place_ref, shifted_ref, sigma_ref, row_ref)
    near = row_ref[:, at(2 - 2 * odd, 2)]
    near_ref[...] = near
    far_ref[:, width:] = near
    far_ref[:, :width] = row_ref[:, at(3 * odd)]
    last_ref[...] = row_ref[:, at(3 - 3 * odd)]


def prior_parts(place, shifted, sigma):
    rows, nodes = sigma.shape
    chunk = 128
    width = nodes // 4
    out = lambda blocks: jax.ShapeDtypeStruct((rows, blocks * width), BF16)
    spec = lambda blocks: pl.BlockSpec((chunk, blocks * width), lambda i, place: (i, 0))
    return pl.pallas_call(
        parts_kernel,
        out_shape=(out(4), out(3), out(2), out(1)),
        grid_spec=pltpu.PrefetchScalarGridSpec(
            num_scalar_prefetch=1,
            grid=(rows // chunk,),
            in_specs=[
                pl.BlockSpec(
                    (chunk, nodes), lambda i, place: (jnp.where(place[3] == 0, i, 0), 0)
                ),
                pl.BlockSpec(
                    (chunk, nodes), lambda i, place: (jnp.where(place[3] == 0, 0, i), 0)
                ),
            ],
            out_specs=(spec(4), spec(3), spec(2), spec(1)),
        ),
        compiler_params=pltpu.CompilerParams(vmem_limit_bytes=8 * MIB),
        cost_estimate=LIGHT,
        name="prior_parts",
    )(place, shifted, sigma)


def assemble_kernel(place_ref, own, near_two, last_three, far_zero, out_ref):
    @pl.when(place_ref[1] == 1)
    def _():
        odd = place_ref[0]
        width = last_three.shape[1]

        def at(block):
            return pl.ds(pl.multiple_of(block * width, 128), width)

        near = 2 * (1 - odd)
        half = pl.ds(pl.multiple_of(near * width, 128), 2 * width)
        row = [turned(block, odd) for block in range(4)]
        out_ref[at(row[1]), :] = own[...]
        out_ref[at(row[2]), half] = near_two[...]
        out_ref[at(row[0]), at(row[0])] = far_zero[:, :width]
        out_ref[at(row[0]), half] = far_zero[:, width:]
        out_ref[at(row[3]), at(row[3])] = last_three[...]
        for step in range(2):
            out_ref[at(near + step), at(row[1])] = own[:, at(near + step)].T
            piece = slice((1 + step) * width, (2 + step) * width)
            out_ref[at(near + step), at(row[0])] = far_zero[:, piece].T
        out_ref[at(row[0]), at(row[1])] = own[:, at(row[0])].T
        out_ref[at(row[3]), at(row[2])] = near_two[:, at(1 - odd)].T


def assemble(place, *parts):
    nodes = parts[0].shape[1]
    vmem = pl.BlockSpec(memory_space=pltpu.VMEM)
    return pl.pallas_call(
        assemble_kernel,
        out_shape=jax.ShapeDtypeStruct((nodes, nodes), BF16),
        in_specs=[pl.BlockSpec(memory_space=pltpu.SMEM)] + [vmem] * 4,
        out_specs=vmem,
        compiler_params=pltpu.CompilerParams(vmem_limit_bytes=6 * MIB),
        cost_estimate=LIGHT,
        name="assemble",
    )(place, *parts)


def tick(place, *values, cost=HEAVY):
    def kernel(place_ref, *refs):
        for which in range(place.shape[0]):
            refs[-1][which] = place_ref[which]

    scalars = pl.BlockSpec(memory_space=pltpu.SMEM)
    return pl.pallas_call(
        kernel,
        out_shape=jax.ShapeDtypeStruct(place.shape, place.dtype),
        in_specs=[scalars] + [pl.BlockSpec(memory_space=pl.ANY)] * len(values),
        out_specs=scalars,
        compiler_params=pltpu.CompilerParams(vmem_limit_bytes=MIB),
        cost_estimate=cost,
        name="tick",
    )(place, *values)


def finish_kernel(
    place_ref, pivot_ref, sigma_ref,
    q0, q0_last, q2, q2_zero, q3_two,
    q01, q11, q21, q31,
    out_ref, var_ref,
):
    rows, nodes = pivot_ref.shape
    width = nodes // 4
    odd, place = place_ref[0], place_ref[1]
    here = pl.multiple_of(pl.program_id(0) * rows, 128)
    diagonal = diagonal_of(rows)

    def at(block, count=1):
        return pl.ds(pl.multiple_of(block * width, 128), count * width)

    def own(block):
        return pl.ds(pl.multiple_of(block * width + here, 128), rows)

    def add(columns, product):
        out_ref[:, columns] = (pivot_ref[:, columns].astype(F32) + product.astype(F32)).astype(BF16)

    def trace(product):
        var_ref[...] = diagonal(
            pivot_ref[:, own(place_ref[2])].astype(F32) + product.astype(F32)
        )

    active = place_ref[4] != 0

    @pl.when(active & (place == 0))
    def _():
        add(at(odd, 3), q0[...])
        add(at(turned(3, odd)), q0_last[:, pl.ds(here, rows)].T)
        trace(q0[:, own(2 * odd)])

    @pl.when(active & (place == 1))
    def _():
        add(at(turned(0, odd)), q01[...].T)
        add(at(turned(1, odd)), q11[...])
        add(at(turned(2, odd)), q21[...].T)
        add(at(turned(3, odd)), q31[...].T)
        trace(q11[:, pl.ds(here, rows)])

    @pl.when(active & (place == 2))
    def _():
        add(at(turned(0, odd)), q2_zero[:, pl.ds(here, rows)].T)
        add(at(1, 2), q2[...])
        trace(q2[:, own(1 - odd)])

    @pl.when(active & (place == 3))
    def _():
        add(at(turned(2, odd)), q3_two[...])

    @pl.when(place_ref[4] == 0)
    def _():
        out_ref[...] = sigma_ref[...]
        var_ref[...] = diagonal(sigma_ref[:, own(place_ref[2])].astype(F32))


def finish(place, pivot, sigma, received, kept):
    rows, nodes = pivot.shape
    chunk = 128
    width = nodes // 4

    def picked(which, blocks):
        return pl.BlockSpec(
            (chunk, blocks * width), lambda i, place: (jnp.where(place[1] == which, i, 0), 0)
        )

    def turned_block(start):
        return pl.BlockSpec(
            (rows, chunk),
            lambda i, place: (
                0,
                jnp.where(place[1] == 1, start(place[0]) * (width // chunk) + i, 0),
            ),
        )

    whole = lambda block: pl.BlockSpec((rows, width), lambda i, place: (0, block))
    return pl.pallas_call(
        finish_kernel,
        out_shape=(
            jax.ShapeDtypeStruct((rows, nodes), BF16),
            jax.ShapeDtypeStruct((1, rows), F32),
        ),
        grid_spec=pltpu.PrefetchScalarGridSpec(
            num_scalar_prefetch=1,
            grid=(rows // chunk,),
            in_specs=[
                pl.BlockSpec((chunk, nodes), lambda i, place: (i, 0)),
                pl.BlockSpec(
                    (chunk, nodes), lambda i, place: (jnp.where(place[4] == 0, i, 0), 0)
                ),
                picked(0, 3),
                whole(0),
                picked(2, 2),
                whole(2),
                picked(3, 1),
                turned_block(lambda odd: 1),
                picked(1, 1),
                turned_block(lambda odd: odd),
                turned_block(lambda odd: 1 - odd),
            ],
            out_specs=(
                pl.BlockSpec((chunk, nodes), lambda i, place: (i, 0)),
                pl.BlockSpec((1, chunk), lambda i, place: (0, i)),
            ),
        ),
        compiler_params=pltpu.CompilerParams(vmem_limit_bytes=12 * MIB),
        cost_estimate=HEAVY,
        name="finish",
    )(place, pivot, sigma, *received, *kept)


def last_kernel(place_ref, pivot_ref, q2_last, q3, old_ref, old_var_ref, out_ref, var_ref, sum_ref, sems):
    rows, nodes = pivot_ref.shape
    width = nodes // 4
    chunk = 128
    odd, place = place_ref[0], place_ref[1]
    active = place_ref[4] != 0

    def at(block, count=1):
        return pl.ds(pl.multiple_of(block * width, 128), count * width)

    def copies(here, pieces):
        return [
            pltpu.make_async_copy(
                sum_ref.at[here, source], out_ref.at[here, target], sems.at[which, here.start // chunk]
            )
            for which, (source, target, _) in enumerate(pieces)
        ]

    def write(pieces):
        for start in range(0, rows, chunk):
            here = pl.ds(start, chunk)
            for source, target, product in pieces:
                value = pivot_ref[here, target].astype(F32) + product(here).astype(F32)
                sum_ref[here, source] = value.astype(BF16)
            for copy in copies(here, pieces):
                copy.start()
        for start in range(0, rows, chunk):
            for copy in copies(pl.ds(start, chunk), pieces):
                copy.wait()

    var_ref[...] = old_var_ref[...]

    @pl.when(active & (place == 2))
    def _():
        write([(pl.ds(0, width), at(3 - 3 * odd), lambda here: q2_last[:, here].T)])

    @pl.when(active & (place == 3))
    def _():
        both, last = pl.ds(0, 2 * width), pl.ds(2 * width, width)
        for start in range(0, rows, chunk):
            here = pl.ds(start, chunk)
            own = pl.ds(pl.multiple_of(place_ref[2] * width + start, 128), chunk)
            value = pivot_ref[here, own].astype(F32)
            value = value + q3[here, pl.ds(2 * width + start, chunk)].astype(F32)
            var_ref[:, here] = diagonal_of(chunk)(value)
        write(
            [
                (both, at(2 * odd, 2), lambda here: q3[here, both]),
                (last, at(3 - 3 * odd), lambda here: q3[here, last]),
            ]
        )


def diagonal_of(rows):
    square = (rows, rows)
    on_diagonal = lax.broadcasted_iota(jnp.int32, square, 0) == lax.broadcasted_iota(
        jnp.int32, square, 1
    )
    return lambda value: jnp.sum(jnp.where(on_diagonal, value, 0.0), axis=0, keepdims=True)


def finish_last(place, pivot, q2_last, q3, covariance, variances):
    rows, nodes = pivot.shape
    width = nodes // 4
    vmem = pl.BlockSpec(memory_space=pltpu.VMEM)
    anywhere = pl.BlockSpec(memory_space=pl.ANY)
    return pl.pallas_call(
        last_kernel,
        out_shape=(
            jax.ShapeDtypeStruct((rows, nodes), BF16),
            jax.ShapeDtypeStruct((1, rows), F32),
        ),
        in_specs=[pl.BlockSpec(memory_space=pltpu.SMEM)] + [vmem] * 3 + [anywhere, vmem],
        out_specs=(anywhere, vmem),
        scratch_shapes=[
            pltpu.VMEM((rows, 3 * width), BF16),
            pltpu.SemaphoreType.DMA((2, rows // 128)),
        ],
        input_output_aliases={4: 0},
        compiler_params=pltpu.CompilerParams(vmem_limit_bytes=8 * MIB),
        cost_estimate=LIGHT,
        name="finish_last",
    )(place, pivot, q2_last, q3, covariance, variances)


def owned(sigma_next, separator, inverse_pivot, coupling_rate, lengths, step_index, node_class):
    sigma, pivot = sigma_next[0], inverse_pivot[0]
    odd = lax.axis_index("dom") % 2
    col = lax.axis_index("col")
    step = step_index[0]
    place = jnp.stack([odd, turned(col, odd), col, step, step < lengths[0]]).astype(jnp.int32)
    after = lambda value, *others: lax.optimization_barrier((value, *others))[0]

    shifted = passed_along(separator, "dom", -1)[0]
    p2 = moved(pivot, 2, 1)
    p0 = moved(pivot, 0, 1)
    c1 = [couple(pivot, node_class, coupling_rate, part, 2) for part in range(2)]
    across = turn(place, 1, 0, c1[0], None)
    across = turn(place, 1, 1, c1[1], across)

    row, far, near, last = prior_parts(place, after(shifted, across), sigma)
    far_zero, near_two, last_three = moved(far, 0, 1), moved(near, 2, 1), moved(last, 3, 1)

    c2 = couple_here(place, after(p2, last), node_class, coupling_rate)
    across = turn(place, 2, 0, c2, across)
    c0 = couple_here(place, after(p0, across), node_class, coupling_rate)
    across = turn(place, 0, 0, c0, across)
    c3 = [
        moved(after(c1[0], last_three, near_two, across), 3, 1),
        moved(after(c1[1], far_zero), 3, 1),
    ]
    prior = assemble(place, row, near_two, last_three, far_zero)

    h0 = multiply(place, [c0], prior)
    q0_own = multiply(place, [h0], across, lambda odd: odd, 3)
    q0 = moved(q0_own, 1, 0)
    h2 = multiply(place, [after(c2, q0_own)], prior)
    q2_own = product_two(place, h2, across, q0_own)
    q2 = moved(q2_own, 1, 2)

    h3 = multiply(place, c3, prior)
    q30, q32 = product_ends(place, h3, across)
    q0_last, q3_two = moved(q30, 1, 0), moved(q32, 1, 3)
    across = turn(place, 3, 0, c3[0], after(across, q30))
    across = turn(place, 3, 1, c3[1], across)
    q3_own = product_rest(place, h3, across, q30)
    q3 = moved(q3_own, 1, 3)
    q2_last = moved(q3_two, 3, 2)
    h1 = multiply(place, [after(c1[0], q3_own), c1[1]], prior)
    q11 = multiply(place, [h1], across, lambda odd: 1 + odd, 1)
    received = (q0, q0_last, q2, q2, q3_two)
    kept = (q0_own, q11, q2_own, q3_own)
    place_then = tick(place, q0, cost=LIGHT)
    covariance, variances = finish(place_then, pivot, sigma, received, kept)
    covariance, variances = finish_last(place, pivot, q2_last, q3, covariance, variances)
    return (covariance[None], variances)


def gathered(sigma_next, separator, inverse_pivot, coupling_rate, lengths, step_index, node_class):
    shifted = passed_along(separator, "dom", -1)
    prior = jnp.where(step_index[0] == 0, shifted[0], sigma_next[0])
    pivot = inverse_pivot[0].astype(F32)
    coupled = couple(inverse_pivot[0], node_class, coupling_rate)
    rows = coupled.shape[0]
    half = jnp.dot(
        coupled,
        lax.all_gather(prior, "col", axis=0, tiled=True),
        preferred_element_type=F32,
    ).astype(BF16)
    product = lax.dot_general(
        half,
        lax.all_gather(coupled, "col", axis=0, tiled=True),
        (((1,), (1,)), ((), ())),
        preferred_element_type=F32,
    )
    full = pivot + product
    active = step_index[0] < lengths[0]
    old = sigma_next[0]
    covariance = jnp.where(active, full.astype(BF16), old)
    first_col = lax.axis_index("col") * rows
    new_block = lax.dynamic_slice_in_dim(full, first_col, rows, 1)
    old_block = lax.dynamic_slice_in_dim(old, first_col, rows, 1)
    variances = jnp.where(active, jnp.diagonal(new_block), jnp.diagonal(old_block).astype(F32))
    return (covariance[None], variances[None])


def solution(mesh):
    local = owned if mesh.shape["col"] == 4 and mesh.shape["dom"] % 2 == 0 else gathered
    return jax.shard_map(
        local,
        mesh=mesh,
        in_specs=(
            P(("groups", "dom"), "col", None),
            P(("groups", "dom"), "col", None),
            P(("groups", "dom"), "col", None),
            P(("groups", "dom")),
            P(("groups", "dom")),
            P(("groups", "dom")),
            P("groups"),
        ),
        out_specs=(P(("groups", "dom"), "col", None), P(("groups", "dom"), "col")),
        check_vma=False,
    )
```

```python
import functools

import jax
import jax.numpy as jnp
from jax import lax
from jax.experimental import pallas as pl
from jax.experimental.pallas import tpu as pltpu
from jax.sharding import PartitionSpec as P

GX = 64
GY = 32
BF16 = jnp.bfloat16
F32 = jnp.float32
MIB = 1 << 20


def passed_along(value, axis, steps):
    count = lax.axis_size(axis)
    initial, last = (max(0, -steps), min(count, count - steps))
    return lax.ppermute(value, axis, [(source, source + steps) for source in range(initial, last)])


LIGHT = pl.CostEstimate(flops=1 << 20, bytes_accessed=1 << 16, transcendentals=0)
MEDIUM = pl.CostEstimate(flops=2000000000, bytes_accessed=1 << 16, transcendentals=0)
HEAVY = pl.CostEstimate(flops=14000000000, bytes_accessed=1 << 16, transcendentals=0)


def couple_kernel(rate_ref, class_ref, pivot_ref, out_ref, weight_ref):
    nodes = pivot_ref.shape[1]

    @pl.when(pl.program_id(0) == 0)
    def _():
        kind = class_ref[...]
        across = jnp.where(
            kind == 0, 0.25, jnp.where(kind == 1, 0.375, jnp.where(kind == 2, 0.125, 0.5))
        ).astype(F32)
        along = jnp.where(
            kind == 0, 0.25, jnp.where(kind == 1, 0.125, jnp.where(kind == 2, 0.375, 0.0))
        ).astype(F32)
        node = lax.broadcasted_iota(jnp.int32, (1, nodes), 1)
        column = node % GX
        parts = (
            jnp.where(column > 0, across, 0.0),
            jnp.where(column < GX - 1, across, 0.0),
            jnp.where(node >= GX, along, 0.0),
            jnp.where(node < nodes - GX, along, 0.0),
        )
        for which, part in enumerate(parts):
            weight_ref[which] = jnp.broadcast_to(part, (16, nodes))

    rate = rate_ref[0]

    def group(step, carry):
        rows = pl.ds(pl.multiple_of(step * 16, 16), 16)
        value = pivot_ref[rows, :].astype(F32)
        total = (
            value
            + weight_ref[0] * pltpu.roll(value, 1, 1)
            + weight_ref[1] * pltpu.roll(value, nodes - 1, 1)
            + weight_ref[2] * pltpu.roll(value, GX, 1)
            + weight_ref[3] * pltpu.roll(value, nodes - GX, 1)
        )
        out_ref[rows, :] = (rate * total).astype(BF16)
        return carry

    lax.fori_loop(0, pivot_ref.shape[0] // 16, group, 0)


def couple(pivot, node_class, rate, part=0, parts=1):
    rows, nodes = pivot.shape[0] // parts, pivot.shape[1]
    chunk = min(rows, 128)
    steps = rows // chunk
    return pl.pallas_call(
        couple_kernel,
        out_shape=jax.ShapeDtypeStruct((rows, nodes), BF16),
        grid=(steps,),
        in_specs=[
            pl.BlockSpec(memory_space=pltpu.SMEM),
            pl.BlockSpec((1, nodes), lambda i: (0, 0)),
            pl.BlockSpec((chunk, nodes), lambda i: (part * steps + i, 0)),
        ],
        out_specs=pl.BlockSpec((chunk, nodes), lambda i: (i, 0)),
        scratch_shapes=[pltpu.VMEM((4, 16, nodes), F32)],
        compiler_params=pltpu.CompilerParams(vmem_limit_bytes=6 * MIB),
        cost_estimate=LIGHT,
        name="couple",
    )(rate, node_class.reshape(1, nodes), pivot)


def turned(block, odd):
    return block + odd * (3 - 2 * block)


def route(source, target, doms):
    pairs = []
    for dom in range(doms):
        odd = dom % 2
        pairs.append((dom * 4 + turned(source, odd), dom * 4 + turned(target, odd)))
    return pairs


def moved(value, source, target):
    return lax.ppermute(value, ("dom", "col"), route(source, target, lax.axis_size("dom")))


def couple_here(place, pivot, node_class, rate):
    rows, nodes = pivot.shape
    chunk = 128

    def kernel(place_ref, *refs):
        @pl.when(place_ref[1] == 1)
        def _():
            couple_kernel(*refs)

    return pl.pallas_call(
        kernel,
        out_shape=jax.ShapeDtypeStruct((rows, nodes), BF16),
        grid_spec=pltpu.PrefetchScalarGridSpec(
            num_scalar_prefetch=1,
            grid=(rows // chunk,),
            in_specs=[
                pl.BlockSpec(memory_space=pltpu.SMEM),
                pl.BlockSpec((1, nodes), lambda i, place: (0, 0)),
                pl.BlockSpec((chunk, nodes), lambda i, place: (i, 0)),
            ],
            out_specs=pl.BlockSpec((chunk, nodes), lambda i, place: (i, 0)),
            scratch_shapes=[pltpu.VMEM((4, 16, nodes), F32)],
        ),
        compiler_params=pltpu.CompilerParams(vmem_limit_bytes=8 * MIB),
        cost_estimate=LIGHT,
        name="couple_here",
    )(place, rate, node_class.reshape(1, nodes), pivot)


def turn_kernel(place_ref, coupled_ref, *refs):
    @pl.when(place_ref[1] == 1)
    def _():
        refs[-1][...] = coupled_ref[...].T


def turn(place, panel, part, coupled, across):
    rows, nodes = coupled.shape
    chunk = 128
    steps = rows // chunk
    ratio = nodes // 4 // chunk
    return pl.pallas_call(
        turn_kernel,
        out_shape=jax.ShapeDtypeStruct((nodes, nodes), BF16),
        grid_spec=pltpu.PrefetchScalarGridSpec(
            num_scalar_prefetch=1,
            grid=(steps,),
            in_specs=[pl.BlockSpec((chunk, nodes), lambda i, place: (i, 0))]
            + ([] if across is None else [pl.BlockSpec(memory_space=pl.ANY)]),
            out_specs=pl.BlockSpec(
                (nodes, chunk),
                lambda i, place: (0, turned(panel, place[0]) * ratio + part * steps + i),
            ),
        ),
        input_output_aliases={} if across is None else {2: 0},
        compiler_params=pltpu.CompilerParams(vmem_limit_bytes=4 * MIB),
        cost_estimate=LIGHT,
        name="turn",
    )(place, coupled, *(() if across is None else (across,)))


def multiply_kernel(first, count, lefts, place_ref, *refs):
    left_refs, right_ref, out_ref = refs[:lefts], refs[lefts], refs[-1]
    width = right_ref.shape[0] // 4

    @pl.when(place_ref[1] == 1)
    def _():
        def block(step, carry):
            source = pl.multiple_of((first(place_ref[0]) + step) * width, 128)
            target = pl.multiple_of(step * width, 128)
            row = 0
            for left_ref in left_refs:
                rows = left_ref.shape[0]
                out_ref[row : row + rows, pl.ds(target, width)] = jnp.dot(
                    left_ref[...], right_ref[:, pl.ds(source, width)], preferred_element_type=F32
                ).astype(BF16)
                row += rows
            return carry

        lax.fori_loop(0, count, block, 0)


def multiply(place, lefts, right, first=lambda odd: 0, count=4):
    rows = sum(left.shape[0] for left in lefts)
    width = right.shape[0] // 4
    vmem = pl.BlockSpec(memory_space=pltpu.VMEM)
    return pl.pallas_call(
        functools.partial(multiply_kernel, first, count, len(lefts)),
        out_shape=jax.ShapeDtypeStruct((rows, count * width), BF16),
        in_specs=[pl.BlockSpec(memory_space=pltpu.SMEM)] + [vmem] * (len(lefts) + 1),
        out_specs=vmem,
        compiler_params=pltpu.CompilerParams(vmem_limit_bytes=6 * MIB),
        cost_estimate=LIGHT,
        name="multiply",
    )(place, *lefts, right)


def two_kernel(place_ref, left_ref, right_ref, zero_ref, out_ref):
    odd = place_ref[0]
    width = right_ref.shape[0] // 4
    multiply_kernel(lambda odd: 1, 2, 1, place_ref, left_ref, right_ref, out_ref)

    @pl.when(place_ref[1] == 1)
    def _():
        out_ref[:, 2 * width :] = zero_ref[:, pl.ds(pl.multiple_of((2 - 2 * odd) * width, 128), width)]


def product_two(place, half, across, zero):
    rows = half.shape[0]
    width = across.shape[0] // 4
    vmem = pl.BlockSpec(memory_space=pltpu.VMEM)
    return pl.pallas_call(
        two_kernel,
        out_shape=jax.ShapeDtypeStruct((rows, 3 * width), BF16),
        in_specs=[pl.BlockSpec(memory_space=pltpu.SMEM)] + [vmem] * 3,
        out_specs=vmem,
        compiler_params=pltpu.CompilerParams(vmem_limit_bytes=6 * MIB),
        cost_estimate=LIGHT,
        name="product_two",
    )(place, half, across, zero)


def half_kernel(place_ref, left_ref, right_ref, one_ref, out_ref):
    width = one_ref.shape[1]

    @pl.when(place_ref[1] == 1)
    def _():
        def block(step, carry):
            which = turned(step + (step > 0).astype(jnp.int32), place_ref[0])
            columns = pl.ds(pl.multiple_of(which * width, 128), width)
            out_ref[:, columns] = jnp.dot(
                left_ref[...], right_ref[:, columns], preferred_element_type=F32
            ).astype(BF16)
            return carry

        lax.fori_loop(0, 3, block, 0)
        columns = pl.ds(pl.multiple_of(turned(1, place_ref[0]) * width, 128), width)
        out_ref[:, columns] = one_ref[...]


def half_product(place, left, right, one):
    vmem = pl.BlockSpec(memory_space=pltpu.VMEM)
    return pl.pallas_call(
        half_kernel,
        out_shape=jax.ShapeDtypeStruct(left.shape, BF16),
        in_specs=[pl.BlockSpec(memory_space=pltpu.SMEM)] + [vmem] * 3,
        out_specs=vmem,
        compiler_params=pltpu.CompilerParams(vmem_limit_bytes=6 * MIB),
        cost_estimate=LIGHT,
        name="half_product",
    )(place, left, right, one)


def column_kernel(place_ref, own_ref, first_ref, second_ref, *refs):
    column_ref, out_refs = refs[0], refs[1:]

    @pl.when(place_ref[1] == 1)
    def _():
        width = own_ref.shape[0]
        for block in range(4):
            rows = pl.ds(block * width, width)
            column_ref[rows, :] = own_ref[:, rows].T
        for left_ref, out_ref in zip((first_ref, second_ref), out_refs):
            out_ref[...] = jnp.dot(
                left_ref[...], column_ref[...], preferred_element_type=F32
            ).astype(BF16)


def own_column(place, own, first, second):
    rows, nodes = own.shape
    vmem = pl.BlockSpec(memory_space=pltpu.VMEM)
    return pl.pallas_call(
        column_kernel,
        out_shape=(
            jax.ShapeDtypeStruct((nodes, rows), BF16),
            jax.ShapeDtypeStruct((rows, rows), BF16),
            jax.ShapeDtypeStruct((rows, rows), BF16),
        ),
        in_specs=[pl.BlockSpec(memory_space=pltpu.SMEM)] + [vmem] * 3,
        out_specs=(vmem, vmem, vmem),
        compiler_params=pltpu.CompilerParams(vmem_limit_bytes=6 * MIB),
        cost_estimate=LIGHT,
        name="own_column",
    )(place, own, first, second)


def rest_kernel(place_ref, left_ref, right_ref, zero_ref, out_ref):
    odd = place_ref[0]
    width = zero_ref.shape[1]

    @pl.when(place_ref[1] == 1)
    def _():
        out_ref[:, pl.ds(pl.multiple_of(odd * width, 128), width)] = zero_ref[...]
        for source, target in ((1 + odd, 1 - odd), (3 - 3 * odd, 2)):
            source = pl.multiple_of(source * width, 128)
            target = pl.multiple_of(target * width, 128)
            out_ref[:, pl.ds(target, width)] = jnp.dot(
                left_ref[...], right_ref[:, pl.ds(source, width)], preferred_element_type=F32
            ).astype(BF16)


def product_rest(place, half, across, zero):
    rows = half.shape[0]
    width = across.shape[0] // 4
    vmem = pl.BlockSpec(memory_space=pltpu.VMEM)
    return pl.pallas_call(
        rest_kernel,
        out_shape=jax.ShapeDtypeStruct((rows, 3 * width), BF16),
        in_specs=[pl.BlockSpec(memory_space=pltpu.SMEM)] + [vmem] * 3,
        out_specs=vmem,
        compiler_params=pltpu.CompilerParams(vmem_limit_bytes=6 * MIB),
        cost_estimate=LIGHT,
        name="product_rest",
    )(place, half, across, zero)


def prior_kernel(place_ref, shifted_ref, sigma_ref, out_ref):
    @pl.when(place_ref[3] == 0)
    def _():
        out_ref[...] = shifted_ref[...]

    @pl.when(place_ref[3] != 0)
    def _():
        out_ref[...] = sigma_ref[...]


def parts_kernel(place_ref, shifted_ref, sigma_ref, row_ref, far_ref, near_ref, last_ref):
    odd = place_ref[0]
    width = last_ref.shape[1]

    def at(block, count=1):
        return pl.ds(pl.multiple_of(block * width, 128), count * width)

    prior_kernel(place_ref, shifted_ref, sigma_ref, row_ref)
    near = row_ref[:, at(2 - 2 * odd, 2)]
    near_ref[...] = near
    far_ref[:, width:] = near
    far_ref[:, :width] = row_ref[:, at(3 * odd)]
    last_ref[...] = row_ref[:, at(3 - 3 * odd)]


def prior_parts(place, shifted, sigma):
    rows, nodes = sigma.shape
    chunk = 128
    width = nodes // 4
    out = lambda blocks: jax.ShapeDtypeStruct((rows, blocks * width), BF16)
    spec = lambda blocks: pl.BlockSpec((chunk, blocks * width), lambda i, place: (i, 0))
    return pl.pallas_call(
        parts_kernel,
        out_shape=(out(4), out(3), out(2), out(1)),
        grid_spec=pltpu.PrefetchScalarGridSpec(
            num_scalar_prefetch=1,
            grid=(rows // chunk,),
            in_specs=[
                pl.BlockSpec(
                    (chunk, nodes), lambda i, place: (jnp.where(place[3] == 0, i, 0), 0)
                ),
                pl.BlockSpec(
                    (chunk, nodes), lambda i, place: (jnp.where(place[3] == 0, 0, i), 0)
                ),
            ],
            out_specs=(spec(4), spec(3), spec(2), spec(1)),
        ),
        compiler_params=pltpu.CompilerParams(vmem_limit_bytes=8 * MIB),
        cost_estimate=LIGHT,
        name="prior_parts",
    )(place, shifted, sigma)


def assemble_kernel(place_ref, own, column, near_two, last_three, far_zero, out_ref):
    @pl.when(place_ref[1] == 1)
    def _():
        odd = place_ref[0]
        width = last_three.shape[1]

        def at(block):
            return pl.ds(pl.multiple_of(block * width, 128), width)

        near = 2 * (1 - odd)
        half = pl.ds(pl.multiple_of(near * width, 128), 2 * width)
        row = [turned(block, odd) for block in range(4)]
        out_ref[at(row[1]), :] = own[...]
        out_ref[at(row[2]), half] = near_two[...]
        out_ref[at(row[0]), at(row[0])] = far_zero[:, :width]
        out_ref[at(row[0]), half] = far_zero[:, width:]
        out_ref[at(row[3]), at(row[3])] = last_three[...]
        for block in (0, 2, 3):
            out_ref[at(row[block]), at(row[1])] = column[at(row[block]), :]
        for step in range(2):
            piece = slice((1 + step) * width, (2 + step) * width)
            out_ref[at(near + step), at(row[0])] = far_zero[:, piece].T
        out_ref[at(row[3]), at(row[2])] = near_two[:, at(1 - odd)].T


def assemble(place, *parts):
    nodes = parts[0].shape[1]
    vmem = pl.BlockSpec(memory_space=pltpu.VMEM)
    return pl.pallas_call(
        assemble_kernel,
        out_shape=jax.ShapeDtypeStruct((nodes, nodes), BF16),
        in_specs=[pl.BlockSpec(memory_space=pltpu.SMEM)] + [vmem] * 5,
        out_specs=vmem,
        compiler_params=pltpu.CompilerParams(vmem_limit_bytes=6 * MIB),
        cost_estimate=LIGHT,
        name="assemble",
    )(place, *parts)


def tick(place, *values, cost=HEAVY):
    def kernel(place_ref, *refs):
        for which in range(place.shape[0]):
            refs[-1][which] = place_ref[which]

    scalars = pl.BlockSpec(memory_space=pltpu.SMEM)
    return pl.pallas_call(
        kernel,
        out_shape=jax.ShapeDtypeStruct(place.shape, place.dtype),
        in_specs=[scalars] + [pl.BlockSpec(memory_space=pl.ANY)] * len(values),
        out_specs=scalars,
        compiler_params=pltpu.CompilerParams(vmem_limit_bytes=MIB),
        cost_estimate=cost,
        name="tick",
    )(place, *values)


def finish_kernel(
    place_ref, pivot_ref, sigma_ref,
    q0, q0_last, q2, q2_zero, q3_two,
    q01, q11, q21, q31,
    out_ref, var_ref,
):
    rows, nodes = pivot_ref.shape
    width = nodes // 4
    odd, place = place_ref[0], place_ref[1]
    here = pl.multiple_of(pl.program_id(0) * rows, 128)
    diagonal = diagonal_of(rows)

    def at(block, count=1):
        return pl.ds(pl.multiple_of(block * width, 128), count * width)

    def own(block):
        return pl.ds(pl.multiple_of(block * width + here, 128), rows)

    def add(columns, product):
        out_ref[:, columns] = (pivot_ref[:, columns].astype(F32) + product.astype(F32)).astype(BF16)

    def trace(product):
        var_ref[...] = diagonal(
            pivot_ref[:, own(place_ref[2])].astype(F32) + product.astype(F32)
        )

    active = place_ref[4] != 0

    @pl.when(active & (place == 0))
    def _():
        add(at(odd, 3), q0[...])
        add(at(turned(3, odd)), q0_last[:, pl.ds(here, rows)].T)
        trace(q0[:, own(2 * odd)])

    @pl.when(active & (place == 1))
    def _():
        add(at(turned(0, odd)), q01[...].T)
        add(at(turned(1, odd)), q11[...])
        add(at(turned(2, odd)), q21[...].T)
        add(at(turned(3, odd)), q31[...].T)
        trace(q11[:, pl.ds(here, rows)])

    @pl.when(active & (place == 2))
    def _():
        add(at(turned(0, odd)), q2_zero[:, pl.ds(here, rows)].T)
        add(at(1, 2), q2[...])
        trace(q2[:, own(1 - odd)])

    @pl.when(active & (place == 3))
    def _():
        add(at(turned(2, odd)), q3_two[...])

    @pl.when(place_ref[4] == 0)
    def _():
        out_ref[...] = sigma_ref[...]
        var_ref[...] = diagonal(sigma_ref[:, own(place_ref[2])].astype(F32))


def finish(place, pivot, sigma, received, kept):
    rows, nodes = pivot.shape
    chunk = 128
    width = nodes // 4

    def picked(which, blocks):
        return pl.BlockSpec(
            (chunk, blocks * width), lambda i, place: (jnp.where(place[1] == which, i, 0), 0)
        )

    def turned_block(start):
        return pl.BlockSpec(
            (rows, chunk),
            lambda i, place: (
                0,
                jnp.where(place[1] == 1, start(place[0]) * (width // chunk) + i, 0),
            ),
        )

    whole = lambda block: pl.BlockSpec((rows, width), lambda i, place: (0, block))
    return pl.pallas_call(
        finish_kernel,
        out_shape=(
            jax.ShapeDtypeStruct((rows, nodes), BF16),
            jax.ShapeDtypeStruct((1, rows), F32),
        ),
        grid_spec=pltpu.PrefetchScalarGridSpec(
            num_scalar_prefetch=1,
            grid=(rows // chunk,),
            in_specs=[
                pl.BlockSpec((chunk, nodes), lambda i, place: (i, 0)),
                pl.BlockSpec(
                    (chunk, nodes), lambda i, place: (jnp.where(place[4] == 0, i, 0), 0)
                ),
                picked(0, 3),
                whole(0),
                picked(2, 2),
                whole(2),
                picked(3, 1),
                turned_block(lambda odd: 1),
                picked(1, 1),
                turned_block(lambda odd: odd),
                turned_block(lambda odd: 1 - odd),
            ],
            out_specs=(
                pl.BlockSpec((chunk, nodes), lambda i, place: (i, 0)),
                pl.BlockSpec((1, chunk), lambda i, place: (0, i)),
            ),
        ),
        compiler_params=pltpu.CompilerParams(vmem_limit_bytes=12 * MIB),
        cost_estimate=HEAVY,
        name="finish",
    )(place, pivot, sigma, *received, *kept)


def last_kernel(place_ref, pivot_ref, q2_last, q3, old_ref, old_var_ref, out_ref, var_ref, sum_ref, sems):
    rows, nodes = pivot_ref.shape
    width = nodes // 4
    chunk = 128
    odd, place = place_ref[0], place_ref[1]
    active = place_ref[4] != 0

    def at(block, count=1):
        return pl.ds(pl.multiple_of(block * width, 128), count * width)

    def copies(here, pieces):
        return [
            pltpu.make_async_copy(
                sum_ref.at[here, source], out_ref.at[here, target], sems.at[which, here.start // chunk]
            )
            for which, (source, target, _) in enumerate(pieces)
        ]

    def write(pieces):
        for start in range(0, rows, chunk):
            here = pl.ds(start, chunk)
            for source, target, product in pieces:
                value = pivot_ref[here, target].astype(F32) + product(here).astype(F32)
                sum_ref[here, source] = value.astype(BF16)
            for copy in copies(here, pieces):
                copy.start()
        for start in range(0, rows, chunk):
            for copy in copies(pl.ds(start, chunk), pieces):
                copy.wait()

    var_ref[...] = old_var_ref[...]

    @pl.when(active & (place == 2))
    def _():
        write([(pl.ds(0, width), at(3 - 3 * odd), lambda here: q2_last[:, here].T)])

    @pl.when(active & (place == 3))
    def _():
        both, last = pl.ds(0, 2 * width), pl.ds(2 * width, width)
        for start in range(0, rows, chunk):
            here = pl.ds(start, chunk)
            own = pl.ds(pl.multiple_of(place_ref[2] * width + start, 128), chunk)
            value = pivot_ref[here, own].astype(F32)
            value = value + q3[here, pl.ds(2 * width + start, chunk)].astype(F32)
            var_ref[:, here] = diagonal_of(chunk)(value)
        write(
            [
                (both, at(2 * odd, 2), lambda here: q3[here, both]),
                (last, at(3 - 3 * odd), lambda here: q3[here, last]),
            ]
        )


def diagonal_of(rows):
    square = (rows, rows)
    on_diagonal = lax.broadcasted_iota(jnp.int32, square, 0) == lax.broadcasted_iota(
        jnp.int32, square, 1
    )
    return lambda value: jnp.sum(jnp.where(on_diagonal, value, 0.0), axis=0, keepdims=True)


def finish_last(place, pivot, q2_last, q3, covariance, variances):
    rows, nodes = pivot.shape
    width = nodes // 4
    vmem = pl.BlockSpec(memory_space=pltpu.VMEM)
    anywhere = pl.BlockSpec(memory_space=pl.ANY)
    return pl.pallas_call(
        last_kernel,
        out_shape=(
            jax.ShapeDtypeStruct((rows, nodes), BF16),
            jax.ShapeDtypeStruct((1, rows), F32),
        ),
        in_specs=[pl.BlockSpec(memory_space=pltpu.SMEM)] + [vmem] * 3 + [anywhere, vmem],
        out_specs=(anywhere, vmem),
        scratch_shapes=[
            pltpu.VMEM((rows, 3 * width), BF16),
            pltpu.SemaphoreType.DMA((2, rows // 128)),
        ],
        input_output_aliases={4: 0},
        compiler_params=pltpu.CompilerParams(vmem_limit_bytes=8 * MIB),
        cost_estimate=LIGHT,
        name="finish_last",
    )(place, pivot, q2_last, q3, covariance, variances)


def owned(sigma_next, separator, inverse_pivot, coupling_rate, lengths, step_index, node_class):
    sigma, pivot = sigma_next[0], inverse_pivot[0]
    odd = lax.axis_index("dom") % 2
    col = lax.axis_index("col")
    step = step_index[0]
    place = jnp.stack([odd, turned(col, odd), col, step, step < lengths[0]]).astype(jnp.int32)
    after = lambda value, *others: lax.optimization_barrier((value, *others))[0]

    shifted = passed_along(separator, "dom", -1)[0]
    p2 = moved(pivot, 2, 1)
    p0 = moved(pivot, 0, 1)
    c1 = [couple(pivot, node_class, coupling_rate, part, 2) for part in range(2)]
    across = turn(place, 1, 0, c1[0], None)
    across = turn(place, 1, 1, c1[1], across)

    row, far, near, last = prior_parts(place, after(shifted, across), sigma)
    far_zero, near_two, last_three = moved(far, 0, 1), moved(near, 2, 1), moved(last, 3, 1)

    c2 = couple_here(place, after(p2, last), node_class, coupling_rate)
    across = turn(place, 2, 0, c2, across)
    c0 = couple_here(place, after(p0, across), node_class, coupling_rate)
    across = turn(place, 0, 0, c0, across)
    column, h0_one, h2_one = own_column(place, row, c0, c2)
    c3 = [
        moved(after(c1[0], last_three, near_two, across), 3, 1),
        moved(after(c1[1], far_zero, h2_one), 3, 1),
    ]
    prior = assemble(place, row, column, near_two, last_three, far_zero)

    h0 = half_product(place, c0, prior, h0_one)
    q0_own = multiply(place, [h0], across, lambda odd: odd, 3)
    q0 = moved(q0_own, 1, 0)
    h2 = half_product(place, after(c2, q0_own), prior, h2_one)
    q2_own = product_two(place, h2, across, q0_own)
    q2 = moved(q2_own, 1, 2)

    h3 = multiply(place, c3, prior)
    q30 = multiply(place, [h3], across, lambda odd: 3 * odd, 1)
    q0_last = moved(q30, 1, 0)
    q32 = multiply(place, [after(h3, q30)], across, lambda odd: 2 - odd, 1)
    q3_two = moved(q32, 1, 3)
    across = turn(place, 3, 0, c3[0], after(across, q32))
    across = turn(place, 3, 1, c3[1], across)
    q3_own = product_rest(place, h3, across, q30)
    q3 = moved(q3_own, 1, 3)
    h1 = multiply(place, [after(c1[0], q3_own), c1[1]], prior)
    q11 = multiply(place, [h1], across, lambda odd: 1 + odd, 1)
    received = (q0, q0_last, q2, q2, q3_two)
    kept = (q0_own, q11, q2_own, q3_own)
    place_then = tick(tick(place, q0, cost=LIGHT), q0_last, cost=MEDIUM)
    q2_last = moved(after(q3_two, place_then), 3, 2)
    covariance, variances = finish(place_then, pivot, sigma, received, kept)
    covariance, variances = finish_last(place, pivot, q2_last, q3, covariance, variances)
    return (covariance[None], variances)


def gathered(sigma_next, separator, inverse_pivot, coupling_rate, lengths, step_index, node_class):
    shifted = passed_along(separator, "dom", -1)
    prior = jnp.where(step_index[0] == 0, shifted[0], sigma_next[0])
    pivot = inverse_pivot[0].astype(F32)
    coupled = couple(inverse_pivot[0], node_class, coupling_rate)
    rows = coupled.shape[0]
    half = jnp.dot(
        coupled,
        lax.all_gather(prior, "col", axis=0, tiled=True),
        preferred_element_type=F32,
    ).astype(BF16)
    product = lax.dot_general(
        half,
        lax.all_gather(coupled, "col", axis=0, tiled=True),
        (((1,), (1,)), ((), ())),
        preferred_element_type=F32,
    )
    full = pivot + product
    active = step_index[0] < lengths[0]
    old = sigma_next[0]
    covariance = jnp.where(active, full.astype(BF16), old)
    first_col = lax.axis_index("col") * rows
    new_block = lax.dynamic_slice_in_dim(full, first_col, rows, 1)
    old_block = lax.dynamic_slice_in_dim(old, first_col, rows, 1)
    variances = jnp.where(active, jnp.diagonal(new_block), jnp.diagonal(old_block).astype(F32))
    return (covariance[None], variances[None])


def solution(mesh):
    local = owned if mesh.shape["col"] == 4 and mesh.shape["dom"] % 2 == 0 else gathered
    return jax.shard_map(
        local,
        mesh=mesh,
        in_specs=(
            P(("groups", "dom"), "col", None),
            P(("groups", "dom"), "col", None),
            P(("groups", "dom"), "col", None),
            P(("groups", "dom")),
            P(("groups", "dom")),
            P(("groups", "dom")),
            P("groups"),
        ),
        out_specs=(P(("groups", "dom"), "col", None), P(("groups", "dom"), "col")),
        check_vma=False,
    )
```

```python
import functools

import jax
import jax.numpy as jnp
from jax import lax
from jax.experimental import pallas as pl
from jax.experimental.pallas import tpu as pltpu
from jax.sharding import PartitionSpec as P

GX = 64
GY = 32
BF16 = jnp.bfloat16
F32 = jnp.float32
MIB = 1 << 20


def passed_along(value, axis, steps):
    count = lax.axis_size(axis)
    initial, last = (max(0, -steps), min(count, count - steps))
    return lax.ppermute(value, axis, [(source, source + steps) for source in range(initial, last)])


LIGHT = pl.CostEstimate(flops=1 << 20, bytes_accessed=1 << 16, transcendentals=0)
MEDIUM = pl.CostEstimate(flops=2000000000, bytes_accessed=1 << 16, transcendentals=0)
HEAVY = pl.CostEstimate(flops=14000000000, bytes_accessed=1 << 16, transcendentals=0)


def couple_kernel(rate_ref, class_ref, pivot_ref, out_ref, weight_ref):
    nodes = pivot_ref.shape[1]

    @pl.when(pl.program_id(0) == 0)
    def _():
        kind = class_ref[...]
        across = jnp.where(
            kind == 0, 0.25, jnp.where(kind == 1, 0.375, jnp.where(kind == 2, 0.125, 0.5))
        ).astype(F32)
        along = jnp.where(
            kind == 0, 0.25, jnp.where(kind == 1, 0.125, jnp.where(kind == 2, 0.375, 0.0))
        ).astype(F32)
        node = lax.broadcasted_iota(jnp.int32, (1, nodes), 1)
        column = node % GX
        parts = (
            jnp.where(column > 0, across, 0.0),
            jnp.where(column < GX - 1, across, 0.0),
            jnp.where(node >= GX, along, 0.0),
            jnp.where(node < nodes - GX, along, 0.0),
        )
        for which, part in enumerate(parts):
            weight_ref[which] = jnp.broadcast_to(part, (16, nodes))

    rate = rate_ref[0]

    def group(step, carry):
        rows = pl.ds(pl.multiple_of(step * 16, 16), 16)
        value = pivot_ref[rows, :].astype(F32)
        total = (
            value
            + weight_ref[0] * pltpu.roll(value, 1, 1)
            + weight_ref[1] * pltpu.roll(value, nodes - 1, 1)
            + weight_ref[2] * pltpu.roll(value, GX, 1)
            + weight_ref[3] * pltpu.roll(value, nodes - GX, 1)
        )
        out_ref[rows, :] = (rate * total).astype(BF16)
        return carry

    lax.fori_loop(0, pivot_ref.shape[0] // 16, group, 0)


def couple(pivot, node_class, rate, part=0, parts=1):
    rows, nodes = pivot.shape[0] // parts, pivot.shape[1]
    chunk = min(rows, 128)
    steps = rows // chunk
    return pl.pallas_call(
        couple_kernel,
        out_shape=jax.ShapeDtypeStruct((rows, nodes), BF16),
        grid=(steps,),
        in_specs=[
            pl.BlockSpec(memory_space=pltpu.SMEM),
            pl.BlockSpec((1, nodes), lambda i: (0, 0)),
            pl.BlockSpec((chunk, nodes), lambda i: (part * steps + i, 0)),
        ],
        out_specs=pl.BlockSpec((chunk, nodes), lambda i: (i, 0)),
        scratch_shapes=[pltpu.VMEM((4, 16, nodes), F32)],
        compiler_params=pltpu.CompilerParams(vmem_limit_bytes=6 * MIB),
        cost_estimate=LIGHT,
        name="couple",
    )(rate, node_class.reshape(1, nodes), pivot)


def turned(block, odd):
    return block + odd * (3 - 2 * block)


def route(source, target, doms):
    pairs = []
    for dom in range(doms):
        odd = dom % 2
        pairs.append((dom * 4 + turned(source, odd), dom * 4 + turned(target, odd)))
    return pairs


def moved(value, source, target):
    return lax.ppermute(value, ("dom", "col"), route(source, target, lax.axis_size("dom")))


def couple_here(place, pivot, node_class, rate):
    rows, nodes = pivot.shape
    chunk = 128

    def kernel(place_ref, *refs):
        @pl.when(place_ref[1] == 1)
        def _():
            couple_kernel(*refs)

    return pl.pallas_call(
        kernel,
        out_shape=jax.ShapeDtypeStruct((rows, nodes), BF16),
        grid_spec=pltpu.PrefetchScalarGridSpec(
            num_scalar_prefetch=1,
            grid=(rows // chunk,),
            in_specs=[
                pl.BlockSpec(memory_space=pltpu.SMEM),
                pl.BlockSpec((1, nodes), lambda i, place: (0, 0)),
                pl.BlockSpec((chunk, nodes), lambda i, place: (i, 0)),
            ],
            out_specs=pl.BlockSpec((chunk, nodes), lambda i, place: (i, 0)),
            scratch_shapes=[pltpu.VMEM((4, 16, nodes), F32)],
        ),
        compiler_params=pltpu.CompilerParams(vmem_limit_bytes=8 * MIB),
        cost_estimate=LIGHT,
        name="couple_here",
    )(place, rate, node_class.reshape(1, nodes), pivot)


def turn_kernel(place_ref, coupled_ref, *refs):
    @pl.when(place_ref[1] == 1)
    def _():
        refs[-1][...] = coupled_ref[...].T


def turn(place, panel, part, coupled, across):
    rows, nodes = coupled.shape
    chunk = 128
    steps = rows // chunk
    ratio = nodes // 4 // chunk
    return pl.pallas_call(
        turn_kernel,
        out_shape=jax.ShapeDtypeStruct((nodes, nodes), BF16),
        grid_spec=pltpu.PrefetchScalarGridSpec(
            num_scalar_prefetch=1,
            grid=(steps,),
            in_specs=[pl.BlockSpec((chunk, nodes), lambda i, place: (i, 0))]
            + ([] if across is None else [pl.BlockSpec(memory_space=pl.ANY)]),
            out_specs=pl.BlockSpec(
                (nodes, chunk),
                lambda i, place: (0, turned(panel, place[0]) * ratio + part * steps + i),
            ),
        ),
        input_output_aliases={} if across is None else {2: 0},
        compiler_params=pltpu.CompilerParams(vmem_limit_bytes=4 * MIB),
        cost_estimate=LIGHT,
        name="turn",
    )(place, coupled, *(() if across is None else (across,)))


def multiply_kernel(first, count, lefts, place_ref, *refs):
    left_refs, right_ref, out_ref = refs[:lefts], refs[lefts], refs[-1]
    width = right_ref.shape[0] // 4

    @pl.when(place_ref[1] == 1)
    def _():
        def block(step, carry):
            source = pl.multiple_of((first(place_ref[0]) + step) * width, 128)
            target = pl.multiple_of(step * width, 128)
            row = 0
            for left_ref in left_refs:
                rows = left_ref.shape[0]
                out_ref[row : row + rows, pl.ds(target, width)] = jnp.dot(
                    left_ref[...], right_ref[:, pl.ds(source, width)], preferred_element_type=F32
                ).astype(BF16)
                row += rows
            return carry

        lax.fori_loop(0, count, block, 0)


def multiply(place, lefts, right, first=lambda odd: 0, count=4):
    rows = sum(left.shape[0] for left in lefts)
    width = right.shape[0] // 4
    vmem = pl.BlockSpec(memory_space=pltpu.VMEM)
    return pl.pallas_call(
        functools.partial(multiply_kernel, first, count, len(lefts)),
        out_shape=jax.ShapeDtypeStruct((rows, count * width), BF16),
        in_specs=[pl.BlockSpec(memory_space=pltpu.SMEM)] + [vmem] * (len(lefts) + 1),
        out_specs=vmem,
        compiler_params=pltpu.CompilerParams(vmem_limit_bytes=6 * MIB),
        cost_estimate=LIGHT,
        name="multiply",
    )(place, *lefts, right)


def pack(value, out_ref, column):
    half = value.shape[0] // 2
    for part in range(2):
        rows = pl.ds(part * half, half)
        pack_rows(part, value[part * half : (part + 1) * half], out_ref.at[rows], column)


def two_kernel(place_ref, left_ref, right_ref, zero_ref, out_ref):
    odd = place_ref[0]
    width = right_ref.shape[0] // 4

    def product(block):
        columns = pl.ds(pl.multiple_of(block * width, 128), width)
        value = jnp.dot(left_ref[...], right_ref[:, columns], preferred_element_type=F32)
        return value.astype(BF16)

    @pl.when(place_ref[1] == 1)
    def _():
        out_ref[:, :width] = product(1 + odd)
        zero = pl.ds(pl.multiple_of((2 - 2 * odd) * width, 128), width)
        out_ref[:, width : 2 * width] = zero_ref[:, zero]
        pack(product(2 - odd), out_ref, 2 * width)


def product_two(place, half, across, zero):
    rows = half.shape[0]
    width = across.shape[0] // 4
    vmem = pl.BlockSpec(memory_space=pltpu.VMEM)
    return pl.pallas_call(
        two_kernel,
        out_shape=jax.ShapeDtypeStruct((rows, 11 * width // 4), BF16),
        in_specs=[pl.BlockSpec(memory_space=pltpu.SMEM)] + [vmem] * 3,
        out_specs=vmem,
        compiler_params=pltpu.CompilerParams(vmem_limit_bytes=6 * MIB),
        cost_estimate=LIGHT,
        name="product_two",
    )(place, half, across, zero)


def half_kernel(place_ref, left_ref, right_ref, one_ref, out_ref):
    width = one_ref.shape[1]

    @pl.when(place_ref[1] == 1)
    def _():
        def block(step, carry):
            which = turned(step + (step > 0).astype(jnp.int32), place_ref[0])
            columns = pl.ds(pl.multiple_of(which * width, 128), width)
            out_ref[:, columns] = jnp.dot(
                left_ref[...], right_ref[:, columns], preferred_element_type=F32
            ).astype(BF16)
            return carry

        lax.fori_loop(0, 3, block, 0)
        columns = pl.ds(pl.multiple_of(turned(1, place_ref[0]) * width, 128), width)
        out_ref[:, columns] = one_ref[...]


def half_product(place, left, right, one):
    vmem = pl.BlockSpec(memory_space=pltpu.VMEM)
    return pl.pallas_call(
        half_kernel,
        out_shape=jax.ShapeDtypeStruct(left.shape, BF16),
        in_specs=[pl.BlockSpec(memory_space=pltpu.SMEM)] + [vmem] * 3,
        out_specs=vmem,
        compiler_params=pltpu.CompilerParams(vmem_limit_bytes=6 * MIB),
        cost_estimate=LIGHT,
        name="half_product",
    )(place, left, right, one)


def column_kernel(place_ref, own_ref, first_ref, second_ref, *refs):
    column_ref, out_refs = refs[0], refs[1:]

    @pl.when(place_ref[1] == 1)
    def _():
        width = own_ref.shape[0]
        for block in range(4):
            rows = pl.ds(block * width, width)
            column_ref[rows, :] = own_ref[:, rows].T
        for left_ref, out_ref in zip((first_ref, second_ref), out_refs):
            out_ref[...] = jnp.dot(
                left_ref[...], column_ref[...], preferred_element_type=F32
            ).astype(BF16)


def own_column(place, own, first, second):
    rows, nodes = own.shape
    vmem = pl.BlockSpec(memory_space=pltpu.VMEM)
    return pl.pallas_call(
        column_kernel,
        out_shape=(
            jax.ShapeDtypeStruct((nodes, rows), BF16),
            jax.ShapeDtypeStruct((rows, rows), BF16),
            jax.ShapeDtypeStruct((rows, rows), BF16),
        ),
        in_specs=[pl.BlockSpec(memory_space=pltpu.SMEM)] + [vmem] * 3,
        out_specs=(vmem, vmem, vmem),
        compiler_params=pltpu.CompilerParams(vmem_limit_bytes=6 * MIB),
        cost_estimate=LIGHT,
        name="own_column",
    )(place, own, first, second)


def rest_kernel(place_ref, left_ref, right_ref, zero_ref, out_ref):
    odd = place_ref[0]
    width = zero_ref.shape[1]

    def product(block):
        columns = pl.ds(pl.multiple_of(block * width, 128), width)
        value = jnp.dot(left_ref[...], right_ref[:, columns], preferred_element_type=F32)
        return value.astype(BF16)

    @pl.when(place_ref[1] == 1)
    def _():
        out_ref[:, pl.ds(pl.multiple_of(odd * width, 128), width)] = zero_ref[...]
        out_ref[:, pl.ds(pl.multiple_of((1 - odd) * width, 128), width)] = product(1 + odd)
        pack(product(3 - 3 * odd), out_ref, 2 * width)


def product_rest(place, half, across, zero):
    rows = half.shape[0]
    width = across.shape[0] // 4
    vmem = pl.BlockSpec(memory_space=pltpu.VMEM)
    return pl.pallas_call(
        rest_kernel,
        out_shape=jax.ShapeDtypeStruct((rows, 11 * width // 4), BF16),
        in_specs=[pl.BlockSpec(memory_space=pltpu.SMEM)] + [vmem] * 3,
        out_specs=vmem,
        compiler_params=pltpu.CompilerParams(vmem_limit_bytes=6 * MIB),
        cost_estimate=LIGHT,
        name="product_rest",
    )(place, half, across, zero)


def pack_rows(part, value, out_ref, column):
    half, width = value.shape
    quarter = half // 2
    if part == 0:
        out_ref[:, column : column + half] = value[:, :half]
        out_ref[:, column + half : column + half + quarter] = value[:, half : half + quarter]
    else:
        out_ref[:, column : column + half] = value[:, half:]
        beside = slice(column + half, column + half + quarter)
        out_ref[:quarter, beside] = value[quarter:, :quarter]
        out_ref[quarter:, beside] = value[quarter:, quarter:half]


def unpacked_rows(part, packed_ref, column):
    quarter = packed_ref.shape[0] // 4
    half = 2 * quarter
    beside = slice(column + half, column + half + quarter)
    rows = slice(part * quarter, (part + 1) * quarter)
    diagonal = packed_ref[rows, column : column + half]
    lower = [packed_ref[start : start + quarter, beside] for start in (half, half + quarter)]
    if part < 2:
        return diagonal, jnp.concatenate([packed_ref[rows, beside], lower[part].T], axis=1)
    if part == 2:
        return packed_ref[:half, beside].T, diagonal
    return jnp.concatenate(lower, axis=1), diagonal


def prior_kernel(place_ref, shifted_ref, sigma_ref, out_ref):
    @pl.when(place_ref[3] == 0)
    def _():
        out_ref[...] = shifted_ref[...]

    @pl.when(place_ref[3] != 0)
    def _():
        out_ref[...] = sigma_ref[...]


def parts_kernel(place_ref, shifted_ref, sigma_ref, row_ref, far_ref, near_ref, last_ref):
    odd = place_ref[0]
    width = row_ref.shape[1] // 4

    def at(block, count=1):
        return pl.ds(pl.multiple_of(block * width, 128), count * width)

    prior_kernel(place_ref, shifted_ref, sigma_ref, row_ref)
    far_ref[:, : 2 * width] = row_ref[:, at(2 - 2 * odd, 2)]
    near_ref[:, :width] = row_ref[:, at(3 - 3 * odd)]
    for part in range(2):

        @pl.when(pl.program_id(0) == part)
        def _():
            pack_rows(part, row_ref[:, at(3 * odd)], far_ref, 2 * width)
            pack_rows(part, row_ref[:, at(2 - odd)], near_ref, width)
            pack_rows(part, row_ref[:, at(3 - 3 * odd)], last_ref, 0)


def prior_parts(place, shifted, sigma):
    rows, nodes = sigma.shape
    chunk = rows // 2
    width = nodes // 4
    out = lambda quarters: jax.ShapeDtypeStruct((rows, quarters * width // 4), BF16)
    spec = lambda quarters: pl.BlockSpec((chunk, quarters * width // 4), lambda i, place: (i, 0))
    return pl.pallas_call(
        parts_kernel,
        out_shape=(out(16), out(11), out(7), out(3)),
        grid_spec=pltpu.PrefetchScalarGridSpec(
            num_scalar_prefetch=1,
            grid=(rows // chunk,),
            in_specs=[
                pl.BlockSpec(
                    (chunk, nodes), lambda i, place: (jnp.where(place[3] == 0, i, 0), 0)
                ),
                pl.BlockSpec(
                    (chunk, nodes), lambda i, place: (jnp.where(place[3] == 0, 0, i), 0)
                ),
            ],
            out_specs=(spec(16), spec(11), spec(7), spec(3)),
        ),
        compiler_params=pltpu.CompilerParams(vmem_limit_bytes=14 * MIB),
        cost_estimate=LIGHT,
        name="prior_parts",
    )(place, shifted, sigma)


def assemble_kernel(place_ref, own, column, near_two, last_three, far_zero, out_ref):
    @pl.when(place_ref[1] == 1)
    def _():
        odd = place_ref[0]
        width = own.shape[0]
        half, quarter = width // 2, width // 4

        def at(block, count=1):
            return pl.ds(pl.multiple_of(block * width, 128), count * width)

        near = 2 * (1 - odd)
        row = [turned(block, odd) for block in range(4)]
        out_ref[at(row[1]), :] = own[...]
        out_ref[at(row[2]), at(row[3])] = near_two[:, :width]
        out_ref[at(row[3]), at(row[2])] = near_two[:, :width].T
        out_ref[at(row[0]), at(near, 2)] = far_zero[:, : 2 * width]
        for step in range(2):
            out_ref[at(near + step), at(row[0])] = far_zero[:, step * width : (1 + step) * width].T
        for block in (0, 2, 3):
            out_ref[at(row[block]), at(row[1])] = column[at(row[block]), :]
        packed = ((0, far_zero, 2 * width), (2, near_two, width), (3, last_three, 0))
        for block, packed_ref, start in packed:
            for part in range(4):
                rows = pl.ds(pl.multiple_of(row[block] * width + part * quarter, 128), quarter)
                for side, value in enumerate(unpacked_rows(part, packed_ref, start)):
                    columns = pl.ds(pl.multiple_of(row[block] * width + side * half, 128), half)
                    out_ref[rows, columns] = value


def assemble(place, *parts):
    nodes = parts[0].shape[1]
    vmem = pl.BlockSpec(memory_space=pltpu.VMEM)
    return pl.pallas_call(
        assemble_kernel,
        out_shape=jax.ShapeDtypeStruct((nodes, nodes), BF16),
        in_specs=[pl.BlockSpec(memory_space=pltpu.SMEM)] + [vmem] * 5,
        out_specs=vmem,
        compiler_params=pltpu.CompilerParams(vmem_limit_bytes=6 * MIB),
        cost_estimate=LIGHT,
        name="assemble",
    )(place, *parts)


def tick(place, *values, cost=HEAVY):
    def kernel(place_ref, *refs):
        for which in range(place.shape[0]):
            refs[-1][which] = place_ref[which]

    scalars = pl.BlockSpec(memory_space=pltpu.SMEM)
    return pl.pallas_call(
        kernel,
        out_shape=jax.ShapeDtypeStruct(place.shape, place.dtype),
        in_specs=[scalars] + [pl.BlockSpec(memory_space=pl.ANY)] * len(values),
        out_specs=scalars,
        compiler_params=pltpu.CompilerParams(vmem_limit_bytes=MIB),
        cost_estimate=cost,
        name="tick",
    )(place, *values)


def finish_kernel(
    place_ref, pivot_ref, sigma_ref,
    q0, q0_last, q2, q3_two,
    q01, q11, q21, q31,
    out_ref, var_ref,
):
    rows, nodes = pivot_ref.shape
    width = nodes // 4
    odd, place = place_ref[0], place_ref[1]
    here = pl.multiple_of(pl.program_id(0) * rows, 128)
    diagonal = diagonal_of(rows)

    def at(block, count=1):
        return pl.ds(pl.multiple_of(block * width, 128), count * width)

    def own(block):
        return pl.ds(pl.multiple_of(block * width + here, 128), rows)

    def add(columns, product):
        out_ref[:, columns] = (pivot_ref[:, columns].astype(F32) + product.astype(F32)).astype(BF16)

    def trace(product):
        var_ref[...] = diagonal(
            pivot_ref[:, own(place_ref[2])].astype(F32) + product.astype(F32)
        )

    active = place_ref[4] != 0

    @pl.when(active & (place == 0))
    def _():
        add(at(odd, 3), q0[...])
        add(at(turned(3, odd)), q0_last[:, pl.ds(here, rows)].T)
        trace(q0[:, own(2 * odd)])

    @pl.when(active & (place == 1))
    def _():
        add(at(turned(0, odd)), q01[...].T)
        add(at(turned(1, odd)), q11[...])
        add(at(turned(2, odd)), q21[...].T)
        add(at(turned(3, odd)), q31[...].T)
        trace(q11[:, pl.ds(here, rows)])

    @pl.when(active & (place == 2))
    def _():
        add(at(turned(0, odd)), q2[pl.ds(0, width), pl.ds(pl.multiple_of(width + here, 128), rows)].T)
        add(at(turned(1, odd)), q2[pl.ds(here, rows), pl.ds(0, width)])
        start = pl.program_id(0) % 2 * rows + 2 * width
        trace(q2[pl.ds(here, rows), pl.ds(pl.multiple_of(start, 128), rows)])
        for part in range(4):

            @pl.when(pl.program_id(0) == part)
            def _():
                for side, value in enumerate(unpacked_rows(part, q2, 2 * width)):
                    start = turned(2, odd) * width + side * width // 2
                    add(pl.ds(pl.multiple_of(start, 128), width // 2), value)

    @pl.when(active & (place == 3))
    def _():
        add(at(turned(2, odd)), q3_two[...])

    @pl.when(place_ref[4] == 0)
    def _():
        out_ref[...] = sigma_ref[...]
        var_ref[...] = diagonal(sigma_ref[:, own(place_ref[2])].astype(F32))


def finish(place, pivot, sigma, received, kept):
    rows, nodes = pivot.shape
    chunk = 128
    width = nodes // 4

    def picked(which, blocks):
        return pl.BlockSpec(
            (chunk, blocks * width), lambda i, place: (jnp.where(place[1] == which, i, 0), 0)
        )

    def turned_block(start):
        return pl.BlockSpec(
            (rows, chunk),
            lambda i, place: (
                0,
                jnp.where(place[1] == 1, start(place[0]) * (width // chunk) + i, 0),
            ),
        )

    whole = lambda block: pl.BlockSpec((rows, width), lambda i, place: (0, block))
    return pl.pallas_call(
        finish_kernel,
        out_shape=(
            jax.ShapeDtypeStruct((rows, nodes), BF16),
            jax.ShapeDtypeStruct((1, rows), F32),
        ),
        grid_spec=pltpu.PrefetchScalarGridSpec(
            num_scalar_prefetch=1,
            grid=(rows // chunk,),
            in_specs=[
                pl.BlockSpec((chunk, nodes), lambda i, place: (i, 0)),
                pl.BlockSpec(
                    (chunk, nodes), lambda i, place: (jnp.where(place[4] == 0, i, 0), 0)
                ),
                picked(0, 3),
                whole(0),
                pl.BlockSpec((rows, 11 * width // 4), lambda i, place: (0, 0)),
                picked(3, 1),
                turned_block(lambda odd: 1),
                picked(1, 1),
                turned_block(lambda odd: 0),
                turned_block(lambda odd: 1 - odd),
            ],
            out_specs=(
                pl.BlockSpec((chunk, nodes), lambda i, place: (i, 0)),
                pl.BlockSpec((1, chunk), lambda i, place: (0, i)),
            ),
        ),
        compiler_params=pltpu.CompilerParams(vmem_limit_bytes=12 * MIB),
        cost_estimate=HEAVY,
        name="finish",
    )(place, pivot, sigma, *received, *kept)


def last_kernel(place_ref, pivot_ref, q2_last, q3, old_ref, old_var_ref, out_ref, var_ref, sum_ref, sems):
    rows, nodes = pivot_ref.shape
    width = nodes // 4
    chunk = 128
    odd, place = place_ref[0], place_ref[1]
    active = place_ref[4] != 0

    def at(block, count=1):
        return pl.ds(pl.multiple_of(block * width, 128), count * width)

    def copies(part, pieces):
        here = pl.ds(part * chunk, chunk)
        return [
            pltpu.make_async_copy(
                sum_ref.at[here, source], out_ref.at[here, target], sems.at[which, part]
            )
            for which, (source, target, _) in enumerate(pieces)
        ]

    def write(pieces):
        for part in range(4):
            here = pl.ds(part * chunk, chunk)
            for source, target, product in pieces:
                value = pivot_ref[here, target].astype(F32) + product(part, here).astype(F32)
                sum_ref[here, source] = value.astype(BF16)
            for copy in copies(part, pieces):
                copy.start()
        for part in range(4):
            for copy in copies(part, pieces):
                copy.wait()

    var_ref[...] = old_var_ref[...]

    @pl.when(active & (place == 2))
    def _():
        write([(pl.ds(0, width), at(3 - 3 * odd), lambda part, here: q2_last[:, here].T)])

    @pl.when(active & (place == 3))
    def _():
        both, last = pl.ds(0, 2 * width), pl.ds(2 * width, width)
        for start in range(0, rows, chunk):
            here = pl.ds(start, chunk)
            own = pl.ds(pl.multiple_of(place_ref[2] * width + start, 128), chunk)
            value = pivot_ref[here, own].astype(F32)
            value = value + q3[here, pl.ds(2 * width + start % (2 * chunk), chunk)].astype(F32)
            var_ref[:, here] = diagonal_of(chunk)(value)
        write(
            [
                (both, at(2 * odd, 2), lambda part, here: q3[here, both]),
                (
                    last,
                    at(3 - 3 * odd),
                    lambda part, here: jnp.concatenate(unpacked_rows(part, q3, 2 * width), axis=1),
                ),
            ]
        )


def diagonal_of(rows):
    square = (rows, rows)
    on_diagonal = lax.broadcasted_iota(jnp.int32, square, 0) == lax.broadcasted_iota(
        jnp.int32, square, 1
    )
    return lambda value: jnp.sum(jnp.where(on_diagonal, value, 0.0), axis=0, keepdims=True)


def finish_last(place, pivot, q2_last, q3, covariance, variances):
    rows, nodes = pivot.shape
    width = nodes // 4
    vmem = pl.BlockSpec(memory_space=pltpu.VMEM)
    anywhere = pl.BlockSpec(memory_space=pl.ANY)
    return pl.pallas_call(
        last_kernel,
        out_shape=(
            jax.ShapeDtypeStruct((rows, nodes), BF16),
            jax.ShapeDtypeStruct((1, rows), F32),
        ),
        in_specs=[pl.BlockSpec(memory_space=pltpu.SMEM)] + [vmem] * 3 + [anywhere, vmem],
        out_specs=(anywhere, vmem),
        scratch_shapes=[
            pltpu.VMEM((rows, 3 * width), BF16),
            pltpu.SemaphoreType.DMA((2, rows // 128)),
        ],
        input_output_aliases={4: 0},
        compiler_params=pltpu.CompilerParams(vmem_limit_bytes=8 * MIB),
        cost_estimate=LIGHT,
        name="finish_last",
    )(place, pivot, q2_last, q3, covariance, variances)


def owned(sigma_next, separator, inverse_pivot, coupling_rate, lengths, step_index, node_class):
    sigma, pivot = sigma_next[0], inverse_pivot[0]
    odd = lax.axis_index("dom") % 2
    col = lax.axis_index("col")
    step = step_index[0]
    place = jnp.stack([odd, turned(col, odd), col, step, step < lengths[0]]).astype(jnp.int32)
    after = lambda value, *others: lax.optimization_barrier((value, *others))[0]

    shifted = passed_along(separator, "dom", -1)[0]
    p2 = moved(pivot, 2, 1)
    p0 = moved(pivot, 0, 1)
    c1 = [couple(pivot, node_class, coupling_rate, part, 2) for part in range(2)]
    across = turn(place, 1, 0, c1[0], None)
    across = turn(place, 1, 1, c1[1], across)

    row, far, near, last = prior_parts(place, after(shifted, across), sigma)
    far_zero, near_two, last_three = moved(far, 0, 1), moved(near, 2, 1), moved(last, 3, 1)

    c2 = couple_here(place, after(p2, last), node_class, coupling_rate)
    across = turn(place, 2, 0, c2, across)
    c0 = couple_here(place, after(p0, across), node_class, coupling_rate)
    across = turn(place, 0, 0, c0, across)
    column, h0_one, h2_one = own_column(place, row, c0, c2)
    c3 = [
        moved(after(c1[0], last_three, near_two, across), 3, 1),
        moved(after(c1[1], far_zero, h2_one), 3, 1),
    ]
    prior = assemble(place, row, column, near_two, last_three, far_zero)

    h0 = half_product(place, c0, prior, h0_one)
    q0_own = multiply(place, [h0], across, lambda odd: odd, 3)
    q0 = moved(q0_own, 1, 0)
    h2 = half_product(place, after(c2, q0_own), prior, h2_one)
    q2_own = product_two(place, h2, across, q0_own)
    q2 = moved(q2_own, 1, 2)

    h3 = multiply(place, c3, prior)
    q30 = multiply(place, [h3], across, lambda odd: 3 * odd, 1)
    q0_last = moved(q30, 1, 0)
    q32 = multiply(place, [after(h3, q30)], across, lambda odd: 2 - odd, 1)
    q3_two = moved(q32, 1, 3)
    across = turn(place, 3, 0, c3[0], after(across, q32))
    across = turn(place, 3, 1, c3[1], across)
    q3_own = product_rest(place, h3, across, q30)
    q3 = moved(q3_own, 1, 3)
    h1 = multiply(place, [after(c1[0], q3_own), c1[1]], prior)
    q11 = multiply(place, [h1], across, lambda odd: 1 + odd, 1)
    received = (q0, q0_last, q2, q3_two)
    kept = (q0_own, q11, q2_own, q3_own)
    place_then = tick(tick(place, q0, cost=LIGHT), q0_last, cost=MEDIUM)
    q2_last = moved(after(q3_two, place_then), 3, 2)
    covariance, variances = finish(place_then, pivot, sigma, received, kept)
    covariance, variances = finish_last(place, pivot, q2_last, q3, covariance, variances)
    return (covariance[None], variances)


def gathered(sigma_next, separator, inverse_pivot, coupling_rate, lengths, step_index, node_class):
    shifted = passed_along(separator, "dom", -1)
    prior = jnp.where(step_index[0] == 0, shifted[0], sigma_next[0])
    pivot = inverse_pivot[0].astype(F32)
    coupled = couple(inverse_pivot[0], node_class, coupling_rate)
    rows = coupled.shape[0]
    half = jnp.dot(
        coupled,
        lax.all_gather(prior, "col", axis=0, tiled=True),
        preferred_element_type=F32,
    ).astype(BF16)
    product = lax.dot_general(
        half,
        lax.all_gather(coupled, "col", axis=0, tiled=True),
        (((1,), (1,)), ((), ())),
        preferred_element_type=F32,
    )
    full = pivot + product
    active = step_index[0] < lengths[0]
    old = sigma_next[0]
    covariance = jnp.where(active, full.astype(BF16), old)
    first_col = lax.axis_index("col") * rows
    new_block = lax.dynamic_slice_in_dim(full, first_col, rows, 1)
    old_block = lax.dynamic_slice_in_dim(old, first_col, rows, 1)
    variances = jnp.where(active, jnp.diagonal(new_block), jnp.diagonal(old_block).astype(F32))
    return (covariance[None], variances[None])


def solution(mesh):
    local = owned if mesh.shape["col"] == 4 and mesh.shape["dom"] % 2 == 0 else gathered
    return jax.shard_map(
        local,
        mesh=mesh,
        in_specs=(
            P(("groups", "dom"), "col", None),
            P(("groups", "dom"), "col", None),
            P(("groups", "dom"), "col", None),
            P(("groups", "dom")),
            P(("groups", "dom")),
            P(("groups", "dom")),
            P("groups"),
        ),
        out_specs=(P(("groups", "dom"), "col", None), P(("groups", "dom"), "col")),
        check_vma=False,
    )
```

```python
import functools

import jax
import jax.numpy as jnp
from jax import lax
from jax.experimental import pallas as pl
from jax.experimental.pallas import tpu as pltpu
from jax.sharding import PartitionSpec as P

GX = 64
GY = 32
BF16 = jnp.bfloat16
F32 = jnp.float32
MIB = 1 << 20


def passed_along(value, axis, steps):
    count = lax.axis_size(axis)
    initial, last = (max(0, -steps), min(count, count - steps))
    return lax.ppermute(value, axis, [(source, source + steps) for source in range(initial, last)])


LIGHT = pl.CostEstimate(flops=1 << 20, bytes_accessed=1 << 16, transcendentals=0)
MEDIUM = pl.CostEstimate(flops=2000000000, bytes_accessed=1 << 16, transcendentals=0)
HEAVY = pl.CostEstimate(flops=14000000000, bytes_accessed=1 << 16, transcendentals=0)


def couple_kernel(rate_ref, class_ref, pivot_ref, out_ref, weight_ref):
    nodes = pivot_ref.shape[1]

    @pl.when(pl.program_id(0) == 0)
    def _():
        kind = class_ref[...]
        across = jnp.where(
            kind == 0, 0.25, jnp.where(kind == 1, 0.375, jnp.where(kind == 2, 0.125, 0.5))
        ).astype(F32)
        along = jnp.where(
            kind == 0, 0.25, jnp.where(kind == 1, 0.125, jnp.where(kind == 2, 0.375, 0.0))
        ).astype(F32)
        node = lax.broadcasted_iota(jnp.int32, (1, nodes), 1)
        column = node % GX
        parts = (
            jnp.where(column > 0, across, 0.0),
            jnp.where(column < GX - 1, across, 0.0),
            jnp.where(node >= GX, along, 0.0),
            jnp.where(node < nodes - GX, along, 0.0),
        )
        for which, part in enumerate(parts):
            weight_ref[which] = jnp.broadcast_to(part, (16, nodes))

    rate = rate_ref[0]

    def group(step, carry):
        rows = pl.ds(pl.multiple_of(step * 16, 16), 16)
        value = pivot_ref[rows, :].astype(F32)
        total = (
            value
            + weight_ref[0] * pltpu.roll(value, 1, 1)
            + weight_ref[1] * pltpu.roll(value, nodes - 1, 1)
            + weight_ref[2] * pltpu.roll(value, GX, 1)
            + weight_ref[3] * pltpu.roll(value, nodes - GX, 1)
        )
        out_ref[rows, :] = (rate * total).astype(BF16)
        return carry

    lax.fori_loop(0, pivot_ref.shape[0] // 16, group, 0)


def couple(pivot, node_class, rate, part=0, parts=1):
    rows, nodes = pivot.shape[0] // parts, pivot.shape[1]
    chunk = min(rows, 128)
    steps = rows // chunk
    return pl.pallas_call(
        couple_kernel,
        out_shape=jax.ShapeDtypeStruct((rows, nodes), BF16),
        grid=(steps,),
        in_specs=[
            pl.BlockSpec(memory_space=pltpu.SMEM),
            pl.BlockSpec((1, nodes), lambda i: (0, 0)),
            pl.BlockSpec((chunk, nodes), lambda i: (part * steps + i, 0)),
        ],
        out_specs=pl.BlockSpec((chunk, nodes), lambda i: (i, 0)),
        scratch_shapes=[pltpu.VMEM((4, 16, nodes), F32)],
        compiler_params=pltpu.CompilerParams(vmem_limit_bytes=6 * MIB),
        cost_estimate=LIGHT,
        name="couple",
    )(rate, node_class.reshape(1, nodes), pivot)


def turned(block, odd):
    return block + odd * (3 - 2 * block)


def route(source, target, doms):
    pairs = []
    for dom in range(doms):
        odd = dom % 2
        pairs.append((dom * 4 + turned(source, odd), dom * 4 + turned(target, odd)))
    return pairs


def moved(value, source, target):
    return lax.ppermute(value, ("dom", "col"), route(source, target, lax.axis_size("dom")))


def couple_here(place, pivot, node_class, rate):
    rows, nodes = pivot.shape
    chunk = 128

    def kernel(place_ref, *refs):
        @pl.when(place_ref[1] == 1)
        def _():
            couple_kernel(*refs)

    return pl.pallas_call(
        kernel,
        out_shape=jax.ShapeDtypeStruct((rows, nodes), BF16),
        grid_spec=pltpu.PrefetchScalarGridSpec(
            num_scalar_prefetch=1,
            grid=(rows // chunk,),
            in_specs=[
                pl.BlockSpec(memory_space=pltpu.SMEM),
                pl.BlockSpec((1, nodes), lambda i, place: (0, 0)),
                pl.BlockSpec((chunk, nodes), lambda i, place: (i, 0)),
            ],
            out_specs=pl.BlockSpec((chunk, nodes), lambda i, place: (i, 0)),
            scratch_shapes=[pltpu.VMEM((4, 16, nodes), F32)],
        ),
        compiler_params=pltpu.CompilerParams(vmem_limit_bytes=8 * MIB),
        cost_estimate=LIGHT,
        name="couple_here",
    )(place, rate, node_class.reshape(1, nodes), pivot)


def turn_kernel(place_ref, coupled_ref, *refs):
    @pl.when(place_ref[1] == 1)
    def _():
        refs[-1][...] = coupled_ref[...].T


def turn(place, panel, part, coupled, across):
    rows, nodes = coupled.shape
    chunk = 128
    steps = rows // chunk
    ratio = nodes // 4 // chunk
    return pl.pallas_call(
        turn_kernel,
        out_shape=jax.ShapeDtypeStruct((nodes, nodes), BF16),
        grid_spec=pltpu.PrefetchScalarGridSpec(
            num_scalar_prefetch=1,
            grid=(steps,),
            in_specs=[pl.BlockSpec((chunk, nodes), lambda i, place: (i, 0))]
            + ([] if across is None else [pl.BlockSpec(memory_space=pl.ANY)]),
            out_specs=pl.BlockSpec(
                (nodes, chunk),
                lambda i, place: (0, turned(panel, place[0]) * ratio + part * steps + i),
            ),
        ),
        input_output_aliases={} if across is None else {2: 0},
        compiler_params=pltpu.CompilerParams(vmem_limit_bytes=4 * MIB),
        cost_estimate=LIGHT,
        name="turn",
    )(place, coupled, *(() if across is None else (across,)))


def multiply_kernel(first, count, lefts, place_ref, *refs):
    left_refs, right_ref, out_ref = refs[:lefts], refs[lefts], refs[-1]
    width = right_ref.shape[0] // 4

    @pl.when(place_ref[1] == 1)
    def _():
        def block(step, carry):
            source = pl.multiple_of((first(place_ref[0]) + step) * width, 128)
            target = pl.multiple_of(step * width, 128)
            row = 0
            for left_ref in left_refs:
                rows = left_ref.shape[0]
                out_ref[row : row + rows, pl.ds(target, width)] = jnp.dot(
                    left_ref[...], right_ref[:, pl.ds(source, width)], preferred_element_type=F32
                ).astype(BF16)
                row += rows
            return carry

        lax.fori_loop(0, count, block, 0)


def multiply(place, lefts, right, first=lambda odd: 0, count=4):
    rows = sum(left.shape[0] for left in lefts)
    width = right.shape[0] // 4
    vmem = pl.BlockSpec(memory_space=pltpu.VMEM)
    return pl.pallas_call(
        functools.partial(multiply_kernel, first, count, len(lefts)),
        out_shape=jax.ShapeDtypeStruct((rows, count * width), BF16),
        in_specs=[pl.BlockSpec(memory_space=pltpu.SMEM)] + [vmem] * (len(lefts) + 1),
        out_specs=vmem,
        compiler_params=pltpu.CompilerParams(vmem_limit_bytes=6 * MIB),
        cost_estimate=LIGHT,
        name="multiply",
    )(place, *lefts, right)


def pack(value, out_ref, column):
    half = value.shape[0] // 2
    for part in range(2):
        rows = pl.ds(part * half, half)
        pack_rows(part, value[part * half : (part + 1) * half], out_ref.at[rows], column)


def two_kernel(place_ref, left_ref, right_ref, zero_ref, out_ref):
    odd = place_ref[0]
    width = right_ref.shape[0] // 4

    def product(block):
        columns = pl.ds(pl.multiple_of(block * width, 128), width)
        value = jnp.dot(left_ref[...], right_ref[:, columns], preferred_element_type=F32)
        return value.astype(BF16)

    @pl.when(place_ref[1] == 1)
    def _():
        out_ref[:, :width] = product(1 + odd)
        zero = pl.ds(pl.multiple_of((2 - 2 * odd) * width, 128), width)
        out_ref[:, width : 2 * width] = zero_ref[:, zero]
        pack(product(2 - odd), out_ref, 2 * width)


def product_two(place, half, across, zero):
    rows = half.shape[0]
    width = across.shape[0] // 4
    vmem = pl.BlockSpec(memory_space=pltpu.VMEM)
    return pl.pallas_call(
        two_kernel,
        out_shape=jax.ShapeDtypeStruct((rows, 11 * width // 4), BF16),
        in_specs=[pl.BlockSpec(memory_space=pltpu.SMEM)] + [vmem] * 3,
        out_specs=vmem,
        compiler_params=pltpu.CompilerParams(vmem_limit_bytes=6 * MIB),
        cost_estimate=LIGHT,
        name="product_two",
    )(place, half, across, zero)


def half_kernel(place_ref, left_ref, right_ref, one_ref, out_ref):
    width = one_ref.shape[1]

    @pl.when(place_ref[1] == 1)
    def _():
        def block(step, carry):
            which = turned(step + (step > 0).astype(jnp.int32), place_ref[0])
            columns = pl.ds(pl.multiple_of(which * width, 128), width)
            out_ref[:, columns] = jnp.dot(
                left_ref[...], right_ref[:, columns], preferred_element_type=F32
            ).astype(BF16)
            return carry

        lax.fori_loop(0, 3, block, 0)
        columns = pl.ds(pl.multiple_of(turned(1, place_ref[0]) * width, 128), width)
        out_ref[:, columns] = one_ref[...]


def half_product(place, left, right, one):
    vmem = pl.BlockSpec(memory_space=pltpu.VMEM)
    return pl.pallas_call(
        half_kernel,
        out_shape=jax.ShapeDtypeStruct(left.shape, BF16),
        in_specs=[pl.BlockSpec(memory_space=pltpu.SMEM)] + [vmem] * 3,
        out_specs=vmem,
        compiler_params=pltpu.CompilerParams(vmem_limit_bytes=6 * MIB),
        cost_estimate=LIGHT,
        name="half_product",
    )(place, left, right, one)


def column_kernel(place_ref, own_ref, first_ref, second_ref, *refs):
    column_ref, out_refs = refs[0], refs[1:]

    @pl.when(place_ref[1] == 1)
    def _():
        width = own_ref.shape[0]
        for block in range(4):
            rows = pl.ds(block * width, width)
            column_ref[rows, :] = own_ref[:, rows].T
        for left_ref, out_ref in zip((first_ref, second_ref), out_refs):
            out_ref[...] = jnp.dot(
                left_ref[...], column_ref[...], preferred_element_type=F32
            ).astype(BF16)


def own_column(place, own, first, second):
    rows, nodes = own.shape
    vmem = pl.BlockSpec(memory_space=pltpu.VMEM)
    return pl.pallas_call(
        column_kernel,
        out_shape=(
            jax.ShapeDtypeStruct((nodes, rows), BF16),
            jax.ShapeDtypeStruct((rows, rows), BF16),
            jax.ShapeDtypeStruct((rows, rows), BF16),
        ),
        in_specs=[pl.BlockSpec(memory_space=pltpu.SMEM)] + [vmem] * 3,
        out_specs=(vmem, vmem, vmem),
        compiler_params=pltpu.CompilerParams(vmem_limit_bytes=6 * MIB),
        cost_estimate=LIGHT,
        name="own_column",
    )(place, own, first, second)


def rest_kernel(place_ref, left_ref, right_ref, zero_ref, out_ref):
    odd = place_ref[0]
    width = zero_ref.shape[1]

    def product(block):
        columns = pl.ds(pl.multiple_of(block * width, 128), width)
        value = jnp.dot(left_ref[...], right_ref[:, columns], preferred_element_type=F32)
        return value.astype(BF16)

    @pl.when(place_ref[1] == 1)
    def _():
        out_ref[:, pl.ds(pl.multiple_of(odd * width, 128), width)] = zero_ref[...].T
        out_ref[:, pl.ds(pl.multiple_of((1 - odd) * width, 128), width)] = product(1 + odd)
        pack(product(3 - 3 * odd), out_ref, 2 * width)


def product_rest(place, half, across, zero):
    rows = half.shape[0]
    width = across.shape[0] // 4
    vmem = pl.BlockSpec(memory_space=pltpu.VMEM)
    return pl.pallas_call(
        rest_kernel,
        out_shape=jax.ShapeDtypeStruct((rows, 11 * width // 4), BF16),
        in_specs=[pl.BlockSpec(memory_space=pltpu.SMEM)] + [vmem] * 3,
        out_specs=vmem,
        compiler_params=pltpu.CompilerParams(vmem_limit_bytes=6 * MIB),
        cost_estimate=LIGHT,
        name="product_rest",
    )(place, half, across, zero)


def pack_rows(part, value, out_ref, column):
    half, width = value.shape
    quarter = half // 2
    if part == 0:
        out_ref[:, column : column + half] = value[:, :half]
        out_ref[:, column + half : column + half + quarter] = value[:, half : half + quarter]
    else:
        out_ref[:, column : column + half] = value[:, half:]
        beside = slice(column + half, column + half + quarter)
        out_ref[:quarter, beside] = value[quarter:, :quarter]
        out_ref[quarter:, beside] = value[quarter:, quarter:half]


def unpacked_rows(part, packed_ref, column):
    quarter = packed_ref.shape[0] // 4
    half = 2 * quarter
    beside = slice(column + half, column + half + quarter)
    rows = slice(part * quarter, (part + 1) * quarter)
    diagonal = packed_ref[rows, column : column + half]
    lower = [packed_ref[start : start + quarter, beside] for start in (half, half + quarter)]
    if part < 2:
        return diagonal, jnp.concatenate([packed_ref[rows, beside], lower[part].T], axis=1)
    if part == 2:
        return packed_ref[:half, beside].T, diagonal
    return jnp.concatenate(lower, axis=1), diagonal


def prior_kernel(place_ref, shifted_ref, sigma_ref, out_ref):
    @pl.when(place_ref[3] == 0)
    def _():
        out_ref[...] = shifted_ref[...]

    @pl.when(place_ref[3] != 0)
    def _():
        out_ref[...] = sigma_ref[...]


def parts_kernel(place_ref, shifted_ref, sigma_ref, row_ref, far_ref, near_ref, last_ref):
    odd = place_ref[0]
    width = row_ref.shape[1] // 4

    def at(block, count=1):
        return pl.ds(pl.multiple_of(block * width, 128), count * width)

    prior_kernel(place_ref, shifted_ref, sigma_ref, row_ref)
    far_ref[:, : 2 * width] = row_ref[:, at(2 - 2 * odd, 2)]
    near_ref[:, :width] = row_ref[:, at(3 - 3 * odd)]
    for part in range(2):

        @pl.when(pl.program_id(0) == part)
        def _():
            pack_rows(part, row_ref[:, at(3 * odd)], far_ref, 2 * width)
            pack_rows(part, row_ref[:, at(2 - odd)], near_ref, width)
            pack_rows(part, row_ref[:, at(3 - 3 * odd)], last_ref, 0)


def prior_parts(place, shifted, sigma):
    rows, nodes = sigma.shape
    chunk = rows // 2
    width = nodes // 4
    out = lambda quarters: jax.ShapeDtypeStruct((rows, quarters * width // 4), BF16)
    spec = lambda quarters: pl.BlockSpec((chunk, quarters * width // 4), lambda i, place: (i, 0))
    return pl.pallas_call(
        parts_kernel,
        out_shape=(out(16), out(11), out(7), out(3)),
        grid_spec=pltpu.PrefetchScalarGridSpec(
            num_scalar_prefetch=1,
            grid=(rows // chunk,),
            in_specs=[
                pl.BlockSpec(
                    (chunk, nodes), lambda i, place: (jnp.where(place[3] == 0, i, 0), 0)
                ),
                pl.BlockSpec(
                    (chunk, nodes), lambda i, place: (jnp.where(place[3] == 0, 0, i), 0)
                ),
            ],
            out_specs=(spec(16), spec(11), spec(7), spec(3)),
        ),
        compiler_params=pltpu.CompilerParams(vmem_limit_bytes=14 * MIB),
        cost_estimate=LIGHT,
        name="prior_parts",
    )(place, shifted, sigma)


def assemble_kernel(place_ref, own, column, near_two, last_three, far_zero, out_ref):
    @pl.when(place_ref[1] == 1)
    def _():
        odd = place_ref[0]
        width = own.shape[0]
        half, quarter = width // 2, width // 4

        def at(block, count=1):
            return pl.ds(pl.multiple_of(block * width, 128), count * width)

        near = 2 * (1 - odd)
        row = [turned(block, odd) for block in range(4)]
        out_ref[at(row[1]), :] = own[...]
        out_ref[at(row[2]), at(row[3])] = near_two[:, :width]
        out_ref[at(row[3]), at(row[2])] = near_two[:, :width].T
        out_ref[at(row[0]), at(near, 2)] = far_zero[:, : 2 * width]
        for step in range(2):
            out_ref[at(near + step), at(row[0])] = far_zero[:, step * width : (1 + step) * width].T
        for block in (0, 2, 3):
            out_ref[at(row[block]), at(row[1])] = column[at(row[block]), :]
        packed = ((0, far_zero, 2 * width), (2, near_two, width), (3, last_three, 0))
        for block, packed_ref, start in packed:
            for part in range(4):
                rows = pl.ds(pl.multiple_of(row[block] * width + part * quarter, 128), quarter)
                for side, value in enumerate(unpacked_rows(part, packed_ref, start)):
                    columns = pl.ds(pl.multiple_of(row[block] * width + side * half, 128), half)
                    out_ref[rows, columns] = value


def assemble(place, *parts):
    nodes = parts[0].shape[1]
    vmem = pl.BlockSpec(memory_space=pltpu.VMEM)
    return pl.pallas_call(
        assemble_kernel,
        out_shape=jax.ShapeDtypeStruct((nodes, nodes), BF16),
        in_specs=[pl.BlockSpec(memory_space=pltpu.SMEM)] + [vmem] * 5,
        out_specs=vmem,
        compiler_params=pltpu.CompilerParams(vmem_limit_bytes=6 * MIB),
        cost_estimate=LIGHT,
        name="assemble",
    )(place, *parts)


def tick(place, *values, cost=HEAVY):
    def kernel(place_ref, *refs):
        for which in range(place.shape[0]):
            refs[-1][which] = place_ref[which]

    scalars = pl.BlockSpec(memory_space=pltpu.SMEM)
    return pl.pallas_call(
        kernel,
        out_shape=jax.ShapeDtypeStruct(place.shape, place.dtype),
        in_specs=[scalars] + [pl.BlockSpec(memory_space=pl.ANY)] * len(values),
        out_specs=scalars,
        compiler_params=pltpu.CompilerParams(vmem_limit_bytes=MIB),
        cost_estimate=cost,
        name="tick",
    )(place, *values)


def finish_kernel(
    place_ref, pivot_ref, sigma_ref,
    q0, q0_last, q2, q3_two,
    q01, q11, q21, q31,
    out_ref, var_ref,
):
    rows, nodes = pivot_ref.shape
    width = nodes // 4
    odd, place = place_ref[0], place_ref[1]
    here = pl.multiple_of(pl.program_id(0) * rows, 128)
    diagonal = diagonal_of(rows)

    def at(block, count=1):
        return pl.ds(pl.multiple_of(block * width, 128), count * width)

    def own(block):
        return pl.ds(pl.multiple_of(block * width + here, 128), rows)

    def add(columns, product):
        out_ref[:, columns] = (pivot_ref[:, columns].astype(F32) + product.astype(F32)).astype(BF16)

    def trace(product):
        var_ref[...] = diagonal(
            pivot_ref[:, own(place_ref[2])].astype(F32) + product.astype(F32)
        )

    active = place_ref[4] != 0

    @pl.when(active & (place == 0))
    def _():
        add(at(odd, 3), q0[...])
        add(at(turned(3, odd)), q0_last[...])
        trace(q0[:, own(2 * odd)])

    @pl.when(active & (place == 1))
    def _():
        add(at(turned(0, odd)), q01[...].T)
        add(at(turned(1, odd)), q11[...])
        add(at(turned(2, odd)), q21[...].T)
        add(at(turned(3, odd)), q31[...].T)
        trace(q11[:, pl.ds(here, rows)])

    @pl.when(active & (place == 2))
    def _():
        add(at(turned(0, odd)), q2[pl.ds(0, width), pl.ds(pl.multiple_of(width + here, 128), rows)].T)
        add(at(turned(1, odd)), q2[pl.ds(here, rows), pl.ds(0, width)])
        start = pl.program_id(0) % 2 * rows + 2 * width
        trace(q2[pl.ds(here, rows), pl.ds(pl.multiple_of(start, 128), rows)])
        for part in range(4):

            @pl.when(pl.program_id(0) == part)
            def _():
                for side, value in enumerate(unpacked_rows(part, q2, 2 * width)):
                    start = turned(2, odd) * width + side * width // 2
                    add(pl.ds(pl.multiple_of(start, 128), width // 2), value)

    @pl.when(active & (place == 3))
    def _():
        add(at(turned(2, odd)), q3_two[...])

    @pl.when(place_ref[4] == 0)
    def _():
        out_ref[...] = sigma_ref[...]
        var_ref[...] = diagonal(sigma_ref[:, own(place_ref[2])].astype(F32))


def finish(place, pivot, sigma, received, kept):
    rows, nodes = pivot.shape
    chunk = 128
    width = nodes // 4

    def picked(which, blocks):
        return pl.BlockSpec(
            (chunk, blocks * width), lambda i, place: (jnp.where(place[1] == which, i, 0), 0)
        )

    def turned_block(start):
        return pl.BlockSpec(
            (rows, chunk),
            lambda i, place: (
                0,
                jnp.where(place[1] == 1, start(place[0]) * (width // chunk) + i, 0),
            ),
        )

    return pl.pallas_call(
        finish_kernel,
        out_shape=(
            jax.ShapeDtypeStruct((rows, nodes), BF16),
            jax.ShapeDtypeStruct((1, rows), F32),
        ),
        grid_spec=pltpu.PrefetchScalarGridSpec(
            num_scalar_prefetch=1,
            grid=(rows // chunk,),
            in_specs=[
                pl.BlockSpec((chunk, nodes), lambda i, place: (i, 0)),
                pl.BlockSpec(
                    (chunk, nodes), lambda i, place: (jnp.where(place[4] == 0, i, 0), 0)
                ),
                picked(0, 3),
                picked(0, 1),
                pl.BlockSpec((rows, 11 * width // 4), lambda i, place: (0, 0)),
                picked(3, 1),
                turned_block(lambda odd: 1),
                picked(1, 1),
                turned_block(lambda odd: 0),
                turned_block(lambda odd: 1 - odd),
            ],
            out_specs=(
                pl.BlockSpec((chunk, nodes), lambda i, place: (i, 0)),
                pl.BlockSpec((1, chunk), lambda i, place: (0, i)),
            ),
        ),
        compiler_params=pltpu.CompilerParams(vmem_limit_bytes=12 * MIB),
        cost_estimate=HEAVY,
        name="finish",
    )(place, pivot, sigma, *received, *kept)


def last_kernel(place_ref, pivot_ref, q2_last, q3, old_ref, old_var_ref, out_ref, var_ref, sum_ref, sems):
    rows, nodes = pivot_ref.shape
    width = nodes // 4
    chunk = 128
    odd, place = place_ref[0], place_ref[1]
    active = place_ref[4] != 0

    def at(block, count=1):
        return pl.ds(pl.multiple_of(block * width, 128), count * width)

    def copies(part, pieces):
        here = pl.ds(part * chunk, chunk)
        return [
            pltpu.make_async_copy(
                sum_ref.at[here, source], out_ref.at[here, target], sems.at[which, part]
            )
            for which, (source, target, _) in enumerate(pieces)
        ]

    def write(pieces):
        for part in range(4):
            here = pl.ds(part * chunk, chunk)
            for source, target, product in pieces:
                value = pivot_ref[here, target].astype(F32) + product(part, here).astype(F32)
                sum_ref[here, source] = value.astype(BF16)
            for copy in copies(part, pieces):
                copy.start()
        for part in range(4):
            for copy in copies(part, pieces):
                copy.wait()

    var_ref[...] = old_var_ref[...]

    @pl.when(active & (place == 2))
    def _():
        write([(pl.ds(0, width), at(3 - 3 * odd), lambda part, here: q2_last[:, here].T)])

    @pl.when(active & (place == 3))
    def _():
        both, last = pl.ds(0, 2 * width), pl.ds(2 * width, width)
        for start in range(0, rows, chunk):
            here = pl.ds(start, chunk)
            own = pl.ds(pl.multiple_of(place_ref[2] * width + start, 128), chunk)
            value = pivot_ref[here, own].astype(F32)
            value = value + q3[here, pl.ds(2 * width + start % (2 * chunk), chunk)].astype(F32)
            var_ref[:, here] = diagonal_of(chunk)(value)
        write(
            [
                (both, at(2 * odd, 2), lambda part, here: q3[here, both]),
                (
                    last,
                    at(3 - 3 * odd),
                    lambda part, here: jnp.concatenate(unpacked_rows(part, q3, 2 * width), axis=1),
                ),
            ]
        )


def diagonal_of(rows):
    square = (rows, rows)
    on_diagonal = lax.broadcasted_iota(jnp.int32, square, 0) == lax.broadcasted_iota(
        jnp.int32, square, 1
    )
    return lambda value: jnp.sum(jnp.where(on_diagonal, value, 0.0), axis=0, keepdims=True)


def finish_last(place, pivot, q2_last, q3, covariance, variances):
    rows, nodes = pivot.shape
    width = nodes // 4
    vmem = pl.BlockSpec(memory_space=pltpu.VMEM)
    anywhere = pl.BlockSpec(memory_space=pl.ANY)
    return pl.pallas_call(
        last_kernel,
        out_shape=(
            jax.ShapeDtypeStruct((rows, nodes), BF16),
            jax.ShapeDtypeStruct((1, rows), F32),
        ),
        in_specs=[pl.BlockSpec(memory_space=pltpu.SMEM)] + [vmem] * 3 + [anywhere, vmem],
        out_specs=(anywhere, vmem),
        scratch_shapes=[
            pltpu.VMEM((rows, 3 * width), BF16),
            pltpu.SemaphoreType.DMA((2, rows // 128)),
        ],
        input_output_aliases={4: 0},
        compiler_params=pltpu.CompilerParams(vmem_limit_bytes=8 * MIB),
        cost_estimate=LIGHT,
        name="finish_last",
    )(place, pivot, q2_last, q3, covariance, variances)


def owned(sigma_next, separator, inverse_pivot, coupling_rate, lengths, step_index, node_class):
    sigma, pivot = sigma_next[0], inverse_pivot[0]
    odd = lax.axis_index("dom") % 2
    col = lax.axis_index("col")
    step = step_index[0]
    place = jnp.stack([odd, turned(col, odd), col, step, step < lengths[0]]).astype(jnp.int32)
    after = lambda value, *others: lax.optimization_barrier((value, *others))[0]

    shifted = passed_along(separator, "dom", -1)[0]
    p2 = moved(pivot, 2, 1)
    p0 = moved(pivot, 0, 1)
    c1 = [couple(pivot, node_class, coupling_rate, part, 2) for part in range(2)]
    across = turn(place, 1, 0, c1[0], None)
    across = turn(place, 1, 1, c1[1], across)

    row, far, near, last = prior_parts(place, after(shifted, across), sigma)
    far_zero, near_two, last_three = moved(far, 0, 1), moved(near, 2, 1), moved(last, 3, 1)

    c2 = couple_here(place, after(p2, last), node_class, coupling_rate)
    across = turn(place, 2, 0, c2, across)
    c0 = couple_here(place, after(p0, across), node_class, coupling_rate)
    across = turn(place, 0, 0, c0, across)
    column, h0_one, h2_one = own_column(place, row, c0, c2)
    c3 = [
        moved(after(c1[0], last_three, near_two, across), 3, 1),
        moved(after(c1[1], far_zero, h2_one), 3, 1),
    ]
    prior = assemble(place, row, column, near_two, last_three, far_zero)

    h0 = half_product(place, c0, prior, h0_one)
    q0_own = multiply(place, [h0], across, lambda odd: odd, 3)
    q0 = moved(q0_own, 1, 0)
    h2 = half_product(place, after(c2, q0_own), prior, h2_one)
    q2_own = product_two(place, h2, across, q0_own)
    q2 = moved(q2_own, 1, 2)

    across = turn(place, 3, 0, c3[0], after(across, q2_own))
    across = turn(place, 3, 1, c3[1], across)
    q03 = multiply(place, [h0], across, lambda odd: 3 - 3 * odd, 1)
    q0_last = moved(q03, 1, 0)
    h3 = multiply(place, [after(c3[0], q03), c3[1]], prior)
    q32 = multiply(place, [h3], across, lambda odd: 2 - odd, 1)
    q3_two = moved(q32, 1, 3)
    q3_own = product_rest(place, after(h3, q32), across, q03)
    q3 = moved(q3_own, 1, 3)
    h1 = multiply(place, [after(c1[0], q3_own), c1[1]], prior)
    q11 = multiply(place, [h1], across, lambda odd: 1 + odd, 1)
    received = (q0, q0_last, q2, q3_two)
    kept = (q0_own, q11, q2_own, q3_own)
    place_then = tick(tick(place, q0, cost=LIGHT), q0_last, cost=MEDIUM)
    q2_last = moved(after(q3_two, place_then), 3, 2)
    covariance, variances = finish(place_then, pivot, sigma, received, kept)
    covariance, variances = finish_last(place, pivot, q2_last, q3, covariance, variances)
    return (covariance[None], variances)


def gathered(sigma_next, separator, inverse_pivot, coupling_rate, lengths, step_index, node_class):
    shifted = passed_along(separator, "dom", -1)
    prior = jnp.where(step_index[0] == 0, shifted[0], sigma_next[0])
    pivot = inverse_pivot[0].astype(F32)
    coupled = couple(inverse_pivot[0], node_class, coupling_rate)
    rows = coupled.shape[0]
    half = jnp.dot(
        coupled,
        lax.all_gather(prior, "col", axis=0, tiled=True),
        preferred_element_type=F32,
    ).astype(BF16)
    product = lax.dot_general(
        half,
        lax.all_gather(coupled, "col", axis=0, tiled=True),
        (((1,), (1,)), ((), ())),
        preferred_element_type=F32,
    )
    full = pivot + product
    active = step_index[0] < lengths[0]
    old = sigma_next[0]
    covariance = jnp.where(active, full.astype(BF16), old)
    first_col = lax.axis_index("col") * rows
    new_block = lax.dynamic_slice_in_dim(full, first_col, rows, 1)
    old_block = lax.dynamic_slice_in_dim(old, first_col, rows, 1)
    variances = jnp.where(active, jnp.diagonal(new_block), jnp.diagonal(old_block).astype(F32))
    return (covariance[None], variances[None])


def solution(mesh):
    local = owned if mesh.shape["col"] == 4 and mesh.shape["dom"] % 2 == 0 else gathered
    return jax.shard_map(
        local,
        mesh=mesh,
        in_specs=(
            P(("groups", "dom"), "col", None),
            P(("groups", "dom"), "col", None),
            P(("groups", "dom"), "col", None),
            P(("groups", "dom")),
            P(("groups", "dom")),
            P(("groups", "dom")),
            P("groups"),
        ),
        out_specs=(P(("groups", "dom"), "col", None), P(("groups", "dom"), "col")),
        check_vma=False,
    )
```

```python
import functools

import jax
import jax.numpy as jnp
from jax import lax
from jax.experimental import pallas as pl
from jax.experimental.pallas import tpu as pltpu
from jax.sharding import PartitionSpec as P

GX = 64
GY = 32
BF16 = jnp.bfloat16
F32 = jnp.float32
MIB = 1 << 20


def passed_along(value, axis, steps):
    count = lax.axis_size(axis)
    initial, last = (max(0, -steps), min(count, count - steps))
    return lax.ppermute(value, axis, [(source, source + steps) for source in range(initial, last)])


LIGHT = pl.CostEstimate(flops=1 << 20, bytes_accessed=1 << 16, transcendentals=0)
MEDIUM = pl.CostEstimate(flops=2000000000, bytes_accessed=1 << 16, transcendentals=0)
HEAVY = pl.CostEstimate(flops=14000000000, bytes_accessed=1 << 16, transcendentals=0)


def couple_kernel(rate_ref, class_ref, pivot_ref, out_ref, weight_ref):
    nodes = pivot_ref.shape[1]

    @pl.when(pl.program_id(0) == 0)
    def _():
        kind = class_ref[...]
        across = jnp.where(
            kind == 0, 0.25, jnp.where(kind == 1, 0.375, jnp.where(kind == 2, 0.125, 0.5))
        ).astype(F32)
        along = jnp.where(
            kind == 0, 0.25, jnp.where(kind == 1, 0.125, jnp.where(kind == 2, 0.375, 0.0))
        ).astype(F32)
        node = lax.broadcasted_iota(jnp.int32, (1, nodes), 1)
        column = node % GX
        parts = (
            jnp.where(column > 0, across, 0.0),
            jnp.where(column < GX - 1, across, 0.0),
            jnp.where(node >= GX, along, 0.0),
            jnp.where(node < nodes - GX, along, 0.0),
        )
        for which, part in enumerate(parts):
            weight_ref[which] = jnp.broadcast_to(part, (16, nodes))

    rate = rate_ref[0]

    def group(step, carry):
        rows = pl.ds(pl.multiple_of(step * 16, 16), 16)
        value = pivot_ref[rows, :].astype(F32)
        total = (
            value
            + weight_ref[0] * pltpu.roll(value, 1, 1)
            + weight_ref[1] * pltpu.roll(value, nodes - 1, 1)
            + weight_ref[2] * pltpu.roll(value, GX, 1)
            + weight_ref[3] * pltpu.roll(value, nodes - GX, 1)
        )
        out_ref[rows, :] = (rate * total).astype(BF16)
        return carry

    lax.fori_loop(0, pivot_ref.shape[0] // 16, group, 0)


def couple(pivot, node_class, rate, part=0, parts=1):
    rows, nodes = pivot.shape[0] // parts, pivot.shape[1]
    chunk = min(rows, 128)
    steps = rows // chunk
    return pl.pallas_call(
        couple_kernel,
        out_shape=jax.ShapeDtypeStruct((rows, nodes), BF16),
        grid=(steps,),
        in_specs=[
            pl.BlockSpec(memory_space=pltpu.SMEM),
            pl.BlockSpec((1, nodes), lambda i: (0, 0)),
            pl.BlockSpec((chunk, nodes), lambda i: (part * steps + i, 0)),
        ],
        out_specs=pl.BlockSpec((chunk, nodes), lambda i: (i, 0)),
        scratch_shapes=[pltpu.VMEM((4, 16, nodes), F32)],
        compiler_params=pltpu.CompilerParams(vmem_limit_bytes=6 * MIB),
        cost_estimate=LIGHT,
        name="couple",
    )(rate, node_class.reshape(1, nodes), pivot)


def turned(block, odd):
    return block + odd * (3 - 2 * block)


def route(source, target, doms):
    pairs = []
    for dom in range(doms):
        odd = dom % 2
        pairs.append((dom * 4 + turned(source, odd), dom * 4 + turned(target, odd)))
    return pairs


def moved(value, source, target):
    return lax.ppermute(value, ("dom", "col"), route(source, target, lax.axis_size("dom")))


def couple_here(place, pivot, node_class, rate):
    rows, nodes = pivot.shape
    chunk = 128

    def kernel(place_ref, *refs):
        @pl.when(place_ref[1] == 1)
        def _():
            couple_kernel(*refs)

    return pl.pallas_call(
        kernel,
        out_shape=jax.ShapeDtypeStruct((rows, nodes), BF16),
        grid_spec=pltpu.PrefetchScalarGridSpec(
            num_scalar_prefetch=1,
            grid=(rows // chunk,),
            in_specs=[
                pl.BlockSpec(memory_space=pltpu.SMEM),
                pl.BlockSpec((1, nodes), lambda i, place: (0, 0)),
                pl.BlockSpec((chunk, nodes), lambda i, place: (i, 0)),
            ],
            out_specs=pl.BlockSpec((chunk, nodes), lambda i, place: (i, 0)),
            scratch_shapes=[pltpu.VMEM((4, 16, nodes), F32)],
        ),
        compiler_params=pltpu.CompilerParams(vmem_limit_bytes=8 * MIB),
        cost_estimate=LIGHT,
        name="couple_here",
    )(place, rate, node_class.reshape(1, nodes), pivot)


def turn_kernel(place_ref, coupled_ref, *refs):
    @pl.when(place_ref[1] == 1)
    def _():
        refs[-1][...] = coupled_ref[...].T


def turn(place, panel, part, coupled, across):
    rows, nodes = coupled.shape
    chunk = 128
    steps = rows // chunk
    ratio = nodes // 4 // chunk
    return pl.pallas_call(
        turn_kernel,
        out_shape=jax.ShapeDtypeStruct((nodes, nodes), BF16),
        grid_spec=pltpu.PrefetchScalarGridSpec(
            num_scalar_prefetch=1,
            grid=(steps,),
            in_specs=[pl.BlockSpec((chunk, nodes), lambda i, place: (i, 0))]
            + ([] if across is None else [pl.BlockSpec(memory_space=pl.ANY)]),
            out_specs=pl.BlockSpec(
                (nodes, chunk),
                lambda i, place: (0, turned(panel, place[0]) * ratio + part * steps + i),
            ),
        ),
        input_output_aliases={} if across is None else {2: 0},
        compiler_params=pltpu.CompilerParams(vmem_limit_bytes=4 * MIB),
        cost_estimate=LIGHT,
        name="turn",
    )(place, coupled, *(() if across is None else (across,)))


def multiply_kernel(first, count, lefts, place_ref, *refs):
    left_refs, right_ref, out_ref = refs[:lefts], refs[lefts], refs[-1]
    width = right_ref.shape[0] // 4

    @pl.when(place_ref[1] == 1)
    def _():
        def block(step, carry):
            source = pl.multiple_of((first(place_ref[0]) + step) * width, 128)
            target = pl.multiple_of(step * width, 128)
            row = 0
            for left_ref in left_refs:
                rows = left_ref.shape[0]
                out_ref[row : row + rows, pl.ds(target, width)] = jnp.dot(
                    left_ref[...], right_ref[:, pl.ds(source, width)], preferred_element_type=F32
                ).astype(BF16)
                row += rows
            return carry

        lax.fori_loop(0, count, block, 0)


def multiply(place, lefts, right, first=lambda odd: 0, count=4):
    rows = sum(left.shape[0] for left in lefts)
    width = right.shape[0] // 4
    vmem = pl.BlockSpec(memory_space=pltpu.VMEM)
    return pl.pallas_call(
        functools.partial(multiply_kernel, first, count, len(lefts)),
        out_shape=jax.ShapeDtypeStruct((rows, count * width), BF16),
        in_specs=[pl.BlockSpec(memory_space=pltpu.SMEM)] + [vmem] * (len(lefts) + 1),
        out_specs=vmem,
        compiler_params=pltpu.CompilerParams(vmem_limit_bytes=6 * MIB),
        cost_estimate=LIGHT,
        name="multiply",
    )(place, *lefts, right)


def pack(value, out_ref, column):
    half = value.shape[0] // 2
    for part in range(2):
        rows = pl.ds(part * half, half)
        pack_rows(part, value[part * half : (part + 1) * half], out_ref.at[rows], column)


def two_kernel(place_ref, left_ref, right_ref, zero_ref, out_ref):
    odd = place_ref[0]
    width = right_ref.shape[0] // 4

    def product(block):
        columns = pl.ds(pl.multiple_of(block * width, 128), width)
        value = jnp.dot(left_ref[...], right_ref[:, columns], preferred_element_type=F32)
        return value.astype(BF16)

    @pl.when(place_ref[1] == 1)
    def _():
        out_ref[:, :width] = product(1 + odd)
        zero = pl.ds(pl.multiple_of((2 - 2 * odd) * width, 128), width)
        out_ref[:, width : 2 * width] = zero_ref[:, zero]
        pack(product(2 - odd), out_ref, 2 * width)


def product_two(place, half, across, zero):
    rows = half.shape[0]
    width = across.shape[0] // 4
    vmem = pl.BlockSpec(memory_space=pltpu.VMEM)
    return pl.pallas_call(
        two_kernel,
        out_shape=jax.ShapeDtypeStruct((rows, 11 * width // 4), BF16),
        in_specs=[pl.BlockSpec(memory_space=pltpu.SMEM)] + [vmem] * 3,
        out_specs=vmem,
        compiler_params=pltpu.CompilerParams(vmem_limit_bytes=6 * MIB),
        cost_estimate=LIGHT,
        name="product_two",
    )(place, half, across, zero)


def half_kernel(place_ref, left_ref, right_ref, one_ref, out_ref):
    width = one_ref.shape[1]

    @pl.when(place_ref[1] == 1)
    def _():
        def block(step, carry):
            which = turned(step + (step > 0).astype(jnp.int32), place_ref[0])
            columns = pl.ds(pl.multiple_of(which * width, 128), width)
            out_ref[:, columns] = jnp.dot(
                left_ref[...], right_ref[:, columns], preferred_element_type=F32
            ).astype(BF16)
            return carry

        lax.fori_loop(0, 3, block, 0)
        columns = pl.ds(pl.multiple_of(turned(1, place_ref[0]) * width, 128), width)
        out_ref[:, columns] = one_ref[...]


def half_product(place, left, right, one):
    vmem = pl.BlockSpec(memory_space=pltpu.VMEM)
    return pl.pallas_call(
        half_kernel,
        out_shape=jax.ShapeDtypeStruct(left.shape, BF16),
        in_specs=[pl.BlockSpec(memory_space=pltpu.SMEM)] + [vmem] * 3,
        out_specs=vmem,
        compiler_params=pltpu.CompilerParams(vmem_limit_bytes=6 * MIB),
        cost_estimate=LIGHT,
        name="half_product",
    )(place, left, right, one)


def column_kernel(place_ref, own_ref, first_ref, second_ref, *refs):
    column_ref, out_refs = refs[0], refs[1:]

    @pl.when(place_ref[1] == 1)
    def _():
        width = own_ref.shape[0]
        for block in range(4):
            rows = pl.ds(block * width, width)
            column_ref[rows, :] = own_ref[:, rows].T
        for left_ref, out_ref in zip((first_ref, second_ref), out_refs):
            out_ref[...] = jnp.dot(
                left_ref[...], column_ref[...], preferred_element_type=F32
            ).astype(BF16)


def own_column(place, own, first, second):
    rows, nodes = own.shape
    vmem = pl.BlockSpec(memory_space=pltpu.VMEM)
    return pl.pallas_call(
        column_kernel,
        out_shape=(
            jax.ShapeDtypeStruct((nodes, rows), BF16),
            jax.ShapeDtypeStruct((rows, rows), BF16),
            jax.ShapeDtypeStruct((rows, rows), BF16),
        ),
        in_specs=[pl.BlockSpec(memory_space=pltpu.SMEM)] + [vmem] * 3,
        out_specs=(vmem, vmem, vmem),
        compiler_params=pltpu.CompilerParams(vmem_limit_bytes=6 * MIB),
        cost_estimate=LIGHT,
        name="own_column",
    )(place, own, first, second)


def rest_kernel(place_ref, upper_ref, lower_ref, right_ref, zero_ref, out_ref):
    odd = place_ref[0]
    width = zero_ref.shape[1]
    half = width // 2

    def product(left_ref, block):
        columns = pl.ds(pl.multiple_of(block * width, 128), width)
        value = jnp.dot(left_ref[...], right_ref[:, columns], preferred_element_type=F32)
        return value.astype(BF16)

    @pl.when(place_ref[1] == 1)
    def _():
        out_ref[:, pl.ds(pl.multiple_of(odd * width, 128), width)] = zero_ref[...].T
        other = pl.ds(pl.multiple_of((1 - odd) * width, 128), width)
        for part, left_ref in enumerate((upper_ref, lower_ref)):
            rows = pl.ds(part * half, half)
            out_ref[rows, other] = product(left_ref, 1 + odd)
            pack_rows(part, product(left_ref, 3 - 3 * odd), out_ref.at[rows], 2 * width)


def product_rest(place, halves, across, zero):
    rows, width = zero.shape
    vmem = pl.BlockSpec(memory_space=pltpu.VMEM)
    return pl.pallas_call(
        rest_kernel,
        out_shape=jax.ShapeDtypeStruct((rows, 11 * width // 4), BF16),
        in_specs=[pl.BlockSpec(memory_space=pltpu.SMEM)] + [vmem] * 4,
        out_specs=vmem,
        compiler_params=pltpu.CompilerParams(vmem_limit_bytes=6 * MIB),
        cost_estimate=LIGHT,
        name="product_rest",
    )(place, *halves, across, zero)


def pack_rows(part, value, out_ref, column):
    half, width = value.shape
    quarter = half // 2
    if part == 0:
        out_ref[:, column : column + half] = value[:, :half]
        out_ref[:, column + half : column + half + quarter] = value[:, half : half + quarter]
    else:
        out_ref[:, column : column + half] = value[:, half:]
        beside = slice(column + half, column + half + quarter)
        out_ref[:quarter, beside] = value[quarter:, :quarter]
        out_ref[quarter:, beside] = value[quarter:, quarter:half]


def unpacked_rows(part, packed_ref, column):
    quarter = packed_ref.shape[0] // 4
    half = 2 * quarter
    beside = slice(column + half, column + half + quarter)
    rows = slice(part * quarter, (part + 1) * quarter)
    diagonal = packed_ref[rows, column : column + half]
    lower = [packed_ref[start : start + quarter, beside] for start in (half, half + quarter)]
    if part < 2:
        return diagonal, jnp.concatenate([packed_ref[rows, beside], lower[part].T], axis=1)
    if part == 2:
        return packed_ref[:half, beside].T, diagonal
    return jnp.concatenate(lower, axis=1), diagonal


def prior_kernel(place_ref, shifted_ref, sigma_ref, out_ref):
    @pl.when(place_ref[3] == 0)
    def _():
        out_ref[...] = shifted_ref[...]

    @pl.when(place_ref[3] != 0)
    def _():
        out_ref[...] = sigma_ref[...]


def parts_kernel(place_ref, shifted_ref, sigma_ref, row_ref, far_ref, near_ref, last_ref):
    odd = place_ref[0]
    width = row_ref.shape[1] // 4

    def at(block, count=1):
        return pl.ds(pl.multiple_of(block * width, 128), count * width)

    prior_kernel(place_ref, shifted_ref, sigma_ref, row_ref)
    far_ref[:, : 2 * width] = row_ref[:, at(2 - 2 * odd, 2)]
    near_ref[:, :width] = row_ref[:, at(3 - 3 * odd)]
    for part in range(2):

        @pl.when(pl.program_id(0) == part)
        def _():
            pack_rows(part, row_ref[:, at(3 * odd)], far_ref, 2 * width)
            pack_rows(part, row_ref[:, at(2 - odd)], near_ref, width)
            pack_rows(part, row_ref[:, at(3 - 3 * odd)], last_ref, 0)


def prior_parts(place, shifted, sigma):
    rows, nodes = sigma.shape
    chunk = rows // 2
    width = nodes // 4
    out = lambda quarters: jax.ShapeDtypeStruct((rows, quarters * width // 4), BF16)
    spec = lambda quarters: pl.BlockSpec((chunk, quarters * width // 4), lambda i, place: (i, 0))
    return pl.pallas_call(
        parts_kernel,
        out_shape=(out(16), out(11), out(7), out(3)),
        grid_spec=pltpu.PrefetchScalarGridSpec(
            num_scalar_prefetch=1,
            grid=(rows // chunk,),
            in_specs=[
                pl.BlockSpec(
                    (chunk, nodes), lambda i, place: (jnp.where(place[3] == 0, i, 0), 0)
                ),
                pl.BlockSpec(
                    (chunk, nodes), lambda i, place: (jnp.where(place[3] == 0, 0, i), 0)
                ),
            ],
            out_specs=(spec(16), spec(11), spec(7), spec(3)),
        ),
        compiler_params=pltpu.CompilerParams(vmem_limit_bytes=14 * MIB),
        cost_estimate=LIGHT,
        name="prior_parts",
    )(place, shifted, sigma)


def assemble_kernel(place_ref, own, column, near_two, last_three, far_zero, out_ref):
    @pl.when(place_ref[1] == 1)
    def _():
        odd = place_ref[0]
        width = own.shape[0]
        half, quarter = width // 2, width // 4

        def at(block, count=1):
            return pl.ds(pl.multiple_of(block * width, 128), count * width)

        near = 2 * (1 - odd)
        row = [turned(block, odd) for block in range(4)]
        out_ref[at(row[1]), :] = own[...]
        out_ref[at(row[2]), at(row[3])] = near_two[:, :width]
        out_ref[at(row[3]), at(row[2])] = near_two[:, :width].T
        out_ref[at(row[0]), at(near, 2)] = far_zero[:, : 2 * width]
        for step in range(2):
            out_ref[at(near + step), at(row[0])] = far_zero[:, step * width : (1 + step) * width].T
        for block in (0, 2, 3):
            out_ref[at(row[block]), at(row[1])] = column[at(row[block]), :]
        packed = ((0, far_zero, 2 * width), (2, near_two, width), (3, last_three, 0))
        for block, packed_ref, start in packed:
            for part in range(4):
                rows = pl.ds(pl.multiple_of(row[block] * width + part * quarter, 128), quarter)
                for side, value in enumerate(unpacked_rows(part, packed_ref, start)):
                    columns = pl.ds(pl.multiple_of(row[block] * width + side * half, 128), half)
                    out_ref[rows, columns] = value


def assemble(place, *parts):
    nodes = parts[0].shape[1]
    vmem = pl.BlockSpec(memory_space=pltpu.VMEM)
    return pl.pallas_call(
        assemble_kernel,
        out_shape=jax.ShapeDtypeStruct((nodes, nodes), BF16),
        in_specs=[pl.BlockSpec(memory_space=pltpu.SMEM)] + [vmem] * 5,
        out_specs=vmem,
        compiler_params=pltpu.CompilerParams(vmem_limit_bytes=6 * MIB),
        cost_estimate=LIGHT,
        name="assemble",
    )(place, *parts)


def tick(place, *values, cost=HEAVY):
    def kernel(place_ref, *refs):
        for which in range(place.shape[0]):
            refs[-1][which] = place_ref[which]

    scalars = pl.BlockSpec(memory_space=pltpu.SMEM)
    return pl.pallas_call(
        kernel,
        out_shape=jax.ShapeDtypeStruct(place.shape, place.dtype),
        in_specs=[scalars] + [pl.BlockSpec(memory_space=pl.ANY)] * len(values),
        out_specs=scalars,
        compiler_params=pltpu.CompilerParams(vmem_limit_bytes=MIB),
        cost_estimate=cost,
        name="tick",
    )(place, *values)


def finish_kernel(
    place_ref, pivot_ref, sigma_ref,
    q0, q0_last, q2, q3_two,
    q01, q11, q21, q31,
    out_ref, var_ref,
):
    rows, nodes = pivot_ref.shape
    width = nodes // 4
    odd, place = place_ref[0], place_ref[1]
    here = pl.multiple_of(pl.program_id(0) * rows, 128)
    diagonal = diagonal_of(rows)

    def at(block, count=1):
        return pl.ds(pl.multiple_of(block * width, 128), count * width)

    def own(block):
        return pl.ds(pl.multiple_of(block * width + here, 128), rows)

    def add(columns, product):
        out_ref[:, columns] = (pivot_ref[:, columns].astype(F32) + product.astype(F32)).astype(BF16)

    def trace(product):
        var_ref[...] = diagonal(
            pivot_ref[:, own(place_ref[2])].astype(F32) + product.astype(F32)
        )

    active = place_ref[4] != 0

    @pl.when(active & (place == 0))
    def _():
        add(at(odd, 3), q0[...])
        add(at(turned(3, odd)), q0_last[...])
        trace(q0[:, own(2 * odd)])

    @pl.when(active & (place == 1))
    def _():
        add(at(turned(0, odd)), q01[...].T)
        add(at(turned(1, odd)), q11[...])
        add(at(turned(2, odd)), q21[...].T)
        add(at(turned(3, odd)), q31[...].T)
        trace(q11[:, pl.ds(here, rows)])

    @pl.when(active & (place == 2))
    def _():
        add(at(turned(0, odd)), q2[pl.ds(0, width), pl.ds(pl.multiple_of(width + here, 128), rows)].T)
        add(at(turned(1, odd)), q2[pl.ds(here, rows), pl.ds(0, width)])
        start = pl.program_id(0) % 2 * rows + 2 * width
        trace(q2[pl.ds(here, rows), pl.ds(pl.multiple_of(start, 128), rows)])
        for part in range(4):

            @pl.when(pl.program_id(0) == part)
            def _():
                for side, value in enumerate(unpacked_rows(part, q2, 2 * width)):
                    start = turned(2, odd) * width + side * width // 2
                    add(pl.ds(pl.multiple_of(start, 128), width // 2), value)

    @pl.when(active & (place == 3))
    def _():
        add(at(turned(2, odd)), q3_two[...])

    @pl.when(place_ref[4] == 0)
    def _():
        out_ref[...] = sigma_ref[...]
        var_ref[...] = diagonal(sigma_ref[:, own(place_ref[2])].astype(F32))


def finish(place, pivot, sigma, received, kept):
    rows, nodes = pivot.shape
    chunk = 128
    width = nodes // 4

    def picked(which, blocks):
        return pl.BlockSpec(
            (chunk, blocks * width), lambda i, place: (jnp.where(place[1] == which, i, 0), 0)
        )

    def turned_block(start):
        return pl.BlockSpec(
            (rows, chunk),
            lambda i, place: (
                0,
                jnp.where(place[1] == 1, start(place[0]) * (width // chunk) + i, 0),
            ),
        )

    return pl.pallas_call(
        finish_kernel,
        out_shape=(
            jax.ShapeDtypeStruct((rows, nodes), BF16),
            jax.ShapeDtypeStruct((1, rows), F32),
        ),
        grid_spec=pltpu.PrefetchScalarGridSpec(
            num_scalar_prefetch=1,
            grid=(rows // chunk,),
            in_specs=[
                pl.BlockSpec((chunk, nodes), lambda i, place: (i, 0)),
                pl.BlockSpec(
                    (chunk, nodes), lambda i, place: (jnp.where(place[4] == 0, i, 0), 0)
                ),
                picked(0, 3),
                picked(0, 1),
                pl.BlockSpec((rows, 11 * width // 4), lambda i, place: (0, 0)),
                picked(3, 1),
                turned_block(lambda odd: 1),
                picked(1, 1),
                turned_block(lambda odd: 0),
                turned_block(lambda odd: 1 - odd),
            ],
            out_specs=(
                pl.BlockSpec((chunk, nodes), lambda i, place: (i, 0)),
                pl.BlockSpec((1, chunk), lambda i, place: (0, i)),
            ),
        ),
        compiler_params=pltpu.CompilerParams(vmem_limit_bytes=12 * MIB),
        cost_estimate=HEAVY,
        name="finish",
    )(place, pivot, sigma, *received, *kept)


def last_kernel(place_ref, pivot_ref, q2_last, q3, old_ref, old_var_ref, out_ref, var_ref, sum_ref, sems):
    rows, nodes = pivot_ref.shape
    width = nodes // 4
    chunk = 128
    odd, place = place_ref[0], place_ref[1]
    active = place_ref[4] != 0

    def at(block, count=1):
        return pl.ds(pl.multiple_of(block * width, 128), count * width)

    def copies(part, pieces):
        here = pl.ds(part * chunk, chunk)
        return [
            pltpu.make_async_copy(
                sum_ref.at[here, source], out_ref.at[here, target], sems.at[which, part]
            )
            for which, (source, target, _) in enumerate(pieces)
        ]

    def write(pieces):
        for part in range(4):
            here = pl.ds(part * chunk, chunk)
            for source, target, product in pieces:
                value = pivot_ref[here, target].astype(F32) + product(part, here).astype(F32)
                sum_ref[here, source] = value.astype(BF16)
            for copy in copies(part, pieces):
                copy.start()
        for part in range(4):
            for copy in copies(part, pieces):
                copy.wait()

    var_ref[...] = old_var_ref[...]

    @pl.when(active & (place == 2))
    def _():
        write([(pl.ds(0, width), at(3 - 3 * odd), lambda part, here: q2_last[:, here].T)])

    @pl.when(active & (place == 3))
    def _():
        both, last = pl.ds(0, 2 * width), pl.ds(2 * width, width)
        for start in range(0, rows, chunk):
            here = pl.ds(start, chunk)
            own = pl.ds(pl.multiple_of(place_ref[2] * width + start, 128), chunk)
            value = pivot_ref[here, own].astype(F32)
            value = value + q3[here, pl.ds(2 * width + start % (2 * chunk), chunk)].astype(F32)
            var_ref[:, here] = diagonal_of(chunk)(value)
        write(
            [
                (both, at(2 * odd, 2), lambda part, here: q3[here, both]),
                (
                    last,
                    at(3 - 3 * odd),
                    lambda part, here: jnp.concatenate(unpacked_rows(part, q3, 2 * width), axis=1),
                ),
            ]
        )


def diagonal_of(rows):
    square = (rows, rows)
    on_diagonal = lax.broadcasted_iota(jnp.int32, square, 0) == lax.broadcasted_iota(
        jnp.int32, square, 1
    )
    return lambda value: jnp.sum(jnp.where(on_diagonal, value, 0.0), axis=0, keepdims=True)


def finish_last(place, pivot, q2_last, q3, covariance, variances):
    rows, nodes = pivot.shape
    width = nodes // 4
    vmem = pl.BlockSpec(memory_space=pltpu.VMEM)
    anywhere = pl.BlockSpec(memory_space=pl.ANY)
    return pl.pallas_call(
        last_kernel,
        out_shape=(
            jax.ShapeDtypeStruct((rows, nodes), BF16),
            jax.ShapeDtypeStruct((1, rows), F32),
        ),
        in_specs=[pl.BlockSpec(memory_space=pltpu.SMEM)] + [vmem] * 3 + [anywhere, vmem],
        out_specs=(anywhere, vmem),
        scratch_shapes=[
            pltpu.VMEM((rows, 3 * width), BF16),
            pltpu.SemaphoreType.DMA((2, rows // 128)),
        ],
        input_output_aliases={4: 0},
        compiler_params=pltpu.CompilerParams(vmem_limit_bytes=8 * MIB),
        cost_estimate=LIGHT,
        name="finish_last",
    )(place, pivot, q2_last, q3, covariance, variances)


def owned(sigma_next, separator, inverse_pivot, coupling_rate, lengths, step_index, node_class):
    sigma, pivot = sigma_next[0], inverse_pivot[0]
    odd = lax.axis_index("dom") % 2
    col = lax.axis_index("col")
    step = step_index[0]
    place = jnp.stack([odd, turned(col, odd), col, step, step < lengths[0]]).astype(jnp.int32)
    after = lambda value, *others: lax.optimization_barrier((value, *others))[0]

    shifted = passed_along(separator, "dom", -1)[0]
    p2 = moved(pivot, 2, 1)
    p0 = moved(pivot, 0, 1)
    c1 = [couple(pivot, node_class, coupling_rate, part, 2) for part in range(2)]
    across = turn(place, 1, 0, c1[0], None)
    across = turn(place, 1, 1, c1[1], across)

    row, far, near, last = prior_parts(place, after(shifted, across), sigma)
    far_zero, near_two, last_three = moved(far, 0, 1), moved(near, 2, 1), moved(last, 3, 1)

    c2 = couple_here(place, after(p2, last), node_class, coupling_rate)
    across = turn(place, 2, 0, c2, across)
    c0 = couple_here(place, after(p0, across), node_class, coupling_rate)
    across = turn(place, 0, 0, c0, across)
    column, h0_one, h2_one = own_column(place, after(row, last_three, near_two), c0, c2)
    c3 = [
        moved(after(c1[0], last_three, near_two, across), 3, 1),
        moved(after(c1[1], far_zero, h2_one), 3, 1),
    ]
    prior = assemble(place, row, column, near_two, last_three, far_zero)

    h0 = half_product(place, c0, prior, h0_one)
    q0_own = multiply(place, [h0], across, lambda odd: odd, 3)
    q0 = moved(q0_own, 1, 0)
    h2 = half_product(place, after(c2, q0_own), prior, h2_one)
    q2_own = product_two(place, h2, across, q0_own)
    q2 = moved(q2_own, 1, 2)

    across = turn(place, 3, 0, c3[0], after(across, q2_own))
    upper = multiply(place, [c3[0]], prior)
    across = turn(place, 3, 1, c3[1], after(across, upper))
    q03 = multiply(place, [h0], across, lambda odd: 3 - 3 * odd, 1)
    q0_last = moved(q03, 1, 0)
    h3 = [upper, multiply(place, [after(c3[1], q03)], prior)]
    q32 = multiply(place, h3, across, lambda odd: 2 - odd, 1)
    q3_two = moved(q32, 1, 3)
    q3_own = product_rest(place, h3, across, after(q03, q32))
    q3 = moved(q3_own, 1, 3)
    h1 = multiply(place, [after(c1[0], q3_own), c1[1]], prior)
    q11 = multiply(place, [h1], across, lambda odd: 1 + odd, 1)
    received = (q0, q0_last, q2, q3_two)
    kept = (q0_own, q11, q2_own, q3_own)
    place_then = tick(tick(place, q0, cost=LIGHT), q0_last, cost=MEDIUM)
    q2_last = moved(after(q3_two, place_then), 3, 2)
    covariance, variances = finish(place_then, pivot, sigma, received, kept)
    covariance, variances = finish_last(place, pivot, q2_last, q3, covariance, variances)
    return (covariance[None], variances)


def gathered(sigma_next, separator, inverse_pivot, coupling_rate, lengths, step_index, node_class):
    shifted = passed_along(separator, "dom", -1)
    prior = jnp.where(step_index[0] == 0, shifted[0], sigma_next[0])
    pivot = inverse_pivot[0].astype(F32)
    coupled = couple(inverse_pivot[0], node_class, coupling_rate)
    rows = coupled.shape[0]
    half = jnp.dot(
        coupled,
        lax.all_gather(prior, "col", axis=0, tiled=True),
        preferred_element_type=F32,
    ).astype(BF16)
    product = lax.dot_general(
        half,
        lax.all_gather(coupled, "col", axis=0, tiled=True),
        (((1,), (1,)), ((), ())),
        preferred_element_type=F32,
    )
    full = pivot + product
    active = step_index[0] < lengths[0]
    old = sigma_next[0]
    covariance = jnp.where(active, full.astype(BF16), old)
    first_col = lax.axis_index("col") * rows
    new_block = lax.dynamic_slice_in_dim(full, first_col, rows, 1)
    old_block = lax.dynamic_slice_in_dim(old, first_col, rows, 1)
    variances = jnp.where(active, jnp.diagonal(new_block), jnp.diagonal(old_block).astype(F32))
    return (covariance[None], variances[None])


def solution(mesh):
    local = owned if mesh.shape["col"] == 4 and mesh.shape["dom"] % 2 == 0 else gathered
    return jax.shard_map(
        local,
        mesh=mesh,
        in_specs=(
            P(("groups", "dom"), "col", None),
            P(("groups", "dom"), "col", None),
            P(("groups", "dom"), "col", None),
            P(("groups", "dom")),
            P(("groups", "dom")),
            P(("groups", "dom")),
            P("groups"),
        ),
        out_specs=(P(("groups", "dom"), "col", None), P(("groups", "dom"), "col")),
        check_vma=False,
    )
```

```python
import functools

import jax
import jax.numpy as jnp
from jax import lax
from jax.experimental import pallas as pl
from jax.experimental.pallas import tpu as pltpu
from jax.sharding import PartitionSpec as P

GX = 64
GY = 32
BF16 = jnp.bfloat16
F32 = jnp.float32
MIB = 1 << 20


def passed_along(value, axis, steps):
    count = lax.axis_size(axis)
    initial, last = (max(0, -steps), min(count, count - steps))
    return lax.ppermute(value, axis, [(source, source + steps) for source in range(initial, last)])


LIGHT = pl.CostEstimate(flops=1 << 20, bytes_accessed=1 << 16, transcendentals=0)
MEDIUM = pl.CostEstimate(flops=2000000000, bytes_accessed=1 << 16, transcendentals=0)
HEAVY = pl.CostEstimate(flops=14000000000, bytes_accessed=1 << 16, transcendentals=0)


BLOCK = 256
SPAN = 512


def window(block, nodes):
    return pl.multiple_of(jnp.clip(block * BLOCK - (SPAN - BLOCK) // 2, 0, nodes - SPAN), 128)


def weight_kernel(class_ref, out_ref):
    nodes = class_ref.shape[1]

    def fill(block, carry):
        first = pl.multiple_of(block * BLOCK, BLOCK)
        kind = class_ref[:, pl.ds(first, BLOCK)]
        across = jnp.where(
            kind == 0, 0.25, jnp.where(kind == 1, 0.375, jnp.where(kind == 2, 0.125, 0.5))
        ).astype(F32)
        along = jnp.where(
            kind == 0, 0.25, jnp.where(kind == 1, 0.125, jnp.where(kind == 2, 0.375, 0.0))
        ).astype(F32)
        column = (first + lax.broadcasted_iota(jnp.int32, (1, BLOCK), 1)) % GX
        left = jnp.where(column > 0, across, 0.0)
        right = jnp.where(column < GX - 1, across, 0.0)
        shape = (SPAN, BLOCK)
        offset = (
            lax.broadcasted_iota(jnp.int32, shape, 0)
            - lax.broadcasted_iota(jnp.int32, shape, 1)
            + (window(block, nodes) - first)
        )
        value = jnp.where(jnp.abs(offset) == GX, along, 0.0)
        value = jnp.where(offset == -1, left, value)
        value = jnp.where(offset == 1, right, value)
        value = jnp.where(offset == 0, 1.0, value)
        out_ref[block] = value.astype(BF16)
        return carry

    lax.fori_loop(0, nodes // BLOCK, fill, 0)


def coupling(node_class):
    nodes = node_class.shape[0]
    vmem = pl.BlockSpec(memory_space=pltpu.VMEM)
    return pl.pallas_call(
        weight_kernel,
        out_shape=jax.ShapeDtypeStruct((nodes // BLOCK, SPAN, BLOCK), BF16),
        in_specs=[vmem],
        out_specs=vmem,
        compiler_params=pltpu.CompilerParams(vmem_limit_bytes=6 * MIB),
        cost_estimate=LIGHT,
        name="coupling",
    )(node_class.reshape(1, nodes))


def couple_kernel(first, rate_ref, weight_ref, pivot_ref, out_ref):
    rows, nodes = out_ref.shape

    def block_of(block, carry):
        source = pl.ds(window(block, nodes), SPAN)
        target = pl.ds(pl.multiple_of(block * BLOCK, BLOCK), BLOCK)
        value = jnp.dot(
            pivot_ref[first : first + rows, source], weight_ref[block], preferred_element_type=F32
        )
        out_ref[:, target] = (rate_ref[0] * value).astype(BF16)
        return carry

    lax.fori_loop(0, nodes // BLOCK, block_of, 0)


def couple(pivot, weights, rate, part=0, parts=1):
    rows, nodes = pivot.shape[0] // parts, pivot.shape[1]
    vmem = pl.BlockSpec(memory_space=pltpu.VMEM)
    return pl.pallas_call(
        functools.partial(couple_kernel, part * rows),
        out_shape=jax.ShapeDtypeStruct((rows, nodes), BF16),
        in_specs=[pl.BlockSpec(memory_space=pltpu.SMEM), vmem, vmem],
        out_specs=vmem,
        compiler_params=pltpu.CompilerParams(vmem_limit_bytes=8 * MIB),
        cost_estimate=LIGHT,
        name="couple",
    )(rate, weights, pivot)


def turned(block, odd):
    return block + odd * (3 - 2 * block)


def route(source, target, doms):
    pairs = []
    for dom in range(doms):
        odd = dom % 2
        pairs.append((dom * 4 + turned(source, odd), dom * 4 + turned(target, odd)))
    return pairs


def moved(value, source, target):
    return lax.ppermute(value, ("dom", "col"), route(source, target, lax.axis_size("dom")))


def couple_here(place, pivot, weights, rate):
    def kernel(place_ref, *refs):
        @pl.when(place_ref[1] == 1)
        def _():
            couple_kernel(0, *refs)

    scalars, vmem = pl.BlockSpec(memory_space=pltpu.SMEM), pl.BlockSpec(memory_space=pltpu.VMEM)
    return pl.pallas_call(
        kernel,
        out_shape=jax.ShapeDtypeStruct(pivot.shape, BF16),
        in_specs=[scalars, scalars, vmem, vmem],
        out_specs=vmem,
        compiler_params=pltpu.CompilerParams(vmem_limit_bytes=8 * MIB),
        cost_estimate=LIGHT,
        name="couple_here",
    )(place, rate, weights, pivot)


def turn_kernel(place_ref, coupled_ref, *refs):
    @pl.when(place_ref[1] == 1)
    def _():
        refs[-1][...] = coupled_ref[...].T


def turn(place, panel, part, coupled, across):
    rows, nodes = coupled.shape
    chunk = 128
    steps = rows // chunk
    ratio = nodes // 4 // chunk
    return pl.pallas_call(
        turn_kernel,
        out_shape=jax.ShapeDtypeStruct((nodes, nodes), BF16),
        grid_spec=pltpu.PrefetchScalarGridSpec(
            num_scalar_prefetch=1,
            grid=(steps,),
            in_specs=[pl.BlockSpec((chunk, nodes), lambda i, place: (i, 0))]
            + ([] if across is None else [pl.BlockSpec(memory_space=pl.ANY)]),
            out_specs=pl.BlockSpec(
                (nodes, chunk),
                lambda i, place: (0, turned(panel, place[0]) * ratio + part * steps + i),
            ),
        ),
        input_output_aliases={} if across is None else {2: 0},
        compiler_params=pltpu.CompilerParams(vmem_limit_bytes=4 * MIB),
        cost_estimate=LIGHT,
        name="turn",
    )(place, coupled, *(() if across is None else (across,)))


def multiply_kernel(first, count, lefts, place_ref, *refs):
    left_refs, right_ref, out_ref = refs[:lefts], refs[lefts], refs[-1]
    width = right_ref.shape[0] // 4

    @pl.when(place_ref[1] == 1)
    def _():
        def block(step, carry):
            source = pl.multiple_of((first(place_ref[0]) + step) * width, 128)
            target = pl.multiple_of(step * width, 128)
            row = 0
            for left_ref in left_refs:
                rows = left_ref.shape[0]
                out_ref[row : row + rows, pl.ds(target, width)] = jnp.dot(
                    left_ref[...], right_ref[:, pl.ds(source, width)], preferred_element_type=F32
                ).astype(BF16)
                row += rows
            return carry

        lax.fori_loop(0, count, block, 0)


def multiply(place, lefts, right, first=lambda odd: 0, count=4):
    rows = sum(left.shape[0] for left in lefts)
    width = right.shape[0] // 4
    vmem = pl.BlockSpec(memory_space=pltpu.VMEM)
    return pl.pallas_call(
        functools.partial(multiply_kernel, first, count, len(lefts)),
        out_shape=jax.ShapeDtypeStruct((rows, count * width), BF16),
        in_specs=[pl.BlockSpec(memory_space=pltpu.SMEM)] + [vmem] * (len(lefts) + 1),
        out_specs=vmem,
        compiler_params=pltpu.CompilerParams(vmem_limit_bytes=6 * MIB),
        cost_estimate=LIGHT,
        name="multiply",
    )(place, *lefts, right)


def pack(value, out_ref, column):
    half = value.shape[0] // 2
    for part in range(2):
        rows = pl.ds(part * half, half)
        pack_rows(part, value[part * half : (part + 1) * half], out_ref.at[rows], column)


def two_kernel(place_ref, left_ref, right_ref, zero_ref, out_ref):
    odd = place_ref[0]
    width = right_ref.shape[0] // 4

    def product(block):
        columns = pl.ds(pl.multiple_of(block * width, 128), width)
        value = jnp.dot(left_ref[...], right_ref[:, columns], preferred_element_type=F32)
        return value.astype(BF16)

    @pl.when(place_ref[1] == 1)
    def _():
        out_ref[:, :width] = product(1 + odd)
        zero = pl.ds(pl.multiple_of((2 - 2 * odd) * width, 128), width)
        out_ref[:, width : 2 * width] = zero_ref[:, zero]
        pack(product(2 - odd), out_ref, 2 * width)


def product_two(place, half, across, zero):
    rows = half.shape[0]
    width = across.shape[0] // 4
    vmem = pl.BlockSpec(memory_space=pltpu.VMEM)
    return pl.pallas_call(
        two_kernel,
        out_shape=jax.ShapeDtypeStruct((rows, 11 * width // 4), BF16),
        in_specs=[pl.BlockSpec(memory_space=pltpu.SMEM)] + [vmem] * 3,
        out_specs=vmem,
        compiler_params=pltpu.CompilerParams(vmem_limit_bytes=6 * MIB),
        cost_estimate=LIGHT,
        name="product_two",
    )(place, half, across, zero)


def half_kernel(place_ref, left_ref, right_ref, one_ref, out_ref):
    width = one_ref.shape[1]

    @pl.when(place_ref[1] == 1)
    def _():
        def block(step, carry):
            which = turned(step + (step > 0).astype(jnp.int32), place_ref[0])
            columns = pl.ds(pl.multiple_of(which * width, 128), width)
            out_ref[:, columns] = jnp.dot(
                left_ref[...], right_ref[:, columns], preferred_element_type=F32
            ).astype(BF16)
            return carry

        lax.fori_loop(0, 3, block, 0)
        columns = pl.ds(pl.multiple_of(turned(1, place_ref[0]) * width, 128), width)
        out_ref[:, columns] = one_ref[...]


def half_product(place, left, right, one):
    vmem = pl.BlockSpec(memory_space=pltpu.VMEM)
    return pl.pallas_call(
        half_kernel,
        out_shape=jax.ShapeDtypeStruct(left.shape, BF16),
        in_specs=[pl.BlockSpec(memory_space=pltpu.SMEM)] + [vmem] * 3,
        out_specs=vmem,
        compiler_params=pltpu.CompilerParams(vmem_limit_bytes=6 * MIB),
        cost_estimate=LIGHT,
        name="half_product",
    )(place, left, right, one)


def column_kernel(place_ref, own_ref, first_ref, second_ref, *refs):
    column_ref, out_refs = refs[0], refs[1:]

    @pl.when(place_ref[1] == 1)
    def _():
        width = own_ref.shape[0]
        for block in range(4):
            rows = pl.ds(block * width, width)
            column_ref[rows, :] = own_ref[:, rows].T
        for left_ref, out_ref in zip((first_ref, second_ref), out_refs):
            out_ref[...] = jnp.dot(
                left_ref[...], column_ref[...], preferred_element_type=F32
            ).astype(BF16)


def own_column(place, own, first, second):
    rows, nodes = own.shape
    vmem = pl.BlockSpec(memory_space=pltpu.VMEM)
    return pl.pallas_call(
        column_kernel,
        out_shape=(
            jax.ShapeDtypeStruct((nodes, rows), BF16),
            jax.ShapeDtypeStruct((rows, rows), BF16),
            jax.ShapeDtypeStruct((rows, rows), BF16),
        ),
        in_specs=[pl.BlockSpec(memory_space=pltpu.SMEM)] + [vmem] * 3,
        out_specs=(vmem, vmem, vmem),
        compiler_params=pltpu.CompilerParams(vmem_limit_bytes=6 * MIB),
        cost_estimate=LIGHT,
        name="own_column",
    )(place, own, first, second)


def rest_kernel(place_ref, upper_ref, lower_ref, right_ref, zero_ref, out_ref):
    odd = place_ref[0]
    width = zero_ref.shape[1]
    half = width // 2

    def product(left_ref, block):
        columns = pl.ds(pl.multiple_of(block * width, 128), width)
        value = jnp.dot(left_ref[...], right_ref[:, columns], preferred_element_type=F32)
        return value.astype(BF16)

    @pl.when(place_ref[1] == 1)
    def _():
        out_ref[:, pl.ds(pl.multiple_of(odd * width, 128), width)] = zero_ref[...].T
        other = pl.ds(pl.multiple_of((1 - odd) * width, 128), width)
        for part, left_ref in enumerate((upper_ref, lower_ref)):
            rows = pl.ds(part * half, half)
            out_ref[rows, other] = product(left_ref, 1 + odd)
            pack_rows(part, product(left_ref, 3 - 3 * odd), out_ref.at[rows], 2 * width)


def product_rest(place, halves, across, zero):
    rows, width = zero.shape
    vmem = pl.BlockSpec(memory_space=pltpu.VMEM)
    return pl.pallas_call(
        rest_kernel,
        out_shape=jax.ShapeDtypeStruct((rows, 11 * width // 4), BF16),
        in_specs=[pl.BlockSpec(memory_space=pltpu.SMEM)] + [vmem] * 4,
        out_specs=vmem,
        compiler_params=pltpu.CompilerParams(vmem_limit_bytes=6 * MIB),
        cost_estimate=LIGHT,
        name="product_rest",
    )(place, *halves, across, zero)


def pack_rows(part, value, out_ref, column):
    half, width = value.shape
    quarter = half // 2
    if part == 0:
        out_ref[:, column : column + half] = value[:, :half]
        out_ref[:, column + half : column + half + quarter] = value[:, half : half + quarter]
    else:
        out_ref[:, column : column + half] = value[:, half:]
        beside = slice(column + half, column + half + quarter)
        out_ref[:quarter, beside] = value[quarter:, :quarter]
        out_ref[quarter:, beside] = value[quarter:, quarter:half]


def unpacked_rows(part, packed_ref, column):
    quarter = packed_ref.shape[0] // 4
    half = 2 * quarter
    beside = slice(column + half, column + half + quarter)
    rows = slice(part * quarter, (part + 1) * quarter)
    diagonal = packed_ref[rows, column : column + half]
    lower = [packed_ref[start : start + quarter, beside] for start in (half, half + quarter)]
    if part < 2:
        return diagonal, jnp.concatenate([packed_ref[rows, beside], lower[part].T], axis=1)
    if part == 2:
        return packed_ref[:half, beside].T, diagonal
    return jnp.concatenate(lower, axis=1), diagonal


def prior_kernel(place_ref, shifted_ref, sigma_ref, out_ref):
    @pl.when(place_ref[3] == 0)
    def _():
        out_ref[...] = shifted_ref[...]

    @pl.when(place_ref[3] != 0)
    def _():
        out_ref[...] = sigma_ref[...]


def parts_kernel(place_ref, shifted_ref, sigma_ref, row_ref, far_ref, near_ref, last_ref):
    odd = place_ref[0]
    width = row_ref.shape[1] // 4

    def at(block, count=1):
        return pl.ds(pl.multiple_of(block * width, 128), count * width)

    prior_kernel(place_ref, shifted_ref, sigma_ref, row_ref)
    far_ref[:, :width] = row_ref[:, at(3 - 3 * odd)]
    near_ref[:, :width] = row_ref[:, at(3 - 3 * odd)]
    near_ref[:, width : 2 * width] = row_ref[:, at(3 * odd)]
    for part in range(2):

        @pl.when(pl.program_id(0) == part)
        def _():
            pack_rows(part, row_ref[:, at(3 * odd)], far_ref, width)
            pack_rows(part, row_ref[:, at(2 - odd)], near_ref, 2 * width)
            pack_rows(part, row_ref[:, at(3 - 3 * odd)], last_ref, 0)


def prior_parts(place, shifted, sigma):
    rows, nodes = sigma.shape
    chunk = rows // 2
    width = nodes // 4
    out = lambda quarters: jax.ShapeDtypeStruct((rows, quarters * width // 4), BF16)
    spec = lambda quarters: pl.BlockSpec((chunk, quarters * width // 4), lambda i, place: (i, 0))
    return pl.pallas_call(
        parts_kernel,
        out_shape=(out(16), out(7), out(11), out(3)),
        grid_spec=pltpu.PrefetchScalarGridSpec(
            num_scalar_prefetch=1,
            grid=(rows // chunk,),
            in_specs=[
                pl.BlockSpec(
                    (chunk, nodes), lambda i, place: (jnp.where(place[3] == 0, i, 0), 0)
                ),
                pl.BlockSpec(
                    (chunk, nodes), lambda i, place: (jnp.where(place[3] == 0, 0, i), 0)
                ),
            ],
            out_specs=(spec(16), spec(7), spec(11), spec(3)),
        ),
        compiler_params=pltpu.CompilerParams(vmem_limit_bytes=14 * MIB),
        cost_estimate=LIGHT,
        name="prior_parts",
    )(place, shifted, sigma)


def assemble_kernel(place_ref, own, column, near_two, last_three, far_zero, out_ref):
    @pl.when(place_ref[1] == 1)
    def _():
        odd = place_ref[0]
        width = own.shape[0]
        half, quarter = width // 2, width // 4

        def at(block, count=1):
            return pl.ds(pl.multiple_of(block * width, 128), count * width)

        row = [turned(block, odd) for block in range(4)]
        out_ref[at(row[1]), :] = own[...]
        pairs = ((2, 3, near_two, 0), (2, 0, near_two, width), (0, 3, far_zero, 0))
        for first, second, ref, start in pairs:
            value = ref[:, start : start + width]
            out_ref[at(row[first]), at(row[second])] = value
            out_ref[at(row[second]), at(row[first])] = value.T
        for block in (0, 2, 3):
            out_ref[at(row[block]), at(row[1])] = column[at(row[block]), :]
        packed = ((0, far_zero, width), (2, near_two, 2 * width), (3, last_three, 0))
        for block, packed_ref, start in packed:
            for part in range(4):
                rows = pl.ds(pl.multiple_of(row[block] * width + part * quarter, 128), quarter)
                for side, value in enumerate(unpacked_rows(part, packed_ref, start)):
                    columns = pl.ds(pl.multiple_of(row[block] * width + side * half, 128), half)
                    out_ref[rows, columns] = value


def assemble(place, *parts):
    nodes = parts[0].shape[1]
    vmem = pl.BlockSpec(memory_space=pltpu.VMEM)
    return pl.pallas_call(
        assemble_kernel,
        out_shape=jax.ShapeDtypeStruct((nodes, nodes), BF16),
        in_specs=[pl.BlockSpec(memory_space=pltpu.SMEM)] + [vmem] * 5,
        out_specs=vmem,
        compiler_params=pltpu.CompilerParams(vmem_limit_bytes=6 * MIB),
        cost_estimate=LIGHT,
        name="assemble",
    )(place, *parts)


def tick(place, *values, cost=HEAVY):
    def kernel(place_ref, *refs):
        for which in range(place.shape[0]):
            refs[-1][which] = place_ref[which]

    scalars = pl.BlockSpec(memory_space=pltpu.SMEM)
    return pl.pallas_call(
        kernel,
        out_shape=jax.ShapeDtypeStruct(place.shape, place.dtype),
        in_specs=[scalars] + [pl.BlockSpec(memory_space=pl.ANY)] * len(values),
        out_specs=scalars,
        compiler_params=pltpu.CompilerParams(vmem_limit_bytes=MIB),
        cost_estimate=cost,
        name="tick",
    )(place, *values)


def finish_kernel(
    place_ref, pivot_ref, sigma_ref,
    q0, q0_last, q2, q3_two,
    q01, q11, q21, q31,
    out_ref, var_ref,
):
    rows, nodes = pivot_ref.shape
    width = nodes // 4
    odd, place = place_ref[0], place_ref[1]
    here = pl.multiple_of(pl.program_id(0) * rows, 128)
    diagonal = diagonal_of(rows)

    def at(block, count=1):
        return pl.ds(pl.multiple_of(block * width, 128), count * width)

    def own(block):
        return pl.ds(pl.multiple_of(block * width + here, 128), rows)

    def add(columns, product):
        out_ref[:, columns] = (pivot_ref[:, columns].astype(F32) + product.astype(F32)).astype(BF16)

    def trace(product):
        var_ref[...] = diagonal(
            pivot_ref[:, own(place_ref[2])].astype(F32) + product.astype(F32)
        )

    active = place_ref[4] != 0

    @pl.when(active & (place == 0))
    def _():
        add(at(odd, 3), q0[...])
        add(at(turned(3, odd)), q0_last[...])
        trace(q0[:, own(2 * odd)])

    @pl.when(active & (place == 1))
    def _():
        add(at(turned(0, odd)), q01[...].T)
        add(at(turned(1, odd)), q11[...])
        add(at(turned(2, odd)), q21[...].T)
        add(at(turned(3, odd)), q31[...].T)
        trace(q11[:, pl.ds(here, rows)])

    @pl.when(active & (place == 2))
    def _():
        add(at(turned(0, odd)), q2[pl.ds(0, width), pl.ds(pl.multiple_of(width + here, 128), rows)].T)
        add(at(turned(1, odd)), q2[pl.ds(here, rows), pl.ds(0, width)])
        start = pl.program_id(0) % 2 * rows + 2 * width
        trace(q2[pl.ds(here, rows), pl.ds(pl.multiple_of(start, 128), rows)])
        for part in range(4):

            @pl.when(pl.program_id(0) == part)
            def _():
                for side, value in enumerate(unpacked_rows(part, q2, 2 * width)):
                    start = turned(2, odd) * width + side * width // 2
                    add(pl.ds(pl.multiple_of(start, 128), width // 2), value)

    @pl.when(active & (place == 3))
    def _():
        add(at(turned(2, odd)), q3_two[...])

    @pl.when(place_ref[4] == 0)
    def _():
        out_ref[...] = sigma_ref[...]
        var_ref[...] = diagonal(sigma_ref[:, own(place_ref[2])].astype(F32))


def finish(place, pivot, sigma, received, kept):
    rows, nodes = pivot.shape
    chunk = 128
    width = nodes // 4

    def picked(which, blocks):
        return pl.BlockSpec(
            (chunk, blocks * width), lambda i, place: (jnp.where(place[1] == which, i, 0), 0)
        )

    def turned_block(start):
        return pl.BlockSpec(
            (rows, chunk),
            lambda i, place: (
                0,
                jnp.where(place[1] == 1, start(place[0]) * (width // chunk) + i, 0),
            ),
        )

    return pl.pallas_call(
        finish_kernel,
        out_shape=(
            jax.ShapeDtypeStruct((rows, nodes), BF16),
            jax.ShapeDtypeStruct((1, rows), F32),
        ),
        grid_spec=pltpu.PrefetchScalarGridSpec(
            num_scalar_prefetch=1,
            grid=(rows // chunk,),
            in_specs=[
                pl.BlockSpec((chunk, nodes), lambda i, place: (i, 0)),
                pl.BlockSpec(
                    (chunk, nodes), lambda i, place: (jnp.where(place[4] == 0, i, 0), 0)
                ),
                picked(0, 3),
                picked(0, 1),
                pl.BlockSpec((rows, 11 * width // 4), lambda i, place: (0, 0)),
                picked(3, 1),
                turned_block(lambda odd: 1),
                picked(1, 1),
                turned_block(lambda odd: 0),
                turned_block(lambda odd: 1 - odd),
            ],
            out_specs=(
                pl.BlockSpec((chunk, nodes), lambda i, place: (i, 0)),
                pl.BlockSpec((1, chunk), lambda i, place: (0, i)),
            ),
        ),
        compiler_params=pltpu.CompilerParams(vmem_limit_bytes=12 * MIB),
        cost_estimate=HEAVY,
        name="finish",
    )(place, pivot, sigma, *received, *kept)


def last_kernel(place_ref, pivot_ref, q2_last, q3, old_ref, old_var_ref, out_ref, var_ref, sum_ref, sems):
    rows, nodes = pivot_ref.shape
    width = nodes // 4
    chunk = 128
    odd, place = place_ref[0], place_ref[1]
    active = place_ref[4] != 0

    def at(block, count=1):
        return pl.ds(pl.multiple_of(block * width, 128), count * width)

    def copies(part, pieces):
        here = pl.ds(part * chunk, chunk)
        return [
            pltpu.make_async_copy(
                sum_ref.at[here, source], out_ref.at[here, target], sems.at[which, part]
            )
            for which, (source, target, _) in enumerate(pieces)
        ]

    def write(pieces):
        for part in range(4):
            here = pl.ds(part * chunk, chunk)
            for source, target, product in pieces:
                value = pivot_ref[here, target].astype(F32) + product(part, here).astype(F32)
                sum_ref[here, source] = value.astype(BF16)
            for copy in copies(part, pieces):
                copy.start()
        for part in range(4):
            for copy in copies(part, pieces):
                copy.wait()

    var_ref[...] = old_var_ref[...]

    @pl.when(active & (place == 2))
    def _():
        write([(pl.ds(0, width), at(3 - 3 * odd), lambda part, here: q2_last[:, here].T)])

    @pl.when(active & (place == 3))
    def _():
        both, last = pl.ds(0, 2 * width), pl.ds(2 * width, width)
        for start in range(0, rows, chunk):
            here = pl.ds(start, chunk)
            own = pl.ds(pl.multiple_of(place_ref[2] * width + start, 128), chunk)
            value = pivot_ref[here, own].astype(F32)
            value = value + q3[here, pl.ds(2 * width + start % (2 * chunk), chunk)].astype(F32)
            var_ref[:, here] = diagonal_of(chunk)(value)
        write(
            [
                (both, at(2 * odd, 2), lambda part, here: q3[here, both]),
                (
                    last,
                    at(3 - 3 * odd),
                    lambda part, here: jnp.concatenate(unpacked_rows(part, q3, 2 * width), axis=1),
                ),
            ]
        )


def diagonal_of(rows):
    square = (rows, rows)
    on_diagonal = lax.broadcasted_iota(jnp.int32, square, 0) == lax.broadcasted_iota(
        jnp.int32, square, 1
    )
    return lambda value: jnp.sum(jnp.where(on_diagonal, value, 0.0), axis=0, keepdims=True)


def finish_last(place, pivot, q2_last, q3, covariance, variances):
    rows, nodes = pivot.shape
    width = nodes // 4
    vmem = pl.BlockSpec(memory_space=pltpu.VMEM)
    anywhere = pl.BlockSpec(memory_space=pl.ANY)
    return pl.pallas_call(
        last_kernel,
        out_shape=(
            jax.ShapeDtypeStruct((rows, nodes), BF16),
            jax.ShapeDtypeStruct((1, rows), F32),
        ),
        in_specs=[pl.BlockSpec(memory_space=pltpu.SMEM)] + [vmem] * 3 + [anywhere, vmem],
        out_specs=(anywhere, vmem),
        scratch_shapes=[
            pltpu.VMEM((rows, 3 * width), BF16),
            pltpu.SemaphoreType.DMA((2, rows // 128)),
        ],
        input_output_aliases={4: 0},
        compiler_params=pltpu.CompilerParams(vmem_limit_bytes=8 * MIB),
        cost_estimate=LIGHT,
        name="finish_last",
    )(place, pivot, q2_last, q3, covariance, variances)


def owned(sigma_next, separator, inverse_pivot, coupling_rate, lengths, step_index, node_class):
    sigma, pivot = sigma_next[0], inverse_pivot[0]
    odd = lax.axis_index("dom") % 2
    col = lax.axis_index("col")
    step = step_index[0]
    place = jnp.stack([odd, turned(col, odd), col, step, step < lengths[0]]).astype(jnp.int32)
    after = lambda value, *others: lax.optimization_barrier((value, *others))[0]

    shifted = passed_along(separator, "dom", -1)[0]
    p2 = moved(pivot, 2, 1)
    p0 = moved(pivot, 0, 1)
    weights = coupling(node_class)
    c1 = [couple(pivot, weights, coupling_rate, part, 2) for part in range(2)]
    across = turn(place, 1, 0, c1[0], None)
    across = turn(place, 1, 1, c1[1], across)

    row, far, near, last = prior_parts(place, after(shifted, across), sigma)
    far_zero, near_two, last_three = moved(far, 0, 1), moved(near, 2, 1), moved(last, 3, 1)

    c2 = couple_here(place, after(p2, last), weights, coupling_rate)
    across = turn(place, 2, 0, c2, across)
    c0 = couple_here(place, after(p0, across), weights, coupling_rate)
    across = turn(place, 0, 0, c0, across)
    column, h0_one, h2_one = own_column(place, row, c0, c2)
    c3 = [
        moved(after(c1[0], last_three, near_two, across), 3, 1),
        moved(after(c1[1], far_zero, h2_one), 3, 1),
    ]
    prior = assemble(place, row, column, near_two, last_three, far_zero)

    h0 = half_product(place, c0, prior, h0_one)
    q0_own = multiply(place, [h0], across, lambda odd: odd, 3)
    q0 = moved(q0_own, 1, 0)
    h2 = half_product(place, after(c2, q0_own), prior, h2_one)
    q2_own = product_two(place, h2, across, q0_own)
    q2 = moved(q2_own, 1, 2)

    across = turn(place, 3, 0, c3[0], after(across, q2_own))
    upper = multiply(place, [c3[0]], prior)
    across = turn(place, 3, 1, c3[1], after(across, upper))
    q03 = multiply(place, [h0], across, lambda odd: 3 - 3 * odd, 1)
    q0_last = moved(q03, 1, 0)
    h3 = [upper, multiply(place, [after(c3[1], q03)], prior)]
    q32 = multiply(place, h3, across, lambda odd: 2 - odd, 1)
    q3_two = moved(q32, 1, 3)
    q3_own = product_rest(place, h3, across, after(q03, q32))
    q3 = moved(q3_own, 1, 3)
    h1 = multiply(place, [after(c1[0], q3_own), c1[1]], prior)
    q11 = multiply(place, [h1], across, lambda odd: 1 + odd, 1)
    received = (q0, q0_last, q2, q3_two)
    kept = (q0_own, q11, q2_own, q3_own)
    place_then = tick(tick(place, q0, cost=LIGHT), q0_last, cost=MEDIUM)
    q2_last = moved(after(q3_two, place_then), 3, 2)
    covariance, variances = finish(place_then, pivot, sigma, received, kept)
    covariance, variances = finish_last(place, pivot, q2_last, q3, covariance, variances)
    return (covariance[None], variances)


def gathered(sigma_next, separator, inverse_pivot, coupling_rate, lengths, step_index, node_class):
    shifted = passed_along(separator, "dom", -1)
    prior = jnp.where(step_index[0] == 0, shifted[0], sigma_next[0])
    pivot = inverse_pivot[0].astype(F32)
    coupled = couple(inverse_pivot[0], coupling(node_class), coupling_rate)
    rows = coupled.shape[0]
    half = jnp.dot(
        coupled,
        lax.all_gather(prior, "col", axis=0, tiled=True),
        preferred_element_type=F32,
    ).astype(BF16)
    product = lax.dot_general(
        half,
        lax.all_gather(coupled, "col", axis=0, tiled=True),
        (((1,), (1,)), ((), ())),
        preferred_element_type=F32,
    )
    full = pivot + product
    active = step_index[0] < lengths[0]
    old = sigma_next[0]
    covariance = jnp.where(active, full.astype(BF16), old)
    first_col = lax.axis_index("col") * rows
    new_block = lax.dynamic_slice_in_dim(full, first_col, rows, 1)
    old_block = lax.dynamic_slice_in_dim(old, first_col, rows, 1)
    variances = jnp.where(active, jnp.diagonal(new_block), jnp.diagonal(old_block).astype(F32))
    return (covariance[None], variances[None])


def solution(mesh):
    local = owned if mesh.shape["col"] == 4 and mesh.shape["dom"] % 2 == 0 else gathered
    return jax.shard_map(
        local,
        mesh=mesh,
        in_specs=(
            P(("groups", "dom"), "col", None),
            P(("groups", "dom"), "col", None),
            P(("groups", "dom"), "col", None),
            P(("groups", "dom")),
            P(("groups", "dom")),
            P(("groups", "dom")),
            P("groups"),
        ),
        out_specs=(P(("groups", "dom"), "col", None), P(("groups", "dom"), "col")),
        check_vma=False,
    )
```

```python
import functools

import jax
import jax.numpy as jnp
from jax import lax
from jax.experimental import pallas as pl
from jax.experimental.pallas import tpu as pltpu
from jax.sharding import PartitionSpec as P

GX = 64
GY = 32
BF16 = jnp.bfloat16
F32 = jnp.float32
MIB = 1 << 20


def passed_along(value, axis, steps):
    count = lax.axis_size(axis)
    initial, last = (max(0, -steps), min(count, count - steps))
    return lax.ppermute(value, axis, [(source, source + steps) for source in range(initial, last)])


LIGHT = pl.CostEstimate(flops=1 << 20, bytes_accessed=1 << 16, transcendentals=0)
MEDIUM = pl.CostEstimate(flops=2000000000, bytes_accessed=1 << 16, transcendentals=0)
HEAVY = pl.CostEstimate(flops=14000000000, bytes_accessed=1 << 16, transcendentals=0)


BLOCK = 256
SPAN = 512


def window(block, nodes):
    return pl.multiple_of(jnp.clip(block * BLOCK - (SPAN - BLOCK) // 2, 0, nodes - SPAN), 128)


def weight_kernel(class_ref, out_ref):
    nodes = class_ref.shape[1]

    def fill(block, carry):
        first = pl.multiple_of(block * BLOCK, BLOCK)
        kind = class_ref[:, pl.ds(first, BLOCK)]
        across = jnp.where(
            kind == 0, 0.25, jnp.where(kind == 1, 0.375, jnp.where(kind == 2, 0.125, 0.5))
        ).astype(F32)
        along = jnp.where(
            kind == 0, 0.25, jnp.where(kind == 1, 0.125, jnp.where(kind == 2, 0.375, 0.0))
        ).astype(F32)
        column = (first + lax.broadcasted_iota(jnp.int32, (1, BLOCK), 1)) % GX
        left = jnp.where(column > 0, across, 0.0)
        right = jnp.where(column < GX - 1, across, 0.0)
        shape = (SPAN, BLOCK)
        offset = (
            lax.broadcasted_iota(jnp.int32, shape, 0)
            - lax.broadcasted_iota(jnp.int32, shape, 1)
            + (window(block, nodes) - first)
        )
        value = jnp.where(jnp.abs(offset) == GX, along, 0.0)
        value = jnp.where(offset == -1, left, value)
        value = jnp.where(offset == 1, right, value)
        value = jnp.where(offset == 0, 1.0, value)
        out_ref[block] = value.astype(BF16)
        return carry

    lax.fori_loop(0, nodes // BLOCK, fill, 0)


def coupling(node_class):
    nodes = node_class.shape[0]
    vmem = pl.BlockSpec(memory_space=pltpu.VMEM)
    return pl.pallas_call(
        weight_kernel,
        out_shape=jax.ShapeDtypeStruct((nodes // BLOCK, SPAN, BLOCK), BF16),
        in_specs=[vmem],
        out_specs=vmem,
        compiler_params=pltpu.CompilerParams(vmem_limit_bytes=6 * MIB),
        cost_estimate=LIGHT,
        name="coupling",
    )(node_class.reshape(1, nodes))


def couple_kernel(first, rate_ref, weight_ref, pivot_ref, out_ref):
    rows, nodes = out_ref.shape

    def block_of(block, carry):
        source = pl.ds(window(block, nodes), SPAN)
        target = pl.ds(pl.multiple_of(block * BLOCK, BLOCK), BLOCK)
        value = jnp.dot(
            pivot_ref[first : first + rows, source], weight_ref[block], preferred_element_type=F32
        )
        out_ref[:, target] = (rate_ref[0] * value).astype(BF16)
        return carry

    lax.fori_loop(0, nodes // BLOCK, block_of, 0)


def couple(pivot, weights, rate, part=0, parts=1):
    rows, nodes = pivot.shape[0] // parts, pivot.shape[1]
    vmem = pl.BlockSpec(memory_space=pltpu.VMEM)
    return pl.pallas_call(
        functools.partial(couple_kernel, part * rows),
        out_shape=jax.ShapeDtypeStruct((rows, nodes), BF16),
        in_specs=[pl.BlockSpec(memory_space=pltpu.SMEM), vmem, vmem],
        out_specs=vmem,
        compiler_params=pltpu.CompilerParams(vmem_limit_bytes=8 * MIB),
        cost_estimate=LIGHT,
        name="couple",
    )(rate, weights, pivot)


def turned(block, odd):
    return block + odd * (3 - 2 * block)


def route(source, target, doms):
    pairs = []
    for dom in range(doms):
        odd = dom % 2
        pairs.append((dom * 4 + turned(source, odd), dom * 4 + turned(target, odd)))
    return pairs


def moved(value, source, target):
    return lax.ppermute(value, ("dom", "col"), route(source, target, lax.axis_size("dom")))


def couple_here(place, pivot, weights, rate):
    def kernel(place_ref, *refs):
        @pl.when(place_ref[1] == 1)
        def _():
            couple_kernel(0, *refs)

    scalars, vmem = pl.BlockSpec(memory_space=pltpu.SMEM), pl.BlockSpec(memory_space=pltpu.VMEM)
    return pl.pallas_call(
        kernel,
        out_shape=jax.ShapeDtypeStruct(pivot.shape, BF16),
        in_specs=[scalars, scalars, vmem, vmem],
        out_specs=vmem,
        compiler_params=pltpu.CompilerParams(vmem_limit_bytes=8 * MIB),
        cost_estimate=LIGHT,
        name="couple_here",
    )(place, rate, weights, pivot)


def turn_kernel(place_ref, coupled_ref, *refs):
    @pl.when(place_ref[1] == 1)
    def _():
        refs[-1][...] = coupled_ref[...].T


def turn(place, panel, part, coupled, across):
    rows, nodes = coupled.shape
    chunk = 128
    steps = rows // chunk
    ratio = nodes // 4 // chunk
    return pl.pallas_call(
        turn_kernel,
        out_shape=jax.ShapeDtypeStruct((nodes, nodes), BF16),
        grid_spec=pltpu.PrefetchScalarGridSpec(
            num_scalar_prefetch=1,
            grid=(steps,),
            in_specs=[pl.BlockSpec((chunk, nodes), lambda i, place: (i, 0))]
            + ([] if across is None else [pl.BlockSpec(memory_space=pl.ANY)]),
            out_specs=pl.BlockSpec(
                (nodes, chunk),
                lambda i, place: (0, turned(panel, place[0]) * ratio + part * steps + i),
            ),
        ),
        input_output_aliases={} if across is None else {2: 0},
        compiler_params=pltpu.CompilerParams(vmem_limit_bytes=4 * MIB),
        cost_estimate=LIGHT,
        name="turn",
    )(place, coupled, *(() if across is None else (across,)))


def multiply_kernel(first, count, lefts, place_ref, *refs):
    left_refs, right_ref, out_ref = refs[:lefts], refs[lefts], refs[-1]
    width = right_ref.shape[0] // 4

    @pl.when(place_ref[1] == 1)
    def _():
        def block(step, carry):
            source = pl.multiple_of((first(place_ref[0]) + step) * width, 128)
            target = pl.multiple_of(step * width, 128)
            row = 0
            for left_ref in left_refs:
                rows = left_ref.shape[0]
                out_ref[row : row + rows, pl.ds(target, width)] = jnp.dot(
                    left_ref[...], right_ref[:, pl.ds(source, width)], preferred_element_type=F32
                ).astype(BF16)
                row += rows
            return carry

        lax.fori_loop(0, count, block, 0)


def multiply(place, lefts, right, first=lambda odd: 0, count=4):
    rows = sum(left.shape[0] for left in lefts)
    width = right.shape[0] // 4
    vmem = pl.BlockSpec(memory_space=pltpu.VMEM)
    return pl.pallas_call(
        functools.partial(multiply_kernel, first, count, len(lefts)),
        out_shape=jax.ShapeDtypeStruct((rows, count * width), BF16),
        in_specs=[pl.BlockSpec(memory_space=pltpu.SMEM)] + [vmem] * (len(lefts) + 1),
        out_specs=vmem,
        compiler_params=pltpu.CompilerParams(vmem_limit_bytes=6 * MIB),
        cost_estimate=LIGHT,
        name="multiply",
    )(place, *lefts, right)


def pack(value, out_ref, column):
    half = value.shape[0] // 2
    for part in range(2):
        rows = pl.ds(part * half, half)
        pack_rows(part, value[part * half : (part + 1) * half], out_ref.at[rows], column)


def two_kernel(place_ref, left_ref, right_ref, zero_ref, out_ref):
    odd = place_ref[0]
    width = right_ref.shape[0] // 4

    def product(block):
        columns = pl.ds(pl.multiple_of(block * width, 128), width)
        value = jnp.dot(left_ref[...], right_ref[:, columns], preferred_element_type=F32)
        return value.astype(BF16)

    @pl.when(place_ref[1] == 1)
    def _():
        out_ref[:, :width] = product(1 + odd)
        zero = pl.ds(pl.multiple_of((2 - 2 * odd) * width, 128), width)
        out_ref[:, width : 2 * width] = zero_ref[:, zero]
        pack(product(2 - odd), out_ref, 2 * width)


def product_two(place, half, across, zero):
    rows = half.shape[0]
    width = across.shape[0] // 4
    vmem = pl.BlockSpec(memory_space=pltpu.VMEM)
    return pl.pallas_call(
        two_kernel,
        out_shape=jax.ShapeDtypeStruct((rows, 11 * width // 4), BF16),
        in_specs=[pl.BlockSpec(memory_space=pltpu.SMEM)] + [vmem] * 3,
        out_specs=vmem,
        compiler_params=pltpu.CompilerParams(vmem_limit_bytes=6 * MIB),
        cost_estimate=LIGHT,
        name="product_two",
    )(place, half, across, zero)


def half_kernel(place_ref, left_ref, right_ref, one_ref, out_ref):
    width = one_ref.shape[1]

    @pl.when(place_ref[1] == 1)
    def _():
        def block(step, carry):
            which = turned(step + (step > 0).astype(jnp.int32), place_ref[0])
            columns = pl.ds(pl.multiple_of(which * width, 128), width)
            out_ref[:, columns] = jnp.dot(
                left_ref[...], right_ref[:, columns], preferred_element_type=F32
            ).astype(BF16)
            return carry

        lax.fori_loop(0, 3, block, 0)
        columns = pl.ds(pl.multiple_of(turned(1, place_ref[0]) * width, 128), width)
        out_ref[:, columns] = one_ref[...]


def half_product(place, left, right, one):
    vmem = pl.BlockSpec(memory_space=pltpu.VMEM)
    return pl.pallas_call(
        half_kernel,
        out_shape=jax.ShapeDtypeStruct(left.shape, BF16),
        in_specs=[pl.BlockSpec(memory_space=pltpu.SMEM)] + [vmem] * 3,
        out_specs=vmem,
        compiler_params=pltpu.CompilerParams(vmem_limit_bytes=6 * MIB),
        cost_estimate=LIGHT,
        name="half_product",
    )(place, left, right, one)


def column_kernel(place_ref, own_ref, first_ref, second_ref, *refs):
    column_ref, out_refs = refs[0], refs[1:]

    @pl.when(place_ref[1] == 1)
    def _():
        width = own_ref.shape[0]
        for block in range(4):
            rows = pl.ds(block * width, width)
            column_ref[rows, :] = own_ref[:, rows].T
        for left_ref, out_ref in zip((first_ref, second_ref), out_refs):
            out_ref[...] = jnp.dot(
                left_ref[...], column_ref[...], preferred_element_type=F32
            ).astype(BF16)


def own_column(place, own, first, second):
    rows, nodes = own.shape
    vmem = pl.BlockSpec(memory_space=pltpu.VMEM)
    return pl.pallas_call(
        column_kernel,
        out_shape=(
            jax.ShapeDtypeStruct((nodes, rows), BF16),
            jax.ShapeDtypeStruct((rows, rows), BF16),
            jax.ShapeDtypeStruct((rows, rows), BF16),
        ),
        in_specs=[pl.BlockSpec(memory_space=pltpu.SMEM)] + [vmem] * 3,
        out_specs=(vmem, vmem, vmem),
        compiler_params=pltpu.CompilerParams(vmem_limit_bytes=6 * MIB),
        cost_estimate=LIGHT,
        name="own_column",
    )(place, own, first, second)


def rest_kernel(place_ref, upper_ref, lower_ref, right_ref, zero_ref, out_ref):
    odd = place_ref[0]
    width = zero_ref.shape[1]
    half = width // 2

    def product(left_ref, block):
        columns = pl.ds(pl.multiple_of(block * width, 128), width)
        value = jnp.dot(left_ref[...], right_ref[:, columns], preferred_element_type=F32)
        return value.astype(BF16)

    @pl.when(place_ref[1] == 1)
    def _():
        out_ref[:, pl.ds(pl.multiple_of(odd * width, 128), width)] = zero_ref[...].T
        other = pl.ds(pl.multiple_of((1 - odd) * width, 128), width)
        for part, left_ref in enumerate((upper_ref, lower_ref)):
            rows = pl.ds(part * half, half)
            out_ref[rows, other] = product(left_ref, 1 + odd)
            pack_rows(part, product(left_ref, 3 - 3 * odd), out_ref.at[rows], 2 * width)


def product_rest(place, halves, across, zero):
    rows, width = zero.shape
    vmem = pl.BlockSpec(memory_space=pltpu.VMEM)
    return pl.pallas_call(
        rest_kernel,
        out_shape=jax.ShapeDtypeStruct((rows, 11 * width // 4), BF16),
        in_specs=[pl.BlockSpec(memory_space=pltpu.SMEM)] + [vmem] * 4,
        out_specs=vmem,
        compiler_params=pltpu.CompilerParams(vmem_limit_bytes=6 * MIB),
        cost_estimate=LIGHT,
        name="product_rest",
    )(place, *halves, across, zero)


def pack_rows(part, value, out_ref, column):
    half, width = value.shape
    quarter = half // 2
    if part == 0:
        out_ref[:, column : column + half] = value[:, :half]
        out_ref[:, column + half : column + half + quarter] = value[:, half : half + quarter]
    else:
        out_ref[:, column : column + half] = value[:, half:]
        beside = slice(column + half, column + half + quarter)
        out_ref[:quarter, beside] = value[quarter:, :quarter]
        out_ref[quarter:, beside] = value[quarter:, quarter:half]


def unpacked_rows(part, packed_ref, column):
    quarter = packed_ref.shape[0] // 4
    half = 2 * quarter
    beside = slice(column + half, column + half + quarter)
    rows = slice(part * quarter, (part + 1) * quarter)
    diagonal = packed_ref[rows, column : column + half]
    lower = [packed_ref[start : start + quarter, beside] for start in (half, half + quarter)]
    if part < 2:
        return diagonal, jnp.concatenate([packed_ref[rows, beside], lower[part].T], axis=1)
    if part == 2:
        return packed_ref[:half, beside].T, diagonal
    return jnp.concatenate(lower, axis=1), diagonal


def prior_kernel(place_ref, shifted_ref, sigma_ref, out_ref):
    @pl.when(place_ref[3] == 0)
    def _():
        out_ref[...] = shifted_ref[...]

    @pl.when(place_ref[3] != 0)
    def _():
        out_ref[...] = sigma_ref[...]


def parts_kernel(place_ref, shifted_ref, sigma_ref, row_ref, far_ref, near_ref, last_ref):
    odd = place_ref[0]
    width = row_ref.shape[1] // 4

    def at(block, count=1):
        return pl.ds(pl.multiple_of(block * width, 128), count * width)

    prior_kernel(place_ref, shifted_ref, sigma_ref, row_ref)
    far_ref[:, : 2 * width] = row_ref[:, at(2 - 2 * odd, 2)]
    near_ref[:, :width] = row_ref[:, at(3 - 3 * odd)]
    for part in range(2):

        @pl.when(pl.program_id(0) == part)
        def _():
            pack_rows(part, row_ref[:, at(3 * odd)], far_ref, 2 * width)
            pack_rows(part, row_ref[:, at(2 - odd)], near_ref, width)
            pack_rows(part, row_ref[:, at(3 - 3 * odd)], last_ref, 0)


def prior_parts(place, shifted, sigma):
    rows, nodes = sigma.shape
    chunk = rows // 2
    width = nodes // 4
    out = lambda quarters: jax.ShapeDtypeStruct((rows, quarters * width // 4), BF16)
    spec = lambda quarters: pl.BlockSpec((chunk, quarters * width // 4), lambda i, place: (i, 0))
    return pl.pallas_call(
        parts_kernel,
        out_shape=(out(16), out(11), out(7), out(3)),
        grid_spec=pltpu.PrefetchScalarGridSpec(
            num_scalar_prefetch=1,
            grid=(rows // chunk,),
            in_specs=[
                pl.BlockSpec(
                    (chunk, nodes), lambda i, place: (jnp.where(place[3] == 0, i, 0), 0)
                ),
                pl.BlockSpec(
                    (chunk, nodes), lambda i, place: (jnp.where(place[3] == 0, 0, i), 0)
                ),
            ],
            out_specs=(spec(16), spec(11), spec(7), spec(3)),
        ),
        compiler_params=pltpu.CompilerParams(vmem_limit_bytes=14 * MIB),
        cost_estimate=LIGHT,
        name="prior_parts",
    )(place, shifted, sigma)


def assemble_kernel(place_ref, own, column, near_two, last_three, far_zero, out_ref):
    @pl.when(place_ref[1] == 1)
    def _():
        odd = place_ref[0]
        width = own.shape[0]
        half, quarter = width // 2, width // 4

        def at(block, count=1):
            return pl.ds(pl.multiple_of(block * width, 128), count * width)

        near = 2 * (1 - odd)
        row = [turned(block, odd) for block in range(4)]
        out_ref[at(row[1]), :] = own[...]
        out_ref[at(row[2]), at(row[3])] = near_two[:, :width]
        out_ref[at(row[3]), at(row[2])] = near_two[:, :width].T
        out_ref[at(row[0]), at(near, 2)] = far_zero[:, : 2 * width]
        for step in range(2):
            out_ref[at(near + step), at(row[0])] = far_zero[:, step * width : (1 + step) * width].T
        for block in (0, 2, 3):
            out_ref[at(row[block]), at(row[1])] = column[at(row[block]), :]
        packed = ((0, far_zero, 2 * width), (2, near_two, width), (3, last_three, 0))
        for block, packed_ref, start in packed:
            for part in range(4):
                rows = pl.ds(pl.multiple_of(row[block] * width + part * quarter, 128), quarter)
                for side, value in enumerate(unpacked_rows(part, packed_ref, start)):
                    columns = pl.ds(pl.multiple_of(row[block] * width + side * half, 128), half)
                    out_ref[rows, columns] = value


def assemble(place, *parts):
    nodes = parts[0].shape[1]
    vmem = pl.BlockSpec(memory_space=pltpu.VMEM)
    return pl.pallas_call(
        assemble_kernel,
        out_shape=jax.ShapeDtypeStruct((nodes, nodes), BF16),
        in_specs=[pl.BlockSpec(memory_space=pltpu.SMEM)] + [vmem] * 5,
        out_specs=vmem,
        compiler_params=pltpu.CompilerParams(vmem_limit_bytes=6 * MIB),
        cost_estimate=LIGHT,
        name="assemble",
    )(place, *parts)


def tick(place, *values, cost=HEAVY):
    def kernel(place_ref, *refs):
        for which in range(place.shape[0]):
            refs[-1][which] = place_ref[which]

    scalars = pl.BlockSpec(memory_space=pltpu.SMEM)
    return pl.pallas_call(
        kernel,
        out_shape=jax.ShapeDtypeStruct(place.shape, place.dtype),
        in_specs=[scalars] + [pl.BlockSpec(memory_space=pl.ANY)] * len(values),
        out_specs=scalars,
        compiler_params=pltpu.CompilerParams(vmem_limit_bytes=MIB),
        cost_estimate=cost,
        name="tick",
    )(place, *values)


def finish_kernel(
    place_ref, pivot_ref, sigma_ref,
    q0, q0_last, q2, q3_two,
    q01, q11, q21, q31,
    out_ref, var_ref,
):
    rows, nodes = pivot_ref.shape
    width = nodes // 4
    odd, place = place_ref[0], place_ref[1]
    here = pl.multiple_of(pl.program_id(0) * rows, 128)
    diagonal = diagonal_of(rows)

    def at(block, count=1):
        return pl.ds(pl.multiple_of(block * width, 128), count * width)

    def own(block):
        return pl.ds(pl.multiple_of(block * width + here, 128), rows)

    def add(columns, product):
        out_ref[:, columns] = (pivot_ref[:, columns].astype(F32) + product.astype(F32)).astype(BF16)

    def trace(product):
        var_ref[...] = diagonal(
            pivot_ref[:, own(place_ref[2])].astype(F32) + product.astype(F32)
        )

    active = place_ref[4] != 0

    @pl.when(active & (place == 0))
    def _():
        add(at(odd, 3), q0[...])
        add(at(turned(3, odd)), q0_last[...])
        trace(q0[:, own(2 * odd)])

    @pl.when(active & (place == 1))
    def _():
        add(at(turned(0, odd)), q01[...].T)
        add(at(turned(1, odd)), q11[...])
        add(at(turned(2, odd)), q21[...].T)
        add(at(turned(3, odd)), q31[...].T)
        trace(q11[:, pl.ds(here, rows)])

    @pl.when(active & (place == 2))
    def _():
        add(at(turned(0, odd)), q2[pl.ds(0, width), pl.ds(pl.multiple_of(width + here, 128), rows)].T)
        add(at(turned(1, odd)), q2[pl.ds(here, rows), pl.ds(0, width)])
        start = pl.program_id(0) % 2 * rows + 2 * width
        trace(q2[pl.ds(here, rows), pl.ds(pl.multiple_of(start, 128), rows)])
        for part in range(4):

            @pl.when(pl.program_id(0) == part)
            def _():
                for side, value in enumerate(unpacked_rows(part, q2, 2 * width)):
                    start = turned(2, odd) * width + side * width // 2
                    add(pl.ds(pl.multiple_of(start, 128), width // 2), value)

    @pl.when(active & (place == 3))
    def _():
        add(at(turned(2, odd)), q3_two[...])

    @pl.when(place_ref[4] == 0)
    def _():
        out_ref[...] = sigma_ref[...]
        var_ref[...] = diagonal(sigma_ref[:, own(place_ref[2])].astype(F32))


def finish(place, pivot, sigma, received, kept):
    rows, nodes = pivot.shape
    chunk = 128
    width = nodes // 4

    def picked(which, blocks):
        return pl.BlockSpec(
            (chunk, blocks * width), lambda i, place: (jnp.where(place[1] == which, i, 0), 0)
        )

    def turned_block(start):
        return pl.BlockSpec(
            (rows, chunk),
            lambda i, place: (
                0,
                jnp.where(place[1] == 1, start(place[0]) * (width // chunk) + i, 0),
            ),
        )

    return pl.pallas_call(
        finish_kernel,
        out_shape=(
            jax.ShapeDtypeStruct((rows, nodes), BF16),
            jax.ShapeDtypeStruct((1, rows), F32),
        ),
        grid_spec=pltpu.PrefetchScalarGridSpec(
            num_scalar_prefetch=1,
            grid=(rows // chunk,),
            in_specs=[
                pl.BlockSpec((chunk, nodes), lambda i, place: (i, 0)),
                pl.BlockSpec(
                    (chunk, nodes), lambda i, place: (jnp.where(place[4] == 0, i, 0), 0)
                ),
                picked(0, 3),
                picked(0, 1),
                pl.BlockSpec((rows, 11 * width // 4), lambda i, place: (0, 0)),
                picked(3, 1),
                turned_block(lambda odd: 1),
                picked(1, 1),
                turned_block(lambda odd: 0),
                turned_block(lambda odd: 1 - odd),
            ],
            out_specs=(
                pl.BlockSpec((chunk, nodes), lambda i, place: (i, 0)),
                pl.BlockSpec((1, chunk), lambda i, place: (0, i)),
            ),
        ),
        compiler_params=pltpu.CompilerParams(vmem_limit_bytes=12 * MIB),
        cost_estimate=HEAVY,
        name="finish",
    )(place, pivot, sigma, *received, *kept)


def last_kernel(place_ref, pivot_ref, q2_last, q3, old_ref, old_var_ref, out_ref, var_ref, sum_ref, sems):
    rows, nodes = pivot_ref.shape
    width = nodes // 4
    chunk = 128
    odd, place = place_ref[0], place_ref[1]
    active = place_ref[4] != 0

    def at(block, count=1):
        return pl.ds(pl.multiple_of(block * width, 128), count * width)

    def copies(part, pieces):
        here = pl.ds(part * chunk, chunk)
        return [
            pltpu.make_async_copy(
                sum_ref.at[here, source], out_ref.at[here, target], sems.at[which, part]
            )
            for which, (source, target, _) in enumerate(pieces)
        ]

    def write(pieces):
        for part in range(4):
            here = pl.ds(part * chunk, chunk)
            for source, target, product in pieces:
                value = pivot_ref[here, target].astype(F32) + product(part, here).astype(F32)
                sum_ref[here, source] = value.astype(BF16)
            for copy in copies(part, pieces):
                copy.start()
        for part in range(4):
            for copy in copies(part, pieces):
                copy.wait()

    var_ref[...] = old_var_ref[...]

    @pl.when(active & (place == 2))
    def _():
        write([(pl.ds(0, width), at(3 - 3 * odd), lambda part, here: q2_last[:, here].T)])

    @pl.when(active & (place == 3))
    def _():
        both, last = pl.ds(0, 2 * width), pl.ds(2 * width, width)
        for start in range(0, rows, chunk):
            here = pl.ds(start, chunk)
            own = pl.ds(pl.multiple_of(place_ref[2] * width + start, 128), chunk)
            value = pivot_ref[here, own].astype(F32)
            value = value + q3[here, pl.ds(2 * width + start % (2 * chunk), chunk)].astype(F32)
            var_ref[:, here] = diagonal_of(chunk)(value)
        write(
            [
                (both, at(2 * odd, 2), lambda part, here: q3[here, both]),
                (
                    last,
                    at(3 - 3 * odd),
                    lambda part, here: jnp.concatenate(unpacked_rows(part, q3, 2 * width), axis=1),
                ),
            ]
        )


def diagonal_of(rows):
    square = (rows, rows)
    on_diagonal = lax.broadcasted_iota(jnp.int32, square, 0) == lax.broadcasted_iota(
        jnp.int32, square, 1
    )
    return lambda value: jnp.sum(jnp.where(on_diagonal, value, 0.0), axis=0, keepdims=True)


def finish_last(place, pivot, q2_last, q3, covariance, variances):
    rows, nodes = pivot.shape
    width = nodes // 4
    vmem = pl.BlockSpec(memory_space=pltpu.VMEM)
    anywhere = pl.BlockSpec(memory_space=pl.ANY)
    return pl.pallas_call(
        last_kernel,
        out_shape=(
            jax.ShapeDtypeStruct((rows, nodes), BF16),
            jax.ShapeDtypeStruct((1, rows), F32),
        ),
        in_specs=[pl.BlockSpec(memory_space=pltpu.SMEM)] + [vmem] * 3 + [anywhere, vmem],
        out_specs=(anywhere, vmem),
        scratch_shapes=[
            pltpu.VMEM((rows, 3 * width), BF16),
            pltpu.SemaphoreType.DMA((2, rows // 128)),
        ],
        input_output_aliases={4: 0},
        compiler_params=pltpu.CompilerParams(vmem_limit_bytes=8 * MIB),
        cost_estimate=LIGHT,
        name="finish_last",
    )(place, pivot, q2_last, q3, covariance, variances)


def owned(sigma_next, separator, inverse_pivot, coupling_rate, lengths, step_index, node_class):
    sigma, pivot = sigma_next[0], inverse_pivot[0]
    odd = lax.axis_index("dom") % 2
    col = lax.axis_index("col")
    step = step_index[0]
    place = jnp.stack([odd, turned(col, odd), col, step, step < lengths[0]]).astype(jnp.int32)
    after = lambda value, *others: lax.optimization_barrier((value, *others))[0]

    shifted = passed_along(separator, "dom", -1)[0]
    p2 = moved(pivot, 2, 1)
    p0 = moved(pivot, 0, 1)
    weights = coupling(node_class)
    c1 = [couple(pivot, weights, coupling_rate, part, 2) for part in range(2)]
    across = turn(place, 1, 0, c1[0], None)
    across = turn(place, 1, 1, c1[1], across)

    row, far, near, last = prior_parts(place, after(shifted, across), sigma)
    far_zero, near_two, last_three = moved(far, 0, 1), moved(near, 2, 1), moved(last, 3, 1)

    c2 = couple_here(place, after(p2, last), weights, coupling_rate)
    across = turn(place, 2, 0, c2, across)
    c0 = couple_here(place, after(p0, across), weights, coupling_rate)
    across = turn(place, 0, 0, c0, across)
    column, h0_one, h2_one = own_column(place, after(row, last_three, near_two), c0, c2)
    c3 = [
        moved(after(c1[0], last_three, near_two, across), 3, 1),
        moved(after(c1[1], far_zero, h2_one), 3, 1),
    ]
    prior = assemble(place, row, column, near_two, last_three, far_zero)

    h0 = half_product(place, c0, prior, h0_one)
    q0_own = multiply(place, [h0], across, lambda odd: odd, 3)
    q0 = moved(q0_own, 1, 0)
    h2 = half_product(place, after(c2, q0_own), prior, h2_one)
    q2_own = product_two(place, h2, across, q0_own)
    q2 = moved(q2_own, 1, 2)

    across = turn(place, 3, 0, c3[0], after(across, q2_own))
    upper = multiply(place, [c3[0]], prior)
    across = turn(place, 3, 1, c3[1], after(across, upper))
    q03 = multiply(place, [h0], across, lambda odd: 3 - 3 * odd, 1)
    q0_last = moved(q03, 1, 0)
    h3 = [upper, multiply(place, [after(c3[1], q03)], prior)]
    q32 = multiply(place, h3, across, lambda odd: 2 - odd, 1)
    q3_two = moved(q32, 1, 3)
    q3_own = product_rest(place, h3, across, after(q03, q32))
    q3 = moved(q3_own, 1, 3)
    h1 = multiply(place, [after(c1[0], q3_own), c1[1]], prior)
    q11 = multiply(place, [h1], across, lambda odd: 1 + odd, 1)
    received = (q0, q0_last, q2, q3_two)
    kept = (q0_own, q11, q2_own, q3_own)
    place_then = tick(tick(place, q0, cost=LIGHT), q0_last, cost=MEDIUM)
    q2_last = moved(after(q3_two, place_then), 3, 2)
    covariance, variances = finish(place_then, pivot, sigma, received, kept)
    covariance, variances = finish_last(place, pivot, q2_last, q3, covariance, variances)
    return (covariance[None], variances)


def gathered(sigma_next, separator, inverse_pivot, coupling_rate, lengths, step_index, node_class):
    shifted = passed_along(separator, "dom", -1)
    prior = jnp.where(step_index[0] == 0, shifted[0], sigma_next[0])
    pivot = inverse_pivot[0].astype(F32)
    coupled = couple(inverse_pivot[0], coupling(node_class), coupling_rate)
    rows = coupled.shape[0]
    half = jnp.dot(
        coupled,
        lax.all_gather(prior, "col", axis=0, tiled=True),
        preferred_element_type=F32,
    ).astype(BF16)
    product = lax.dot_general(
        half,
        lax.all_gather(coupled, "col", axis=0, tiled=True),
        (((1,), (1,)), ((), ())),
        preferred_element_type=F32,
    )
    full = pivot + product
    active = step_index[0] < lengths[0]
    old = sigma_next[0]
    covariance = jnp.where(active, full.astype(BF16), old)
    first_col = lax.axis_index("col") * rows
    new_block = lax.dynamic_slice_in_dim(full, first_col, rows, 1)
    old_block = lax.dynamic_slice_in_dim(old, first_col, rows, 1)
    variances = jnp.where(active, jnp.diagonal(new_block), jnp.diagonal(old_block).astype(F32))
    return (covariance[None], variances[None])


def solution(mesh):
    local = owned if mesh.shape["col"] == 4 and mesh.shape["dom"] % 2 == 0 else gathered
    return jax.shard_map(
        local,
        mesh=mesh,
        in_specs=(
            P(("groups", "dom"), "col", None),
            P(("groups", "dom"), "col", None),
            P(("groups", "dom"), "col", None),
            P(("groups", "dom")),
            P(("groups", "dom")),
            P(("groups", "dom")),
            P("groups"),
        ),
        out_specs=(P(("groups", "dom"), "col", None), P(("groups", "dom"), "col")),
        check_vma=False,
    )
```

```python
import functools

import jax
import jax.numpy as jnp
from jax import lax
from jax.experimental import pallas as pl
from jax.experimental.pallas import tpu as pltpu
from jax.sharding import PartitionSpec as P

GX = 64
GY = 32
BF16 = jnp.bfloat16
F32 = jnp.float32
MIB = 1 << 20


def passed_along(value, axis, steps):
    count = lax.axis_size(axis)
    initial, last = (max(0, -steps), min(count, count - steps))
    return lax.ppermute(value, axis, [(source, source + steps) for source in range(initial, last)])


LIGHT = pl.CostEstimate(flops=1 << 20, bytes_accessed=1 << 16, transcendentals=0)
MEDIUM = pl.CostEstimate(flops=2000000000, bytes_accessed=1 << 16, transcendentals=0)
HEAVY = pl.CostEstimate(flops=14000000000, bytes_accessed=1 << 16, transcendentals=0)


BLOCK = 256
SPAN = 512


def window(block, nodes):
    return pl.multiple_of(jnp.clip(block * BLOCK - (SPAN - BLOCK) // 2, 0, nodes - SPAN), 128)


def weight_kernel(class_ref, out_ref):
    nodes = class_ref.shape[1]

    def fill(block, carry):
        first = pl.multiple_of(block * BLOCK, BLOCK)
        kind = class_ref[:, pl.ds(first, BLOCK)]
        across = jnp.where(
            kind == 0, 0.25, jnp.where(kind == 1, 0.375, jnp.where(kind == 2, 0.125, 0.5))
        ).astype(F32)
        along = jnp.where(
            kind == 0, 0.25, jnp.where(kind == 1, 0.125, jnp.where(kind == 2, 0.375, 0.0))
        ).astype(F32)
        column = (first + lax.broadcasted_iota(jnp.int32, (1, BLOCK), 1)) % GX
        left = jnp.where(column > 0, across, 0.0)
        right = jnp.where(column < GX - 1, across, 0.0)
        shape = (SPAN, BLOCK)
        offset = (
            lax.broadcasted_iota(jnp.int32, shape, 0)
            - lax.broadcasted_iota(jnp.int32, shape, 1)
            + (window(block, nodes) - first)
        )
        value = jnp.where(jnp.abs(offset) == GX, along, 0.0)
        value = jnp.where(offset == -1, left, value)
        value = jnp.where(offset == 1, right, value)
        value = jnp.where(offset == 0, 1.0, value)
        out_ref[block] = value.astype(BF16)
        return carry

    lax.fori_loop(0, nodes // BLOCK, fill, 0)


def coupling(node_class):
    nodes = node_class.shape[0]
    vmem = pl.BlockSpec(memory_space=pltpu.VMEM)
    return pl.pallas_call(
        weight_kernel,
        out_shape=jax.ShapeDtypeStruct((nodes // BLOCK, SPAN, BLOCK), BF16),
        in_specs=[vmem],
        out_specs=vmem,
        compiler_params=pltpu.CompilerParams(vmem_limit_bytes=6 * MIB),
        cost_estimate=LIGHT,
        name="coupling",
    )(node_class.reshape(1, nodes))


def couple_kernel(first, rate_ref, weight_ref, pivot_ref, out_ref):
    rows, nodes = out_ref.shape

    def block_of(block, carry):
        source = pl.ds(window(block, nodes), SPAN)
        target = pl.ds(pl.multiple_of(block * BLOCK, BLOCK), BLOCK)
        value = jnp.dot(
            pivot_ref[first : first + rows, source], weight_ref[block], preferred_element_type=F32
        )
        out_ref[:, target] = (rate_ref[0] * value).astype(BF16)
        return carry

    lax.fori_loop(0, nodes // BLOCK, block_of, 0)


def couple(pivot, weights, rate, part=0, parts=1):
    rows, nodes = pivot.shape[0] // parts, pivot.shape[1]
    vmem = pl.BlockSpec(memory_space=pltpu.VMEM)
    return pl.pallas_call(
        functools.partial(couple_kernel, part * rows),
        out_shape=jax.ShapeDtypeStruct((rows, nodes), BF16),
        in_specs=[pl.BlockSpec(memory_space=pltpu.SMEM), vmem, vmem],
        out_specs=vmem,
        compiler_params=pltpu.CompilerParams(vmem_limit_bytes=8 * MIB),
        cost_estimate=LIGHT,
        name="couple",
    )(rate, weights, pivot)


def turned(block, odd):
    return block + odd * (3 - 2 * block)


def route(source, target, doms):
    pairs = []
    for dom in range(doms):
        odd = dom % 2
        pairs.append((dom * 4 + turned(source, odd), dom * 4 + turned(target, odd)))
    return pairs


def moved(value, source, target):
    return lax.ppermute(value, ("dom", "col"), route(source, target, lax.axis_size("dom")))


def couple_here(place, pivot, weights, rate):
    def kernel(place_ref, *refs):
        @pl.when(place_ref[1] == 1)
        def _():
            couple_kernel(0, *refs)

    scalars, vmem = pl.BlockSpec(memory_space=pltpu.SMEM), pl.BlockSpec(memory_space=pltpu.VMEM)
    return pl.pallas_call(
        kernel,
        out_shape=jax.ShapeDtypeStruct(pivot.shape, BF16),
        in_specs=[scalars, scalars, vmem, vmem],
        out_specs=vmem,
        compiler_params=pltpu.CompilerParams(vmem_limit_bytes=8 * MIB),
        cost_estimate=LIGHT,
        name="couple_here",
    )(place, rate, weights, pivot)


def turn_kernel(place_ref, coupled_ref, *refs):
    @pl.when(place_ref[1] == 1)
    def _():
        refs[-1][...] = coupled_ref[...].T


def turn(place, panel, part, coupled, across):
    rows, nodes = coupled.shape
    chunk = 128
    steps = rows // chunk
    ratio = nodes // 4 // chunk
    return pl.pallas_call(
        turn_kernel,
        out_shape=jax.ShapeDtypeStruct((nodes, nodes), BF16),
        grid_spec=pltpu.PrefetchScalarGridSpec(
            num_scalar_prefetch=1,
            grid=(steps,),
            in_specs=[pl.BlockSpec((chunk, nodes), lambda i, place: (i, 0))]
            + ([] if across is None else [pl.BlockSpec(memory_space=pl.ANY)]),
            out_specs=pl.BlockSpec(
                (nodes, chunk),
                lambda i, place: (0, turned(panel, place[0]) * ratio + part * steps + i),
            ),
        ),
        input_output_aliases={} if across is None else {2: 0},
        compiler_params=pltpu.CompilerParams(vmem_limit_bytes=4 * MIB),
        cost_estimate=LIGHT,
        name="turn",
    )(place, coupled, *(() if across is None else (across,)))


def multiply_kernel(first, count, lefts, place_ref, *refs):
    left_refs, right_ref, out_ref = refs[:lefts], refs[lefts], refs[-1]
    width = right_ref.shape[0] // 4

    @pl.when(place_ref[1] == 1)
    def _():
        def block(step, carry):
            source = pl.multiple_of((first(place_ref[0]) + step) * width, 128)
            target = pl.multiple_of(step * width, 128)
            row = 0
            for left_ref in left_refs:
                rows = left_ref.shape[0]
                out_ref[row : row + rows, pl.ds(target, width)] = jnp.dot(
                    left_ref[...], right_ref[:, pl.ds(source, width)], preferred_element_type=F32
                ).astype(BF16)
                row += rows
            return carry

        lax.fori_loop(0, count, block, 0)


def multiply(place, lefts, right, first=lambda odd: 0, count=4):
    rows = sum(left.shape[0] for left in lefts)
    width = right.shape[0] // 4
    vmem = pl.BlockSpec(memory_space=pltpu.VMEM)
    return pl.pallas_call(
        functools.partial(multiply_kernel, first, count, len(lefts)),
        out_shape=jax.ShapeDtypeStruct((rows, count * width), BF16),
        in_specs=[pl.BlockSpec(memory_space=pltpu.SMEM)] + [vmem] * (len(lefts) + 1),
        out_specs=vmem,
        compiler_params=pltpu.CompilerParams(vmem_limit_bytes=6 * MIB),
        cost_estimate=LIGHT,
        name="multiply",
    )(place, *lefts, right)


def pack(value, out_ref, column):
    half = value.shape[0] // 2
    for part in range(2):
        rows = pl.ds(part * half, half)
        pack_rows(part, value[part * half : (part + 1) * half], out_ref.at[rows], column)


def two_kernel(place_ref, left_ref, right_ref, zero_ref, out_ref):
    odd = place_ref[0]
    width = right_ref.shape[0] // 4

    def product(block):
        columns = pl.ds(pl.multiple_of(block * width, 128), width)
        value = jnp.dot(left_ref[...], right_ref[:, columns], preferred_element_type=F32)
        return value.astype(BF16)

    @pl.when(place_ref[1] == 1)
    def _():
        out_ref[:, :width] = product(1 + odd)
        zero = pl.ds(pl.multiple_of((2 - 2 * odd) * width, 128), width)
        out_ref[:, width : 2 * width] = zero_ref[:, zero]
        pack(product(2 - odd), out_ref, 2 * width)


def product_two(place, half, across, zero):
    rows = half.shape[0]
    width = across.shape[0] // 4
    vmem = pl.BlockSpec(memory_space=pltpu.VMEM)
    return pl.pallas_call(
        two_kernel,
        out_shape=jax.ShapeDtypeStruct((rows, 11 * width // 4), BF16),
        in_specs=[pl.BlockSpec(memory_space=pltpu.SMEM)] + [vmem] * 3,
        out_specs=vmem,
        compiler_params=pltpu.CompilerParams(vmem_limit_bytes=6 * MIB),
        cost_estimate=LIGHT,
        name="product_two",
    )(place, half, across, zero)


def half_kernel(place_ref, left_ref, right_ref, one_ref, out_ref):
    width = one_ref.shape[1]

    @pl.when(place_ref[1] == 1)
    def _():
        def block(step, carry):
            which = turned(step + (step > 0).astype(jnp.int32), place_ref[0])
            columns = pl.ds(pl.multiple_of(which * width, 128), width)
            out_ref[:, columns] = jnp.dot(
                left_ref[...], right_ref[:, columns], preferred_element_type=F32
            ).astype(BF16)
            return carry

        lax.fori_loop(0, 3, block, 0)
        columns = pl.ds(pl.multiple_of(turned(1, place_ref[0]) * width, 128), width)
        out_ref[:, columns] = one_ref[...]


def half_product(place, left, right, one):
    vmem = pl.BlockSpec(memory_space=pltpu.VMEM)
    return pl.pallas_call(
        half_kernel,
        out_shape=jax.ShapeDtypeStruct(left.shape, BF16),
        in_specs=[pl.BlockSpec(memory_space=pltpu.SMEM)] + [vmem] * 3,
        out_specs=vmem,
        compiler_params=pltpu.CompilerParams(vmem_limit_bytes=6 * MIB),
        cost_estimate=LIGHT,
        name="half_product",
    )(place, left, right, one)


def column_kernel(place_ref, own_ref, first_ref, second_ref, *refs):
    column_ref, out_refs = refs[0], refs[1:]

    @pl.when(place_ref[1] == 1)
    def _():
        width = own_ref.shape[0]
        for block in range(4):
            rows = pl.ds(block * width, width)
            column_ref[rows, :] = own_ref[:, rows].T
        for left_ref, out_ref in zip((first_ref, second_ref), out_refs):
            out_ref[...] = jnp.dot(
                left_ref[...], column_ref[...], preferred_element_type=F32
            ).astype(BF16)


def own_column(place, own, first, second):
    rows, nodes = own.shape
    vmem = pl.BlockSpec(memory_space=pltpu.VMEM)
    return pl.pallas_call(
        column_kernel,
        out_shape=(
            jax.ShapeDtypeStruct((nodes, rows), BF16),
            jax.ShapeDtypeStruct((rows, rows), BF16),
            jax.ShapeDtypeStruct((rows, rows), BF16),
        ),
        in_specs=[pl.BlockSpec(memory_space=pltpu.SMEM)] + [vmem] * 3,
        out_specs=(vmem, vmem, vmem),
        compiler_params=pltpu.CompilerParams(vmem_limit_bytes=6 * MIB),
        cost_estimate=LIGHT,
        name="own_column",
    )(place, own, first, second)


def rest_kernel(place_ref, upper_ref, lower_ref, right_ref, zero_ref, out_ref, last_ref):
    odd = place_ref[0]
    width = zero_ref.shape[1]
    half = width // 2

    def product(left_ref, block):
        columns = pl.ds(pl.multiple_of(block * width, 128), width)
        value = jnp.dot(left_ref[...], right_ref[:, columns], preferred_element_type=F32)
        return value.astype(BF16)

    @pl.when(place_ref[1] == 1)
    def _():
        out_ref[:, pl.ds(pl.multiple_of(odd * width, 128), width)] = zero_ref[...].T
        other = pl.ds(pl.multiple_of((1 - odd) * width, 128), width)
        for part, left_ref in enumerate((upper_ref, lower_ref)):
            rows = pl.ds(part * half, half)
            out_ref[rows, other] = product(left_ref, 1 + odd)
            pack_rows(part, product(left_ref, 3 - 3 * odd), last_ref.at[rows], 0)


def product_rest(place, halves, across, zero):
    rows, width = zero.shape
    vmem = pl.BlockSpec(memory_space=pltpu.VMEM)
    return pl.pallas_call(
        rest_kernel,
        out_shape=(
            jax.ShapeDtypeStruct((rows, 2 * width), BF16),
            jax.ShapeDtypeStruct((rows, 3 * width // 4), BF16),
        ),
        in_specs=[pl.BlockSpec(memory_space=pltpu.SMEM)] + [vmem] * 4,
        out_specs=(vmem, vmem),
        compiler_params=pltpu.CompilerParams(vmem_limit_bytes=6 * MIB),
        cost_estimate=LIGHT,
        name="product_rest",
    )(place, *halves, across, zero)


def pack_rows(part, value, out_ref, column):
    half, width = value.shape
    quarter = half // 2
    if part == 0:
        out_ref[:, column : column + half] = value[:, :half]
        out_ref[:, column + half : column + half + quarter] = value[:, half : half + quarter]
    else:
        out_ref[:, column : column + half] = value[:, half:]
        beside = slice(column + half, column + half + quarter)
        out_ref[:quarter, beside] = value[quarter:, :quarter]
        out_ref[quarter:, beside] = value[quarter:, quarter:half]


def unpacked_rows(part, packed_ref, column):
    quarter = packed_ref.shape[0] // 4
    half = 2 * quarter
    beside = slice(column + half, column + half + quarter)
    rows = slice(part * quarter, (part + 1) * quarter)
    diagonal = packed_ref[rows, column : column + half]
    lower = [packed_ref[start : start + quarter, beside] for start in (half, half + quarter)]
    if part < 2:
        return diagonal, jnp.concatenate([packed_ref[rows, beside], lower[part].T], axis=1)
    if part == 2:
        return packed_ref[:half, beside].T, diagonal
    return jnp.concatenate(lower, axis=1), diagonal


def prior_kernel(place_ref, shifted_ref, sigma_ref, out_ref):
    @pl.when(place_ref[3] == 0)
    def _():
        out_ref[...] = shifted_ref[...]

    @pl.when(place_ref[3] != 0)
    def _():
        out_ref[...] = sigma_ref[...]


def parts_kernel(place_ref, shifted_ref, sigma_ref, row_ref, far_ref, near_ref, last_ref):
    odd = place_ref[0]
    width = row_ref.shape[1] // 4

    def at(block, count=1):
        return pl.ds(pl.multiple_of(block * width, 128), count * width)

    prior_kernel(place_ref, shifted_ref, sigma_ref, row_ref)
    far_ref[:, : 2 * width] = row_ref[:, at(2 - 2 * odd, 2)]
    near_ref[:, :width] = row_ref[:, at(3 - 3 * odd)]
    for part in range(2):

        @pl.when(pl.program_id(0) == part)
        def _():
            pack_rows(part, row_ref[:, at(3 * odd)], far_ref, 2 * width)
            pack_rows(part, row_ref[:, at(2 - odd)], near_ref, width)
            pack_rows(part, row_ref[:, at(3 - 3 * odd)], last_ref, 0)


def prior_parts(place, shifted, sigma):
    rows, nodes = sigma.shape
    chunk = rows // 2
    width = nodes // 4
    out = lambda quarters: jax.ShapeDtypeStruct((rows, quarters * width // 4), BF16)
    spec = lambda quarters: pl.BlockSpec((chunk, quarters * width // 4), lambda i, place: (i, 0))
    return pl.pallas_call(
        parts_kernel,
        out_shape=(out(16), out(11), out(7), out(3)),
        grid_spec=pltpu.PrefetchScalarGridSpec(
            num_scalar_prefetch=1,
            grid=(rows // chunk,),
            in_specs=[
                pl.BlockSpec(
                    (chunk, nodes), lambda i, place: (jnp.where(place[3] == 0, i, 0), 0)
                ),
                pl.BlockSpec(
                    (chunk, nodes), lambda i, place: (jnp.where(place[3] == 0, 0, i), 0)
                ),
            ],
            out_specs=(spec(16), spec(11), spec(7), spec(3)),
        ),
        compiler_params=pltpu.CompilerParams(vmem_limit_bytes=14 * MIB),
        cost_estimate=LIGHT,
        name="prior_parts",
    )(place, shifted, sigma)


def assemble_kernel(place_ref, own, column, near_two, last_three, far_zero, out_ref):
    @pl.when(place_ref[1] == 1)
    def _():
        odd = place_ref[0]
        width = own.shape[0]
        half, quarter = width // 2, width // 4

        def at(block, count=1):
            return pl.ds(pl.multiple_of(block * width, 128), count * width)

        near = 2 * (1 - odd)
        row = [turned(block, odd) for block in range(4)]
        out_ref[at(row[1]), :] = own[...]
        out_ref[at(row[2]), at(row[3])] = near_two[:, :width]
        out_ref[at(row[3]), at(row[2])] = near_two[:, :width].T
        out_ref[at(row[0]), at(near, 2)] = far_zero[:, : 2 * width]
        for step in range(2):
            out_ref[at(near + step), at(row[0])] = far_zero[:, step * width : (1 + step) * width].T
        for block in (0, 2, 3):
            out_ref[at(row[block]), at(row[1])] = column[at(row[block]), :]
        packed = ((0, far_zero, 2 * width), (2, near_two, width), (3, last_three, 0))
        for block, packed_ref, start in packed:
            for part in range(4):
                rows = pl.ds(pl.multiple_of(row[block] * width + part * quarter, 128), quarter)
                for side, value in enumerate(unpacked_rows(part, packed_ref, start)):
                    columns = pl.ds(pl.multiple_of(row[block] * width + side * half, 128), half)
                    out_ref[rows, columns] = value


def assemble(place, *parts):
    nodes = parts[0].shape[1]
    vmem = pl.BlockSpec(memory_space=pltpu.VMEM)
    return pl.pallas_call(
        assemble_kernel,
        out_shape=jax.ShapeDtypeStruct((nodes, nodes), BF16),
        in_specs=[pl.BlockSpec(memory_space=pltpu.SMEM)] + [vmem] * 5,
        out_specs=vmem,
        compiler_params=pltpu.CompilerParams(vmem_limit_bytes=6 * MIB),
        cost_estimate=LIGHT,
        name="assemble",
    )(place, *parts)


def tick(place, *values, cost=HEAVY):
    def kernel(place_ref, *refs):
        for which in range(place.shape[0]):
            refs[-1][which] = place_ref[which]

    scalars = pl.BlockSpec(memory_space=pltpu.SMEM)
    return pl.pallas_call(
        kernel,
        out_shape=jax.ShapeDtypeStruct(place.shape, place.dtype),
        in_specs=[scalars] + [pl.BlockSpec(memory_space=pl.ANY)] * len(values),
        out_specs=scalars,
        compiler_params=pltpu.CompilerParams(vmem_limit_bytes=MIB),
        cost_estimate=cost,
        name="tick",
    )(place, *values)


def finish_kernel(
    place_ref, pivot_ref, sigma_ref,
    q0, q0_last, q2, q3_two,
    q01, q11, q21, q31,
    out_ref, var_ref,
):
    rows, nodes = pivot_ref.shape
    width = nodes // 4
    odd, place = place_ref[0], place_ref[1]
    here = pl.multiple_of(pl.program_id(0) * rows, 128)
    diagonal = diagonal_of(rows)

    def at(block, count=1):
        return pl.ds(pl.multiple_of(block * width, 128), count * width)

    def own(block):
        return pl.ds(pl.multiple_of(block * width + here, 128), rows)

    def add(columns, product):
        out_ref[:, columns] = (pivot_ref[:, columns].astype(F32) + product.astype(F32)).astype(BF16)

    def trace(product):
        var_ref[...] = diagonal(
            pivot_ref[:, own(place_ref[2])].astype(F32) + product.astype(F32)
        )

    active = place_ref[4] != 0

    @pl.when(active & (place == 0))
    def _():
        add(at(odd, 3), q0[...])
        add(at(turned(3, odd)), q0_last[...])
        trace(q0[:, own(2 * odd)])

    @pl.when(active & (place == 1))
    def _():
        add(at(turned(0, odd)), q01[...].T)
        add(at(turned(1, odd)), q11[...])
        add(at(turned(2, odd)), q21[...].T)
        add(at(turned(3, odd)), q31[...].T)
        trace(q11[:, pl.ds(here, rows)])

    @pl.when(active & (place == 2))
    def _():
        add(at(turned(0, odd)), q2[pl.ds(0, width), pl.ds(pl.multiple_of(width + here, 128), rows)].T)
        add(at(turned(1, odd)), q2[pl.ds(here, rows), pl.ds(0, width)])
        start = pl.program_id(0) % 2 * rows + 2 * width
        trace(q2[pl.ds(here, rows), pl.ds(pl.multiple_of(start, 128), rows)])
        for part in range(4):

            @pl.when(pl.program_id(0) == part)
            def _():
                for side, value in enumerate(unpacked_rows(part, q2, 2 * width)):
                    start = turned(2, odd) * width + side * width // 2
                    add(pl.ds(pl.multiple_of(start, 128), width // 2), value)

    @pl.when(active & (place == 3))
    def _():
        add(at(turned(2, odd)), q3_two[...])

    @pl.when(place_ref[4] == 0)
    def _():
        out_ref[...] = sigma_ref[...]
        var_ref[...] = diagonal(sigma_ref[:, own(place_ref[2])].astype(F32))


def finish(place, pivot, sigma, received, kept):
    rows, nodes = pivot.shape
    chunk = 128
    width = nodes // 4

    def picked(which, blocks):
        return pl.BlockSpec(
            (chunk, blocks * width), lambda i, place: (jnp.where(place[1] == which, i, 0), 0)
        )

    def turned_block(start):
        return pl.BlockSpec(
            (rows, chunk),
            lambda i, place: (
                0,
                jnp.where(place[1] == 1, start(place[0]) * (width // chunk) + i, 0),
            ),
        )

    return pl.pallas_call(
        finish_kernel,
        out_shape=(
            jax.ShapeDtypeStruct((rows, nodes), BF16),
            jax.ShapeDtypeStruct((1, rows), F32),
        ),
        grid_spec=pltpu.PrefetchScalarGridSpec(
            num_scalar_prefetch=1,
            grid=(rows // chunk,),
            in_specs=[
                pl.BlockSpec((chunk, nodes), lambda i, place: (i, 0)),
                pl.BlockSpec(
                    (chunk, nodes), lambda i, place: (jnp.where(place[4] == 0, i, 0), 0)
                ),
                picked(0, 3),
                picked(0, 1),
                pl.BlockSpec((rows, 11 * width // 4), lambda i, place: (0, 0)),
                picked(3, 1),
                turned_block(lambda odd: 1),
                picked(1, 1),
                turned_block(lambda odd: 0),
                turned_block(lambda odd: 1 - odd),
            ],
            out_specs=(
                pl.BlockSpec((chunk, nodes), lambda i, place: (i, 0)),
                pl.BlockSpec((1, chunk), lambda i, place: (0, i)),
            ),
        ),
        compiler_params=pltpu.CompilerParams(vmem_limit_bytes=12 * MIB),
        cost_estimate=HEAVY,
        name="finish",
    )(place, pivot, sigma, *received, *kept)


def add_in_place(pivot_ref, out_ref, sum_ref, sems, column, product):
    chunk = pivot_ref.shape[0] // 4
    copies = []
    for part in range(4):
        here = pl.ds(part * chunk, chunk)
        value = pivot_ref[here, column].astype(F32) + product(part, here).astype(F32)
        sum_ref[here, :] = value.astype(BF16)
        copies.append(
            pltpu.make_async_copy(sum_ref.at[here], out_ref.at[here, column], sems.at[part])
        )
        copies[-1].start()
    for copy in copies:
        copy.wait()


def other_kernel(place_ref, pivot_ref, q3_other, old_ref, out_ref, sum_ref, sems):
    width = pivot_ref.shape[1] // 4
    column = pl.ds(pl.multiple_of(2 * place_ref[0] * width, 128), 2 * width)

    @pl.when((place_ref[4] != 0) & (place_ref[1] == 3))
    def _():
        add_in_place(
            pivot_ref, out_ref, sum_ref, sems, column, lambda part, here: q3_other[here, :]
        )


def last_kernel(
    place_ref, pivot_ref, q2_last, q3_last, old_ref, old_var_ref, out_ref, var_ref, sum_ref, sems
):
    rows, nodes = pivot_ref.shape
    width = nodes // 4
    chunk = rows // 4
    active = place_ref[4] != 0
    column = pl.ds(pl.multiple_of(turned(3, place_ref[0]) * width, 128), width)
    add = functools.partial(add_in_place, pivot_ref, out_ref, sum_ref, sems, column)
    var_ref[...] = old_var_ref[...]

    @pl.when(active & (place_ref[1] == 2))
    def _():
        add(lambda part, here: q2_last[:, here].T)

    @pl.when(active & (place_ref[1] == 3))
    def _():
        add(lambda part, here: jnp.concatenate(unpacked_rows(part, q3_last, 0), axis=1))
        for start in range(0, rows, chunk):
            here = pl.ds(start, chunk)
            own = pl.ds(pl.multiple_of(place_ref[2] * width + start, 128), chunk)
            value = pivot_ref[here, own].astype(F32)
            value = value + q3_last[here, pl.ds(start % (2 * chunk), chunk)].astype(F32)
            var_ref[:, here] = diagonal_of(chunk)(value)


def diagonal_of(rows):
    square = (rows, rows)
    on_diagonal = lax.broadcasted_iota(jnp.int32, square, 0) == lax.broadcasted_iota(
        jnp.int32, square, 1
    )
    return lambda value: jnp.sum(jnp.where(on_diagonal, value, 0.0), axis=0, keepdims=True)


def finish_other(place, pivot, q3_other, covariance):
    rows, nodes = pivot.shape
    vmem = pl.BlockSpec(memory_space=pltpu.VMEM)
    anywhere = pl.BlockSpec(memory_space=pl.ANY)
    return pl.pallas_call(
        other_kernel,
        out_shape=jax.ShapeDtypeStruct((rows, nodes), BF16),
        in_specs=[pl.BlockSpec(memory_space=pltpu.SMEM), vmem, vmem, anywhere],
        out_specs=anywhere,
        scratch_shapes=[pltpu.VMEM((rows, nodes // 2), BF16), pltpu.SemaphoreType.DMA((4,))],
        input_output_aliases={3: 0},
        compiler_params=pltpu.CompilerParams(vmem_limit_bytes=8 * MIB),
        cost_estimate=LIGHT,
        name="finish_other",
    )(place, pivot, q3_other, covariance)


def finish_last(place, pivot, q2_last, q3_last, covariance, variances):
    rows, nodes = pivot.shape
    vmem = pl.BlockSpec(memory_space=pltpu.VMEM)
    anywhere = pl.BlockSpec(memory_space=pl.ANY)
    return pl.pallas_call(
        last_kernel,
        out_shape=(
            jax.ShapeDtypeStruct((rows, nodes), BF16),
            jax.ShapeDtypeStruct((1, rows), F32),
        ),
        in_specs=[pl.BlockSpec(memory_space=pltpu.SMEM)] + [vmem] * 3 + [anywhere, vmem],
        out_specs=(anywhere, vmem),
        scratch_shapes=[pltpu.VMEM((rows, nodes // 4), BF16), pltpu.SemaphoreType.DMA((4,))],
        input_output_aliases={4: 0},
        compiler_params=pltpu.CompilerParams(vmem_limit_bytes=8 * MIB),
        cost_estimate=LIGHT,
        name="finish_last",
    )(place, pivot, q2_last, q3_last, covariance, variances)


def owned(sigma_next, separator, inverse_pivot, coupling_rate, lengths, step_index, node_class):
    sigma, pivot = sigma_next[0], inverse_pivot[0]
    odd = lax.axis_index("dom") % 2
    col = lax.axis_index("col")
    step = step_index[0]
    place = jnp.stack([odd, turned(col, odd), col, step, step < lengths[0]]).astype(jnp.int32)
    after = lambda value, *others: lax.optimization_barrier((value, *others))[0]

    shifted = passed_along(separator, "dom", -1)[0]
    p2 = moved(pivot, 2, 1)
    p0 = moved(pivot, 0, 1)
    weights = coupling(node_class)
    c1 = [couple(pivot, weights, coupling_rate, part, 2) for part in range(2)]
    across = turn(place, 1, 0, c1[0], None)
    across = turn(place, 1, 1, c1[1], across)

    row, far, near, last = prior_parts(place, after(shifted, across), sigma)
    far_zero, near_two, last_three = moved(far, 0, 1), moved(near, 2, 1), moved(last, 3, 1)

    c2 = couple_here(place, after(p2, last), weights, coupling_rate)
    across = turn(place, 2, 0, c2, across)
    c0 = couple_here(place, after(p0, across), weights, coupling_rate)
    across = turn(place, 0, 0, c0, across)
    column, h0_one, h2_one = own_column(place, after(row, last_three), c0, c2)
    c3 = [
        moved(after(c1[0], last_three, near_two, across), 3, 1),
        moved(after(c1[1], far_zero, h2_one), 3, 1),
    ]
    prior = assemble(place, row, column, near_two, last_three, far_zero)

    h0 = half_product(place, c0, prior, h0_one)
    q0_own = multiply(place, [h0], across, lambda odd: odd, 3)
    q0 = moved(q0_own, 1, 0)
    h2 = half_product(place, after(c2, q0_own), prior, h2_one)
    q2_own = product_two(place, h2, across, q0_own)
    q2 = moved(q2_own, 1, 2)

    across = turn(place, 3, 0, c3[0], after(across, q2_own))
    upper = multiply(place, [c3[0]], prior)
    across = turn(place, 3, 1, c3[1], after(across, upper))
    q03 = multiply(place, [h0], across, lambda odd: 3 - 3 * odd, 1)
    q0_last = moved(q03, 1, 0)
    h3 = [upper, multiply(place, [after(c3[1], q03)], prior)]
    q32 = multiply(place, h3, across, lambda odd: 2 - odd, 1)
    q3_two = moved(q32, 1, 3)
    q3_own, q33 = product_rest(place, h3, across, after(q03, q32))
    q3_other, q3_last = moved(q3_own, 1, 3), moved(q33, 1, 3)
    h1 = multiply(place, [after(c1[0], q3_own), c1[1]], prior)
    q11 = multiply(place, [h1], across, lambda odd: 1 + odd, 1)
    received = (q0, q0_last, q2, q3_two)
    kept = (q0_own, q11, q2_own, q3_own)
    place_then = tick(tick(place, q0, cost=LIGHT), q0_last, cost=MEDIUM)
    q2_last = moved(after(q3_two, place_then), 3, 2)
    covariance, variances = finish(place_then, pivot, sigma, received, kept)
    covariance = finish_other(place, pivot, q3_other, covariance)
    covariance, variances = finish_last(place, pivot, q2_last, q3_last, covariance, variances)
    return (covariance[None], variances)


def gathered(sigma_next, separator, inverse_pivot, coupling_rate, lengths, step_index, node_class):
    shifted = passed_along(separator, "dom", -1)
    prior = jnp.where(step_index[0] == 0, shifted[0], sigma_next[0])
    pivot = inverse_pivot[0].astype(F32)
    coupled = couple(inverse_pivot[0], coupling(node_class), coupling_rate)
    rows = coupled.shape[0]
    half = jnp.dot(
        coupled,
        lax.all_gather(prior, "col", axis=0, tiled=True),
        preferred_element_type=F32,
    ).astype(BF16)
    product = lax.dot_general(
        half,
        lax.all_gather(coupled, "col", axis=0, tiled=True),
        (((1,), (1,)), ((), ())),
        preferred_element_type=F32,
    )
    full = pivot + product
    active = step_index[0] < lengths[0]
    old = sigma_next[0]
    covariance = jnp.where(active, full.astype(BF16), old)
    first_col = lax.axis_index("col") * rows
    new_block = lax.dynamic_slice_in_dim(full, first_col, rows, 1)
    old_block = lax.dynamic_slice_in_dim(old, first_col, rows, 1)
    variances = jnp.where(active, jnp.diagonal(new_block), jnp.diagonal(old_block).astype(F32))
    return (covariance[None], variances[None])


def solution(mesh):
    local = owned if mesh.shape["col"] == 4 and mesh.shape["dom"] % 2 == 0 else gathered
    return jax.shard_map(
        local,
        mesh=mesh,
        in_specs=(
            P(("groups", "dom"), "col", None),
            P(("groups", "dom"), "col", None),
            P(("groups", "dom"), "col", None),
            P(("groups", "dom")),
            P(("groups", "dom")),
            P(("groups", "dom")),
            P("groups"),
        ),
        out_specs=(P(("groups", "dom"), "col", None), P(("groups", "dom"), "col")),
        check_vma=False,
    )
```

```python
import functools

import jax
import jax.numpy as jnp
from jax import lax
from jax.experimental import pallas as pl
from jax.experimental.pallas import tpu as pltpu
from jax.sharding import PartitionSpec as P

GX = 64
GY = 32
BF16 = jnp.bfloat16
F32 = jnp.float32
MIB = 1 << 20


def passed_along(value, axis, steps):
    count = lax.axis_size(axis)
    initial, last = (max(0, -steps), min(count, count - steps))
    return lax.ppermute(value, axis, [(source, source + steps) for source in range(initial, last)])


LIGHT = pl.CostEstimate(flops=1 << 20, bytes_accessed=1 << 16, transcendentals=0)
MEDIUM = pl.CostEstimate(flops=2000000000, bytes_accessed=1 << 16, transcendentals=0)
HEAVY = pl.CostEstimate(flops=14000000000, bytes_accessed=1 << 16, transcendentals=0)


BLOCK = 256
SPAN = 512


def window(block, nodes):
    return pl.multiple_of(jnp.clip(block * BLOCK - (SPAN - BLOCK) // 2, 0, nodes - SPAN), 128)


def weight_kernel(class_ref, out_ref):
    nodes = class_ref.shape[1]

    def fill(block, carry):
        first = pl.multiple_of(block * BLOCK, BLOCK)
        kind = class_ref[:, pl.ds(first, BLOCK)]
        across = jnp.where(
            kind == 0, 0.25, jnp.where(kind == 1, 0.375, jnp.where(kind == 2, 0.125, 0.5))
        ).astype(F32)
        along = jnp.where(
            kind == 0, 0.25, jnp.where(kind == 1, 0.125, jnp.where(kind == 2, 0.375, 0.0))
        ).astype(F32)
        column = (first + lax.broadcasted_iota(jnp.int32, (1, BLOCK), 1)) % GX
        left = jnp.where(column > 0, across, 0.0)
        right = jnp.where(column < GX - 1, across, 0.0)
        shape = (SPAN, BLOCK)
        offset = (
            lax.broadcasted_iota(jnp.int32, shape, 0)
            - lax.broadcasted_iota(jnp.int32, shape, 1)
            + (window(block, nodes) - first)
        )
        value = jnp.where(jnp.abs(offset) == GX, along, 0.0)
        value = jnp.where(offset == -1, left, value)
        value = jnp.where(offset == 1, right, value)
        value = jnp.where(offset == 0, 1.0, value)
        out_ref[block] = value.astype(BF16)
        return carry

    lax.fori_loop(0, nodes // BLOCK, fill, 0)


def coupling(node_class):
    nodes = node_class.shape[0]
    vmem = pl.BlockSpec(memory_space=pltpu.VMEM)
    return pl.pallas_call(
        weight_kernel,
        out_shape=jax.ShapeDtypeStruct((nodes // BLOCK, SPAN, BLOCK), BF16),
        in_specs=[vmem],
        out_specs=vmem,
        compiler_params=pltpu.CompilerParams(vmem_limit_bytes=6 * MIB),
        cost_estimate=LIGHT,
        name="coupling",
    )(node_class.reshape(1, nodes))


def couple_kernel(first, rate_ref, weight_ref, pivot_ref, out_ref):
    rows, nodes = out_ref.shape

    def block_of(block, carry):
        source = pl.ds(window(block, nodes), SPAN)
        target = pl.ds(pl.multiple_of(block * BLOCK, BLOCK), BLOCK)
        value = jnp.dot(
            pivot_ref[first : first + rows, source], weight_ref[block], preferred_element_type=F32
        )
        out_ref[:, target] = (rate_ref[0] * value).astype(BF16)
        return carry

    lax.fori_loop(0, nodes // BLOCK, block_of, 0)


def couple(pivot, weights, rate, part=0, parts=1):
    rows, nodes = pivot.shape[0] // parts, pivot.shape[1]
    vmem = pl.BlockSpec(memory_space=pltpu.VMEM)
    return pl.pallas_call(
        functools.partial(couple_kernel, part * rows),
        out_shape=jax.ShapeDtypeStruct((rows, nodes), BF16),
        in_specs=[pl.BlockSpec(memory_space=pltpu.SMEM), vmem, vmem],
        out_specs=vmem,
        compiler_params=pltpu.CompilerParams(vmem_limit_bytes=8 * MIB),
        cost_estimate=LIGHT,
        name="couple",
    )(rate, weights, pivot)


def turned(block, odd):
    return block + odd * (3 - 2 * block)


def route(source, target, doms):
    pairs = []
    for dom in range(doms):
        odd = dom % 2
        pairs.append((dom * 4 + turned(source, odd), dom * 4 + turned(target, odd)))
    return pairs


def moved(value, source, target):
    return lax.ppermute(value, ("dom", "col"), route(source, target, lax.axis_size("dom")))


def couple_here(place, pivot, weights, rate):
    def kernel(place_ref, *refs):
        @pl.when(place_ref[1] == 1)
        def _():
            couple_kernel(0, *refs)

    scalars, vmem = pl.BlockSpec(memory_space=pltpu.SMEM), pl.BlockSpec(memory_space=pltpu.VMEM)
    return pl.pallas_call(
        kernel,
        out_shape=jax.ShapeDtypeStruct(pivot.shape, BF16),
        in_specs=[scalars, scalars, vmem, vmem],
        out_specs=vmem,
        compiler_params=pltpu.CompilerParams(vmem_limit_bytes=8 * MIB),
        cost_estimate=LIGHT,
        name="couple_here",
    )(place, rate, weights, pivot)


def turn_kernel(place_ref, coupled_ref, *refs):
    @pl.when(place_ref[1] == 1)
    def _():
        refs[-1][...] = coupled_ref[...].T


def turn(place, panel, part, coupled, across):
    rows, nodes = coupled.shape
    chunk = 128
    steps = rows // chunk
    ratio = nodes // 4 // chunk
    return pl.pallas_call(
        turn_kernel,
        out_shape=jax.ShapeDtypeStruct((nodes, nodes), BF16),
        grid_spec=pltpu.PrefetchScalarGridSpec(
            num_scalar_prefetch=1,
            grid=(steps,),
            in_specs=[pl.BlockSpec((chunk, nodes), lambda i, place: (i, 0))]
            + ([] if across is None else [pl.BlockSpec(memory_space=pl.ANY)]),
            out_specs=pl.BlockSpec(
                (nodes, chunk),
                lambda i, place: (0, turned(panel, place[0]) * ratio + part * steps + i),
            ),
        ),
        input_output_aliases={} if across is None else {2: 0},
        compiler_params=pltpu.CompilerParams(vmem_limit_bytes=4 * MIB),
        cost_estimate=LIGHT,
        name="turn",
    )(place, coupled, *(() if across is None else (across,)))


def multiply_kernel(first, count, lefts, place_ref, *refs):
    left_refs, right_ref, out_ref = refs[:lefts], refs[lefts], refs[-1]
    width = right_ref.shape[0] // 4

    @pl.when(place_ref[1] == 1)
    def _():
        def block(step, carry):
            source = pl.multiple_of((first(place_ref[0]) + step) * width, 128)
            target = pl.multiple_of(step * width, 128)
            row = 0
            for left_ref in left_refs:
                rows = left_ref.shape[0]
                out_ref[row : row + rows, pl.ds(target, width)] = jnp.dot(
                    left_ref[...], right_ref[:, pl.ds(source, width)], preferred_element_type=F32
                ).astype(BF16)
                row += rows
            return carry

        lax.fori_loop(0, count, block, 0)


def multiply(place, lefts, right, first=lambda odd: 0, count=4):
    rows = sum(left.shape[0] for left in lefts)
    width = right.shape[0] // 4
    vmem = pl.BlockSpec(memory_space=pltpu.VMEM)
    return pl.pallas_call(
        functools.partial(multiply_kernel, first, count, len(lefts)),
        out_shape=jax.ShapeDtypeStruct((rows, count * width), BF16),
        in_specs=[pl.BlockSpec(memory_space=pltpu.SMEM)] + [vmem] * (len(lefts) + 1),
        out_specs=vmem,
        compiler_params=pltpu.CompilerParams(vmem_limit_bytes=6 * MIB),
        cost_estimate=LIGHT,
        name="multiply",
    )(place, *lefts, right)


def pack(value, out_ref, column):
    quarter = value.shape[1] // 4
    for part in range(4):
        rows = pl.ds(part * quarter, quarter)
        pack_rows(part, value[part * quarter : (part + 1) * quarter], out_ref.at[rows], column)


def two_kernel(place_ref, left_ref, right_ref, zero_ref, out_ref):
    odd = place_ref[0]
    width = right_ref.shape[0] // 4

    def product(block):
        columns = pl.ds(pl.multiple_of(block * width, 128), width)
        value = jnp.dot(left_ref[...], right_ref[:, columns], preferred_element_type=F32)
        return value.astype(BF16)

    @pl.when(place_ref[1] == 1)
    def _():
        out_ref[:, :width] = product(1 + odd)
        zero = pl.ds(pl.multiple_of((2 - 2 * odd) * width, 128), width)
        out_ref[:, width : 2 * width] = zero_ref[:, zero]
        pack(product(2 - odd), out_ref, 2 * width)


def product_two(place, half, across, zero):
    rows = half.shape[0]
    width = across.shape[0] // 4
    vmem = pl.BlockSpec(memory_space=pltpu.VMEM)
    return pl.pallas_call(
        two_kernel,
        out_shape=jax.ShapeDtypeStruct((rows, 11 * width // 4), BF16),
        in_specs=[pl.BlockSpec(memory_space=pltpu.SMEM)] + [vmem] * 3,
        out_specs=vmem,
        compiler_params=pltpu.CompilerParams(vmem_limit_bytes=6 * MIB),
        cost_estimate=LIGHT,
        name="product_two",
    )(place, half, across, zero)


def half_kernel(place_ref, left_ref, right_ref, one_ref, out_ref):
    width = one_ref.shape[1]

    @pl.when(place_ref[1] == 1)
    def _():
        def block(step, carry):
            which = turned(step + (step > 0).astype(jnp.int32), place_ref[0])
            columns = pl.ds(pl.multiple_of(which * width, 128), width)
            out_ref[:, columns] = jnp.dot(
                left_ref[...], right_ref[:, columns], preferred_element_type=F32
            ).astype(BF16)
            return carry

        lax.fori_loop(0, 3, block, 0)
        columns = pl.ds(pl.multiple_of(turned(1, place_ref[0]) * width, 128), width)
        out_ref[:, columns] = one_ref[...]


def half_product(place, left, right, one):
    vmem = pl.BlockSpec(memory_space=pltpu.VMEM)
    return pl.pallas_call(
        half_kernel,
        out_shape=jax.ShapeDtypeStruct(left.shape, BF16),
        in_specs=[pl.BlockSpec(memory_space=pltpu.SMEM)] + [vmem] * 3,
        out_specs=vmem,
        compiler_params=pltpu.CompilerParams(vmem_limit_bytes=6 * MIB),
        cost_estimate=LIGHT,
        name="half_product",
    )(place, left, right, one)


def column_kernel(place_ref, own_ref, first_ref, second_ref, *refs):
    column_ref, out_refs = refs[0], refs[1:]

    @pl.when(place_ref[1] == 1)
    def _():
        width = own_ref.shape[0]
        for block in range(4):
            rows = pl.ds(block * width, width)
            column_ref[rows, :] = own_ref[:, rows].T
        for left_ref, out_ref in zip((first_ref, second_ref), out_refs):
            out_ref[...] = jnp.dot(
                left_ref[...], column_ref[...], preferred_element_type=F32
            ).astype(BF16)


def own_column(place, own, first, second):
    rows, nodes = own.shape
    vmem = pl.BlockSpec(memory_space=pltpu.VMEM)
    return pl.pallas_call(
        column_kernel,
        out_shape=(
            jax.ShapeDtypeStruct((nodes, rows), BF16),
            jax.ShapeDtypeStruct((rows, rows), BF16),
            jax.ShapeDtypeStruct((rows, rows), BF16),
        ),
        in_specs=[pl.BlockSpec(memory_space=pltpu.SMEM)] + [vmem] * 3,
        out_specs=(vmem, vmem, vmem),
        compiler_params=pltpu.CompilerParams(vmem_limit_bytes=6 * MIB),
        cost_estimate=LIGHT,
        name="own_column",
    )(place, own, first, second)


def rest_kernel(place_ref, upper_ref, lower_ref, right_ref, zero_ref, out_ref, last_ref):
    odd = place_ref[0]
    width = zero_ref.shape[1]
    half = width // 2

    def product(left_ref, block):
        columns = pl.ds(pl.multiple_of(block * width, 128), width)
        value = jnp.dot(left_ref[...], right_ref[:, columns], preferred_element_type=F32)
        return value.astype(BF16)

    @pl.when(place_ref[1] == 1)
    def _():
        out_ref[:, pl.ds(pl.multiple_of(odd * width, 128), width)] = zero_ref[...].T
        other = pl.ds(pl.multiple_of((1 - odd) * width, 128), width)
        for part, left_ref in enumerate((upper_ref, lower_ref)):
            out_ref[pl.ds(part * half, half), other] = product(left_ref, 1 + odd)
            value = product(left_ref, 3 - 3 * odd)
            for quarter in range(2):
                start = quarter * half // 2
                rows = pl.ds(part * half + start, half // 2)
                rows_of = value[start : start + half // 2]
                pack_rows(2 * part + quarter, rows_of, last_ref.at[rows], 0)


def product_rest(place, halves, across, zero):
    rows, width = zero.shape
    vmem = pl.BlockSpec(memory_space=pltpu.VMEM)
    return pl.pallas_call(
        rest_kernel,
        out_shape=(
            jax.ShapeDtypeStruct((rows, 2 * width), BF16),
            jax.ShapeDtypeStruct((rows, 3 * width // 4), BF16),
        ),
        in_specs=[pl.BlockSpec(memory_space=pltpu.SMEM)] + [vmem] * 4,
        out_specs=(vmem, vmem),
        compiler_params=pltpu.CompilerParams(vmem_limit_bytes=6 * MIB),
        cost_estimate=LIGHT,
        name="product_rest",
    )(place, *halves, across, zero)


def pack_rows(part, value, out_ref, column):
    quarter, width = value.shape
    half = width // 2
    beside = (2, 3, 1, 0)[part] * quarter
    out_ref[:, column : column + half] = value[:, part // 2 * half : (part // 2 + 1) * half]
    out_ref[:, column + half : column + half + quarter] = value[:, beside : beside + quarter]


def unpacked_rows(part, packed_ref, column):
    quarter = packed_ref.shape[0] // 4
    half = 2 * quarter

    def beside(which):
        rows = slice(which * quarter, (which + 1) * quarter)
        return packed_ref[rows, column + half : column + half + quarter]

    rows = slice(part * quarter, (part + 1) * quarter)
    diagonal = packed_ref[rows, column : column + half]
    if part == 0:
        return diagonal, jnp.concatenate([beside(0), beside(3).T], axis=1)
    if part == 1:
        return diagonal, jnp.concatenate([beside(2).T, beside(1)], axis=1)
    if part == 2:
        return jnp.concatenate([beside(0).T, beside(2)], axis=1), diagonal
    return jnp.concatenate([beside(3), beside(1).T], axis=1), diagonal


def prior_kernel(place_ref, shifted_ref, sigma_ref, out_ref):
    @pl.when(place_ref[3] == 0)
    def _():
        out_ref[...] = shifted_ref[...]

    @pl.when(place_ref[3] != 0)
    def _():
        out_ref[...] = sigma_ref[...]


def parts_kernel(place_ref, shifted_ref, sigma_ref, row_ref, far_ref, near_ref, last_ref):
    odd = place_ref[0]
    width = row_ref.shape[1] // 4

    def at(block, count=1):
        return pl.ds(pl.multiple_of(block * width, 128), count * width)

    prior_kernel(place_ref, shifted_ref, sigma_ref, row_ref)
    far_ref[:, : 2 * width] = row_ref[:, at(2 - 2 * odd, 2)]
    near_ref[:, :width] = row_ref[:, at(3 - 3 * odd)]
    for part in range(4):

        @pl.when(pl.program_id(0) == part)
        def _():
            pack_rows(part, row_ref[:, at(3 * odd)], far_ref, 2 * width)
            pack_rows(part, row_ref[:, at(2 - odd)], near_ref, width)
            pack_rows(part, row_ref[:, at(3 - 3 * odd)], last_ref, 0)


def prior_parts(place, shifted, sigma):
    rows, nodes = sigma.shape
    chunk = rows // 4
    width = nodes // 4
    out = lambda quarters: jax.ShapeDtypeStruct((rows, quarters * width // 4), BF16)
    spec = lambda quarters: pl.BlockSpec((chunk, quarters * width // 4), lambda i, place: (i, 0))
    return pl.pallas_call(
        parts_kernel,
        out_shape=(out(16), out(11), out(7), out(3)),
        grid_spec=pltpu.PrefetchScalarGridSpec(
            num_scalar_prefetch=1,
            grid=(rows // chunk,),
            in_specs=[
                pl.BlockSpec(
                    (chunk, nodes), lambda i, place: (jnp.where(place[3] == 0, i, 0), 0)
                ),
                pl.BlockSpec(
                    (chunk, nodes), lambda i, place: (jnp.where(place[3] == 0, 0, i), 0)
                ),
            ],
            out_specs=(spec(16), spec(11), spec(7), spec(3)),
        ),
        compiler_params=pltpu.CompilerParams(vmem_limit_bytes=8 * MIB),
        cost_estimate=LIGHT,
        name="prior_parts",
    )(place, shifted, sigma)


def assemble_kernel(place_ref, own, column, near_two, last_three, far_zero, out_ref):
    @pl.when(place_ref[1] == 1)
    def _():
        odd = place_ref[0]
        width = own.shape[0]
        half, quarter = width // 2, width // 4

        def at(block, count=1):
            return pl.ds(pl.multiple_of(block * width, 128), count * width)

        near = 2 * (1 - odd)
        row = [turned(block, odd) for block in range(4)]
        out_ref[at(row[1]), :] = own[...]
        out_ref[at(row[2]), at(row[3])] = near_two[:, :width]
        out_ref[at(row[3]), at(row[2])] = near_two[:, :width].T
        out_ref[at(row[0]), at(near, 2)] = far_zero[:, : 2 * width]
        for step in range(2):
            out_ref[at(near + step), at(row[0])] = far_zero[:, step * width : (1 + step) * width].T
        for block in (0, 2, 3):
            out_ref[at(row[block]), at(row[1])] = column[at(row[block]), :]
        packed = ((0, far_zero, 2 * width), (2, near_two, width), (3, last_three, 0))
        for block, packed_ref, start in packed:
            for part in range(4):
                rows = pl.ds(pl.multiple_of(row[block] * width + part * quarter, 128), quarter)
                for side, value in enumerate(unpacked_rows(part, packed_ref, start)):
                    columns = pl.ds(pl.multiple_of(row[block] * width + side * half, 128), half)
                    out_ref[rows, columns] = value


def assemble(place, *parts):
    nodes = parts[0].shape[1]
    vmem = pl.BlockSpec(memory_space=pltpu.VMEM)
    return pl.pallas_call(
        assemble_kernel,
        out_shape=jax.ShapeDtypeStruct((nodes, nodes), BF16),
        in_specs=[pl.BlockSpec(memory_space=pltpu.SMEM)] + [vmem] * 5,
        out_specs=vmem,
        compiler_params=pltpu.CompilerParams(vmem_limit_bytes=6 * MIB),
        cost_estimate=LIGHT,
        name="assemble",
    )(place, *parts)


def tick(place, *values, cost=HEAVY):
    def kernel(place_ref, *refs):
        for which in range(place.shape[0]):
            refs[-1][which] = place_ref[which]

    scalars = pl.BlockSpec(memory_space=pltpu.SMEM)
    return pl.pallas_call(
        kernel,
        out_shape=jax.ShapeDtypeStruct(place.shape, place.dtype),
        in_specs=[scalars] + [pl.BlockSpec(memory_space=pl.ANY)] * len(values),
        out_specs=scalars,
        compiler_params=pltpu.CompilerParams(vmem_limit_bytes=MIB),
        cost_estimate=cost,
        name="tick",
    )(place, *values)


def finish_kernel(
    place_ref, pivot_ref, sigma_ref,
    q0, q0_last, q2, q3_two,
    q01, q11, q21, q31,
    out_ref, var_ref,
):
    rows, nodes = pivot_ref.shape
    width = nodes // 4
    odd, place = place_ref[0], place_ref[1]
    here = pl.multiple_of(pl.program_id(0) * rows, 128)
    diagonal = diagonal_of(rows)

    def at(block, count=1):
        return pl.ds(pl.multiple_of(block * width, 128), count * width)

    def own(block):
        return pl.ds(pl.multiple_of(block * width + here, 128), rows)

    def add(columns, product):
        out_ref[:, columns] = (pivot_ref[:, columns].astype(F32) + product.astype(F32)).astype(BF16)

    def trace(product):
        var_ref[...] = diagonal(
            pivot_ref[:, own(place_ref[2])].astype(F32) + product.astype(F32)
        )

    active = place_ref[4] != 0

    @pl.when(active & (place == 0))
    def _():
        add(at(odd, 3), q0[...])
        add(at(turned(3, odd)), q0_last[...])
        trace(q0[:, own(2 * odd)])

    @pl.when(active & (place == 1))
    def _():
        add(at(turned(0, odd)), q01[...].T)
        add(at(turned(1, odd)), q11[...])
        add(at(turned(2, odd)), q21[...].T)
        add(at(turned(3, odd)), q31[...].T)
        trace(q11[:, pl.ds(here, rows)])

    @pl.when(active & (place == 2))
    def _():
        add(at(turned(0, odd)), q2[pl.ds(0, width), pl.ds(pl.multiple_of(width + here, 128), rows)].T)
        add(at(turned(1, odd)), q2[pl.ds(here, rows), pl.ds(0, width)])
        start = pl.program_id(0) % 2 * rows + 2 * width
        trace(q2[pl.ds(here, rows), pl.ds(pl.multiple_of(start, 128), rows)])
        for part in range(4):

            @pl.when(pl.program_id(0) == part)
            def _():
                for side, value in enumerate(unpacked_rows(part, q2, 2 * width)):
                    start = turned(2, odd) * width + side * width // 2
                    add(pl.ds(pl.multiple_of(start, 128), width // 2), value)

    @pl.when(active & (place == 3))
    def _():
        add(at(turned(2, odd)), q3_two[...])

    @pl.when(place_ref[4] == 0)
    def _():
        out_ref[...] = sigma_ref[...]
        var_ref[...] = diagonal(sigma_ref[:, own(place_ref[2])].astype(F32))


def finish(place, pivot, sigma, received, kept):
    rows, nodes = pivot.shape
    chunk = 128
    width = nodes // 4

    def picked(which, blocks):
        return pl.BlockSpec(
            (chunk, blocks * width), lambda i, place: (jnp.where(place[1] == which, i, 0), 0)
        )

    def turned_block(start):
        return pl.BlockSpec(
            (rows, chunk),
            lambda i, place: (
                0,
                jnp.where(place[1] == 1, start(place[0]) * (width // chunk) + i, 0),
            ),
        )

    return pl.pallas_call(
        finish_kernel,
        out_shape=(
            jax.ShapeDtypeStruct((rows, nodes), BF16),
            jax.ShapeDtypeStruct((1, rows), F32),
        ),
        grid_spec=pltpu.PrefetchScalarGridSpec(
            num_scalar_prefetch=1,
            grid=(rows // chunk,),
            in_specs=[
                pl.BlockSpec((chunk, nodes), lambda i, place: (i, 0)),
                pl.BlockSpec(
                    (chunk, nodes), lambda i, place: (jnp.where(place[4] == 0, i, 0), 0)
                ),
                picked(0, 3),
                picked(0, 1),
                pl.BlockSpec((rows, 11 * width // 4), lambda i, place: (0, 0)),
                picked(3, 1),
                turned_block(lambda odd: 1),
                picked(1, 1),
                turned_block(lambda odd: 0),
                turned_block(lambda odd: 1 - odd),
            ],
            out_specs=(
                pl.BlockSpec((chunk, nodes), lambda i, place: (i, 0)),
                pl.BlockSpec((1, chunk), lambda i, place: (0, i)),
            ),
        ),
        compiler_params=pltpu.CompilerParams(vmem_limit_bytes=12 * MIB),
        cost_estimate=HEAVY,
        name="finish",
    )(place, pivot, sigma, *received, *kept)


def add_in_place(pivot_ref, out_ref, sum_ref, sems, column, product):
    chunk = pivot_ref.shape[0] // 4
    copies = []
    for part in range(4):
        here = pl.ds(part * chunk, chunk)
        value = pivot_ref[here, :].astype(F32) + product(part, here).astype(F32)
        sum_ref[here, :] = value.astype(BF16)
        copies.append(
            pltpu.make_async_copy(sum_ref.at[here], out_ref.at[here, column], sems.at[part])
        )
        copies[-1].start()
    for copy in copies:
        copy.wait()


def other_kernel(place_ref, pivot_ref, q3_other, old_ref, out_ref, sum_ref, sems):
    both = pivot_ref.shape[1]
    column = pl.ds(pl.multiple_of(place_ref[0] * both, 128), both)

    @pl.when((place_ref[4] != 0) & (place_ref[1] == 3))
    def _():
        add_in_place(
            pivot_ref, out_ref, sum_ref, sems, column, lambda part, here: q3_other[here, :]
        )


def last_kernel(
    place_ref, pivot_ref, q2_last, q3_last, old_ref, old_var_ref, out_ref, var_ref, sum_ref, sems
):
    rows, width = pivot_ref.shape
    chunk = rows // 4
    active = place_ref[4] != 0
    column = pl.ds(pl.multiple_of(turned(3, place_ref[0]) * width, 128), width)
    add = functools.partial(add_in_place, pivot_ref, out_ref, sum_ref, sems, column)
    var_ref[...] = old_var_ref[...]

    @pl.when(active & (place_ref[1] == 2))
    def _():
        add(lambda part, here: q2_last[:, here].T)

    @pl.when(active & (place_ref[1] == 3))
    def _():
        add(lambda part, here: jnp.concatenate(unpacked_rows(part, q3_last, 0), axis=1))
        for start in range(0, rows, chunk):
            here = pl.ds(start, chunk)
            value = pivot_ref[here, here].astype(F32)
            value = value + q3_last[here, pl.ds(start % (2 * chunk), chunk)].astype(F32)
            var_ref[:, here] = diagonal_of(chunk)(value)


def diagonal_of(rows):
    square = (rows, rows)
    on_diagonal = lax.broadcasted_iota(jnp.int32, square, 0) == lax.broadcasted_iota(
        jnp.int32, square, 1
    )
    return lambda value: jnp.sum(jnp.where(on_diagonal, value, 0.0), axis=0, keepdims=True)


def finish_other(place, pivot, q3_other, covariance):
    rows, nodes = pivot.shape
    vmem = pl.BlockSpec(memory_space=pltpu.VMEM)
    anywhere = pl.BlockSpec(memory_space=pl.ANY)
    return pl.pallas_call(
        other_kernel,
        out_shape=jax.ShapeDtypeStruct((rows, nodes), BF16),
        grid_spec=pltpu.PrefetchScalarGridSpec(
            num_scalar_prefetch=1,
            grid=(1,),
            in_specs=[
                pl.BlockSpec((rows, nodes // 2), lambda i, place: (0, place[0])),
                vmem,
                anywhere,
            ],
            out_specs=anywhere,
            scratch_shapes=[pltpu.VMEM((rows, nodes // 2), BF16), pltpu.SemaphoreType.DMA((4,))],
        ),
        input_output_aliases={3: 0},
        compiler_params=pltpu.CompilerParams(vmem_limit_bytes=8 * MIB),
        cost_estimate=LIGHT,
        name="finish_other",
    )(place, pivot, q3_other, covariance)


def finish_last(place, pivot, q2_last, q3_last, covariance, variances):
    rows, nodes = pivot.shape
    vmem = pl.BlockSpec(memory_space=pltpu.VMEM)
    anywhere = pl.BlockSpec(memory_space=pl.ANY)
    return pl.pallas_call(
        last_kernel,
        out_shape=(
            jax.ShapeDtypeStruct((rows, nodes), BF16),
            jax.ShapeDtypeStruct((1, rows), F32),
        ),
        grid_spec=pltpu.PrefetchScalarGridSpec(
            num_scalar_prefetch=1,
            grid=(1,),
            in_specs=[
                pl.BlockSpec((rows, nodes // 4), lambda i, place: (0, turned(3, place[0]))),
                vmem,
                vmem,
                anywhere,
                vmem,
            ],
            out_specs=(anywhere, vmem),
            scratch_shapes=[pltpu.VMEM((rows, nodes // 4), BF16), pltpu.SemaphoreType.DMA((4,))],
        ),
        input_output_aliases={4: 0},
        compiler_params=pltpu.CompilerParams(vmem_limit_bytes=8 * MIB),
        cost_estimate=LIGHT,
        name="finish_last",
    )(place, pivot, q2_last, q3_last, covariance, variances)


def owned(sigma_next, separator, inverse_pivot, coupling_rate, lengths, step_index, node_class):
    sigma, pivot = sigma_next[0], inverse_pivot[0]
    odd = lax.axis_index("dom") % 2
    col = lax.axis_index("col")
    step = step_index[0]
    place = jnp.stack([odd, turned(col, odd), col, step, step < lengths[0]]).astype(jnp.int32)
    after = lambda value, *others: lax.optimization_barrier((value, *others))[0]

    shifted = passed_along(separator, "dom", -1)[0]
    p2 = moved(pivot, 2, 1)
    p0 = moved(pivot, 0, 1)
    weights = coupling(node_class)
    c1 = [couple(pivot, weights, coupling_rate, part, 2) for part in range(2)]
    across = turn(place, 1, 0, c1[0], None)
    across = turn(place, 1, 1, c1[1], across)

    row, far, near, last = prior_parts(place, after(shifted, across), sigma)
    far_zero, near_two, last_three = moved(far, 0, 1), moved(near, 2, 1), moved(last, 3, 1)

    c2 = couple_here(place, after(p2, last), weights, coupling_rate)
    across = turn(place, 2, 0, c2, across)
    c0 = couple_here(place, after(p0, across), weights, coupling_rate)
    across = turn(place, 0, 0, c0, across)
    column, h0_one, h2_one = own_column(place, after(row, last_three), c0, c2)
    c3 = [
        moved(after(c1[0], last_three, near_two, across), 3, 1),
        moved(after(c1[1], far_zero, h2_one), 3, 1),
    ]
    prior = assemble(place, row, column, near_two, last_three, far_zero)

    h0 = half_product(place, c0, prior, h0_one)
    q0_own = multiply(place, [h0], across, lambda odd: odd, 3)
    q0 = moved(q0_own, 1, 0)
    h2 = half_product(place, after(c2, q0_own), prior, h2_one)
    q2_own = product_two(place, h2, across, q0_own)
    q2 = moved(q2_own, 1, 2)

    across = turn(place, 3, 0, c3[0], after(across, q2_own))
    upper = multiply(place, [c3[0]], prior)
    across = turn(place, 3, 1, c3[1], after(across, upper))
    q03 = multiply(place, [h0], across, lambda odd: 3 - 3 * odd, 1)
    q0_last = moved(q03, 1, 0)
    h3 = [upper, multiply(place, [after(c3[1], q03)], prior)]
    q32 = multiply(place, h3, across, lambda odd: 2 - odd, 1)
    q3_two = moved(q32, 1, 3)
    q3_own, q33 = product_rest(place, h3, across, after(q03, q32))
    q3_other, q3_last = moved(q3_own, 1, 3), moved(q33, 1, 3)
    h1 = multiply(place, [after(c1[0], q3_own), c1[1]], prior)
    q11 = multiply(place, [h1], across, lambda odd: 1 + odd, 1)
    received = (q0, q0_last, q2, q3_two)
    kept = (q0_own, q11, q2_own, q3_own)
    place_then = tick(tick(place, q0, cost=LIGHT), q0_last, cost=MEDIUM)
    q2_last = moved(after(q3_two, place_then), 3, 2)
    covariance, variances = finish(place_then, pivot, sigma, received, kept)
    covariance = finish_other(place, pivot, q3_other, covariance)
    covariance, variances = finish_last(place, pivot, q2_last, q3_last, covariance, variances)
    return (covariance[None], variances)


def gathered(sigma_next, separator, inverse_pivot, coupling_rate, lengths, step_index, node_class):
    shifted = passed_along(separator, "dom", -1)
    prior = jnp.where(step_index[0] == 0, shifted[0], sigma_next[0])
    pivot = inverse_pivot[0].astype(F32)
    coupled = couple(inverse_pivot[0], coupling(node_class), coupling_rate)
    rows = coupled.shape[0]
    half = jnp.dot(
        coupled,
        lax.all_gather(prior, "col", axis=0, tiled=True),
        preferred_element_type=F32,
    ).astype(BF16)
    product = lax.dot_general(
        half,
        lax.all_gather(coupled, "col", axis=0, tiled=True),
        (((1,), (1,)), ((), ())),
        preferred_element_type=F32,
    )
    full = pivot + product
    active = step_index[0] < lengths[0]
    old = sigma_next[0]
    covariance = jnp.where(active, full.astype(BF16), old)
    first_col = lax.axis_index("col") * rows
    new_block = lax.dynamic_slice_in_dim(full, first_col, rows, 1)
    old_block = lax.dynamic_slice_in_dim(old, first_col, rows, 1)
    variances = jnp.where(active, jnp.diagonal(new_block), jnp.diagonal(old_block).astype(F32))
    return (covariance[None], variances[None])


def solution(mesh):
    local = owned if mesh.shape["col"] == 4 and mesh.shape["dom"] % 2 == 0 else gathered
    return jax.shard_map(
        local,
        mesh=mesh,
        in_specs=(
            P(("groups", "dom"), "col", None),
            P(("groups", "dom"), "col", None),
            P(("groups", "dom"), "col", None),
            P(("groups", "dom")),
            P(("groups", "dom")),
            P(("groups", "dom")),
            P("groups"),
        ),
        out_specs=(P(("groups", "dom"), "col", None), P(("groups", "dom"), "col")),
        check_vma=False,
    )
```

```python
import functools

import jax
import jax.numpy as jnp
from jax import lax
from jax.experimental import pallas as pl
from jax.experimental.pallas import tpu as pltpu
from jax.sharding import PartitionSpec as P

GX = 64
GY = 32
BF16 = jnp.bfloat16
F32 = jnp.float32
MIB = 1 << 20


def passed_along(value, axis, steps):
    count = lax.axis_size(axis)
    initial, last = (max(0, -steps), min(count, count - steps))
    return lax.ppermute(value, axis, [(source, source + steps) for source in range(initial, last)])


LIGHT = pl.CostEstimate(flops=1 << 20, bytes_accessed=1 << 16, transcendentals=0)
MEDIUM = pl.CostEstimate(flops=2000000000, bytes_accessed=1 << 16, transcendentals=0)
HEAVY = pl.CostEstimate(flops=14000000000, bytes_accessed=1 << 16, transcendentals=0)


BLOCK = 256
SPAN = 512


def window(block, nodes):
    return pl.multiple_of(jnp.clip(block * BLOCK - (SPAN - BLOCK) // 2, 0, nodes - SPAN), 128)


def weight_kernel(class_ref, out_ref):
    nodes = class_ref.shape[1]

    def fill(block, carry):
        first = pl.multiple_of(block * BLOCK, BLOCK)
        kind = class_ref[:, pl.ds(first, BLOCK)]
        across = jnp.where(
            kind == 0, 0.25, jnp.where(kind == 1, 0.375, jnp.where(kind == 2, 0.125, 0.5))
        ).astype(F32)
        along = jnp.where(
            kind == 0, 0.25, jnp.where(kind == 1, 0.125, jnp.where(kind == 2, 0.375, 0.0))
        ).astype(F32)
        column = (first + lax.broadcasted_iota(jnp.int32, (1, BLOCK), 1)) % GX
        left = jnp.where(column > 0, across, 0.0)
        right = jnp.where(column < GX - 1, across, 0.0)
        shape = (SPAN, BLOCK)
        offset = (
            lax.broadcasted_iota(jnp.int32, shape, 0)
            - lax.broadcasted_iota(jnp.int32, shape, 1)
            + (window(block, nodes) - first)
        )
        value = jnp.where(jnp.abs(offset) == GX, along, 0.0)
        value = jnp.where(offset == -1, left, value)
        value = jnp.where(offset == 1, right, value)
        value = jnp.where(offset == 0, 1.0, value)
        out_ref[block] = value.astype(BF16)
        return carry

    lax.fori_loop(0, nodes // BLOCK, fill, 0)


def coupling(node_class):
    nodes = node_class.shape[0]
    vmem = pl.BlockSpec(memory_space=pltpu.VMEM)
    return pl.pallas_call(
        weight_kernel,
        out_shape=jax.ShapeDtypeStruct((nodes // BLOCK, SPAN, BLOCK), BF16),
        in_specs=[vmem],
        out_specs=vmem,
        compiler_params=pltpu.CompilerParams(vmem_limit_bytes=6 * MIB),
        cost_estimate=LIGHT,
        name="coupling",
    )(node_class.reshape(1, nodes))


def couple_kernel(first, rate_ref, weight_ref, pivot_ref, out_ref):
    rows, nodes = out_ref.shape

    def block_of(block, carry):
        source = pl.ds(window(block, nodes), SPAN)
        target = pl.ds(pl.multiple_of(block * BLOCK, BLOCK), BLOCK)
        value = jnp.dot(
            pivot_ref[first : first + rows, source], weight_ref[block], preferred_element_type=F32
        )
        out_ref[:, target] = (rate_ref[0] * value).astype(BF16)
        return carry

    lax.fori_loop(0, nodes // BLOCK, block_of, 0)


def couple(pivot, weights, rate, part=0, parts=1):
    rows, nodes = pivot.shape[0] // parts, pivot.shape[1]
    vmem = pl.BlockSpec(memory_space=pltpu.VMEM)
    return pl.pallas_call(
        functools.partial(couple_kernel, part * rows),
        out_shape=jax.ShapeDtypeStruct((rows, nodes), BF16),
        in_specs=[pl.BlockSpec(memory_space=pltpu.SMEM), vmem, vmem],
        out_specs=vmem,
        compiler_params=pltpu.CompilerParams(vmem_limit_bytes=8 * MIB),
        cost_estimate=LIGHT,
        name="couple",
    )(rate, weights, pivot)


def turned(block, odd):
    return block + odd * (3 - 2 * block)


def route(source, target, doms):
    pairs = []
    for dom in range(doms):
        odd = dom % 2
        pairs.append((dom * 4 + turned(source, odd), dom * 4 + turned(target, odd)))
    return pairs


def moved(value, source, target):
    return lax.ppermute(value, ("dom", "col"), route(source, target, lax.axis_size("dom")))


def couple_here(place, pivot, weights, rate):
    def kernel(place_ref, *refs):
        @pl.when(place_ref[1] == 1)
        def _():
            couple_kernel(0, *refs)

    scalars, vmem = pl.BlockSpec(memory_space=pltpu.SMEM), pl.BlockSpec(memory_space=pltpu.VMEM)
    return pl.pallas_call(
        kernel,
        out_shape=jax.ShapeDtypeStruct(pivot.shape, BF16),
        in_specs=[scalars, scalars, vmem, vmem],
        out_specs=vmem,
        compiler_params=pltpu.CompilerParams(vmem_limit_bytes=8 * MIB),
        cost_estimate=LIGHT,
        name="couple_here",
    )(place, rate, weights, pivot)


def turn_kernel(place_ref, coupled_ref, *refs):
    @pl.when(place_ref[1] == 1)
    def _():
        refs[-1][...] = coupled_ref[...].T


def turn(place, panel, part, coupled, across):
    rows, nodes = coupled.shape
    chunk = 128
    steps = rows // chunk
    ratio = nodes // 4 // chunk
    return pl.pallas_call(
        turn_kernel,
        out_shape=jax.ShapeDtypeStruct((nodes, nodes), BF16),
        grid_spec=pltpu.PrefetchScalarGridSpec(
            num_scalar_prefetch=1,
            grid=(steps,),
            in_specs=[pl.BlockSpec((chunk, nodes), lambda i, place: (i, 0))]
            + ([] if across is None else [pl.BlockSpec(memory_space=pl.ANY)]),
            out_specs=pl.BlockSpec(
                (nodes, chunk),
                lambda i, place: (0, turned(panel, place[0]) * ratio + part * steps + i),
            ),
        ),
        input_output_aliases={} if across is None else {2: 0},
        compiler_params=pltpu.CompilerParams(vmem_limit_bytes=4 * MIB),
        cost_estimate=LIGHT,
        name="turn",
    )(place, coupled, *(() if across is None else (across,)))


def multiply_kernel(first, count, lefts, place_ref, *refs):
    left_refs, right_ref, out_ref = refs[:lefts], refs[lefts], refs[-1]
    width = right_ref.shape[0] // 4

    @pl.when(place_ref[1] == 1)
    def _():
        def block(step, carry):
            source = pl.multiple_of((first(place_ref[0]) + step) * width, 128)
            target = pl.multiple_of(step * width, 128)
            row = 0
            for left_ref in left_refs:
                rows = left_ref.shape[0]
                out_ref[row : row + rows, pl.ds(target, width)] = jnp.dot(
                    left_ref[...], right_ref[:, pl.ds(source, width)], preferred_element_type=F32
                ).astype(BF16)
                row += rows
            return carry

        lax.fori_loop(0, count, block, 0)


def multiply(place, lefts, right, first=lambda odd: 0, count=4):
    rows = sum(left.shape[0] for left in lefts)
    width = right.shape[0] // 4
    vmem = pl.BlockSpec(memory_space=pltpu.VMEM)
    return pl.pallas_call(
        functools.partial(multiply_kernel, first, count, len(lefts)),
        out_shape=jax.ShapeDtypeStruct((rows, count * width), BF16),
        in_specs=[pl.BlockSpec(memory_space=pltpu.SMEM)] + [vmem] * (len(lefts) + 1),
        out_specs=vmem,
        compiler_params=pltpu.CompilerParams(vmem_limit_bytes=6 * MIB),
        cost_estimate=LIGHT,
        name="multiply",
    )(place, *lefts, right)


def pack(value, out_ref, column):
    quarter = value.shape[1] // 4
    for part in range(4):
        rows = pl.ds(part * quarter, quarter)
        pack_rows(part, value[part * quarter : (part + 1) * quarter], out_ref.at[rows], column)


def two_kernel(place_ref, left_ref, right_ref, zero_ref, out_ref):
    odd = place_ref[0]
    width = right_ref.shape[0] // 4

    def product(block):
        columns = pl.ds(pl.multiple_of(block * width, 128), width)
        value = jnp.dot(left_ref[...], right_ref[:, columns], preferred_element_type=F32)
        return value.astype(BF16)

    @pl.when(place_ref[1] == 1)
    def _():
        out_ref[:, :width] = product(1 + odd)
        zero = pl.ds(pl.multiple_of((2 - 2 * odd) * width, 128), width)
        out_ref[:, width : 2 * width] = zero_ref[:, zero]
        pack(product(2 - odd), out_ref, 2 * width)


def product_two(place, half, across, zero):
    rows = half.shape[0]
    width = across.shape[0] // 4
    vmem = pl.BlockSpec(memory_space=pltpu.VMEM)
    return pl.pallas_call(
        two_kernel,
        out_shape=jax.ShapeDtypeStruct((rows, 11 * width // 4), BF16),
        in_specs=[pl.BlockSpec(memory_space=pltpu.SMEM)] + [vmem] * 3,
        out_specs=vmem,
        compiler_params=pltpu.CompilerParams(vmem_limit_bytes=6 * MIB),
        cost_estimate=LIGHT,
        name="product_two",
    )(place, half, across, zero)


def half_kernel(place_ref, left_ref, right_ref, one_ref, out_ref):
    width = one_ref.shape[1]

    @pl.when(place_ref[1] == 1)
    def _():
        def block(step, carry):
            which = turned(step + (step > 0).astype(jnp.int32), place_ref[0])
            columns = pl.ds(pl.multiple_of(which * width, 128), width)
            out_ref[:, columns] = jnp.dot(
                left_ref[...], right_ref[:, columns], preferred_element_type=F32
            ).astype(BF16)
            return carry

        lax.fori_loop(0, 3, block, 0)
        columns = pl.ds(pl.multiple_of(turned(1, place_ref[0]) * width, 128), width)
        out_ref[:, columns] = one_ref[...]


def half_product(place, left, right, one):
    vmem = pl.BlockSpec(memory_space=pltpu.VMEM)
    return pl.pallas_call(
        half_kernel,
        out_shape=jax.ShapeDtypeStruct(left.shape, BF16),
        in_specs=[pl.BlockSpec(memory_space=pltpu.SMEM)] + [vmem] * 3,
        out_specs=vmem,
        compiler_params=pltpu.CompilerParams(vmem_limit_bytes=6 * MIB),
        cost_estimate=LIGHT,
        name="half_product",
    )(place, left, right, one)


def column_kernel(place_ref, near_ref, other_ref, first_ref, second_ref, *refs):
    column_ref, out_refs = refs[0], refs[1:]

    @pl.when(place_ref[1] == 1)
    def _():
        odd = place_ref[0]
        width = near_ref.shape[0]
        for half, half_ref in ((1 - odd, near_ref), (odd, other_ref)):
            for block in range(2):
                rows = pl.ds(pl.multiple_of((2 * half + block) * width, 128), width)
                column_ref[rows, :] = half_ref[:, block * width : (block + 1) * width].T
        for left_ref, out_ref in zip((first_ref, second_ref), out_refs):
            out_ref[...] = jnp.dot(
                left_ref[...], column_ref[...], preferred_element_type=F32
            ).astype(BF16)


def own_column(place, near, other, first, second):
    rows, nodes = first.shape
    vmem = pl.BlockSpec(memory_space=pltpu.VMEM)
    return pl.pallas_call(
        column_kernel,
        out_shape=(
            jax.ShapeDtypeStruct((nodes, rows), BF16),
            jax.ShapeDtypeStruct((rows, rows), BF16),
            jax.ShapeDtypeStruct((rows, rows), BF16),
        ),
        in_specs=[pl.BlockSpec(memory_space=pltpu.SMEM)] + [vmem] * 4,
        out_specs=(vmem, vmem, vmem),
        compiler_params=pltpu.CompilerParams(vmem_limit_bytes=6 * MIB),
        cost_estimate=LIGHT,
        name="own_column",
    )(place, near, other, first, second)


def rest_kernel(place_ref, upper_ref, lower_ref, right_ref, zero_ref, out_ref, last_ref):
    odd = place_ref[0]
    width = zero_ref.shape[1]
    half = width // 2

    def product(left_ref, block):
        columns = pl.ds(pl.multiple_of(block * width, 128), width)
        value = jnp.dot(left_ref[...], right_ref[:, columns], preferred_element_type=F32)
        return value.astype(BF16)

    @pl.when(place_ref[1] == 1)
    def _():
        out_ref[:, pl.ds(pl.multiple_of(odd * width, 128), width)] = zero_ref[...].T
        other = pl.ds(pl.multiple_of((1 - odd) * width, 128), width)
        for part, left_ref in enumerate((upper_ref, lower_ref)):
            out_ref[pl.ds(part * half, half), other] = product(left_ref, 1 + odd)
            value = product(left_ref, 3 - 3 * odd)
            for quarter in range(2):
                start = quarter * half // 2
                rows = pl.ds(part * half + start, half // 2)
                rows_of = value[start : start + half // 2]
                pack_rows(2 * part + quarter, rows_of, last_ref.at[rows], 0)


def product_rest(place, halves, across, zero):
    rows, width = zero.shape
    vmem = pl.BlockSpec(memory_space=pltpu.VMEM)
    return pl.pallas_call(
        rest_kernel,
        out_shape=(
            jax.ShapeDtypeStruct((rows, 2 * width), BF16),
            jax.ShapeDtypeStruct((rows, 3 * width // 4), BF16),
        ),
        in_specs=[pl.BlockSpec(memory_space=pltpu.SMEM)] + [vmem] * 4,
        out_specs=(vmem, vmem),
        compiler_params=pltpu.CompilerParams(vmem_limit_bytes=6 * MIB),
        cost_estimate=LIGHT,
        name="product_rest",
    )(place, *halves, across, zero)


def pack_rows(part, value, out_ref, column):
    quarter, width = value.shape
    half = width // 2
    beside = (2, 3, 1, 0)[part] * quarter
    out_ref[:, column : column + half] = value[:, part // 2 * half : (part // 2 + 1) * half]
    out_ref[:, column + half : column + half + quarter] = value[:, beside : beside + quarter]


def unpacked_rows(part, packed_ref, column):
    quarter = packed_ref.shape[0] // 4
    half = 2 * quarter

    def beside(which):
        rows = slice(which * quarter, (which + 1) * quarter)
        return packed_ref[rows, column + half : column + half + quarter]

    rows = slice(part * quarter, (part + 1) * quarter)
    diagonal = packed_ref[rows, column : column + half]
    if part == 0:
        return diagonal, jnp.concatenate([beside(0), beside(3).T], axis=1)
    if part == 1:
        return diagonal, jnp.concatenate([beside(2).T, beside(1)], axis=1)
    if part == 2:
        return jnp.concatenate([beside(0).T, beside(2)], axis=1), diagonal
    return jnp.concatenate([beside(3), beside(1).T], axis=1), diagonal


def prior_kernel(place_ref, shifted_ref, sigma_ref, out_ref):
    @pl.when(place_ref[3] == 0)
    def _():
        out_ref[...] = shifted_ref[...]

    @pl.when(place_ref[3] != 0)
    def _():
        out_ref[...] = sigma_ref[...]


def halves_kernel(place_ref, first_ref, second_ref, near_ref, other_ref):
    near_ref[...] = first_ref[...]
    other_ref[...] = second_ref[...]


def halves(place, separator):
    rows, nodes = separator.shape
    chunk = rows // 4
    half = lambda side: pl.BlockSpec((chunk, nodes // 2), lambda i, place: (i, side(place[0])))
    out = jax.ShapeDtypeStruct((rows, nodes // 2), BF16)
    return pl.pallas_call(
        halves_kernel,
        out_shape=(out, out),
        grid_spec=pltpu.PrefetchScalarGridSpec(
            num_scalar_prefetch=1,
            grid=(4,),
            in_specs=[half(lambda odd: odd), half(lambda odd: 1 - odd)],
            out_specs=(half(lambda odd: 0), half(lambda odd: 0)),
        ),
        compiler_params=pltpu.CompilerParams(vmem_limit_bytes=6 * MIB),
        cost_estimate=LIGHT,
        name="halves",
    )(place, separator, separator)


def near_kernel(place_ref, shifted_ref, sigma_ref, row_ref, near_ref, last_ref):
    odd = place_ref[0]
    width = row_ref.shape[1] // 2
    prior_kernel(place_ref, shifted_ref, sigma_ref, row_ref)
    two = pl.ds(pl.multiple_of(odd * width, 128), width)
    three = pl.ds(pl.multiple_of((1 - odd) * width, 128), width)
    near_ref[:, :width] = row_ref[:, three]
    for part in range(4):

        @pl.when(pl.program_id(0) == part)
        def _():
            pack_rows(part, row_ref[:, two], near_ref, width)
            pack_rows(part, row_ref[:, three], last_ref, 0)


def other_half_kernel(place_ref, shifted_ref, sigma_ref, row_ref, far_ref):
    width = row_ref.shape[1] // 2
    prior_kernel(place_ref, shifted_ref, sigma_ref, row_ref)
    zero = pl.ds(pl.multiple_of(place_ref[0] * width, 128), width)
    for part in range(4):

        @pl.when(pl.program_id(0) == part)
        def _():
            pack_rows(part, row_ref[:, zero], far_ref, 0)


def prior_half(kernel, side, sent, place, shifted, sigma):
    rows, nodes = sigma.shape
    chunk = rows // 4
    quarters = (8,) + sent
    out = lambda count: jax.ShapeDtypeStruct((rows, count * nodes // 16), BF16)
    spec = lambda count: pl.BlockSpec((chunk, count * nodes // 16), lambda i, place: (i, 0))
    return pl.pallas_call(
        kernel,
        out_shape=tuple(out(count) for count in quarters),
        grid_spec=pltpu.PrefetchScalarGridSpec(
            num_scalar_prefetch=1,
            grid=(4,),
            in_specs=[
                pl.BlockSpec(
                    (chunk, nodes // 2), lambda i, place: (jnp.where(place[3] == 0, i, 0), 0)
                ),
                pl.BlockSpec(
                    (chunk, nodes // 2),
                    lambda i, place: (jnp.where(place[3] == 0, 0, i), side(place[0])),
                ),
            ],
            out_specs=tuple(spec(count) for count in quarters),
        ),
        compiler_params=pltpu.CompilerParams(vmem_limit_bytes=6 * MIB),
        cost_estimate=LIGHT,
        name="prior_half",
    )(place, shifted, sigma)


def assemble_kernel(place_ref, near, other, column, near_two, last_three, near_zero, far_zero, out_ref):
    @pl.when(place_ref[1] == 1)
    def _():
        odd = place_ref[0]
        width = near.shape[0]
        half, quarter = width // 2, width // 4

        def at(block, count=1):
            return pl.ds(pl.multiple_of(block * width, 128), count * width)

        first = 2 * (1 - odd)
        row = [turned(block, odd) for block in range(4)]
        out_ref[at(row[1]), at(first, 2)] = near[...]
        out_ref[at(row[1]), at(2 * odd, 2)] = other[...]
        out_ref[at(row[2]), at(row[3])] = near_two[:, :width]
        out_ref[at(row[3]), at(row[2])] = near_two[:, :width].T
        out_ref[at(row[0]), at(first, 2)] = near_zero[...]
        for step in range(2):
            out_ref[at(first + step), at(row[0])] = near_zero[:, step * width : (1 + step) * width].T
        for block in (0, 2, 3):
            out_ref[at(row[block]), at(row[1])] = column[at(row[block]), :]
        packed = ((0, far_zero, 0), (2, near_two, width), (3, last_three, 0))
        for block, packed_ref, start in packed:
            for part in range(4):
                rows = pl.ds(pl.multiple_of(row[block] * width + part * quarter, 128), quarter)
                for side, value in enumerate(unpacked_rows(part, packed_ref, start)):
                    columns = pl.ds(pl.multiple_of(row[block] * width + side * half, 128), half)
                    out_ref[rows, columns] = value


def assemble(place, *parts):
    nodes = 2 * parts[0].shape[1]
    vmem = pl.BlockSpec(memory_space=pltpu.VMEM)
    return pl.pallas_call(
        assemble_kernel,
        out_shape=jax.ShapeDtypeStruct((nodes, nodes), BF16),
        in_specs=[pl.BlockSpec(memory_space=pltpu.SMEM)] + [vmem] * 7,
        out_specs=vmem,
        compiler_params=pltpu.CompilerParams(vmem_limit_bytes=6 * MIB),
        cost_estimate=LIGHT,
        name="assemble",
    )(place, *parts)


def tick(place, *values, cost=HEAVY):
    def kernel(place_ref, *refs):
        for which in range(place.shape[0]):
            refs[-1][which] = place_ref[which]

    scalars = pl.BlockSpec(memory_space=pltpu.SMEM)
    return pl.pallas_call(
        kernel,
        out_shape=jax.ShapeDtypeStruct(place.shape, place.dtype),
        in_specs=[scalars] + [pl.BlockSpec(memory_space=pl.ANY)] * len(values),
        out_specs=scalars,
        compiler_params=pltpu.CompilerParams(vmem_limit_bytes=MIB),
        cost_estimate=cost,
        name="tick",
    )(place, *values)


def finish_kernel(
    place_ref, pivot_ref, sigma_ref,
    q0, q0_last, q2, q3_two,
    q01, q11, q21, q31,
    out_ref, var_ref,
):
    rows, nodes = pivot_ref.shape
    width = nodes // 4
    odd, place = place_ref[0], place_ref[1]
    here = pl.multiple_of(pl.program_id(0) * rows, 128)
    diagonal = diagonal_of(rows)

    def at(block, count=1):
        return pl.ds(pl.multiple_of(block * width, 128), count * width)

    def own(block):
        return pl.ds(pl.multiple_of(block * width + here, 128), rows)

    def add(columns, product):
        out_ref[:, columns] = (pivot_ref[:, columns].astype(F32) + product.astype(F32)).astype(BF16)

    def trace(product):
        var_ref[...] = diagonal(
            pivot_ref[:, own(place_ref[2])].astype(F32) + product.astype(F32)
        )

    active = place_ref[4] != 0

    @pl.when(active & (place == 0))
    def _():
        add(at(odd, 3), q0[...])
        add(at(turned(3, odd)), q0_last[...])
        trace(q0[:, own(2 * odd)])

    @pl.when(active & (place == 1))
    def _():
        add(at(turned(0, odd)), q01[...].T)
        add(at(turned(1, odd)), q11[...])
        add(at(turned(2, odd)), q21[...].T)
        add(at(turned(3, odd)), q31[...].T)
        trace(q11[:, pl.ds(here, rows)])

    @pl.when(active & (place == 2))
    def _():
        add(at(turned(0, odd)), q2[pl.ds(0, width), pl.ds(pl.multiple_of(width + here, 128), rows)].T)
        add(at(turned(1, odd)), q2[pl.ds(here, rows), pl.ds(0, width)])
        start = pl.program_id(0) % 2 * rows + 2 * width
        trace(q2[pl.ds(here, rows), pl.ds(pl.multiple_of(start, 128), rows)])
        for part in range(4):

            @pl.when(pl.program_id(0) == part)
            def _():
                for side, value in enumerate(unpacked_rows(part, q2, 2 * width)):
                    start = turned(2, odd) * width + side * width // 2
                    add(pl.ds(pl.multiple_of(start, 128), width // 2), value)

    @pl.when(active & (place == 3))
    def _():
        add(at(turned(2, odd)), q3_two[...])

    @pl.when(place_ref[4] == 0)
    def _():
        out_ref[...] = sigma_ref[...]
        var_ref[...] = diagonal(sigma_ref[:, own(place_ref[2])].astype(F32))


def finish(place, pivot, sigma, received, kept):
    rows, nodes = pivot.shape
    chunk = 128
    width = nodes // 4

    def picked(which, blocks):
        return pl.BlockSpec(
            (chunk, blocks * width), lambda i, place: (jnp.where(place[1] == which, i, 0), 0)
        )

    def turned_block(start):
        return pl.BlockSpec(
            (rows, chunk),
            lambda i, place: (
                0,
                jnp.where(place[1] == 1, start(place[0]) * (width // chunk) + i, 0),
            ),
        )

    return pl.pallas_call(
        finish_kernel,
        out_shape=(
            jax.ShapeDtypeStruct((rows, nodes), BF16),
            jax.ShapeDtypeStruct((1, rows), F32),
        ),
        grid_spec=pltpu.PrefetchScalarGridSpec(
            num_scalar_prefetch=1,
            grid=(rows // chunk,),
            in_specs=[
                pl.BlockSpec((chunk, nodes), lambda i, place: (i, 0)),
                pl.BlockSpec(
                    (chunk, nodes), lambda i, place: (jnp.where(place[4] == 0, i, 0), 0)
                ),
                picked(0, 3),
                picked(0, 1),
                pl.BlockSpec((rows, 11 * width // 4), lambda i, place: (0, 0)),
                picked(3, 1),
                turned_block(lambda odd: 1),
                picked(1, 1),
                turned_block(lambda odd: 0),
                turned_block(lambda odd: 1 - odd),
            ],
            out_specs=(
                pl.BlockSpec((chunk, nodes), lambda i, place: (i, 0)),
                pl.BlockSpec((1, chunk), lambda i, place: (0, i)),
            ),
        ),
        compiler_params=pltpu.CompilerParams(vmem_limit_bytes=12 * MIB),
        cost_estimate=HEAVY,
        name="finish",
    )(place, pivot, sigma, *received, *kept)


def add_in_place(pivot_ref, out_ref, sum_ref, sems, column, product):
    chunk = pivot_ref.shape[0] // 4
    copies = []
    for part in range(4):
        here = pl.ds(part * chunk, chunk)
        value = pivot_ref[here, :].astype(F32) + product(part, here).astype(F32)
        sum_ref[here, :] = value.astype(BF16)
        copies.append(
            pltpu.make_async_copy(sum_ref.at[here], out_ref.at[here, column], sems.at[part])
        )
        copies[-1].start()
    for copy in copies:
        copy.wait()


def other_kernel(place_ref, pivot_ref, q3_other, old_ref, out_ref, sum_ref, sems):
    both = pivot_ref.shape[1]
    column = pl.ds(pl.multiple_of(place_ref[0] * both, 128), both)

    @pl.when((place_ref[4] != 0) & (place_ref[1] == 3))
    def _():
        add_in_place(
            pivot_ref, out_ref, sum_ref, sems, column, lambda part, here: q3_other[here, :]
        )


def last_kernel(
    place_ref, pivot_ref, q2_last, q3_last, old_ref, old_var_ref, out_ref, var_ref, sum_ref, sems
):
    rows, width = pivot_ref.shape
    chunk = rows // 4
    active = place_ref[4] != 0
    column = pl.ds(pl.multiple_of(turned(3, place_ref[0]) * width, 128), width)
    add = functools.partial(add_in_place, pivot_ref, out_ref, sum_ref, sems, column)
    var_ref[...] = old_var_ref[...]

    @pl.when(active & (place_ref[1] == 2))
    def _():
        add(lambda part, here: q2_last[:, here].T)

    @pl.when(active & (place_ref[1] == 3))
    def _():
        add(lambda part, here: jnp.concatenate(unpacked_rows(part, q3_last, 0), axis=1))
        for start in range(0, rows, chunk):
            here = pl.ds(start, chunk)
            value = pivot_ref[here, here].astype(F32)
            value = value + q3_last[here, pl.ds(start % (2 * chunk), chunk)].astype(F32)
            var_ref[:, here] = diagonal_of(chunk)(value)


def diagonal_of(rows):
    square = (rows, rows)
    on_diagonal = lax.broadcasted_iota(jnp.int32, square, 0) == lax.broadcasted_iota(
        jnp.int32, square, 1
    )
    return lambda value: jnp.sum(jnp.where(on_diagonal, value, 0.0), axis=0, keepdims=True)


def finish_other(place, pivot, q3_other, covariance):
    rows, nodes = pivot.shape
    vmem = pl.BlockSpec(memory_space=pltpu.VMEM)
    anywhere = pl.BlockSpec(memory_space=pl.ANY)
    return pl.pallas_call(
        other_kernel,
        out_shape=jax.ShapeDtypeStruct((rows, nodes), BF16),
        grid_spec=pltpu.PrefetchScalarGridSpec(
            num_scalar_prefetch=1,
            grid=(1,),
            in_specs=[
                pl.BlockSpec((rows, nodes // 2), lambda i, place: (0, place[0])),
                vmem,
                anywhere,
            ],
            out_specs=anywhere,
            scratch_shapes=[pltpu.VMEM((rows, nodes // 2), BF16), pltpu.SemaphoreType.DMA((4,))],
        ),
        input_output_aliases={3: 0},
        compiler_params=pltpu.CompilerParams(vmem_limit_bytes=8 * MIB),
        cost_estimate=LIGHT,
        name="finish_other",
    )(place, pivot, q3_other, covariance)


def finish_last(place, pivot, q2_last, q3_last, covariance, variances):
    rows, nodes = pivot.shape
    vmem = pl.BlockSpec(memory_space=pltpu.VMEM)
    anywhere = pl.BlockSpec(memory_space=pl.ANY)
    return pl.pallas_call(
        last_kernel,
        out_shape=(
            jax.ShapeDtypeStruct((rows, nodes), BF16),
            jax.ShapeDtypeStruct((1, rows), F32),
        ),
        grid_spec=pltpu.PrefetchScalarGridSpec(
            num_scalar_prefetch=1,
            grid=(1,),
            in_specs=[
                pl.BlockSpec((rows, nodes // 4), lambda i, place: (0, turned(3, place[0]))),
                vmem,
                vmem,
                anywhere,
                vmem,
            ],
            out_specs=(anywhere, vmem),
            scratch_shapes=[pltpu.VMEM((rows, nodes // 4), BF16), pltpu.SemaphoreType.DMA((4,))],
        ),
        input_output_aliases={4: 0},
        compiler_params=pltpu.CompilerParams(vmem_limit_bytes=8 * MIB),
        cost_estimate=LIGHT,
        name="finish_last",
    )(place, pivot, q2_last, q3_last, covariance, variances)


def owned(sigma_next, separator, inverse_pivot, coupling_rate, lengths, step_index, node_class):
    sigma, pivot = sigma_next[0], inverse_pivot[0]
    odd = lax.axis_index("dom") % 2
    col = lax.axis_index("col")
    step = step_index[0]
    place = jnp.stack([odd, turned(col, odd), col, step, step < lengths[0]]).astype(jnp.int32)
    after = lambda value, *others: lax.optimization_barrier((value, *others))[0]

    p2 = moved(pivot, 2, 1)
    p0 = moved(pivot, 0, 1)
    weights = coupling(node_class)
    c1 = [couple(pivot, weights, coupling_rate, part, 2) for part in range(2)]
    across = turn(place, 1, 0, c1[0], None)
    across = turn(place, 1, 1, c1[1], across)

    near, other = halves(place, separator[0])
    near, other = passed_along(near, "dom", -1), passed_along(other, "dom", -1)
    sides = (lambda odd: 1 - odd, lambda odd: odd)
    row_near, near, last = prior_half(
        near_kernel, sides[0], (7, 3), place, after(near, across), sigma
    )
    near_zero, near_two = moved(row_near, 0, 1), moved(near, 2, 1)
    last_three = moved(last, 3, 1)
    row_other, far = prior_half(
        other_half_kernel, sides[1], (3,), place, after(other, p0, p2), sigma
    )
    far_zero = moved(far, 0, 1)

    c2 = couple_here(place, after(p2, last), weights, coupling_rate)
    across = turn(place, 2, 0, c2, across)
    c0 = couple_here(place, after(p0, across), weights, coupling_rate)
    across = turn(place, 0, 0, c0, across)
    column, h0_one, h2_one = own_column(place, row_near, row_other, c0, c2)
    c3 = [
        moved(after(c1[0], last_three, near_two, near_zero, across), 3, 1),
        moved(after(c1[1], far_zero, h2_one), 3, 1),
    ]
    prior = assemble(place, row_near, row_other, column, near_two, last_three, near_zero, far_zero)

    h0 = half_product(place, c0, prior, h0_one)
    q0_own = multiply(place, [h0], across, lambda odd: odd, 3)
    q0 = moved(q0_own, 1, 0)
    h2 = half_product(place, after(c2, q0_own), prior, h2_one)
    q2_own = product_two(place, h2, across, q0_own)
    q2 = moved(q2_own, 1, 2)

    across = turn(place, 3, 0, c3[0], after(across, q2_own))
    upper = multiply(place, [c3[0]], prior)
    across = turn(place, 3, 1, c3[1], after(across, upper))
    q03 = multiply(place, [h0], across, lambda odd: 3 - 3 * odd, 1)
    q0_last = moved(q03, 1, 0)
    h3 = [upper, multiply(place, [after(c3[1], q03)], prior)]
    q32 = multiply(place, h3, across, lambda odd: 2 - odd, 1)
    q3_two = moved(q32, 1, 3)
    q3_own, q33 = product_rest(place, h3, across, after(q03, q32))
    q3_other, q3_last = moved(q3_own, 1, 3), moved(q33, 1, 3)
    h1 = multiply(place, [after(c1[0], q3_own), c1[1]], prior)
    q11 = multiply(place, [h1], across, lambda odd: 1 + odd, 1)
    received = (q0, q0_last, q2, q3_two)
    kept = (q0_own, q11, q2_own, q3_own)
    place_then = tick(tick(place, q0, cost=LIGHT), q0_last, cost=MEDIUM)
    q2_last = moved(after(q3_two, place_then), 3, 2)
    covariance, variances = finish(place_then, pivot, sigma, received, kept)
    covariance = finish_other(place, pivot, q3_other, covariance)
    covariance, variances = finish_last(place, pivot, q2_last, q3_last, covariance, variances)
    return (covariance[None], variances)


def gathered(sigma_next, separator, inverse_pivot, coupling_rate, lengths, step_index, node_class):
    shifted = passed_along(separator, "dom", -1)
    prior = jnp.where(step_index[0] == 0, shifted[0], sigma_next[0])
    pivot = inverse_pivot[0].astype(F32)
    coupled = couple(inverse_pivot[0], coupling(node_class), coupling_rate)
    rows = coupled.shape[0]
    half = jnp.dot(
        coupled,
        lax.all_gather(prior, "col", axis=0, tiled=True),
        preferred_element_type=F32,
    ).astype(BF16)
    product = lax.dot_general(
        half,
        lax.all_gather(coupled, "col", axis=0, tiled=True),
        (((1,), (1,)), ((), ())),
        preferred_element_type=F32,
    )
    full = pivot + product
    active = step_index[0] < lengths[0]
    old = sigma_next[0]
    covariance = jnp.where(active, full.astype(BF16), old)
    first_col = lax.axis_index("col") * rows
    new_block = lax.dynamic_slice_in_dim(full, first_col, rows, 1)
    old_block = lax.dynamic_slice_in_dim(old, first_col, rows, 1)
    variances = jnp.where(active, jnp.diagonal(new_block), jnp.diagonal(old_block).astype(F32))
    return (covariance[None], variances[None])


def solution(mesh):
    local = owned if mesh.shape["col"] == 4 and mesh.shape["dom"] % 2 == 0 else gathered
    return jax.shard_map(
        local,
        mesh=mesh,
        in_specs=(
            P(("groups", "dom"), "col", None),
            P(("groups", "dom"), "col", None),
            P(("groups", "dom"), "col", None),
            P(("groups", "dom")),
            P(("groups", "dom")),
            P(("groups", "dom")),
            P("groups"),
        ),
        out_specs=(P(("groups", "dom"), "col", None), P(("groups", "dom"), "col")),
        check_vma=False,
    )
```

```python
import functools

import jax
import jax.numpy as jnp
from jax import lax
from jax.experimental import pallas as pl
from jax.experimental.pallas import tpu as pltpu
from jax.sharding import PartitionSpec as P

GX = 64
GY = 32
BF16 = jnp.bfloat16
F32 = jnp.float32
MIB = 1 << 20


def passed_along(value, axis, steps):
    count = lax.axis_size(axis)
    initial, last = (max(0, -steps), min(count, count - steps))
    return lax.ppermute(value, axis, [(source, source + steps) for source in range(initial, last)])


LIGHT = pl.CostEstimate(flops=1 << 20, bytes_accessed=1 << 16, transcendentals=0)
MEDIUM = pl.CostEstimate(flops=2000000000, bytes_accessed=1 << 16, transcendentals=0)
HEAVY = pl.CostEstimate(flops=14000000000, bytes_accessed=1 << 16, transcendentals=0)


BLOCK = 256
SPAN = 512


def window(block, nodes):
    return pl.multiple_of(jnp.clip(block * BLOCK - (SPAN - BLOCK) // 2, 0, nodes - SPAN), 128)


def weight_kernel(class_ref, out_ref):
    nodes = class_ref.shape[1]

    def fill(block, carry):
        first = pl.multiple_of(block * BLOCK, BLOCK)
        kind = class_ref[:, pl.ds(first, BLOCK)]
        across = jnp.where(
            kind == 0, 0.25, jnp.where(kind == 1, 0.375, jnp.where(kind == 2, 0.125, 0.5))
        ).astype(F32)
        along = jnp.where(
            kind == 0, 0.25, jnp.where(kind == 1, 0.125, jnp.where(kind == 2, 0.375, 0.0))
        ).astype(F32)
        column = (first + lax.broadcasted_iota(jnp.int32, (1, BLOCK), 1)) % GX
        left = jnp.where(column > 0, across, 0.0)
        right = jnp.where(column < GX - 1, across, 0.0)
        shape = (SPAN, BLOCK)
        offset = (
            lax.broadcasted_iota(jnp.int32, shape, 0)
            - lax.broadcasted_iota(jnp.int32, shape, 1)
            + (window(block, nodes) - first)
        )
        value = jnp.where(jnp.abs(offset) == GX, along, 0.0)
        value = jnp.where(offset == -1, left, value)
        value = jnp.where(offset == 1, right, value)
        value = jnp.where(offset == 0, 1.0, value)
        out_ref[block] = value.astype(BF16)
        return carry

    lax.fori_loop(0, nodes // BLOCK, fill, 0)


def coupling(node_class):
    nodes = node_class.shape[0]
    vmem = pl.BlockSpec(memory_space=pltpu.VMEM)
    return pl.pallas_call(
        weight_kernel,
        out_shape=jax.ShapeDtypeStruct((nodes // BLOCK, SPAN, BLOCK), BF16),
        in_specs=[vmem],
        out_specs=vmem,
        compiler_params=pltpu.CompilerParams(vmem_limit_bytes=6 * MIB),
        cost_estimate=LIGHT,
        name="coupling",
    )(node_class.reshape(1, nodes))


def couple_kernel(first, rate_ref, weight_ref, pivot_ref, out_ref):
    rows, nodes = out_ref.shape

    def block_of(block, carry):
        source = pl.ds(window(block, nodes), SPAN)
        target = pl.ds(pl.multiple_of(block * BLOCK, BLOCK), BLOCK)
        value = jnp.dot(
            pivot_ref[first : first + rows, source], weight_ref[block], preferred_element_type=F32
        )
        out_ref[:, target] = (rate_ref[0] * value).astype(BF16)
        return carry

    lax.fori_loop(0, nodes // BLOCK, block_of, 0)


def couple(pivot, weights, rate, part=0, parts=1):
    rows, nodes = pivot.shape[0] // parts, pivot.shape[1]
    vmem = pl.BlockSpec(memory_space=pltpu.VMEM)
    return pl.pallas_call(
        functools.partial(couple_kernel, part * rows),
        out_shape=jax.ShapeDtypeStruct((rows, nodes), BF16),
        in_specs=[pl.BlockSpec(memory_space=pltpu.SMEM), vmem, vmem],
        out_specs=vmem,
        compiler_params=pltpu.CompilerParams(vmem_limit_bytes=8 * MIB),
        cost_estimate=LIGHT,
        name="couple",
    )(rate, weights, pivot)


def turned(block, odd):
    return block + odd * (3 - 2 * block)


def route(source, target, doms):
    pairs = []
    for dom in range(doms):
        odd = dom % 2
        pairs.append((dom * 4 + turned(source, odd), dom * 4 + turned(target, odd)))
    return pairs


def moved(value, source, target):
    return lax.ppermute(value, ("dom", "col"), route(source, target, lax.axis_size("dom")))


def couple_here(place, pivot, weights, rate):
    def kernel(place_ref, *refs):
        @pl.when(place_ref[1] == 1)
        def _():
            couple_kernel(0, *refs)

    scalars, vmem = pl.BlockSpec(memory_space=pltpu.SMEM), pl.BlockSpec(memory_space=pltpu.VMEM)
    return pl.pallas_call(
        kernel,
        out_shape=jax.ShapeDtypeStruct(pivot.shape, BF16),
        in_specs=[scalars, scalars, vmem, vmem],
        out_specs=vmem,
        compiler_params=pltpu.CompilerParams(vmem_limit_bytes=8 * MIB),
        cost_estimate=LIGHT,
        name="couple_here",
    )(place, rate, weights, pivot)


def turn_kernel(place_ref, coupled_ref, *refs):
    @pl.when(place_ref[1] == 1)
    def _():
        refs[-1][...] = coupled_ref[...].T


def turn(place, panel, part, coupled, across):
    rows, nodes = coupled.shape
    chunk = 128
    steps = rows // chunk
    ratio = nodes // 4 // chunk
    return pl.pallas_call(
        turn_kernel,
        out_shape=jax.ShapeDtypeStruct((nodes, nodes), BF16),
        grid_spec=pltpu.PrefetchScalarGridSpec(
            num_scalar_prefetch=1,
            grid=(steps,),
            in_specs=[pl.BlockSpec((chunk, nodes), lambda i, place: (i, 0))]
            + ([] if across is None else [pl.BlockSpec(memory_space=pl.ANY)]),
            out_specs=pl.BlockSpec(
                (nodes, chunk),
                lambda i, place: (0, turned(panel, place[0]) * ratio + part * steps + i),
            ),
        ),
        input_output_aliases={} if across is None else {2: 0},
        compiler_params=pltpu.CompilerParams(vmem_limit_bytes=4 * MIB),
        cost_estimate=LIGHT,
        name="turn",
    )(place, coupled, *(() if across is None else (across,)))


def multiply_kernel(first, count, lefts, place_ref, *refs):
    left_refs, right_ref, out_ref = refs[:lefts], refs[lefts], refs[-1]
    width = right_ref.shape[0] // 4

    @pl.when(place_ref[1] == 1)
    def _():
        def block(step, carry):
            source = pl.multiple_of((first(place_ref[0]) + step) * width, 128)
            target = pl.multiple_of(step * width, 128)
            row = 0
            for left_ref in left_refs:
                rows = left_ref.shape[0]
                out_ref[row : row + rows, pl.ds(target, width)] = jnp.dot(
                    left_ref[...], right_ref[:, pl.ds(source, width)], preferred_element_type=F32
                ).astype(BF16)
                row += rows
            return carry

        lax.fori_loop(0, count, block, 0)


def multiply(place, lefts, right, first=lambda odd: 0, count=4):
    rows = sum(left.shape[0] for left in lefts)
    width = right.shape[0] // 4
    vmem = pl.BlockSpec(memory_space=pltpu.VMEM)
    return pl.pallas_call(
        functools.partial(multiply_kernel, first, count, len(lefts)),
        out_shape=jax.ShapeDtypeStruct((rows, count * width), BF16),
        in_specs=[pl.BlockSpec(memory_space=pltpu.SMEM)] + [vmem] * (len(lefts) + 1),
        out_specs=vmem,
        compiler_params=pltpu.CompilerParams(vmem_limit_bytes=6 * MIB),
        cost_estimate=LIGHT,
        name="multiply",
    )(place, *lefts, right)


def pack(value, out_ref, column):
    quarter = value.shape[1] // 4
    for part in range(4):
        rows = pl.ds(part * quarter, quarter)
        pack_rows(part, value[part * quarter : (part + 1) * quarter], out_ref.at[rows], column)


def two_kernel(place_ref, left_ref, right_ref, zero_ref, out_ref):
    odd = place_ref[0]
    width = right_ref.shape[0] // 4

    def product(block):
        columns = pl.ds(pl.multiple_of(block * width, 128), width)
        value = jnp.dot(left_ref[...], right_ref[:, columns], preferred_element_type=F32)
        return value.astype(BF16)

    @pl.when(place_ref[1] == 1)
    def _():
        out_ref[:, :width] = product(1 + odd)
        zero = pl.ds(pl.multiple_of((2 - 2 * odd) * width, 128), width)
        out_ref[:, width : 2 * width] = zero_ref[:, zero]
        pack(product(2 - odd), out_ref, 2 * width)


def product_two(place, half, across, zero):
    rows = half.shape[0]
    width = across.shape[0] // 4
    vmem = pl.BlockSpec(memory_space=pltpu.VMEM)
    return pl.pallas_call(
        two_kernel,
        out_shape=jax.ShapeDtypeStruct((rows, 11 * width // 4), BF16),
        in_specs=[pl.BlockSpec(memory_space=pltpu.SMEM)] + [vmem] * 3,
        out_specs=vmem,
        compiler_params=pltpu.CompilerParams(vmem_limit_bytes=6 * MIB),
        cost_estimate=LIGHT,
        name="product_two",
    )(place, half, across, zero)


def half_kernel(place_ref, left_ref, right_ref, one_ref, out_ref):
    width = one_ref.shape[1]

    @pl.when(place_ref[1] == 1)
    def _():
        def block(step, carry):
            which = turned(step + (step > 0).astype(jnp.int32), place_ref[0])
            columns = pl.ds(pl.multiple_of(which * width, 128), width)
            out_ref[:, columns] = jnp.dot(
                left_ref[...], right_ref[:, columns], preferred_element_type=F32
            ).astype(BF16)
            return carry

        lax.fori_loop(0, 3, block, 0)
        columns = pl.ds(pl.multiple_of(turned(1, place_ref[0]) * width, 128), width)
        out_ref[:, columns] = one_ref[...]


def half_product(place, left, right, one):
    vmem = pl.BlockSpec(memory_space=pltpu.VMEM)
    return pl.pallas_call(
        half_kernel,
        out_shape=jax.ShapeDtypeStruct(left.shape, BF16),
        in_specs=[pl.BlockSpec(memory_space=pltpu.SMEM)] + [vmem] * 3,
        out_specs=vmem,
        compiler_params=pltpu.CompilerParams(vmem_limit_bytes=6 * MIB),
        cost_estimate=LIGHT,
        name="half_product",
    )(place, left, right, one)


def column_kernel(place_ref, near_ref, other_ref, first_ref, second_ref, *refs):
    column_ref, out_refs = refs[0], refs[1:]

    @pl.when(place_ref[1] == 1)
    def _():
        odd = place_ref[0]
        width = near_ref.shape[0]
        for half, half_ref in ((1 - odd, near_ref), (odd, other_ref)):
            for block in range(2):
                rows = pl.ds(pl.multiple_of((2 * half + block) * width, 128), width)
                column_ref[rows, :] = half_ref[:, block * width : (block + 1) * width].T
        for left_ref, out_ref in zip((first_ref, second_ref), out_refs):
            out_ref[...] = jnp.dot(
                left_ref[...], column_ref[...], preferred_element_type=F32
            ).astype(BF16)


def own_column(place, near, other, first, second):
    rows, nodes = first.shape
    vmem = pl.BlockSpec(memory_space=pltpu.VMEM)
    return pl.pallas_call(
        column_kernel,
        out_shape=(
            jax.ShapeDtypeStruct((nodes, rows), BF16),
            jax.ShapeDtypeStruct((rows, rows), BF16),
            jax.ShapeDtypeStruct((rows, rows), BF16),
        ),
        in_specs=[pl.BlockSpec(memory_space=pltpu.SMEM)] + [vmem] * 4,
        out_specs=(vmem, vmem, vmem),
        compiler_params=pltpu.CompilerParams(vmem_limit_bytes=6 * MIB),
        cost_estimate=LIGHT,
        name="own_column",
    )(place, near, other, first, second)


def rest_kernel(place_ref, upper_ref, lower_ref, right_ref, zero_ref, out_ref, last_ref):
    odd = place_ref[0]
    width = zero_ref.shape[1]
    half = width // 2

    def product(left_ref, block):
        columns = pl.ds(pl.multiple_of(block * width, 128), width)
        value = jnp.dot(left_ref[...], right_ref[:, columns], preferred_element_type=F32)
        return value.astype(BF16)

    @pl.when(place_ref[1] == 1)
    def _():
        out_ref[:, pl.ds(pl.multiple_of(odd * width, 128), width)] = zero_ref[...].T
        other = pl.ds(pl.multiple_of((1 - odd) * width, 128), width)
        for part, left_ref in enumerate((upper_ref, lower_ref)):
            out_ref[pl.ds(part * half, half), other] = product(left_ref, 1 + odd)
            value = product(left_ref, 3 - 3 * odd)
            for quarter in range(2):
                start = quarter * half // 2
                rows = pl.ds(part * half + start, half // 2)
                rows_of = value[start : start + half // 2]
                pack_rows(2 * part + quarter, rows_of, last_ref.at[rows], 0)


def product_rest(place, halves, across, zero):
    rows, width = zero.shape
    vmem = pl.BlockSpec(memory_space=pltpu.VMEM)
    return pl.pallas_call(
        rest_kernel,
        out_shape=(
            jax.ShapeDtypeStruct((rows, 2 * width), BF16),
            jax.ShapeDtypeStruct((rows, 3 * width // 4), BF16),
        ),
        in_specs=[pl.BlockSpec(memory_space=pltpu.SMEM)] + [vmem] * 4,
        out_specs=(vmem, vmem),
        compiler_params=pltpu.CompilerParams(vmem_limit_bytes=6 * MIB),
        cost_estimate=LIGHT,
        name="product_rest",
    )(place, *halves, across, zero)


def pack_rows(part, value, out_ref, column):
    quarter, width = value.shape
    half = width // 2
    beside = (2, 3, 1, 0)[part] * quarter
    out_ref[:, column : column + half] = value[:, part // 2 * half : (part // 2 + 1) * half]
    out_ref[:, column + half : column + half + quarter] = value[:, beside : beside + quarter]


def unpacked_rows(part, packed_ref, column):
    quarter = packed_ref.shape[0] // 4
    half = 2 * quarter

    def beside(which):
        rows = slice(which * quarter, (which + 1) * quarter)
        return packed_ref[rows, column + half : column + half + quarter]

    rows = slice(part * quarter, (part + 1) * quarter)
    diagonal = packed_ref[rows, column : column + half]
    if part == 0:
        return diagonal, jnp.concatenate([beside(0), beside(3).T], axis=1)
    if part == 1:
        return diagonal, jnp.concatenate([beside(2).T, beside(1)], axis=1)
    if part == 2:
        return jnp.concatenate([beside(0).T, beside(2)], axis=1), diagonal
    return jnp.concatenate([beside(3), beside(1).T], axis=1), diagonal


def prior_kernel(place_ref, shifted_ref, sigma_ref, out_ref):
    @pl.when(place_ref[3] == 0)
    def _():
        out_ref[...] = shifted_ref[...]

    @pl.when(place_ref[3] != 0)
    def _():
        out_ref[...] = sigma_ref[...]


def halves_kernel(place_ref, first_ref, second_ref, near_ref, other_ref):
    near_ref[...] = first_ref[...]
    other_ref[...] = second_ref[...]


def halves(place, separator):
    rows, nodes = separator.shape
    chunk = rows // 4
    half = lambda side: pl.BlockSpec((chunk, nodes // 2), lambda i, place: (i, side(place[0])))
    out = jax.ShapeDtypeStruct((rows, nodes // 2), BF16)
    return pl.pallas_call(
        halves_kernel,
        out_shape=(out, out),
        grid_spec=pltpu.PrefetchScalarGridSpec(
            num_scalar_prefetch=1,
            grid=(4,),
            in_specs=[half(lambda odd: odd), half(lambda odd: 1 - odd)],
            out_specs=(half(lambda odd: 0), half(lambda odd: 0)),
        ),
        compiler_params=pltpu.CompilerParams(vmem_limit_bytes=6 * MIB),
        cost_estimate=LIGHT,
        name="halves",
    )(place, separator, separator)


def near_kernel(place_ref, shifted_ref, sigma_ref, row_ref, near_ref, last_ref):
    odd = place_ref[0]
    width = row_ref.shape[1] // 2
    prior_kernel(place_ref, shifted_ref, sigma_ref, row_ref)
    two = pl.ds(pl.multiple_of(odd * width, 128), width)
    three = pl.ds(pl.multiple_of((1 - odd) * width, 128), width)
    near_ref[:, :width] = row_ref[:, three]
    for part in range(4):

        @pl.when(pl.program_id(0) == part)
        def _():
            pack_rows(part, row_ref[:, two], near_ref, width)
            pack_rows(part, row_ref[:, three], last_ref, 0)


def other_half_kernel(place_ref, shifted_ref, sigma_ref, row_ref, far_ref):
    width = row_ref.shape[1] // 2
    prior_kernel(place_ref, shifted_ref, sigma_ref, row_ref)
    zero = pl.ds(pl.multiple_of(place_ref[0] * width, 128), width)
    for part in range(4):

        @pl.when(pl.program_id(0) == part)
        def _():
            pack_rows(part, row_ref[:, zero], far_ref, 0)


def prior_half(kernel, side, sent, place, shifted, sigma):
    rows, nodes = sigma.shape
    chunk = rows // 4
    quarters = (8,) + sent
    out = lambda count: jax.ShapeDtypeStruct((rows, count * nodes // 16), BF16)
    spec = lambda count: pl.BlockSpec((chunk, count * nodes // 16), lambda i, place: (i, 0))
    return pl.pallas_call(
        kernel,
        out_shape=tuple(out(count) for count in quarters),
        grid_spec=pltpu.PrefetchScalarGridSpec(
            num_scalar_prefetch=1,
            grid=(4,),
            in_specs=[
                pl.BlockSpec(
                    (chunk, nodes // 2), lambda i, place: (jnp.where(place[3] == 0, i, 0), 0)
                ),
                pl.BlockSpec(
                    (chunk, nodes // 2),
                    lambda i, place: (jnp.where(place[3] == 0, 0, i), side(place[0])),
                ),
            ],
            out_specs=tuple(spec(count) for count in quarters),
        ),
        compiler_params=pltpu.CompilerParams(vmem_limit_bytes=6 * MIB),
        cost_estimate=LIGHT,
        name="prior_half",
    )(place, shifted, sigma)


def assemble_kernel(place_ref, near, other, column, near_two, last_three, near_zero, far_zero, out_ref):
    @pl.when(place_ref[1] == 1)
    def _():
        odd = place_ref[0]
        width = near.shape[0]
        half, quarter = width // 2, width // 4

        def at(block, count=1):
            return pl.ds(pl.multiple_of(block * width, 128), count * width)

        first = 2 * (1 - odd)
        row = [turned(block, odd) for block in range(4)]
        out_ref[at(row[1]), at(first, 2)] = near[...]
        out_ref[at(row[1]), at(2 * odd, 2)] = other[...]
        out_ref[at(row[2]), at(row[3])] = near_two[:, :width]
        out_ref[at(row[3]), at(row[2])] = near_two[:, :width].T
        out_ref[at(row[0]), at(first, 2)] = near_zero[...]
        for step in range(2):
            out_ref[at(first + step), at(row[0])] = near_zero[:, step * width : (1 + step) * width].T
        for block in (0, 2, 3):
            out_ref[at(row[block]), at(row[1])] = column[at(row[block]), :]
        packed = ((0, far_zero, 0), (2, near_two, width), (3, last_three, 0))
        for block, packed_ref, start in packed:
            for part in range(4):
                rows = pl.ds(pl.multiple_of(row[block] * width + part * quarter, 128), quarter)
                for side, value in enumerate(unpacked_rows(part, packed_ref, start)):
                    columns = pl.ds(pl.multiple_of(row[block] * width + side * half, 128), half)
                    out_ref[rows, columns] = value


def assemble(place, *parts):
    nodes = 2 * parts[0].shape[1]
    vmem = pl.BlockSpec(memory_space=pltpu.VMEM)
    return pl.pallas_call(
        assemble_kernel,
        out_shape=jax.ShapeDtypeStruct((nodes, nodes), BF16),
        in_specs=[pl.BlockSpec(memory_space=pltpu.SMEM)] + [vmem] * 7,
        out_specs=vmem,
        compiler_params=pltpu.CompilerParams(vmem_limit_bytes=6 * MIB),
        cost_estimate=LIGHT,
        name="assemble",
    )(place, *parts)


def tick(place, *values, cost=HEAVY):
    def kernel(place_ref, *refs):
        for which in range(place.shape[0]):
            refs[-1][which] = place_ref[which]

    scalars = pl.BlockSpec(memory_space=pltpu.SMEM)
    return pl.pallas_call(
        kernel,
        out_shape=jax.ShapeDtypeStruct(place.shape, place.dtype),
        in_specs=[scalars] + [pl.BlockSpec(memory_space=pl.ANY)] * len(values),
        out_specs=scalars,
        compiler_params=pltpu.CompilerParams(vmem_limit_bytes=MIB),
        cost_estimate=cost,
        name="tick",
    )(place, *values)


def finish_kernel(
    place_ref, pivot_ref, sigma_ref,
    q0, q0_last, q2, q3_two,
    q01, q11, q21, q31,
    out_ref, var_ref,
):
    rows, nodes = pivot_ref.shape
    width = nodes // 4
    odd, place = place_ref[0], place_ref[1]
    here = pl.multiple_of(pl.program_id(0) * rows, 128)
    diagonal = diagonal_of(rows)

    def at(block, count=1):
        return pl.ds(pl.multiple_of(block * width, 128), count * width)

    def own(block):
        return pl.ds(pl.multiple_of(block * width + here, 128), rows)

    def add(columns, product):
        out_ref[:, columns] = (pivot_ref[:, columns].astype(F32) + product.astype(F32)).astype(BF16)

    def trace(product):
        var_ref[...] = diagonal(
            pivot_ref[:, own(place_ref[2])].astype(F32) + product.astype(F32)
        )

    active = place_ref[4] != 0

    @pl.when(active & (place == 0))
    def _():
        add(at(odd, 3), q0[...])
        add(at(turned(3, odd)), q0_last[...])
        trace(q0[:, own(2 * odd)])

    @pl.when(active & (place == 1))
    def _():
        add(at(turned(0, odd)), q01[...].T)
        add(at(turned(1, odd)), q11[...])
        add(at(turned(2, odd)), q21[...].T)
        add(at(turned(3, odd)), q31[...].T)
        trace(q11[:, pl.ds(here, rows)])

    @pl.when(active & (place == 2))
    def _():
        add(at(turned(0, odd)), q2[pl.ds(0, width), pl.ds(pl.multiple_of(width + here, 128), rows)].T)
        add(at(turned(1, odd)), q2[pl.ds(here, rows), pl.ds(0, width)])
        start = pl.program_id(0) % 2 * rows + 2 * width
        trace(q2[pl.ds(here, rows), pl.ds(pl.multiple_of(start, 128), rows)])
        for part in range(4):

            @pl.when(pl.program_id(0) == part)
            def _():
                for side, value in enumerate(unpacked_rows(part, q2, 2 * width)):
                    start = turned(2, odd) * width + side * width // 2
                    add(pl.ds(pl.multiple_of(start, 128), width // 2), value)

    @pl.when(active & (place == 3))
    def _():
        add(at(turned(2, odd)), q3_two[...])

    @pl.when(place_ref[4] == 0)
    def _():
        out_ref[...] = sigma_ref[...]
        var_ref[...] = diagonal(sigma_ref[:, own(place_ref[2])].astype(F32))


def finish(place, pivot, sigma, received, kept):
    rows, nodes = pivot.shape
    chunk = 128
    width = nodes // 4

    def picked(which, blocks):
        return pl.BlockSpec(
            (chunk, blocks * width), lambda i, place: (jnp.where(place[1] == which, i, 0), 0)
        )

    def turned_block(start):
        return pl.BlockSpec(
            (rows, chunk),
            lambda i, place: (
                0,
                jnp.where(place[1] == 1, start(place[0]) * (width // chunk) + i, 0),
            ),
        )

    return pl.pallas_call(
        finish_kernel,
        out_shape=(
            jax.ShapeDtypeStruct((rows, nodes), BF16),
            jax.ShapeDtypeStruct((1, rows), F32),
        ),
        grid_spec=pltpu.PrefetchScalarGridSpec(
            num_scalar_prefetch=1,
            grid=(rows // chunk,),
            in_specs=[
                pl.BlockSpec((chunk, nodes), lambda i, place: (i, 0)),
                pl.BlockSpec(
                    (chunk, nodes), lambda i, place: (jnp.where(place[4] == 0, i, 0), 0)
                ),
                picked(0, 3),
                picked(0, 1),
                pl.BlockSpec((rows, 11 * width // 4), lambda i, place: (0, 0)),
                picked(3, 1),
                turned_block(lambda odd: 1),
                picked(1, 1),
                turned_block(lambda odd: 0),
                turned_block(lambda odd: 1 - odd),
            ],
            out_specs=(
                pl.BlockSpec((chunk, nodes), lambda i, place: (i, 0)),
                pl.BlockSpec((1, chunk), lambda i, place: (0, i)),
            ),
        ),
        compiler_params=pltpu.CompilerParams(vmem_limit_bytes=12 * MIB),
        cost_estimate=HEAVY,
        name="finish",
    )(place, pivot, sigma, *received, *kept)


def add_in_place(pivot_ref, out_ref, sum_ref, sems, column, product):
    chunk = pivot_ref.shape[0] // 4
    copies = []
    for part in range(4):
        here = pl.ds(part * chunk, chunk)
        value = pivot_ref[here, :].astype(F32) + product(part, here).astype(F32)
        sum_ref[here, :] = value.astype(BF16)
        copies.append(
            pltpu.make_async_copy(sum_ref.at[here], out_ref.at[here, column], sems.at[part])
        )
        copies[-1].start()
    for copy in copies:
        copy.wait()


def other_kernel(place_ref, pivot_ref, q3_other, old_ref, out_ref, sum_ref, sems):
    both = pivot_ref.shape[1]
    column = pl.ds(pl.multiple_of(place_ref[0] * both, 128), both)

    @pl.when((place_ref[4] != 0) & (place_ref[1] == 3))
    def _():
        add_in_place(
            pivot_ref, out_ref, sum_ref, sems, column, lambda part, here: q3_other[here, :]
        )


def last_kernel(
    place_ref, pivot_ref, q2_last, q3_last, old_ref, old_var_ref, out_ref, var_ref, sum_ref, sems
):
    rows, width = pivot_ref.shape
    chunk = rows // 4
    active = place_ref[4] != 0
    column = pl.ds(pl.multiple_of(turned(3, place_ref[0]) * width, 128), width)
    add = functools.partial(add_in_place, pivot_ref, out_ref, sum_ref, sems, column)
    var_ref[...] = old_var_ref[...]

    @pl.when(active & (place_ref[1] == 2))
    def _():
        add(lambda part, here: q2_last[:, here].T)

    @pl.when(active & (place_ref[1] == 3))
    def _():
        add(lambda part, here: jnp.concatenate(unpacked_rows(part, q3_last, 0), axis=1))
        for start in range(0, rows, chunk):
            here = pl.ds(start, chunk)
            value = pivot_ref[here, here].astype(F32)
            value = value + q3_last[here, pl.ds(start % (2 * chunk), chunk)].astype(F32)
            var_ref[:, here] = diagonal_of(chunk)(value)


def diagonal_of(rows):
    square = (rows, rows)
    on_diagonal = lax.broadcasted_iota(jnp.int32, square, 0) == lax.broadcasted_iota(
        jnp.int32, square, 1
    )
    return lambda value: jnp.sum(jnp.where(on_diagonal, value, 0.0), axis=0, keepdims=True)


def finish_other(place, pivot, q3_other, covariance):
    rows, nodes = pivot.shape
    vmem = pl.BlockSpec(memory_space=pltpu.VMEM)
    anywhere = pl.BlockSpec(memory_space=pl.ANY)
    return pl.pallas_call(
        other_kernel,
        out_shape=jax.ShapeDtypeStruct((rows, nodes), BF16),
        grid_spec=pltpu.PrefetchScalarGridSpec(
            num_scalar_prefetch=1,
            grid=(1,),
            in_specs=[
                pl.BlockSpec((rows, nodes // 2), lambda i, place: (0, place[0])),
                vmem,
                anywhere,
            ],
            out_specs=anywhere,
            scratch_shapes=[pltpu.VMEM((rows, nodes // 2), BF16), pltpu.SemaphoreType.DMA((4,))],
        ),
        input_output_aliases={3: 0},
        compiler_params=pltpu.CompilerParams(vmem_limit_bytes=8 * MIB),
        cost_estimate=LIGHT,
        name="finish_other",
    )(place, pivot, q3_other, covariance)


def finish_last(place, pivot, q2_last, q3_last, covariance, variances):
    rows, nodes = pivot.shape
    vmem = pl.BlockSpec(memory_space=pltpu.VMEM)
    anywhere = pl.BlockSpec(memory_space=pl.ANY)
    return pl.pallas_call(
        last_kernel,
        out_shape=(
            jax.ShapeDtypeStruct((rows, nodes), BF16),
            jax.ShapeDtypeStruct((1, rows), F32),
        ),
        grid_spec=pltpu.PrefetchScalarGridSpec(
            num_scalar_prefetch=1,
            grid=(1,),
            in_specs=[
                pl.BlockSpec((rows, nodes // 4), lambda i, place: (0, turned(3, place[0]))),
                vmem,
                vmem,
                anywhere,
                vmem,
            ],
            out_specs=(anywhere, vmem),
            scratch_shapes=[pltpu.VMEM((rows, nodes // 4), BF16), pltpu.SemaphoreType.DMA((4,))],
        ),
        input_output_aliases={4: 0},
        compiler_params=pltpu.CompilerParams(vmem_limit_bytes=8 * MIB),
        cost_estimate=LIGHT,
        name="finish_last",
    )(place, pivot, q2_last, q3_last, covariance, variances)


def owned(sigma_next, separator, inverse_pivot, coupling_rate, lengths, step_index, node_class):
    sigma, pivot = sigma_next[0], inverse_pivot[0]
    odd = lax.axis_index("dom") % 2
    col = lax.axis_index("col")
    step = step_index[0]
    place = jnp.stack([odd, turned(col, odd), col, step, step < lengths[0]]).astype(jnp.int32)
    after = lambda value, *others: lax.optimization_barrier((value, *others))[0]

    p2 = moved(pivot, 2, 1)
    p0 = moved(pivot, 0, 1)
    weights = coupling(node_class)
    c1 = [couple(pivot, weights, coupling_rate, part, 2) for part in range(2)]
    across = turn(place, 1, 0, c1[0], None)
    across = turn(place, 1, 1, c1[1], across)

    near, other = halves(place, separator[0])
    near, other = passed_along(near, "dom", -1), passed_along(other, "dom", -1)
    sides = (lambda odd: 1 - odd, lambda odd: odd)
    row_near, near, last = prior_half(
        near_kernel, sides[0], (7, 3), place, after(near, across), sigma
    )
    near_zero, near_two = moved(row_near, 0, 1), moved(near, 2, 1)
    last_three = moved(last, 3, 1)
    c2 = couple_here(place, after(p2, last), weights, coupling_rate)
    across = turn(place, 2, 0, c2, across)
    c0 = couple_here(place, after(p0, across), weights, coupling_rate)
    across = turn(place, 0, 0, c0, across)
    row_other, far = prior_half(
        other_half_kernel, sides[1], (3,), place, after(other, across), sigma
    )
    far_zero = moved(far, 0, 1)
    column, h0_one, h2_one = own_column(place, row_near, row_other, c0, c2)
    c3 = [
        moved(after(c1[0], last_three, near_two, near_zero, across), 3, 1),
        moved(after(c1[1], far_zero, h2_one), 3, 1),
    ]
    prior = assemble(place, row_near, row_other, column, near_two, last_three, near_zero, far_zero)

    h0 = half_product(place, c0, prior, h0_one)
    q0_own = multiply(place, [h0], across, lambda odd: odd, 3)
    q0 = moved(q0_own, 1, 0)
    h2 = half_product(place, after(c2, q0_own), prior, h2_one)
    q2_own = product_two(place, h2, across, q0_own)
    q2 = moved(q2_own, 1, 2)

    across = turn(place, 3, 0, c3[0], after(across, q2_own))
    upper = multiply(place, [c3[0]], prior)
    across = turn(place, 3, 1, c3[1], after(across, upper))
    q03 = multiply(place, [h0], across, lambda odd: 3 - 3 * odd, 1)
    q0_last = moved(q03, 1, 0)
    h3 = [upper, multiply(place, [after(c3[1], q03)], prior)]
    q32 = multiply(place, h3, across, lambda odd: 2 - odd, 1)
    q3_two = moved(q32, 1, 3)
    q3_own, q33 = product_rest(place, h3, across, after(q03, q32))
    q3_other, q3_last = moved(q3_own, 1, 3), moved(q33, 1, 3)
    h1 = multiply(place, [after(c1[0], q3_own), c1[1]], prior)
    q11 = multiply(place, [h1], across, lambda odd: 1 + odd, 1)
    received = (q0, q0_last, q2, q3_two)
    kept = (q0_own, q11, q2_own, q3_own)
    place_then = tick(tick(place, q0, cost=LIGHT), q0_last, cost=MEDIUM)
    q2_last = moved(after(q3_two, place_then), 3, 2)
    covariance, variances = finish(place_then, pivot, sigma, received, kept)
    covariance = finish_other(place, pivot, q3_other, covariance)
    covariance, variances = finish_last(place, pivot, q2_last, q3_last, covariance, variances)
    return (covariance[None], variances)


def gathered(sigma_next, separator, inverse_pivot, coupling_rate, lengths, step_index, node_class):
    shifted = passed_along(separator, "dom", -1)
    prior = jnp.where(step_index[0] == 0, shifted[0], sigma_next[0])
    pivot = inverse_pivot[0].astype(F32)
    coupled = couple(inverse_pivot[0], coupling(node_class), coupling_rate)
    rows = coupled.shape[0]
    half = jnp.dot(
        coupled,
        lax.all_gather(prior, "col", axis=0, tiled=True),
        preferred_element_type=F32,
    ).astype(BF16)
    product = lax.dot_general(
        half,
        lax.all_gather(coupled, "col", axis=0, tiled=True),
        (((1,), (1,)), ((), ())),
        preferred_element_type=F32,
    )
    full = pivot + product
    active = step_index[0] < lengths[0]
    old = sigma_next[0]
    covariance = jnp.where(active, full.astype(BF16), old)
    first_col = lax.axis_index("col") * rows
    new_block = lax.dynamic_slice_in_dim(full, first_col, rows, 1)
    old_block = lax.dynamic_slice_in_dim(old, first_col, rows, 1)
    variances = jnp.where(active, jnp.diagonal(new_block), jnp.diagonal(old_block).astype(F32))
    return (covariance[None], variances[None])


def solution(mesh):
    local = owned if mesh.shape["col"] == 4 and mesh.shape["dom"] % 2 == 0 else gathered
    return jax.shard_map(
        local,
        mesh=mesh,
        in_specs=(
            P(("groups", "dom"), "col", None),
            P(("groups", "dom"), "col", None),
            P(("groups", "dom"), "col", None),
            P(("groups", "dom")),
            P(("groups", "dom")),
            P(("groups", "dom")),
            P("groups"),
        ),
        out_specs=(P(("groups", "dom"), "col", None), P(("groups", "dom"), "col")),
        check_vma=False,
    )
```

```python
import functools

import jax
import jax.numpy as jnp
from jax import lax
from jax.experimental import pallas as pl
from jax.experimental.pallas import tpu as pltpu
from jax.sharding import PartitionSpec as P

GX = 64
GY = 32
BF16 = jnp.bfloat16
F32 = jnp.float32
MIB = 1 << 20


def passed_along(value, axis, steps):
    count = lax.axis_size(axis)
    initial, last = (max(0, -steps), min(count, count - steps))
    return lax.ppermute(value, axis, [(source, source + steps) for source in range(initial, last)])


LIGHT = pl.CostEstimate(flops=1 << 20, bytes_accessed=1 << 16, transcendentals=0)
MEDIUM = pl.CostEstimate(flops=2000000000, bytes_accessed=1 << 16, transcendentals=0)
HEAVY = pl.CostEstimate(flops=14000000000, bytes_accessed=1 << 16, transcendentals=0)


BLOCK = 256
SPAN = 512


def window(block, nodes):
    return pl.multiple_of(jnp.clip(block * BLOCK - (SPAN - BLOCK) // 2, 0, nodes - SPAN), 128)


def weight_kernel(class_ref, out_ref):
    nodes = class_ref.shape[1]

    def fill(block, carry):
        first = pl.multiple_of(block * BLOCK, BLOCK)
        kind = class_ref[:, pl.ds(first, BLOCK)]
        across = jnp.where(
            kind == 0, 0.25, jnp.where(kind == 1, 0.375, jnp.where(kind == 2, 0.125, 0.5))
        ).astype(F32)
        along = jnp.where(
            kind == 0, 0.25, jnp.where(kind == 1, 0.125, jnp.where(kind == 2, 0.375, 0.0))
        ).astype(F32)
        column = (first + lax.broadcasted_iota(jnp.int32, (1, BLOCK), 1)) % GX
        left = jnp.where(column > 0, across, 0.0)
        right = jnp.where(column < GX - 1, across, 0.0)
        shape = (SPAN, BLOCK)
        offset = (
            lax.broadcasted_iota(jnp.int32, shape, 0)
            - lax.broadcasted_iota(jnp.int32, shape, 1)
            + (window(block, nodes) - first)
        )
        value = jnp.where(jnp.abs(offset) == GX, along, 0.0)
        value = jnp.where(offset == -1, left, value)
        value = jnp.where(offset == 1, right, value)
        value = jnp.where(offset == 0, 1.0, value)
        out_ref[block] = value.astype(BF16)
        return carry

    lax.fori_loop(0, nodes // BLOCK, fill, 0)


def coupling(node_class):
    nodes = node_class.shape[0]
    vmem = pl.BlockSpec(memory_space=pltpu.VMEM)
    return pl.pallas_call(
        weight_kernel,
        out_shape=jax.ShapeDtypeStruct((nodes // BLOCK, SPAN, BLOCK), BF16),
        in_specs=[vmem],
        out_specs=vmem,
        compiler_params=pltpu.CompilerParams(vmem_limit_bytes=6 * MIB),
        cost_estimate=LIGHT,
        name="coupling",
    )(node_class.reshape(1, nodes))


def couple_kernel(first, rate_ref, weight_ref, pivot_ref, out_ref):
    rows, nodes = out_ref.shape

    def block_of(block, carry):
        source = pl.ds(window(block, nodes), SPAN)
        target = pl.ds(pl.multiple_of(block * BLOCK, BLOCK), BLOCK)
        value = jnp.dot(
            pivot_ref[first : first + rows, source], weight_ref[block], preferred_element_type=F32
        )
        out_ref[:, target] = (rate_ref[0] * value).astype(BF16)
        return carry

    lax.fori_loop(0, nodes // BLOCK, block_of, 0)


def couple(pivot, weights, rate, part=0, parts=1):
    rows, nodes = pivot.shape[0] // parts, pivot.shape[1]
    vmem = pl.BlockSpec(memory_space=pltpu.VMEM)
    return pl.pallas_call(
        functools.partial(couple_kernel, part * rows),
        out_shape=jax.ShapeDtypeStruct((rows, nodes), BF16),
        in_specs=[pl.BlockSpec(memory_space=pltpu.SMEM), vmem, vmem],
        out_specs=vmem,
        compiler_params=pltpu.CompilerParams(vmem_limit_bytes=8 * MIB),
        cost_estimate=LIGHT,
        name="couple",
    )(rate, weights, pivot)


def turned(block, odd):
    return block + odd * (3 - 2 * block)


def route(source, target, doms):
    pairs = []
    for dom in range(doms):
        odd = dom % 2
        pairs.append((dom * 4 + turned(source, odd), dom * 4 + turned(target, odd)))
    return pairs


def moved(value, source, target):
    return lax.ppermute(value, ("dom", "col"), route(source, target, lax.axis_size("dom")))


def couple_here(place, pivot, weights, rate):
    def kernel(place_ref, *refs):
        @pl.when(place_ref[1] == 1)
        def _():
            couple_kernel(0, *refs)

    scalars, vmem = pl.BlockSpec(memory_space=pltpu.SMEM), pl.BlockSpec(memory_space=pltpu.VMEM)
    return pl.pallas_call(
        kernel,
        out_shape=jax.ShapeDtypeStruct(pivot.shape, BF16),
        in_specs=[scalars, scalars, vmem, vmem],
        out_specs=vmem,
        compiler_params=pltpu.CompilerParams(vmem_limit_bytes=8 * MIB),
        cost_estimate=LIGHT,
        name="couple_here",
    )(place, rate, weights, pivot)


def turn_kernel(place_ref, coupled_ref, *refs):
    @pl.when(place_ref[1] == 1)
    def _():
        refs[-1][...] = coupled_ref[...].T


def turn(place, panel, part, coupled, across):
    rows, nodes = coupled.shape
    chunk = 128
    steps = rows // chunk
    ratio = nodes // 4 // chunk
    return pl.pallas_call(
        turn_kernel,
        out_shape=jax.ShapeDtypeStruct((nodes, nodes), BF16),
        grid_spec=pltpu.PrefetchScalarGridSpec(
            num_scalar_prefetch=1,
            grid=(steps,),
            in_specs=[pl.BlockSpec((chunk, nodes), lambda i, place: (i, 0))]
            + ([] if across is None else [pl.BlockSpec(memory_space=pl.ANY)]),
            out_specs=pl.BlockSpec(
                (nodes, chunk),
                lambda i, place: (0, turned(panel, place[0]) * ratio + part * steps + i),
            ),
        ),
        input_output_aliases={} if across is None else {2: 0},
        compiler_params=pltpu.CompilerParams(vmem_limit_bytes=4 * MIB),
        cost_estimate=LIGHT,
        name="turn",
    )(place, coupled, *(() if across is None else (across,)))


def multiply_kernel(first, count, lefts, place_ref, *refs):
    left_refs, right_ref, out_ref = refs[:lefts], refs[lefts], refs[-1]
    width = right_ref.shape[0] // 4

    @pl.when(place_ref[1] == 1)
    def _():
        def block(step, carry):
            source = pl.multiple_of((first(place_ref[0]) + step) * width, 128)
            target = pl.multiple_of(step * width, 128)
            row = 0
            for left_ref in left_refs:
                rows = left_ref.shape[0]
                out_ref[row : row + rows, pl.ds(target, width)] = jnp.dot(
                    left_ref[...], right_ref[:, pl.ds(source, width)], preferred_element_type=F32
                ).astype(BF16)
                row += rows
            return carry

        lax.fori_loop(0, count, block, 0)


def multiply(place, lefts, right, first=lambda odd: 0, count=4):
    rows = sum(left.shape[0] for left in lefts)
    width = right.shape[0] // 4
    vmem = pl.BlockSpec(memory_space=pltpu.VMEM)
    return pl.pallas_call(
        functools.partial(multiply_kernel, first, count, len(lefts)),
        out_shape=jax.ShapeDtypeStruct((rows, count * width), BF16),
        in_specs=[pl.BlockSpec(memory_space=pltpu.SMEM)] + [vmem] * (len(lefts) + 1),
        out_specs=vmem,
        compiler_params=pltpu.CompilerParams(vmem_limit_bytes=6 * MIB),
        cost_estimate=LIGHT,
        name="multiply",
    )(place, *lefts, right)


def pack(value, out_ref, column):
    quarter = value.shape[1] // 4
    for part in range(4):
        rows = pl.ds(part * quarter, quarter)
        pack_rows(part, value[part * quarter : (part + 1) * quarter], out_ref.at[rows], column)


def two_kernel(place_ref, left_ref, right_ref, zero_ref, out_ref):
    odd = place_ref[0]
    width = right_ref.shape[0] // 4

    def product(block):
        columns = pl.ds(pl.multiple_of(block * width, 128), width)
        value = jnp.dot(left_ref[...], right_ref[:, columns], preferred_element_type=F32)
        return value.astype(BF16)

    @pl.when(place_ref[1] == 1)
    def _():
        out_ref[:, :width] = product(1 + odd)
        zero = pl.ds(pl.multiple_of((2 - 2 * odd) * width, 128), width)
        out_ref[:, width : 2 * width] = zero_ref[:, zero]
        pack(product(2 - odd), out_ref, 2 * width)


def product_two(place, half, across, zero):
    rows = half.shape[0]
    width = across.shape[0] // 4
    vmem = pl.BlockSpec(memory_space=pltpu.VMEM)
    return pl.pallas_call(
        two_kernel,
        out_shape=jax.ShapeDtypeStruct((rows, 11 * width // 4), BF16),
        in_specs=[pl.BlockSpec(memory_space=pltpu.SMEM)] + [vmem] * 3,
        out_specs=vmem,
        compiler_params=pltpu.CompilerParams(vmem_limit_bytes=6 * MIB),
        cost_estimate=LIGHT,
        name="product_two",
    )(place, half, across, zero)


def half_kernel(place_ref, left_ref, right_ref, one_ref, out_ref):
    width = one_ref.shape[1]

    @pl.when(place_ref[1] == 1)
    def _():
        def block(step, carry):
            which = turned(step + (step > 0).astype(jnp.int32), place_ref[0])
            columns = pl.ds(pl.multiple_of(which * width, 128), width)
            out_ref[:, columns] = jnp.dot(
                left_ref[...], right_ref[:, columns], preferred_element_type=F32
            ).astype(BF16)
            return carry

        lax.fori_loop(0, 3, block, 0)
        columns = pl.ds(pl.multiple_of(turned(1, place_ref[0]) * width, 128), width)
        out_ref[:, columns] = one_ref[...]


def half_product(place, left, right, one):
    vmem = pl.BlockSpec(memory_space=pltpu.VMEM)
    return pl.pallas_call(
        half_kernel,
        out_shape=jax.ShapeDtypeStruct(left.shape, BF16),
        in_specs=[pl.BlockSpec(memory_space=pltpu.SMEM)] + [vmem] * 3,
        out_specs=vmem,
        compiler_params=pltpu.CompilerParams(vmem_limit_bytes=6 * MIB),
        cost_estimate=LIGHT,
        name="half_product",
    )(place, left, right, one)


def column_kernel(place_ref, near_ref, other_ref, first_ref, second_ref, *refs):
    column_ref, out_refs = refs[0], refs[1:]

    @pl.when(place_ref[1] == 1)
    def _():
        odd = place_ref[0]
        width = near_ref.shape[0]
        for half, half_ref in ((1 - odd, near_ref), (odd, other_ref)):
            for block in range(2):
                rows = pl.ds(pl.multiple_of((2 * half + block) * width, 128), width)
                column_ref[rows, :] = half_ref[:, block * width : (block + 1) * width].T
        for left_ref, out_ref in zip((first_ref, second_ref), out_refs):
            out_ref[...] = jnp.dot(
                left_ref[...], column_ref[...], preferred_element_type=F32
            ).astype(BF16)


def own_column(place, near, other, first, second):
    rows, nodes = first.shape
    vmem = pl.BlockSpec(memory_space=pltpu.VMEM)
    return pl.pallas_call(
        column_kernel,
        out_shape=(
            jax.ShapeDtypeStruct((nodes, rows), BF16),
            jax.ShapeDtypeStruct((rows, rows), BF16),
            jax.ShapeDtypeStruct((rows, rows), BF16),
        ),
        in_specs=[pl.BlockSpec(memory_space=pltpu.SMEM)] + [vmem] * 4,
        out_specs=(vmem, vmem, vmem),
        compiler_params=pltpu.CompilerParams(vmem_limit_bytes=6 * MIB),
        cost_estimate=LIGHT,
        name="own_column",
    )(place, near, other, first, second)


def rest_kernel(place_ref, upper_ref, lower_ref, right_ref, zero_ref, out_ref, last_ref):
    odd = place_ref[0]
    width = zero_ref.shape[1]
    half = width // 2

    def product(left_ref, block):
        columns = pl.ds(pl.multiple_of(block * width, 128), width)
        value = jnp.dot(left_ref[...], right_ref[:, columns], preferred_element_type=F32)
        return value.astype(BF16)

    @pl.when(place_ref[1] == 1)
    def _():
        out_ref[:, pl.ds(pl.multiple_of(odd * width, 128), width)] = zero_ref[...].T
        other = pl.ds(pl.multiple_of((1 - odd) * width, 128), width)
        for part, left_ref in enumerate((upper_ref, lower_ref)):
            out_ref[pl.ds(part * half, half), other] = product(left_ref, 1 + odd)
            value = product(left_ref, 3 - 3 * odd)
            for quarter in range(2):
                start = quarter * half // 2
                rows = pl.ds(part * half + start, half // 2)
                rows_of = value[start : start + half // 2]
                pack_rows(2 * part + quarter, rows_of, last_ref.at[rows], 0)


def product_rest(place, halves, across, zero):
    rows, width = zero.shape
    vmem = pl.BlockSpec(memory_space=pltpu.VMEM)
    return pl.pallas_call(
        rest_kernel,
        out_shape=(
            jax.ShapeDtypeStruct((rows, 2 * width), BF16),
            jax.ShapeDtypeStruct((rows, 3 * width // 4), BF16),
        ),
        in_specs=[pl.BlockSpec(memory_space=pltpu.SMEM)] + [vmem] * 4,
        out_specs=(vmem, vmem),
        compiler_params=pltpu.CompilerParams(vmem_limit_bytes=6 * MIB),
        cost_estimate=LIGHT,
        name="product_rest",
    )(place, *halves, across, zero)


def pack_rows(part, value, out_ref, column):
    quarter, width = value.shape
    half = width // 2
    beside = (2, 3, 1, 0)[part] * quarter
    out_ref[:, column : column + half] = value[:, part // 2 * half : (part // 2 + 1) * half]
    out_ref[:, column + half : column + half + quarter] = value[:, beside : beside + quarter]


def unpacked_rows(part, packed_ref, column):
    quarter = packed_ref.shape[0] // 4
    half = 2 * quarter

    def beside(which):
        rows = slice(which * quarter, (which + 1) * quarter)
        return packed_ref[rows, column + half : column + half + quarter]

    rows = slice(part * quarter, (part + 1) * quarter)
    diagonal = packed_ref[rows, column : column + half]
    if part == 0:
        return diagonal, jnp.concatenate([beside(0), beside(3).T], axis=1)
    if part == 1:
        return diagonal, jnp.concatenate([beside(2).T, beside(1)], axis=1)
    if part == 2:
        return jnp.concatenate([beside(0).T, beside(2)], axis=1), diagonal
    return jnp.concatenate([beside(3), beside(1).T], axis=1), diagonal


def prior_kernel(place_ref, shifted_ref, sigma_ref, out_ref):
    @pl.when(place_ref[3] == 0)
    def _():
        out_ref[...] = shifted_ref[...]

    @pl.when(place_ref[3] != 0)
    def _():
        out_ref[...] = sigma_ref[...]


def halves_kernel(place_ref, first_ref, second_ref, near_ref, other_ref):
    near_ref[...] = first_ref[...]
    other_ref[...] = second_ref[...]


def halves(place, separator):
    rows, nodes = separator.shape
    chunk = rows // 4
    half = lambda side: pl.BlockSpec((chunk, nodes // 2), lambda i, place: (i, side(place[0])))
    out = jax.ShapeDtypeStruct((rows, nodes // 2), BF16)
    return pl.pallas_call(
        halves_kernel,
        out_shape=(out, out),
        grid_spec=pltpu.PrefetchScalarGridSpec(
            num_scalar_prefetch=1,
            grid=(4,),
            in_specs=[half(lambda odd: odd), half(lambda odd: 1 - odd)],
            out_specs=(half(lambda odd: 0), half(lambda odd: 0)),
        ),
        compiler_params=pltpu.CompilerParams(vmem_limit_bytes=6 * MIB),
        cost_estimate=LIGHT,
        name="halves",
    )(place, separator, separator)


def near_kernel(place_ref, shifted_ref, sigma_ref, row_ref, near_ref, last_ref):
    odd = place_ref[0]
    width = row_ref.shape[1] // 2
    prior_kernel(place_ref, shifted_ref, sigma_ref, row_ref)
    two = pl.ds(pl.multiple_of(odd * width, 128), width)
    three = pl.ds(pl.multiple_of((1 - odd) * width, 128), width)
    near_ref[:, :width] = row_ref[:, three]
    for part in range(4):

        @pl.when(pl.program_id(0) == part)
        def _():
            pack_rows(part, row_ref[:, two], near_ref, width)
            pack_rows(part, row_ref[:, three], last_ref, 0)


def other_half_kernel(place_ref, shifted_ref, sigma_ref, row_ref, far_ref):
    width = row_ref.shape[1] // 2
    prior_kernel(place_ref, shifted_ref, sigma_ref, row_ref)
    zero = pl.ds(pl.multiple_of(place_ref[0] * width, 128), width)
    for part in range(4):

        @pl.when(pl.program_id(0) == part)
        def _():
            pack_rows(part, row_ref[:, zero], far_ref, 0)


def prior_half(kernel, side, sent, place, shifted, sigma):
    rows, nodes = sigma.shape
    chunk = rows // 4
    quarters = (8,) + sent
    out = lambda count: jax.ShapeDtypeStruct((rows, count * nodes // 16), BF16)
    spec = lambda count: pl.BlockSpec((chunk, count * nodes // 16), lambda i, place: (i, 0))
    return pl.pallas_call(
        kernel,
        out_shape=tuple(out(count) for count in quarters),
        grid_spec=pltpu.PrefetchScalarGridSpec(
            num_scalar_prefetch=1,
            grid=(4,),
            in_specs=[
                pl.BlockSpec(
                    (chunk, nodes // 2), lambda i, place: (jnp.where(place[3] == 0, i, 0), 0)
                ),
                pl.BlockSpec(
                    (chunk, nodes // 2),
                    lambda i, place: (jnp.where(place[3] == 0, 0, i), side(place[0])),
                ),
            ],
            out_specs=tuple(spec(count) for count in quarters),
        ),
        compiler_params=pltpu.CompilerParams(vmem_limit_bytes=6 * MIB),
        cost_estimate=LIGHT,
        name="prior_half",
    )(place, shifted, sigma)


def assemble_kernel(place_ref, near, other, column, near_two, last_three, near_zero, far_zero, out_ref):
    @pl.when(place_ref[1] == 1)
    def _():
        odd = place_ref[0]
        width = near.shape[0]
        half, quarter = width // 2, width // 4

        def at(block, count=1):
            return pl.ds(pl.multiple_of(block * width, 128), count * width)

        first = 2 * (1 - odd)
        row = [turned(block, odd) for block in range(4)]
        out_ref[at(row[1]), at(first, 2)] = near[...]
        out_ref[at(row[1]), at(2 * odd, 2)] = other[...]
        out_ref[at(row[2]), at(row[3])] = near_two[:, :width]
        out_ref[at(row[3]), at(row[2])] = near_two[:, :width].T
        out_ref[at(row[0]), at(first, 2)] = near_zero[...]
        for step in range(2):
            out_ref[at(first + step), at(row[0])] = near_zero[:, step * width : (1 + step) * width].T
        for block in (0, 2, 3):
            out_ref[at(row[block]), at(row[1])] = column[at(row[block]), :]
        packed = ((0, far_zero, 0), (2, near_two, width), (3, last_three, 0))
        for block, packed_ref, start in packed:
            for part in range(4):
                rows = pl.ds(pl.multiple_of(row[block] * width + part * quarter, 128), quarter)
                for side, value in enumerate(unpacked_rows(part, packed_ref, start)):
                    columns = pl.ds(pl.multiple_of(row[block] * width + side * half, 128), half)
                    out_ref[rows, columns] = value


def assemble(place, *parts):
    nodes = 2 * parts[0].shape[1]
    vmem = pl.BlockSpec(memory_space=pltpu.VMEM)
    return pl.pallas_call(
        assemble_kernel,
        out_shape=jax.ShapeDtypeStruct((nodes, nodes), BF16),
        in_specs=[pl.BlockSpec(memory_space=pltpu.SMEM)] + [vmem] * 7,
        out_specs=vmem,
        compiler_params=pltpu.CompilerParams(vmem_limit_bytes=6 * MIB),
        cost_estimate=LIGHT,
        name="assemble",
    )(place, *parts)


def tick(place, *values, cost=HEAVY):
    def kernel(place_ref, *refs):
        for which in range(place.shape[0]):
            refs[-1][which] = place_ref[which]

    scalars = pl.BlockSpec(memory_space=pltpu.SMEM)
    return pl.pallas_call(
        kernel,
        out_shape=jax.ShapeDtypeStruct(place.shape, place.dtype),
        in_specs=[scalars] + [pl.BlockSpec(memory_space=pl.ANY)] * len(values),
        out_specs=scalars,
        compiler_params=pltpu.CompilerParams(vmem_limit_bytes=MIB),
        cost_estimate=cost,
        name="tick",
    )(place, *values)


def finish_kernel(
    place_ref, pivot_ref, sigma_ref,
    q0, q0_last, q2, q3_two,
    q01, q11, q21, q31,
    out_ref, var_ref,
):
    rows, nodes = pivot_ref.shape
    width = nodes // 4
    odd, place = place_ref[0], place_ref[1]
    here = pl.multiple_of(pl.program_id(0) * rows, 128)
    diagonal = diagonal_of(rows)

    def at(block, count=1):
        return pl.ds(pl.multiple_of(block * width, 128), count * width)

    def own(block):
        return pl.ds(pl.multiple_of(block * width + here, 128), rows)

    def add(columns, product):
        out_ref[:, columns] = (pivot_ref[:, columns].astype(F32) + product.astype(F32)).astype(BF16)

    def trace(product):
        var_ref[...] = diagonal(
            pivot_ref[:, own(place_ref[2])].astype(F32) + product.astype(F32)
        )

    active = place_ref[4] != 0

    @pl.when(active & (place == 0))
    def _():
        add(at(odd, 3), q0[...])
        add(at(turned(3, odd)), q0_last[...])
        trace(q0[:, own(2 * odd)])

    @pl.when(active & (place == 1))
    def _():
        add(at(turned(0, odd)), q01[...].T)
        add(at(turned(1, odd)), q11[...])
        add(at(turned(2, odd)), q21[...].T)
        add(at(turned(3, odd)), q31[...].T)
        trace(q11[:, pl.ds(here, rows)])

    @pl.when(active & (place == 2))
    def _():
        add(at(turned(0, odd)), q2[pl.ds(0, width), pl.ds(pl.multiple_of(width + here, 128), rows)].T)
        add(at(turned(1, odd)), q2[pl.ds(here, rows), pl.ds(0, width)])
        start = pl.program_id(0) % 2 * rows + 2 * width
        trace(q2[pl.ds(here, rows), pl.ds(pl.multiple_of(start, 128), rows)])
        for part in range(4):

            @pl.when(pl.program_id(0) == part)
            def _():
                for side, value in enumerate(unpacked_rows(part, q2, 2 * width)):
                    start = turned(2, odd) * width + side * width // 2
                    add(pl.ds(pl.multiple_of(start, 128), width // 2), value)

    @pl.when(active & (place == 3))
    def _():
        add(at(turned(2, odd)), q3_two[...])

    @pl.when(place_ref[4] == 0)
    def _():
        out_ref[...] = sigma_ref[...]
        var_ref[...] = diagonal(sigma_ref[:, own(place_ref[2])].astype(F32))


def finish(place, pivot, sigma, received, kept):
    rows, nodes = pivot.shape
    chunk = 128
    width = nodes // 4

    def picked(which, blocks):
        return pl.BlockSpec(
            (chunk, blocks * width), lambda i, place: (jnp.where(place[1] == which, i, 0), 0)
        )

    def turned_block(start):
        return pl.BlockSpec(
            (rows, chunk),
            lambda i, place: (
                0,
                jnp.where(place[1] == 1, start(place[0]) * (width // chunk) + i, 0),
            ),
        )

    return pl.pallas_call(
        finish_kernel,
        out_shape=(
            jax.ShapeDtypeStruct((rows, nodes), BF16),
            jax.ShapeDtypeStruct((1, rows), F32),
        ),
        grid_spec=pltpu.PrefetchScalarGridSpec(
            num_scalar_prefetch=1,
            grid=(rows // chunk,),
            in_specs=[
                pl.BlockSpec((chunk, nodes), lambda i, place: (i, 0)),
                pl.BlockSpec(
                    (chunk, nodes), lambda i, place: (jnp.where(place[4] == 0, i, 0), 0)
                ),
                picked(0, 3),
                picked(0, 1),
                pl.BlockSpec((rows, 11 * width // 4), lambda i, place: (0, 0)),
                picked(3, 1),
                turned_block(lambda odd: 1),
                picked(1, 1),
                turned_block(lambda odd: 0),
                turned_block(lambda odd: 1 - odd),
            ],
            out_specs=(
                pl.BlockSpec((chunk, nodes), lambda i, place: (i, 0)),
                pl.BlockSpec((1, chunk), lambda i, place: (0, i)),
            ),
        ),
        compiler_params=pltpu.CompilerParams(vmem_limit_bytes=12 * MIB),
        cost_estimate=HEAVY,
        name="finish",
    )(place, pivot, sigma, *received, *kept)


def add_in_place(pivot_ref, out_ref, sum_ref, sems, column, product):
    chunk = pivot_ref.shape[0] // 4
    copies = []
    for part in range(4):
        here = pl.ds(part * chunk, chunk)
        value = pivot_ref[here, :].astype(F32) + product(part, here).astype(F32)
        sum_ref[here, :] = value.astype(BF16)
        copies.append(
            pltpu.make_async_copy(sum_ref.at[here], out_ref.at[here, column], sems.at[part])
        )
        copies[-1].start()
    for copy in copies:
        copy.wait()


def other_kernel(place_ref, pivot_ref, q3_other, old_ref, out_ref, sum_ref, sems):
    both = pivot_ref.shape[1]
    column = pl.ds(pl.multiple_of(place_ref[0] * both, 128), both)

    @pl.when((place_ref[4] != 0) & (place_ref[1] == 3))
    def _():
        add_in_place(
            pivot_ref, out_ref, sum_ref, sems, column, lambda part, here: q3_other[here, :]
        )


def last_kernel(
    place_ref, pivot_ref, q2_last, q3_last, old_ref, old_var_ref, out_ref, var_ref, sum_ref, sems
):
    rows, width = pivot_ref.shape
    chunk = rows // 4
    active = place_ref[4] != 0
    column = pl.ds(pl.multiple_of(turned(3, place_ref[0]) * width, 128), width)
    add = functools.partial(add_in_place, pivot_ref, out_ref, sum_ref, sems, column)
    var_ref[...] = old_var_ref[...]

    @pl.when(active & (place_ref[1] == 2))
    def _():
        add(lambda part, here: q2_last[:, here].T)

    @pl.when(active & (place_ref[1] == 3))
    def _():
        add(lambda part, here: jnp.concatenate(unpacked_rows(part, q3_last, 0), axis=1))
        for start in range(0, rows, chunk):
            here = pl.ds(start, chunk)
            value = pivot_ref[here, here].astype(F32)
            value = value + q3_last[here, pl.ds(start % (2 * chunk), chunk)].astype(F32)
            var_ref[:, here] = diagonal_of(chunk)(value)


def diagonal_of(rows):
    square = (rows, rows)
    on_diagonal = lax.broadcasted_iota(jnp.int32, square, 0) == lax.broadcasted_iota(
        jnp.int32, square, 1
    )
    return lambda value: jnp.sum(jnp.where(on_diagonal, value, 0.0), axis=0, keepdims=True)


def finish_other(place, pivot, q3_other, covariance):
    rows, nodes = pivot.shape
    vmem = pl.BlockSpec(memory_space=pltpu.VMEM)
    anywhere = pl.BlockSpec(memory_space=pl.ANY)
    return pl.pallas_call(
        other_kernel,
        out_shape=jax.ShapeDtypeStruct((rows, nodes), BF16),
        grid_spec=pltpu.PrefetchScalarGridSpec(
            num_scalar_prefetch=1,
            grid=(1,),
            in_specs=[
                pl.BlockSpec((rows, nodes // 2), lambda i, place: (0, place[0])),
                vmem,
                anywhere,
            ],
            out_specs=anywhere,
            scratch_shapes=[pltpu.VMEM((rows, nodes // 2), BF16), pltpu.SemaphoreType.DMA((4,))],
        ),
        input_output_aliases={3: 0},
        compiler_params=pltpu.CompilerParams(vmem_limit_bytes=8 * MIB),
        cost_estimate=LIGHT,
        name="finish_other",
    )(place, pivot, q3_other, covariance)


def finish_last(place, pivot, q2_last, q3_last, covariance, variances):
    rows, nodes = pivot.shape
    vmem = pl.BlockSpec(memory_space=pltpu.VMEM)
    anywhere = pl.BlockSpec(memory_space=pl.ANY)
    return pl.pallas_call(
        last_kernel,
        out_shape=(
            jax.ShapeDtypeStruct((rows, nodes), BF16),
            jax.ShapeDtypeStruct((1, rows), F32),
        ),
        grid_spec=pltpu.PrefetchScalarGridSpec(
            num_scalar_prefetch=1,
            grid=(1,),
            in_specs=[
                pl.BlockSpec((rows, nodes // 4), lambda i, place: (0, turned(3, place[0]))),
                vmem,
                vmem,
                anywhere,
                vmem,
            ],
            out_specs=(anywhere, vmem),
            scratch_shapes=[pltpu.VMEM((rows, nodes // 4), BF16), pltpu.SemaphoreType.DMA((4,))],
        ),
        input_output_aliases={4: 0},
        compiler_params=pltpu.CompilerParams(vmem_limit_bytes=8 * MIB),
        cost_estimate=LIGHT,
        name="finish_last",
    )(place, pivot, q2_last, q3_last, covariance, variances)


def owned(sigma_next, separator, inverse_pivot, coupling_rate, lengths, step_index, node_class):
    sigma, pivot = sigma_next[0], inverse_pivot[0]
    odd = lax.axis_index("dom") % 2
    col = lax.axis_index("col")
    step = step_index[0]
    place = jnp.stack([odd, turned(col, odd), col, step, step < lengths[0]]).astype(jnp.int32)
    after = lambda value, *others: lax.optimization_barrier((value, *others))[0]

    p2 = moved(pivot, 2, 1)
    p0 = moved(pivot, 0, 1)
    weights = coupling(node_class)
    c1 = [couple(pivot, weights, coupling_rate, part, 2) for part in range(2)]
    across = turn(place, 1, 0, c1[0], None)
    across = turn(place, 1, 1, c1[1], across)

    near, other = halves(place, separator[0])
    near, other = passed_along(near, "dom", -1), passed_along(other, "dom", -1)
    sides = (lambda odd: 1 - odd, lambda odd: odd)
    row_near, near, last = prior_half(
        near_kernel, sides[0], (7, 3), place, after(near, across), sigma
    )
    near_zero, near_two = moved(row_near, 0, 1), moved(near, 2, 1)
    last_three = moved(last, 3, 1)
    c2 = couple_here(place, after(p2, last), weights, coupling_rate)
    across = turn(place, 2, 0, c2, across)
    row_other, far = prior_half(
        other_half_kernel, sides[1], (3,), place, after(other, across), sigma
    )
    far_zero = moved(far, 0, 1)
    c0 = couple_here(place, after(p0, across, far), weights, coupling_rate)
    across = turn(place, 0, 0, c0, across)
    column, h0_one, h2_one = own_column(place, row_near, row_other, c0, c2)
    c3 = [
        moved(after(c1[0], last_three, near_two, near_zero, across), 3, 1),
        moved(after(c1[1], far_zero, h2_one), 3, 1),
    ]
    prior = assemble(place, row_near, row_other, column, near_two, last_three, near_zero, far_zero)

    h0 = half_product(place, c0, prior, h0_one)
    q0_own = multiply(place, [h0], across, lambda odd: odd, 3)
    q0 = moved(q0_own, 1, 0)
    h2 = half_product(place, after(c2, q0_own), prior, h2_one)
    q2_own = product_two(place, h2, across, q0_own)
    q2 = moved(q2_own, 1, 2)

    across = turn(place, 3, 0, c3[0], after(across, q2_own))
    upper = multiply(place, [c3[0]], prior)
    across = turn(place, 3, 1, c3[1], after(across, upper))
    q03 = multiply(place, [h0], across, lambda odd: 3 - 3 * odd, 1)
    q0_last = moved(q03, 1, 0)
    h3 = [upper, multiply(place, [after(c3[1], q03)], prior)]
    q32 = multiply(place, h3, across, lambda odd: 2 - odd, 1)
    q3_two = moved(q32, 1, 3)
    q3_own, q33 = product_rest(place, h3, across, after(q03, q32))
    q3_other, q3_last = moved(q3_own, 1, 3), moved(q33, 1, 3)
    h1 = multiply(place, [after(c1[0], q3_own), c1[1]], prior)
    q11 = multiply(place, [h1], across, lambda odd: 1 + odd, 1)
    received = (q0, q0_last, q2, q3_two)
    kept = (q0_own, q11, q2_own, q3_own)
    place_then = tick(tick(place, q0, cost=LIGHT), q0_last, cost=MEDIUM)
    q2_last = moved(after(q3_two, place_then), 3, 2)
    covariance, variances = finish(place_then, pivot, sigma, received, kept)
    covariance = finish_other(place, pivot, q3_other, covariance)
    covariance, variances = finish_last(place, pivot, q2_last, q3_last, covariance, variances)
    return (covariance[None], variances)


def gathered(sigma_next, separator, inverse_pivot, coupling_rate, lengths, step_index, node_class):
    shifted = passed_along(separator, "dom", -1)
    prior = jnp.where(step_index[0] == 0, shifted[0], sigma_next[0])
    pivot = inverse_pivot[0].astype(F32)
    coupled = couple(inverse_pivot[0], coupling(node_class), coupling_rate)
    rows = coupled.shape[0]
    half = jnp.dot(
        coupled,
        lax.all_gather(prior, "col", axis=0, tiled=True),
        preferred_element_type=F32,
    ).astype(BF16)
    product = lax.dot_general(
        half,
        lax.all_gather(coupled, "col", axis=0, tiled=True),
        (((1,), (1,)), ((), ())),
        preferred_element_type=F32,
    )
    full = pivot + product
    active = step_index[0] < lengths[0]
    old = sigma_next[0]
    covariance = jnp.where(active, full.astype(BF16), old)
    first_col = lax.axis_index("col") * rows
    new_block = lax.dynamic_slice_in_dim(full, first_col, rows, 1)
    old_block = lax.dynamic_slice_in_dim(old, first_col, rows, 1)
    variances = jnp.where(active, jnp.diagonal(new_block), jnp.diagonal(old_block).astype(F32))
    return (covariance[None], variances[None])


def solution(mesh):
    local = owned if mesh.shape["col"] == 4 and mesh.shape["dom"] % 2 == 0 else gathered
    return jax.shard_map(
        local,
        mesh=mesh,
        in_specs=(
            P(("groups", "dom"), "col", None),
            P(("groups", "dom"), "col", None),
            P(("groups", "dom"), "col", None),
            P(("groups", "dom")),
            P(("groups", "dom")),
            P(("groups", "dom")),
            P("groups"),
        ),
        out_specs=(P(("groups", "dom"), "col", None), P(("groups", "dom"), "col")),
        check_vma=False,
    )
```

```python
import functools

import jax
import jax.numpy as jnp
from jax import lax
from jax.experimental import pallas as pl
from jax.experimental.pallas import tpu as pltpu
from jax.sharding import PartitionSpec as P

GX = 64
GY = 32
BF16 = jnp.bfloat16
F32 = jnp.float32
MIB = 1 << 20


def passed_along(value, axis, steps):
    count = lax.axis_size(axis)
    initial, last = (max(0, -steps), min(count, count - steps))
    return lax.ppermute(value, axis, [(source, source + steps) for source in range(initial, last)])


LIGHT = pl.CostEstimate(flops=1 << 20, bytes_accessed=1 << 16, transcendentals=0)
MEDIUM = pl.CostEstimate(flops=2000000000, bytes_accessed=1 << 16, transcendentals=0)
HEAVY = pl.CostEstimate(flops=14000000000, bytes_accessed=1 << 16, transcendentals=0)


BLOCK = 256
SPAN = 512


def window(block, nodes):
    return pl.multiple_of(jnp.clip(block * BLOCK - (SPAN - BLOCK) // 2, 0, nodes - SPAN), 128)


def weight_kernel(class_ref, out_ref):
    nodes = class_ref.shape[1]

    def fill(block, carry):
        first = pl.multiple_of(block * BLOCK, BLOCK)
        kind = class_ref[:, pl.ds(first, BLOCK)]
        across = jnp.where(
            kind == 0, 0.25, jnp.where(kind == 1, 0.375, jnp.where(kind == 2, 0.125, 0.5))
        ).astype(F32)
        along = jnp.where(
            kind == 0, 0.25, jnp.where(kind == 1, 0.125, jnp.where(kind == 2, 0.375, 0.0))
        ).astype(F32)
        column = (first + lax.broadcasted_iota(jnp.int32, (1, BLOCK), 1)) % GX
        left = jnp.where(column > 0, across, 0.0)
        right = jnp.where(column < GX - 1, across, 0.0)
        shape = (SPAN, BLOCK)
        offset = (
            lax.broadcasted_iota(jnp.int32, shape, 0)
            - lax.broadcasted_iota(jnp.int32, shape, 1)
            + (window(block, nodes) - first)
        )
        value = jnp.where(jnp.abs(offset) == GX, along, 0.0)
        value = jnp.where(offset == -1, left, value)
        value = jnp.where(offset == 1, right, value)
        value = jnp.where(offset == 0, 1.0, value)
        out_ref[block] = value.astype(BF16)
        return carry

    lax.fori_loop(0, nodes // BLOCK, fill, 0)


def coupling(node_class):
    nodes = node_class.shape[0]
    vmem = pl.BlockSpec(memory_space=pltpu.VMEM)
    return pl.pallas_call(
        weight_kernel,
        out_shape=jax.ShapeDtypeStruct((nodes // BLOCK, SPAN, BLOCK), BF16),
        in_specs=[vmem],
        out_specs=vmem,
        compiler_params=pltpu.CompilerParams(vmem_limit_bytes=6 * MIB),
        cost_estimate=LIGHT,
        name="coupling",
    )(node_class.reshape(1, nodes))


def couple_kernel(first, rate_ref, weight_ref, pivot_ref, out_ref):
    rows, nodes = out_ref.shape

    def block_of(block, carry):
        source = pl.ds(window(block, nodes), SPAN)
        target = pl.ds(pl.multiple_of(block * BLOCK, BLOCK), BLOCK)
        value = jnp.dot(
            pivot_ref[first : first + rows, source], weight_ref[block], preferred_element_type=F32
        )
        out_ref[:, target] = (rate_ref[0] * value).astype(BF16)
        return carry

    lax.fori_loop(0, nodes // BLOCK, block_of, 0)


def couple(pivot, weights, rate, part=0, parts=1):
    rows, nodes = pivot.shape[0] // parts, pivot.shape[1]
    vmem = pl.BlockSpec(memory_space=pltpu.VMEM)
    return pl.pallas_call(
        functools.partial(couple_kernel, part * rows),
        out_shape=jax.ShapeDtypeStruct((rows, nodes), BF16),
        in_specs=[pl.BlockSpec(memory_space=pltpu.SMEM), vmem, vmem],
        out_specs=vmem,
        compiler_params=pltpu.CompilerParams(vmem_limit_bytes=8 * MIB),
        cost_estimate=LIGHT,
        name="couple",
    )(rate, weights, pivot)


def turned(block, odd):
    return block + odd * (3 - 2 * block)


def route(source, target, doms):
    pairs = []
    for dom in range(doms):
        odd = dom % 2
        pairs.append((dom * 4 + turned(source, odd), dom * 4 + turned(target, odd)))
    return pairs


def moved(value, source, target):
    return lax.ppermute(value, ("dom", "col"), route(source, target, lax.axis_size("dom")))


def couple_here(place, pivot, weights, rate):
    def kernel(place_ref, *refs):
        @pl.when(place_ref[1] == 1)
        def _():
            couple_kernel(0, *refs)

    scalars, vmem = pl.BlockSpec(memory_space=pltpu.SMEM), pl.BlockSpec(memory_space=pltpu.VMEM)
    return pl.pallas_call(
        kernel,
        out_shape=jax.ShapeDtypeStruct(pivot.shape, BF16),
        in_specs=[scalars, scalars, vmem, vmem],
        out_specs=vmem,
        compiler_params=pltpu.CompilerParams(vmem_limit_bytes=8 * MIB),
        cost_estimate=LIGHT,
        name="couple_here",
    )(place, rate, weights, pivot)


def turn_kernel(place_ref, coupled_ref, *refs):
    @pl.when(place_ref[1] == 1)
    def _():
        refs[-1][...] = coupled_ref[...].T


def turn(place, panel, part, coupled, across):
    rows, nodes = coupled.shape
    chunk = 128
    steps = rows // chunk
    ratio = nodes // 4 // chunk
    return pl.pallas_call(
        turn_kernel,
        out_shape=jax.ShapeDtypeStruct((nodes, nodes), BF16),
        grid_spec=pltpu.PrefetchScalarGridSpec(
            num_scalar_prefetch=1,
            grid=(steps,),
            in_specs=[pl.BlockSpec((chunk, nodes), lambda i, place: (i, 0))]
            + ([] if across is None else [pl.BlockSpec(memory_space=pl.ANY)]),
            out_specs=pl.BlockSpec(
                (nodes, chunk),
                lambda i, place: (0, turned(panel, place[0]) * ratio + part * steps + i),
            ),
        ),
        input_output_aliases={} if across is None else {2: 0},
        compiler_params=pltpu.CompilerParams(vmem_limit_bytes=4 * MIB),
        cost_estimate=LIGHT,
        name="turn",
    )(place, coupled, *(() if across is None else (across,)))


def multiply_kernel(first, count, lefts, place_ref, *refs):
    left_refs, right_ref, out_ref = refs[:lefts], refs[lefts], refs[-1]
    width = right_ref.shape[0] // 4

    @pl.when(place_ref[1] == 1)
    def _():
        def block(step, carry):
            source = pl.multiple_of((first(place_ref[0]) + step) * width, 128)
            target = pl.multiple_of(step * width, 128)
            row = 0
            for left_ref in left_refs:
                rows = left_ref.shape[0]
                out_ref[row : row + rows, pl.ds(target, width)] = jnp.dot(
                    left_ref[...], right_ref[:, pl.ds(source, width)], preferred_element_type=F32
                ).astype(BF16)
                row += rows
            return carry

        lax.fori_loop(0, count, block, 0)


def multiply(place, lefts, right, first=lambda odd: 0, count=4):
    rows = sum(left.shape[0] for left in lefts)
    width = right.shape[0] // 4
    vmem = pl.BlockSpec(memory_space=pltpu.VMEM)
    return pl.pallas_call(
        functools.partial(multiply_kernel, first, count, len(lefts)),
        out_shape=jax.ShapeDtypeStruct((rows, count * width), BF16),
        in_specs=[pl.BlockSpec(memory_space=pltpu.SMEM)] + [vmem] * (len(lefts) + 1),
        out_specs=vmem,
        compiler_params=pltpu.CompilerParams(vmem_limit_bytes=6 * MIB),
        cost_estimate=LIGHT,
        name="multiply",
    )(place, *lefts, right)


def pack(value, out_ref, column):
    quarter = value.shape[1] // 4
    for part in range(4):
        rows = pl.ds(part * quarter, quarter)
        pack_rows(part, value[part * quarter : (part + 1) * quarter], out_ref.at[rows], column)


def two_kernel(place_ref, left_ref, right_ref, zero_ref, out_ref):
    odd = place_ref[0]
    width = right_ref.shape[0] // 4

    def product(block):
        columns = pl.ds(pl.multiple_of(block * width, 128), width)
        value = jnp.dot(left_ref[...], right_ref[:, columns], preferred_element_type=F32)
        return value.astype(BF16)

    @pl.when(place_ref[1] == 1)
    def _():
        out_ref[:, :width] = product(1 + odd)
        zero = pl.ds(pl.multiple_of((2 - 2 * odd) * width, 128), width)
        out_ref[:, width : 2 * width] = zero_ref[:, zero]
        pack(product(2 - odd), out_ref, 2 * width)


def product_two(place, half, across, zero):
    rows = half.shape[0]
    width = across.shape[0] // 4
    vmem = pl.BlockSpec(memory_space=pltpu.VMEM)
    return pl.pallas_call(
        two_kernel,
        out_shape=jax.ShapeDtypeStruct((rows, 11 * width // 4), BF16),
        in_specs=[pl.BlockSpec(memory_space=pltpu.SMEM)] + [vmem] * 3,
        out_specs=vmem,
        compiler_params=pltpu.CompilerParams(vmem_limit_bytes=6 * MIB),
        cost_estimate=LIGHT,
        name="product_two",
    )(place, half, across, zero)


def half_kernel(place_ref, left_ref, right_ref, one_ref, out_ref):
    width = one_ref.shape[1]

    @pl.when(place_ref[1] == 1)
    def _():
        def block(step, carry):
            which = turned(step + (step > 0).astype(jnp.int32), place_ref[0])
            columns = pl.ds(pl.multiple_of(which * width, 128), width)
            out_ref[:, columns] = jnp.dot(
                left_ref[...], right_ref[:, columns], preferred_element_type=F32
            ).astype(BF16)
            return carry

        lax.fori_loop(0, 3, block, 0)
        columns = pl.ds(pl.multiple_of(turned(1, place_ref[0]) * width, 128), width)
        out_ref[:, columns] = one_ref[...]


def half_product(place, left, right, one):
    vmem = pl.BlockSpec(memory_space=pltpu.VMEM)
    return pl.pallas_call(
        half_kernel,
        out_shape=jax.ShapeDtypeStruct(left.shape, BF16),
        in_specs=[pl.BlockSpec(memory_space=pltpu.SMEM)] + [vmem] * 3,
        out_specs=vmem,
        compiler_params=pltpu.CompilerParams(vmem_limit_bytes=6 * MIB),
        cost_estimate=LIGHT,
        name="half_product",
    )(place, left, right, one)


def column_kernel(place_ref, near_ref, other_ref, first_ref, second_ref, *refs):
    column_ref, out_refs = refs[0], refs[1:]

    @pl.when(place_ref[1] == 1)
    def _():
        odd = place_ref[0]
        width = near_ref.shape[0]
        for half, half_ref in ((1 - odd, near_ref), (odd, other_ref)):
            for block in range(2):
                rows = pl.ds(pl.multiple_of((2 * half + block) * width, 128), width)
                column_ref[rows, :] = half_ref[:, block * width : (block + 1) * width].T
        for left_ref, out_ref in zip((first_ref, second_ref), out_refs):
            out_ref[...] = jnp.dot(
                left_ref[...], column_ref[...], preferred_element_type=F32
            ).astype(BF16)


def own_column(place, near, other, first, second):
    rows, nodes = first.shape
    vmem = pl.BlockSpec(memory_space=pltpu.VMEM)
    return pl.pallas_call(
        column_kernel,
        out_shape=(
            jax.ShapeDtypeStruct((nodes, rows), BF16),
            jax.ShapeDtypeStruct((rows, rows), BF16),
            jax.ShapeDtypeStruct((rows, rows), BF16),
        ),
        in_specs=[pl.BlockSpec(memory_space=pltpu.SMEM)] + [vmem] * 4,
        out_specs=(vmem, vmem, vmem),
        compiler_params=pltpu.CompilerParams(vmem_limit_bytes=6 * MIB),
        cost_estimate=LIGHT,
        name="own_column",
    )(place, near, other, first, second)


def rest_kernel(place_ref, upper_ref, lower_ref, right_ref, zero_ref, out_ref, last_ref):
    odd = place_ref[0]
    width = zero_ref.shape[1]
    half = width // 2

    def product(left_ref, block):
        columns = pl.ds(pl.multiple_of(block * width, 128), width)
        value = jnp.dot(left_ref[...], right_ref[:, columns], preferred_element_type=F32)
        return value.astype(BF16)

    @pl.when(place_ref[1] == 1)
    def _():
        out_ref[:, pl.ds(pl.multiple_of(odd * width, 128), width)] = zero_ref[...].T
        other = pl.ds(pl.multiple_of((1 - odd) * width, 128), width)
        for part, left_ref in enumerate((upper_ref, lower_ref)):
            out_ref[pl.ds(part * half, half), other] = product(left_ref, 1 + odd)
            value = product(left_ref, 3 - 3 * odd)
            for quarter in range(2):
                start = quarter * half // 2
                rows = pl.ds(part * half + start, half // 2)
                rows_of = value[start : start + half // 2]
                pack_rows(2 * part + quarter, rows_of, last_ref.at[rows], 0)


def product_rest(place, halves, across, zero):
    rows, width = zero.shape
    vmem = pl.BlockSpec(memory_space=pltpu.VMEM)
    return pl.pallas_call(
        rest_kernel,
        out_shape=(
            jax.ShapeDtypeStruct((rows, 2 * width), BF16),
            jax.ShapeDtypeStruct((rows, 3 * width // 4), BF16),
        ),
        in_specs=[pl.BlockSpec(memory_space=pltpu.SMEM)] + [vmem] * 4,
        out_specs=(vmem, vmem),
        compiler_params=pltpu.CompilerParams(vmem_limit_bytes=6 * MIB),
        cost_estimate=LIGHT,
        name="product_rest",
    )(place, *halves, across, zero)


def pack_rows(part, value, out_ref, column):
    quarter, width = value.shape
    half = width // 2
    beside = (2, 3, 1, 0)[part] * quarter
    out_ref[:, column : column + half] = value[:, part // 2 * half : (part // 2 + 1) * half]
    out_ref[:, column + half : column + half + quarter] = value[:, beside : beside + quarter]


def unpacked_rows(part, packed_ref, column):
    quarter = packed_ref.shape[0] // 4
    half = 2 * quarter

    def beside(which):
        rows = slice(which * quarter, (which + 1) * quarter)
        return packed_ref[rows, column + half : column + half + quarter]

    rows = slice(part * quarter, (part + 1) * quarter)
    diagonal = packed_ref[rows, column : column + half]
    if part == 0:
        return diagonal, jnp.concatenate([beside(0), beside(3).T], axis=1)
    if part == 1:
        return diagonal, jnp.concatenate([beside(2).T, beside(1)], axis=1)
    if part == 2:
        return jnp.concatenate([beside(0).T, beside(2)], axis=1), diagonal
    return jnp.concatenate([beside(3), beside(1).T], axis=1), diagonal


def prior_kernel(place_ref, shifted_ref, sigma_ref, out_ref):
    @pl.when(place_ref[3] == 0)
    def _():
        out_ref[...] = shifted_ref[...]

    @pl.when(place_ref[3] != 0)
    def _():
        out_ref[...] = sigma_ref[...]


def halves_kernel(place_ref, separator_ref, near_ref, other_ref, sems):
    half = near_ref.shape[1]
    copies = []
    for which, (side, out_ref) in enumerate(((place_ref[0], near_ref), (1 - place_ref[0], other_ref))):
        source = separator_ref.at[:, pl.ds(pl.multiple_of(side * half, 128), half)]
        copies.append(pltpu.make_async_copy(source, out_ref, sems.at[which]))
        copies[-1].start()
    for copy in copies:
        copy.wait()


def halves(place, separator):
    rows, nodes = separator.shape
    vmem = pl.BlockSpec(memory_space=pltpu.VMEM)
    return pl.pallas_call(
        halves_kernel,
        out_shape=(jax.ShapeDtypeStruct((rows, nodes // 2), BF16),) * 2,
        in_specs=[pl.BlockSpec(memory_space=pltpu.SMEM), pl.BlockSpec(memory_space=pl.ANY)],
        out_specs=(vmem, vmem),
        scratch_shapes=[pltpu.SemaphoreType.DMA((2,))],
        compiler_params=pltpu.CompilerParams(vmem_limit_bytes=6 * MIB),
        cost_estimate=LIGHT,
        name="halves",
    )(place, separator)


def near_kernel(place_ref, shifted_ref, sigma_ref, row_ref, near_ref, last_ref):
    odd = place_ref[0]
    width = row_ref.shape[1] // 2
    prior_kernel(place_ref, shifted_ref, sigma_ref, row_ref)
    two = pl.ds(pl.multiple_of(odd * width, 128), width)
    three = pl.ds(pl.multiple_of((1 - odd) * width, 128), width)
    near_ref[:, :width] = row_ref[:, three]
    for part in range(4):

        @pl.when(pl.program_id(0) == part)
        def _():
            pack_rows(part, row_ref[:, two], near_ref, width)
            pack_rows(part, row_ref[:, three], last_ref, 0)


def other_half_kernel(place_ref, shifted_ref, sigma_ref, row_ref, far_ref):
    width = row_ref.shape[1] // 2
    prior_kernel(place_ref, shifted_ref, sigma_ref, row_ref)
    zero = pl.ds(pl.multiple_of(place_ref[0] * width, 128), width)
    for part in range(4):

        @pl.when(pl.program_id(0) == part)
        def _():
            pack_rows(part, row_ref[:, zero], far_ref, 0)


def prior_half(kernel, side, sent, place, shifted, sigma):
    rows, nodes = sigma.shape
    chunk = rows // 4
    quarters = (8,) + sent
    out = lambda count: jax.ShapeDtypeStruct((rows, count * nodes // 16), BF16)
    spec = lambda count: pl.BlockSpec((chunk, count * nodes // 16), lambda i, place: (i, 0))
    return pl.pallas_call(
        kernel,
        out_shape=tuple(out(count) for count in quarters),
        grid_spec=pltpu.PrefetchScalarGridSpec(
            num_scalar_prefetch=1,
            grid=(4,),
            in_specs=[
                pl.BlockSpec(
                    (chunk, nodes // 2), lambda i, place: (jnp.where(place[3] == 0, i, 0), 0)
                ),
                pl.BlockSpec(
                    (chunk, nodes // 2),
                    lambda i, place: (jnp.where(place[3] == 0, 0, i), side(place[0])),
                ),
            ],
            out_specs=tuple(spec(count) for count in quarters),
        ),
        compiler_params=pltpu.CompilerParams(vmem_limit_bytes=6 * MIB),
        cost_estimate=LIGHT,
        name="prior_half",
    )(place, shifted, sigma)


def assemble_kernel(place_ref, near, other, column, near_two, last_three, near_zero, far_zero, out_ref):
    @pl.when(place_ref[1] == 1)
    def _():
        odd = place_ref[0]
        width = near.shape[0]
        half, quarter = width // 2, width // 4

        def at(block, count=1):
            return pl.ds(pl.multiple_of(block * width, 128), count * width)

        first = 2 * (1 - odd)
        row = [turned(block, odd) for block in range(4)]
        out_ref[at(row[1]), at(first, 2)] = near[...]
        out_ref[at(row[1]), at(2 * odd, 2)] = other[...]
        out_ref[at(row[2]), at(row[3])] = near_two[:, :width]
        out_ref[at(row[3]), at(row[2])] = near_two[:, :width].T
        out_ref[at(row[0]), at(first, 2)] = near_zero[...]
        for step in range(2):
            out_ref[at(first + step), at(row[0])] = near_zero[:, step * width : (1 + step) * width].T
        for block in (0, 2, 3):
            out_ref[at(row[block]), at(row[1])] = column[at(row[block]), :]
        packed = ((0, far_zero, 0), (2, near_two, width), (3, last_three, 0))
        for block, packed_ref, start in packed:
            for part in range(4):
                rows = pl.ds(pl.multiple_of(row[block] * width + part * quarter, 128), quarter)
                for side, value in enumerate(unpacked_rows(part, packed_ref, start)):
                    columns = pl.ds(pl.multiple_of(row[block] * width + side * half, 128), half)
                    out_ref[rows, columns] = value


def assemble(place, *parts):
    nodes = 2 * parts[0].shape[1]
    vmem = pl.BlockSpec(memory_space=pltpu.VMEM)
    return pl.pallas_call(
        assemble_kernel,
        out_shape=jax.ShapeDtypeStruct((nodes, nodes), BF16),
        in_specs=[pl.BlockSpec(memory_space=pltpu.SMEM)] + [vmem] * 7,
        out_specs=vmem,
        compiler_params=pltpu.CompilerParams(vmem_limit_bytes=6 * MIB),
        cost_estimate=LIGHT,
        name="assemble",
    )(place, *parts)


def tick(place, *values, cost=HEAVY):
    def kernel(place_ref, *refs):
        for which in range(place.shape[0]):
            refs[-1][which] = place_ref[which]

    scalars = pl.BlockSpec(memory_space=pltpu.SMEM)
    return pl.pallas_call(
        kernel,
        out_shape=jax.ShapeDtypeStruct(place.shape, place.dtype),
        in_specs=[scalars] + [pl.BlockSpec(memory_space=pl.ANY)] * len(values),
        out_specs=scalars,
        compiler_params=pltpu.CompilerParams(vmem_limit_bytes=MIB),
        cost_estimate=cost,
        name="tick",
    )(place, *values)


def finish_kernel(
    place_ref, pivot_ref, sigma_ref,
    q0, q0_last, q2, q3_two,
    q01, q11, q21, q31,
    out_ref, var_ref,
):
    rows, nodes = pivot_ref.shape
    width = nodes // 4
    odd, place = place_ref[0], place_ref[1]
    here = pl.multiple_of(pl.program_id(0) * rows, 128)
    diagonal = diagonal_of(rows)

    def at(block, count=1):
        return pl.ds(pl.multiple_of(block * width, 128), count * width)

    def own(block):
        return pl.ds(pl.multiple_of(block * width + here, 128), rows)

    def add(columns, product):
        out_ref[:, columns] = (pivot_ref[:, columns].astype(F32) + product.astype(F32)).astype(BF16)

    def trace(product):
        var_ref[...] = diagonal(
            pivot_ref[:, own(place_ref[2])].astype(F32) + product.astype(F32)
        )

    active = place_ref[4] != 0

    @pl.when(active & (place == 0))
    def _():
        add(at(odd, 3), q0[...])
        add(at(turned(3, odd)), q0_last[...])
        trace(q0[:, own(2 * odd)])

    @pl.when(active & (place == 1))
    def _():
        add(at(turned(0, odd)), q01[...].T)
        add(at(turned(1, odd)), q11[...])
        add(at(turned(2, odd)), q21[...].T)
        add(at(turned(3, odd)), q31[...].T)
        trace(q11[:, pl.ds(here, rows)])

    @pl.when(active & (place == 2))
    def _():
        add(at(turned(0, odd)), q2[pl.ds(0, width), pl.ds(pl.multiple_of(width + here, 128), rows)].T)
        add(at(turned(1, odd)), q2[pl.ds(here, rows), pl.ds(0, width)])
        start = pl.program_id(0) % 2 * rows + 2 * width
        trace(q2[pl.ds(here, rows), pl.ds(pl.multiple_of(start, 128), rows)])
        for part in range(4):

            @pl.when(pl.program_id(0) == part)
            def _():
                for side, value in enumerate(unpacked_rows(part, q2, 2 * width)):
                    start = turned(2, odd) * width + side * width // 2
                    add(pl.ds(pl.multiple_of(start, 128), width // 2), value)

    @pl.when(active & (place == 3))
    def _():
        add(at(turned(2, odd)), q3_two[...])

    @pl.when(place_ref[4] == 0)
    def _():
        out_ref[...] = sigma_ref[...]
        var_ref[...] = diagonal(sigma_ref[:, own(place_ref[2])].astype(F32))


def finish(place, pivot, sigma, received, kept):
    rows, nodes = pivot.shape
    chunk = 128
    width = nodes // 4

    def picked(which, blocks):
        return pl.BlockSpec(
            (chunk, blocks * width), lambda i, place: (jnp.where(place[1] == which, i, 0), 0)
        )

    def turned_block(start):
        return pl.BlockSpec(
            (rows, chunk),
            lambda i, place: (
                0,
                jnp.where(place[1] == 1, start(place[0]) * (width // chunk) + i, 0),
            ),
        )

    return pl.pallas_call(
        finish_kernel,
        out_shape=(
            jax.ShapeDtypeStruct((rows, nodes), BF16),
            jax.ShapeDtypeStruct((1, rows), F32),
        ),
        grid_spec=pltpu.PrefetchScalarGridSpec(
            num_scalar_prefetch=1,
            grid=(rows // chunk,),
            in_specs=[
                pl.BlockSpec((chunk, nodes), lambda i, place: (i, 0)),
                pl.BlockSpec(
                    (chunk, nodes), lambda i, place: (jnp.where(place[4] == 0, i, 0), 0)
                ),
                picked(0, 3),
                picked(0, 1),
                pl.BlockSpec((rows, 11 * width // 4), lambda i, place: (0, 0)),
                picked(3, 1),
                turned_block(lambda odd: 1),
                picked(1, 1),
                turned_block(lambda odd: 0),
                turned_block(lambda odd: 1 - odd),
            ],
            out_specs=(
                pl.BlockSpec((chunk, nodes), lambda i, place: (i, 0)),
                pl.BlockSpec((1, chunk), lambda i, place: (0, i)),
            ),
        ),
        compiler_params=pltpu.CompilerParams(vmem_limit_bytes=12 * MIB),
        cost_estimate=HEAVY,
        name="finish",
    )(place, pivot, sigma, *received, *kept)


def add_in_place(pivot_ref, out_ref, sum_ref, sems, column, product):
    chunk = pivot_ref.shape[0] // 4
    copies = []
    for part in range(4):
        here = pl.ds(part * chunk, chunk)
        value = pivot_ref[here, :].astype(F32) + product(part, here).astype(F32)
        sum_ref[here, :] = value.astype(BF16)
        copies.append(
            pltpu.make_async_copy(sum_ref.at[here], out_ref.at[here, column], sems.at[part])
        )
        copies[-1].start()
    return copies


def other_kernel(place_ref, pivot_ref, q3_other, old_ref, out_ref, sum_ref, sems):
    both = pivot_ref.shape[1]
    column = pl.ds(pl.multiple_of(place_ref[0] * both, 128), both)

    @pl.when((place_ref[4] != 0) & (place_ref[1] == 3))
    def _():
        product = lambda part, here: q3_other[here, :]
        for copy in add_in_place(pivot_ref, out_ref, sum_ref, sems, column, product):
            copy.wait()


def last_kernel(
    place_ref, pivot_ref, q2_last, q3_last, old_ref, old_var_ref, out_ref, var_ref, sum_ref, sems
):
    rows, width = pivot_ref.shape
    chunk = rows // 4
    active = place_ref[4] != 0
    column = pl.ds(pl.multiple_of(turned(3, place_ref[0]) * width, 128), width)
    add = functools.partial(add_in_place, pivot_ref, out_ref, sum_ref, sems, column)
    var_ref[...] = old_var_ref[...]

    @pl.when(active & (place_ref[1] == 2))
    def _():
        for copy in add(lambda part, here: q2_last[:, here].T):
            copy.wait()

    @pl.when(active & (place_ref[1] == 3))
    def _():
        copies = add(lambda part, here: jnp.concatenate(unpacked_rows(part, q3_last, 0), axis=1))
        for start in range(0, rows, chunk):
            here = pl.ds(start, chunk)
            value = pivot_ref[here, here].astype(F32)
            value = value + q3_last[here, pl.ds(start % (2 * chunk), chunk)].astype(F32)
            var_ref[:, here] = diagonal_of(chunk)(value)
        for copy in copies:
            copy.wait()


def diagonal_of(rows):
    square = (rows, rows)
    on_diagonal = lax.broadcasted_iota(jnp.int32, square, 0) == lax.broadcasted_iota(
        jnp.int32, square, 1
    )
    return lambda value: jnp.sum(jnp.where(on_diagonal, value, 0.0), axis=0, keepdims=True)


def finish_other(place, pivot, q3_other, covariance):
    rows, nodes = pivot.shape
    vmem = pl.BlockSpec(memory_space=pltpu.VMEM)
    anywhere = pl.BlockSpec(memory_space=pl.ANY)
    return pl.pallas_call(
        other_kernel,
        out_shape=jax.ShapeDtypeStruct((rows, nodes), BF16),
        grid_spec=pltpu.PrefetchScalarGridSpec(
            num_scalar_prefetch=1,
            grid=(1,),
            in_specs=[
                pl.BlockSpec((rows, nodes // 2), lambda i, place: (0, place[0])),
                vmem,
                anywhere,
            ],
            out_specs=anywhere,
            scratch_shapes=[pltpu.VMEM((rows, nodes // 2), BF16), pltpu.SemaphoreType.DMA((4,))],
        ),
        input_output_aliases={3: 0},
        compiler_params=pltpu.CompilerParams(vmem_limit_bytes=8 * MIB),
        cost_estimate=LIGHT,
        name="finish_other",
    )(place, pivot, q3_other, covariance)


def finish_last(place, pivot, q2_last, q3_last, covariance, variances):
    rows, nodes = pivot.shape
    vmem = pl.BlockSpec(memory_space=pltpu.VMEM)
    anywhere = pl.BlockSpec(memory_space=pl.ANY)
    return pl.pallas_call(
        last_kernel,
        out_shape=(
            jax.ShapeDtypeStruct((rows, nodes), BF16),
            jax.ShapeDtypeStruct((1, rows), F32),
        ),
        grid_spec=pltpu.PrefetchScalarGridSpec(
            num_scalar_prefetch=1,
            grid=(1,),
            in_specs=[
                pl.BlockSpec((rows, nodes // 4), lambda i, place: (0, turned(3, place[0]))),
                vmem,
                vmem,
                anywhere,
                vmem,
            ],
            out_specs=(anywhere, vmem),
            scratch_shapes=[pltpu.VMEM((rows, nodes // 4), BF16), pltpu.SemaphoreType.DMA((4,))],
        ),
        input_output_aliases={4: 0},
        compiler_params=pltpu.CompilerParams(vmem_limit_bytes=8 * MIB),
        cost_estimate=LIGHT,
        name="finish_last",
    )(place, pivot, q2_last, q3_last, covariance, variances)


def owned(sigma_next, separator, inverse_pivot, coupling_rate, lengths, step_index, node_class):
    sigma, pivot = sigma_next[0], inverse_pivot[0]
    odd = lax.axis_index("dom") % 2
    col = lax.axis_index("col")
    step = step_index[0]
    place = jnp.stack([odd, turned(col, odd), col, step, step < lengths[0]]).astype(jnp.int32)
    after = lambda value, *others: lax.optimization_barrier((value, *others))[0]

    p2 = moved(pivot, 2, 1)
    p0 = moved(pivot, 0, 1)
    weights = coupling(node_class)
    c1 = [couple(pivot, weights, coupling_rate, part, 2) for part in range(2)]
    across = turn(place, 1, 0, c1[0], None)
    across = turn(place, 1, 1, c1[1], across)

    near, other = halves(place, separator[0])
    near, other = passed_along(near, "dom", -1), passed_along(other, "dom", -1)
    sides = (lambda odd: 1 - odd, lambda odd: odd)
    row_near, near, last = prior_half(
        near_kernel, sides[0], (7, 3), place, after(near, across), sigma
    )
    near_zero, near_two = moved(row_near, 0, 1), moved(near, 2, 1)
    last_three = moved(last, 3, 1)
    c2 = couple_here(place, after(p2, last), weights, coupling_rate)
    across = turn(place, 2, 0, c2, across)
    row_other, far = prior_half(
        other_half_kernel, sides[1], (3,), place, after(other, across), sigma
    )
    far_zero = moved(far, 0, 1)
    c0 = couple_here(place, after(p0, across, far), weights, coupling_rate)
    across = turn(place, 0, 0, c0, across)
    column, h0_one, h2_one = own_column(place, row_near, row_other, c0, c2)
    c3 = [
        moved(after(c1[0], last_three, near_two, across), 3, 1),
        moved(after(c1[1], far_zero, h2_one), 3, 1),
    ]
    prior = assemble(place, row_near, row_other, column, near_two, last_three, near_zero, far_zero)

    h0 = half_product(place, c0, prior, h0_one)
    q0_own = multiply(place, [h0], across, lambda odd: odd, 3)
    q0 = moved(q0_own, 1, 0)
    h2 = half_product(place, after(c2, q0_own), prior, h2_one)
    q2_own = product_two(place, h2, across, q0_own)
    q2 = moved(q2_own, 1, 2)

    across = turn(place, 3, 0, c3[0], after(across, q2_own))
    upper = multiply(place, [c3[0]], prior)
    across = turn(place, 3, 1, c3[1], after(across, upper))
    q03 = multiply(place, [h0], across, lambda odd: 3 - 3 * odd, 1)
    q0_last = moved(q03, 1, 0)
    h3 = [upper, multiply(place, [after(c3[1], q03)], prior)]
    q32 = multiply(place, h3, across, lambda odd: 2 - odd, 1)
    q3_two = moved(q32, 1, 3)
    q3_own, q33 = product_rest(place, h3, across, after(q03, q32))
    q3_other, q3_last = moved(q3_own, 1, 3), moved(q33, 1, 3)
    h1 = multiply(place, [after(c1[0], q3_own), c1[1]], prior)
    q11 = multiply(place, [h1], across, lambda odd: 1 + odd, 1)
    received = (q0, q0_last, q2, q3_two)
    kept = (q0_own, q11, q2_own, q3_own)
    place_then = tick(tick(place, q0, cost=LIGHT), q0_last, cost=MEDIUM)
    q2_last = moved(after(q3_two, place_then), 3, 2)
    covariance, variances = finish(place_then, pivot, sigma, received, kept)
    covariance = finish_other(place, pivot, q3_other, covariance)
    covariance, variances = finish_last(place, pivot, q2_last, q3_last, covariance, variances)
    return (covariance[None], variances)


def gathered(sigma_next, separator, inverse_pivot, coupling_rate, lengths, step_index, node_class):
    shifted = passed_along(separator, "dom", -1)
    prior = jnp.where(step_index[0] == 0, shifted[0], sigma_next[0])
    pivot = inverse_pivot[0].astype(F32)
    coupled = couple(inverse_pivot[0], coupling(node_class), coupling_rate)
    rows = coupled.shape[0]
    half = jnp.dot(
        coupled,
        lax.all_gather(prior, "col", axis=0, tiled=True),
        preferred_element_type=F32,
    ).astype(BF16)
    product = lax.dot_general(
        half,
        lax.all_gather(coupled, "col", axis=0, tiled=True),
        (((1,), (1,)), ((), ())),
        preferred_element_type=F32,
    )
    full = pivot + product
    active = step_index[0] < lengths[0]
    old = sigma_next[0]
    covariance = jnp.where(active, full.astype(BF16), old)
    first_col = lax.axis_index("col") * rows
    new_block = lax.dynamic_slice_in_dim(full, first_col, rows, 1)
    old_block = lax.dynamic_slice_in_dim(old, first_col, rows, 1)
    variances = jnp.where(active, jnp.diagonal(new_block), jnp.diagonal(old_block).astype(F32))
    return (covariance[None], variances[None])


def solution(mesh):
    local = owned if mesh.shape["col"] == 4 and mesh.shape["dom"] % 2 == 0 else gathered
    return jax.shard_map(
        local,
        mesh=mesh,
        in_specs=(
            P(("groups", "dom"), "col", None),
            P(("groups", "dom"), "col", None),
            P(("groups", "dom"), "col", None),
            P(("groups", "dom")),
            P(("groups", "dom")),
            P(("groups", "dom")),
            P("groups"),
        ),
        out_specs=(P(("groups", "dom"), "col", None), P(("groups", "dom"), "col")),
        check_vma=False,
    )
```

```python
import functools

import jax
import jax.numpy as jnp
from jax import lax
from jax.experimental import pallas as pl
from jax.experimental.pallas import tpu as pltpu
from jax.sharding import PartitionSpec as P

GX = 64
GY = 32
BF16 = jnp.bfloat16
F32 = jnp.float32
MIB = 1 << 20


def passed_along(value, axis, steps):
    count = lax.axis_size(axis)
    initial, last = (max(0, -steps), min(count, count - steps))
    return lax.ppermute(value, axis, [(source, source + steps) for source in range(initial, last)])


LIGHT = pl.CostEstimate(flops=1 << 20, bytes_accessed=1 << 16, transcendentals=0)
MEDIUM = pl.CostEstimate(flops=2000000000, bytes_accessed=1 << 16, transcendentals=0)
HEAVY = pl.CostEstimate(flops=14000000000, bytes_accessed=1 << 16, transcendentals=0)


BLOCK = 256
SPAN = 512


def window(block, nodes):
    return pl.multiple_of(jnp.clip(block * BLOCK - (SPAN - BLOCK) // 2, 0, nodes - SPAN), 128)


def weight_kernel(class_ref, out_ref):
    nodes = class_ref.shape[1]

    def fill(block, carry):
        first = pl.multiple_of(block * BLOCK, BLOCK)
        kind = class_ref[:, pl.ds(first, BLOCK)]
        across = jnp.where(
            kind == 0, 0.25, jnp.where(kind == 1, 0.375, jnp.where(kind == 2, 0.125, 0.5))
        ).astype(F32)
        along = jnp.where(
            kind == 0, 0.25, jnp.where(kind == 1, 0.125, jnp.where(kind == 2, 0.375, 0.0))
        ).astype(F32)
        column = (first + lax.broadcasted_iota(jnp.int32, (1, BLOCK), 1)) % GX
        left = jnp.where(column > 0, across, 0.0)
        right = jnp.where(column < GX - 1, across, 0.0)
        shape = (SPAN, BLOCK)
        offset = (
            lax.broadcasted_iota(jnp.int32, shape, 0)
            - lax.broadcasted_iota(jnp.int32, shape, 1)
            + (window(block, nodes) - first)
        )
        value = jnp.where(jnp.abs(offset) == GX, along, 0.0)
        value = jnp.where(offset == -1, left, value)
        value = jnp.where(offset == 1, right, value)
        value = jnp.where(offset == 0, 1.0, value)
        out_ref[block] = value.astype(BF16)
        return carry

    lax.fori_loop(0, nodes // BLOCK, fill, 0)


def coupling(node_class):
    nodes = node_class.shape[0]
    vmem = pl.BlockSpec(memory_space=pltpu.VMEM)
    return pl.pallas_call(
        weight_kernel,
        out_shape=jax.ShapeDtypeStruct((nodes // BLOCK, SPAN, BLOCK), BF16),
        in_specs=[vmem],
        out_specs=vmem,
        compiler_params=pltpu.CompilerParams(vmem_limit_bytes=6 * MIB),
        cost_estimate=LIGHT,
        name="coupling",
    )(node_class.reshape(1, nodes))


def couple_kernel(first, rate_ref, weight_ref, pivot_ref, out_ref):
    rows, nodes = out_ref.shape

    def block_of(block, carry):
        source = pl.ds(window(block, nodes), SPAN)
        target = pl.ds(pl.multiple_of(block * BLOCK, BLOCK), BLOCK)
        value = jnp.dot(
            pivot_ref[first : first + rows, source], weight_ref[block], preferred_element_type=F32
        )
        out_ref[:, target] = (rate_ref[0] * value).astype(BF16)
        return carry

    lax.fori_loop(0, nodes // BLOCK, block_of, 0)


def couple(pivot, weights, rate, part=0, parts=1):
    rows, nodes = pivot.shape[0] // parts, pivot.shape[1]
    vmem = pl.BlockSpec(memory_space=pltpu.VMEM)
    return pl.pallas_call(
        functools.partial(couple_kernel, part * rows),
        out_shape=jax.ShapeDtypeStruct((rows, nodes), BF16),
        in_specs=[pl.BlockSpec(memory_space=pltpu.SMEM), vmem, vmem],
        out_specs=vmem,
        compiler_params=pltpu.CompilerParams(vmem_limit_bytes=8 * MIB),
        cost_estimate=LIGHT,
        name="couple",
    )(rate, weights, pivot)


def turned(block, odd):
    return block + odd * (3 - 2 * block)


def route(source, target, doms):
    pairs = []
    for dom in range(doms):
        odd = dom % 2
        pairs.append((dom * 4 + turned(source, odd), dom * 4 + turned(target, odd)))
    return pairs


def moved(value, source, target):
    return lax.ppermute(value, ("dom", "col"), route(source, target, lax.axis_size("dom")))


def couple_here(place, pivot, weights, rate):
    def kernel(place_ref, *refs):
        @pl.when(place_ref[1] == 1)
        def _():
            couple_kernel(0, *refs)

    scalars, vmem = pl.BlockSpec(memory_space=pltpu.SMEM), pl.BlockSpec(memory_space=pltpu.VMEM)
    return pl.pallas_call(
        kernel,
        out_shape=jax.ShapeDtypeStruct(pivot.shape, BF16),
        in_specs=[scalars, scalars, vmem, vmem],
        out_specs=vmem,
        compiler_params=pltpu.CompilerParams(vmem_limit_bytes=8 * MIB),
        cost_estimate=LIGHT,
        name="couple_here",
    )(place, rate, weights, pivot)


def turn_kernel(place_ref, coupled_ref, *refs):
    @pl.when(place_ref[1] == 1)
    def _():
        refs[-1][...] = coupled_ref[...].T


def turn(place, panel, part, coupled, across):
    rows, nodes = coupled.shape
    chunk = 128
    steps = rows // chunk
    ratio = nodes // 4 // chunk
    return pl.pallas_call(
        turn_kernel,
        out_shape=jax.ShapeDtypeStruct((nodes, nodes), BF16),
        grid_spec=pltpu.PrefetchScalarGridSpec(
            num_scalar_prefetch=1,
            grid=(steps,),
            in_specs=[pl.BlockSpec((chunk, nodes), lambda i, place: (i, 0))]
            + ([] if across is None else [pl.BlockSpec(memory_space=pl.ANY)]),
            out_specs=pl.BlockSpec(
                (nodes, chunk),
                lambda i, place: (0, turned(panel, place[0]) * ratio + part * steps + i),
            ),
        ),
        input_output_aliases={} if across is None else {2: 0},
        compiler_params=pltpu.CompilerParams(vmem_limit_bytes=4 * MIB),
        cost_estimate=LIGHT,
        name="turn",
    )(place, coupled, *(() if across is None else (across,)))


def multiply_kernel(first, count, lefts, place_ref, *refs):
    left_refs, right_ref, out_ref = refs[:lefts], refs[lefts], refs[-1]
    width = right_ref.shape[0] // 4

    @pl.when(place_ref[1] == 1)
    def _():
        def block(step, carry):
            source = pl.multiple_of((first(place_ref[0]) + step) * width, 128)
            target = pl.multiple_of(step * width, 128)
            row = 0
            for left_ref in left_refs:
                rows = left_ref.shape[0]
                out_ref[row : row + rows, pl.ds(target, width)] = jnp.dot(
                    left_ref[...], right_ref[:, pl.ds(source, width)], preferred_element_type=F32
                ).astype(BF16)
                row += rows
            return carry

        lax.fori_loop(0, count, block, 0)


def multiply(place, lefts, right, first=lambda odd: 0, count=4):
    rows = sum(left.shape[0] for left in lefts)
    width = right.shape[0] // 4
    vmem = pl.BlockSpec(memory_space=pltpu.VMEM)
    return pl.pallas_call(
        functools.partial(multiply_kernel, first, count, len(lefts)),
        out_shape=jax.ShapeDtypeStruct((rows, count * width), BF16),
        in_specs=[pl.BlockSpec(memory_space=pltpu.SMEM)] + [vmem] * (len(lefts) + 1),
        out_specs=vmem,
        compiler_params=pltpu.CompilerParams(vmem_limit_bytes=6 * MIB),
        cost_estimate=LIGHT,
        name="multiply",
    )(place, *lefts, right)


def pack(value, out_ref, column):
    quarter = value.shape[1] // 4
    for part in range(4):
        rows = pl.ds(part * quarter, quarter)
        pack_rows(part, value[part * quarter : (part + 1) * quarter], out_ref.at[rows], column)


def two_kernel(place_ref, left_ref, right_ref, zero_ref, out_ref):
    odd = place_ref[0]
    width = right_ref.shape[0] // 4

    def product(block):
        columns = pl.ds(pl.multiple_of(block * width, 128), width)
        value = jnp.dot(left_ref[...], right_ref[:, columns], preferred_element_type=F32)
        return value.astype(BF16)

    @pl.when(place_ref[1] == 1)
    def _():
        out_ref[:, :width] = product(1 + odd)
        zero = pl.ds(pl.multiple_of((2 - 2 * odd) * width, 128), width)
        out_ref[:, width : 2 * width] = zero_ref[:, zero]
        pack(product(2 - odd), out_ref, 2 * width)


def product_two(place, half, across, zero):
    rows = half.shape[0]
    width = across.shape[0] // 4
    vmem = pl.BlockSpec(memory_space=pltpu.VMEM)
    return pl.pallas_call(
        two_kernel,
        out_shape=jax.ShapeDtypeStruct((rows, 11 * width // 4), BF16),
        in_specs=[pl.BlockSpec(memory_space=pltpu.SMEM)] + [vmem] * 3,
        out_specs=vmem,
        compiler_params=pltpu.CompilerParams(vmem_limit_bytes=6 * MIB),
        cost_estimate=LIGHT,
        name="product_two",
    )(place, half, across, zero)


def half_kernel(place_ref, left_ref, right_ref, one_ref, out_ref):
    width = one_ref.shape[1]

    @pl.when(place_ref[1] == 1)
    def _():
        def block(step, carry):
            which = turned(step + (step > 0).astype(jnp.int32), place_ref[0])
            columns = pl.ds(pl.multiple_of(which * width, 128), width)
            out_ref[:, columns] = jnp.dot(
                left_ref[...], right_ref[:, columns], preferred_element_type=F32
            ).astype(BF16)
            return carry

        lax.fori_loop(0, 3, block, 0)
        columns = pl.ds(pl.multiple_of(turned(1, place_ref[0]) * width, 128), width)
        out_ref[:, columns] = one_ref[...]


def half_product(place, left, right, one):
    vmem = pl.BlockSpec(memory_space=pltpu.VMEM)
    return pl.pallas_call(
        half_kernel,
        out_shape=jax.ShapeDtypeStruct(left.shape, BF16),
        in_specs=[pl.BlockSpec(memory_space=pltpu.SMEM)] + [vmem] * 3,
        out_specs=vmem,
        compiler_params=pltpu.CompilerParams(vmem_limit_bytes=6 * MIB),
        cost_estimate=LIGHT,
        name="half_product",
    )(place, left, right, one)


def column_kernel(place_ref, near_ref, other_ref, first_ref, second_ref, *refs):
    column_ref, out_refs = refs[0], refs[1:]

    @pl.when(place_ref[1] == 1)
    def _():
        odd = place_ref[0]
        width = near_ref.shape[0]
        for half, half_ref in ((1 - odd, near_ref), (odd, other_ref)):
            for block in range(2):
                rows = pl.ds(pl.multiple_of((2 * half + block) * width, 128), width)
                column_ref[rows, :] = half_ref[:, block * width : (block + 1) * width].T
        for left_ref, out_ref in zip((first_ref, second_ref), out_refs):
            out_ref[...] = jnp.dot(
                left_ref[...], column_ref[...], preferred_element_type=F32
            ).astype(BF16)


def own_column(place, near, other, first, second):
    rows, nodes = first.shape
    vmem = pl.BlockSpec(memory_space=pltpu.VMEM)
    return pl.pallas_call(
        column_kernel,
        out_shape=(
            jax.ShapeDtypeStruct((nodes, rows), BF16),
            jax.ShapeDtypeStruct((rows, rows), BF16),
            jax.ShapeDtypeStruct((rows, rows), BF16),
        ),
        in_specs=[pl.BlockSpec(memory_space=pltpu.SMEM)] + [vmem] * 4,
        out_specs=(vmem, vmem, vmem),
        compiler_params=pltpu.CompilerParams(vmem_limit_bytes=6 * MIB),
        cost_estimate=LIGHT,
        name="own_column",
    )(place, near, other, first, second)


def rest_kernel(place_ref, upper_ref, lower_ref, right_ref, zero_ref, out_ref, last_ref):
    odd = place_ref[0]
    width = zero_ref.shape[1]
    half = width // 2

    def product(left_ref, block):
        columns = pl.ds(pl.multiple_of(block * width, 128), width)
        value = jnp.dot(left_ref[...], right_ref[:, columns], preferred_element_type=F32)
        return value.astype(BF16)

    @pl.when(place_ref[1] == 1)
    def _():
        out_ref[:, pl.ds(pl.multiple_of(odd * width, 128), width)] = zero_ref[...].T
        other = pl.ds(pl.multiple_of((1 - odd) * width, 128), width)
        for part, left_ref in enumerate((upper_ref, lower_ref)):
            out_ref[pl.ds(part * half, half), other] = product(left_ref, 1 + odd)
            value = product(left_ref, 3 - 3 * odd)
            for quarter in range(2):
                start = quarter * half // 2
                rows = pl.ds(part * half + start, half // 2)
                rows_of = value[start : start + half // 2]
                pack_rows(2 * part + quarter, rows_of, last_ref.at[rows], 0)


def product_rest(place, halves, across, zero):
    rows, width = zero.shape
    vmem = pl.BlockSpec(memory_space=pltpu.VMEM)
    return pl.pallas_call(
        rest_kernel,
        out_shape=(
            jax.ShapeDtypeStruct((rows, 2 * width), BF16),
            jax.ShapeDtypeStruct((rows, 3 * width // 4), BF16),
        ),
        in_specs=[pl.BlockSpec(memory_space=pltpu.SMEM)] + [vmem] * 4,
        out_specs=(vmem, vmem),
        compiler_params=pltpu.CompilerParams(vmem_limit_bytes=6 * MIB),
        cost_estimate=LIGHT,
        name="product_rest",
    )(place, *halves, across, zero)


def pack_rows(part, value, out_ref, column):
    quarter, width = value.shape
    half = width // 2
    beside = (2, 3, 1, 0)[part] * quarter
    out_ref[:, column : column + half] = value[:, part // 2 * half : (part // 2 + 1) * half]
    out_ref[:, column + half : column + half + quarter] = value[:, beside : beside + quarter]


def unpacked_rows(part, packed_ref, column):
    quarter = packed_ref.shape[0] // 4
    half = 2 * quarter

    def beside(which):
        rows = slice(which * quarter, (which + 1) * quarter)
        return packed_ref[rows, column + half : column + half + quarter]

    rows = slice(part * quarter, (part + 1) * quarter)
    diagonal = packed_ref[rows, column : column + half]
    if part == 0:
        return diagonal, jnp.concatenate([beside(0), beside(3).T], axis=1)
    if part == 1:
        return diagonal, jnp.concatenate([beside(2).T, beside(1)], axis=1)
    if part == 2:
        return jnp.concatenate([beside(0).T, beside(2)], axis=1), diagonal
    return jnp.concatenate([beside(3), beside(1).T], axis=1), diagonal


def prior_kernel(place_ref, shifted_ref, sigma_ref, out_ref):
    @pl.when(place_ref[3] == 0)
    def _():
        out_ref[...] = shifted_ref[...]

    @pl.when(place_ref[3] != 0)
    def _():
        out_ref[...] = sigma_ref[...]


def halves_kernel(place_ref, first_ref, second_ref, near_ref, other_ref):
    near_ref[...] = first_ref[...]
    other_ref[...] = second_ref[...]


def halves(place, separator):
    rows, nodes = separator.shape
    chunk = rows // 4
    half = lambda side: pl.BlockSpec((chunk, nodes // 2), lambda i, place: (i, side(place[0])))
    out = jax.ShapeDtypeStruct((rows, nodes // 2), BF16)
    return pl.pallas_call(
        halves_kernel,
        out_shape=(out, out),
        grid_spec=pltpu.PrefetchScalarGridSpec(
            num_scalar_prefetch=1,
            grid=(4,),
            in_specs=[half(lambda odd: odd), half(lambda odd: 1 - odd)],
            out_specs=(half(lambda odd: 0), half(lambda odd: 0)),
        ),
        compiler_params=pltpu.CompilerParams(vmem_limit_bytes=6 * MIB),
        cost_estimate=LIGHT,
        name="halves",
    )(place, separator, separator)


def near_kernel(place_ref, shifted_ref, sigma_ref, row_ref, near_ref, last_ref):
    odd = place_ref[0]
    width = row_ref.shape[1] // 2
    prior_kernel(place_ref, shifted_ref, sigma_ref, row_ref)
    two = pl.ds(pl.multiple_of(odd * width, 128), width)
    three = pl.ds(pl.multiple_of((1 - odd) * width, 128), width)
    near_ref[:, :width] = row_ref[:, three]
    for part in range(4):

        @pl.when(pl.program_id(0) == part)
        def _():
            pack_rows(part, row_ref[:, two], near_ref, width)
            pack_rows(part, row_ref[:, three], last_ref, 0)


def other_half_kernel(place_ref, shifted_ref, sigma_ref, row_ref, far_ref):
    width = row_ref.shape[1] // 2
    prior_kernel(place_ref, shifted_ref, sigma_ref, row_ref)
    zero = pl.ds(pl.multiple_of(place_ref[0] * width, 128), width)
    for part in range(4):

        @pl.when(pl.program_id(0) == part)
        def _():
            pack_rows(part, row_ref[:, zero], far_ref, 0)


def prior_half(kernel, side, sent, place, shifted, sigma):
    rows, nodes = sigma.shape
    chunk = rows // 4
    quarters = (8,) + sent
    out = lambda count: jax.ShapeDtypeStruct((rows, count * nodes // 16), BF16)
    spec = lambda count: pl.BlockSpec((chunk, count * nodes // 16), lambda i, place: (i, 0))
    return pl.pallas_call(
        kernel,
        out_shape=tuple(out(count) for count in quarters),
        grid_spec=pltpu.PrefetchScalarGridSpec(
            num_scalar_prefetch=1,
            grid=(4,),
            in_specs=[
                pl.BlockSpec(
                    (chunk, nodes // 2), lambda i, place: (jnp.where(place[3] == 0, i, 0), 0)
                ),
                pl.BlockSpec(
                    (chunk, nodes // 2),
                    lambda i, place: (jnp.where(place[3] == 0, 0, i), side(place[0])),
                ),
            ],
            out_specs=tuple(spec(count) for count in quarters),
        ),
        compiler_params=pltpu.CompilerParams(vmem_limit_bytes=6 * MIB),
        cost_estimate=LIGHT,
        name="prior_half",
    )(place, shifted, sigma)


def assemble_kernel(place_ref, near, other, column, near_two, last_three, near_zero, far_zero, out_ref):
    @pl.when(place_ref[1] == 1)
    def _():
        odd = place_ref[0]
        width = near.shape[0]
        half, quarter = width // 2, width // 4

        def at(block, count=1):
            return pl.ds(pl.multiple_of(block * width, 128), count * width)

        first = 2 * (1 - odd)
        row = [turned(block, odd) for block in range(4)]
        out_ref[at(row[1]), at(first, 2)] = near[...]
        out_ref[at(row[1]), at(2 * odd, 2)] = other[...]
        out_ref[at(row[2]), at(row[3])] = near_two[:, :width]
        out_ref[at(row[3]), at(row[2])] = near_two[:, :width].T
        out_ref[at(row[0]), at(first, 2)] = near_zero[...]
        for step in range(2):
            out_ref[at(first + step), at(row[0])] = near_zero[:, step * width : (1 + step) * width].T
        for block in (0, 2, 3):
            out_ref[at(row[block]), at(row[1])] = column[at(row[block]), :]
        packed = ((0, far_zero, 0), (2, near_two, width), (3, last_three, 0))
        for block, packed_ref, start in packed:
            for part in range(4):
                rows = pl.ds(pl.multiple_of(row[block] * width + part * quarter, 128), quarter)
                for side, value in enumerate(unpacked_rows(part, packed_ref, start)):
                    columns = pl.ds(pl.multiple_of(row[block] * width + side * half, 128), half)
                    out_ref[rows, columns] = value


def assemble(place, *parts):
    nodes = 2 * parts[0].shape[1]
    vmem = pl.BlockSpec(memory_space=pltpu.VMEM)
    return pl.pallas_call(
        assemble_kernel,
        out_shape=jax.ShapeDtypeStruct((nodes, nodes), BF16),
        in_specs=[pl.BlockSpec(memory_space=pltpu.SMEM)] + [vmem] * 7,
        out_specs=vmem,
        compiler_params=pltpu.CompilerParams(vmem_limit_bytes=6 * MIB),
        cost_estimate=LIGHT,
        name="assemble",
    )(place, *parts)


def tick(place, *values, cost=HEAVY):
    def kernel(place_ref, *refs):
        for which in range(place.shape[0]):
            refs[-1][which] = place_ref[which]

    scalars = pl.BlockSpec(memory_space=pltpu.SMEM)
    return pl.pallas_call(
        kernel,
        out_shape=jax.ShapeDtypeStruct(place.shape, place.dtype),
        in_specs=[scalars] + [pl.BlockSpec(memory_space=pl.ANY)] * len(values),
        out_specs=scalars,
        compiler_params=pltpu.CompilerParams(vmem_limit_bytes=MIB),
        cost_estimate=cost,
        name="tick",
    )(place, *values)


def finish_kernel(
    place_ref, pivot_ref, sigma_ref,
    q0, q0_last, q2, q3_two,
    q01, q11, q21, q31,
    out_ref, var_ref,
):
    rows, nodes = pivot_ref.shape
    width = nodes // 4
    odd, place = place_ref[0], place_ref[1]
    here = pl.multiple_of(pl.program_id(0) * rows, 128)
    diagonal = diagonal_of(rows)

    def at(block, count=1):
        return pl.ds(pl.multiple_of(block * width, 128), count * width)

    def own(block):
        return pl.ds(pl.multiple_of(block * width + here, 128), rows)

    def add(columns, product):
        out_ref[:, columns] = (pivot_ref[:, columns].astype(F32) + product.astype(F32)).astype(BF16)

    def trace(product):
        var_ref[...] = diagonal(
            pivot_ref[:, own(place_ref[2])].astype(F32) + product.astype(F32)
        )

    active = place_ref[4] != 0

    @pl.when(active & (place == 0))
    def _():
        add(at(odd, 3), q0[...])
        add(at(turned(3, odd)), q0_last[...])
        trace(q0[:, own(2 * odd)])

    @pl.when(active & (place == 1))
    def _():
        add(at(turned(0, odd)), q01[...].T)
        add(at(turned(1, odd)), q11[...])
        add(at(turned(2, odd)), q21[...].T)
        add(at(turned(3, odd)), q31[...].T)
        trace(q11[:, pl.ds(here, rows)])

    @pl.when(active & (place == 2))
    def _():
        add(at(turned(0, odd)), q2[pl.ds(0, width), pl.ds(pl.multiple_of(width + here, 128), rows)].T)
        add(at(turned(1, odd)), q2[pl.ds(here, rows), pl.ds(0, width)])
        start = pl.program_id(0) % 2 * rows + 2 * width
        trace(q2[pl.ds(here, rows), pl.ds(pl.multiple_of(start, 128), rows)])
        for part in range(4):

            @pl.when(pl.program_id(0) == part)
            def _():
                for side, value in enumerate(unpacked_rows(part, q2, 2 * width)):
                    start = turned(2, odd) * width + side * width // 2
                    add(pl.ds(pl.multiple_of(start, 128), width // 2), value)

    @pl.when(active & (place == 3))
    def _():
        add(at(turned(2, odd)), q3_two[...])

    @pl.when(place_ref[4] == 0)
    def _():
        out_ref[...] = sigma_ref[...]
        var_ref[...] = diagonal(sigma_ref[:, own(place_ref[2])].astype(F32))


def finish(place, pivot, sigma, received, kept):
    rows, nodes = pivot.shape
    chunk = 128
    width = nodes // 4

    def picked(which, blocks):
        return pl.BlockSpec(
            (chunk, blocks * width), lambda i, place: (jnp.where(place[1] == which, i, 0), 0)
        )

    def turned_block(start):
        return pl.BlockSpec(
            (rows, chunk),
            lambda i, place: (
                0,
                jnp.where(place[1] == 1, start(place[0]) * (width // chunk) + i, 0),
            ),
        )

    return pl.pallas_call(
        finish_kernel,
        out_shape=(
            jax.ShapeDtypeStruct((rows, nodes), BF16),
            jax.ShapeDtypeStruct((1, rows), F32),
        ),
        grid_spec=pltpu.PrefetchScalarGridSpec(
            num_scalar_prefetch=1,
            grid=(rows // chunk,),
            in_specs=[
                pl.BlockSpec((chunk, nodes), lambda i, place: (i, 0)),
                pl.BlockSpec(
                    (chunk, nodes), lambda i, place: (jnp.where(place[4] == 0, i, 0), 0)
                ),
                picked(0, 3),
                picked(0, 1),
                pl.BlockSpec((rows, 11 * width // 4), lambda i, place: (0, 0)),
                picked(3, 1),
                turned_block(lambda odd: 1),
                picked(1, 1),
                turned_block(lambda odd: 0),
                turned_block(lambda odd: 1 - odd),
            ],
            out_specs=(
                pl.BlockSpec((chunk, nodes), lambda i, place: (i, 0)),
                pl.BlockSpec((1, chunk), lambda i, place: (0, i)),
            ),
        ),
        compiler_params=pltpu.CompilerParams(vmem_limit_bytes=12 * MIB),
        cost_estimate=HEAVY,
        name="finish",
    )(place, pivot, sigma, *received, *kept)


def add_in_place(pivot_ref, out_ref, sum_ref, sems, column, product):
    chunk = pivot_ref.shape[0] // 4
    copies = []
    for part in range(4):
        here = pl.ds(part * chunk, chunk)
        value = pivot_ref[here, :].astype(F32) + product(part, here).astype(F32)
        sum_ref[here, :] = value.astype(BF16)
        copies.append(
            pltpu.make_async_copy(sum_ref.at[here], out_ref.at[here, column], sems.at[part])
        )
        copies[-1].start()
    return copies


def other_kernel(place_ref, pivot_ref, q3_other, old_ref, out_ref, sum_ref, sems):
    both = pivot_ref.shape[1]
    column = pl.ds(pl.multiple_of(place_ref[0] * both, 128), both)

    @pl.when((place_ref[4] != 0) & (place_ref[1] == 3))
    def _():
        product = lambda part, here: q3_other[here, :]
        for copy in add_in_place(pivot_ref, out_ref, sum_ref, sems, column, product):
            copy.wait()


def last_kernel(
    place_ref, pivot_ref, q2_last, q3_last, old_ref, old_var_ref, out_ref, var_ref, sum_ref, sems
):
    rows, width = pivot_ref.shape
    chunk = rows // 4
    active = place_ref[4] != 0
    column = pl.ds(pl.multiple_of(turned(3, place_ref[0]) * width, 128), width)
    add = functools.partial(add_in_place, pivot_ref, out_ref, sum_ref, sems, column)
    var_ref[...] = old_var_ref[...]

    @pl.when(active & (place_ref[1] == 2))
    def _():
        for copy in add(lambda part, here: q2_last[:, here].T):
            copy.wait()

    @pl.when(active & (place_ref[1] == 3))
    def _():
        copies = add(lambda part, here: jnp.concatenate(unpacked_rows(part, q3_last, 0), axis=1))
        for start in range(0, rows, chunk):
            here = pl.ds(start, chunk)
            value = pivot_ref[here, here].astype(F32)
            value = value + q3_last[here, pl.ds(start % (2 * chunk), chunk)].astype(F32)
            var_ref[:, here] = diagonal_of(chunk)(value)
        for copy in copies:
            copy.wait()


def diagonal_of(rows):
    square = (rows, rows)
    on_diagonal = lax.broadcasted_iota(jnp.int32, square, 0) == lax.broadcasted_iota(
        jnp.int32, square, 1
    )
    return lambda value: jnp.sum(jnp.where(on_diagonal, value, 0.0), axis=0, keepdims=True)


def finish_other(place, pivot, q3_other, covariance):
    rows, nodes = pivot.shape
    vmem = pl.BlockSpec(memory_space=pltpu.VMEM)
    anywhere = pl.BlockSpec(memory_space=pl.ANY)
    return pl.pallas_call(
        other_kernel,
        out_shape=jax.ShapeDtypeStruct((rows, nodes), BF16),
        grid_spec=pltpu.PrefetchScalarGridSpec(
            num_scalar_prefetch=1,
            grid=(1,),
            in_specs=[
                pl.BlockSpec((rows, nodes // 2), lambda i, place: (0, place[0])),
                vmem,
                anywhere,
            ],
            out_specs=anywhere,
            scratch_shapes=[pltpu.VMEM((rows, nodes // 2), BF16), pltpu.SemaphoreType.DMA((4,))],
        ),
        input_output_aliases={3: 0},
        compiler_params=pltpu.CompilerParams(vmem_limit_bytes=8 * MIB),
        cost_estimate=LIGHT,
        name="finish_other",
    )(place, pivot, q3_other, covariance)


def finish_last(place, pivot, q2_last, q3_last, covariance, variances):
    rows, nodes = pivot.shape
    vmem = pl.BlockSpec(memory_space=pltpu.VMEM)
    anywhere = pl.BlockSpec(memory_space=pl.ANY)
    return pl.pallas_call(
        last_kernel,
        out_shape=(
            jax.ShapeDtypeStruct((rows, nodes), BF16),
            jax.ShapeDtypeStruct((1, rows), F32),
        ),
        grid_spec=pltpu.PrefetchScalarGridSpec(
            num_scalar_prefetch=1,
            grid=(1,),
            in_specs=[
                pl.BlockSpec((rows, nodes // 4), lambda i, place: (0, turned(3, place[0]))),
                vmem,
                vmem,
                anywhere,
                vmem,
            ],
            out_specs=(anywhere, vmem),
            scratch_shapes=[pltpu.VMEM((rows, nodes // 4), BF16), pltpu.SemaphoreType.DMA((4,))],
        ),
        input_output_aliases={4: 0},
        compiler_params=pltpu.CompilerParams(vmem_limit_bytes=8 * MIB),
        cost_estimate=LIGHT,
        name="finish_last",
    )(place, pivot, q2_last, q3_last, covariance, variances)


def owned(sigma_next, separator, inverse_pivot, coupling_rate, lengths, step_index, node_class):
    sigma, pivot = sigma_next[0], inverse_pivot[0]
    odd = lax.axis_index("dom") % 2
    col = lax.axis_index("col")
    step = step_index[0]
    place = jnp.stack([odd, turned(col, odd), col, step, step < lengths[0]]).astype(jnp.int32)
    after = lambda value, *others: lax.optimization_barrier((value, *others))[0]

    p2 = moved(pivot, 2, 1)
    p0 = moved(pivot, 0, 1)
    weights = coupling(node_class)
    c1 = [couple(pivot, weights, coupling_rate, part, 2) for part in range(2)]
    across = turn(place, 1, 0, c1[0], None)
    across = turn(place, 1, 1, c1[1], across)

    near, other = halves(place, separator[0])
    near, other = passed_along(near, "dom", -1), passed_along(other, "dom", -1)
    sides = (lambda odd: 1 - odd, lambda odd: odd)
    row_near, near, last = prior_half(
        near_kernel, sides[0], (7, 3), place, after(near, across), sigma
    )
    near_zero, near_two = moved(row_near, 0, 1), moved(near, 2, 1)
    last_three = moved(last, 3, 1)
    c2 = couple_here(place, after(p2, last), weights, coupling_rate)
    across = turn(place, 2, 0, c2, across)
    row_other, far = prior_half(
        other_half_kernel, sides[1], (3,), place, after(other, across), sigma
    )
    far_zero = moved(far, 0, 1)
    c0 = couple_here(place, after(p0, across, far), weights, coupling_rate)
    across = turn(place, 0, 0, c0, across)
    column, h0_one, h2_one = own_column(place, row_near, row_other, c0, c2)
    c3 = [
        moved(after(c1[0], last_three, near_two, near_zero, across), 3, 1),
        moved(after(c1[1], far_zero, h2_one), 3, 1),
    ]
    prior = assemble(place, row_near, row_other, column, near_two, last_three, near_zero, far_zero)

    h0 = half_product(place, c0, prior, h0_one)
    q0_own = multiply(place, [h0], across, lambda odd: odd, 3)
    q0 = moved(q0_own, 1, 0)
    h2 = half_product(place, after(c2, q0_own), prior, h2_one)
    q2_own = product_two(place, h2, across, q0_own)
    q2 = moved(q2_own, 1, 2)

    across = turn(place, 3, 0, c3[0], after(across, q2_own))
    across = turn(place, 3, 1, c3[1], across)
    q03 = multiply(place, [h0], across, lambda odd: 3 - 3 * odd, 1)
    q0_last = moved(q03, 1, 0)
    h3 = [multiply(place, [after(panel, q03)], prior) for panel in c3]
    q32 = multiply(place, h3, across, lambda odd: 2 - odd, 1)
    q3_two = moved(q32, 1, 3)
    q3_own, q33 = product_rest(place, h3, across, after(q03, q32))
    q3_other, q3_last = moved(q3_own, 1, 3), moved(q33, 1, 3)
    h1 = multiply(place, [after(c1[0], q3_own), c1[1]], prior)
    q11 = multiply(place, [h1], across, lambda odd: 1 + odd, 1)
    received = (q0, q0_last, q2, q3_two)
    kept = (q0_own, q11, q2_own, q3_own)
    place_then = tick(tick(place, q0, cost=LIGHT), q0_last, cost=MEDIUM)
    q2_last = moved(after(q3_two, place_then), 3, 2)
    covariance, variances = finish(place_then, pivot, sigma, received, kept)
    covariance = finish_other(place, pivot, q3_other, covariance)
    covariance, variances = finish_last(place, pivot, q2_last, q3_last, covariance, variances)
    return (covariance[None], variances)


def gathered(sigma_next, separator, inverse_pivot, coupling_rate, lengths, step_index, node_class):
    shifted = passed_along(separator, "dom", -1)
    prior = jnp.where(step_index[0] == 0, shifted[0], sigma_next[0])
    pivot = inverse_pivot[0].astype(F32)
    coupled = couple(inverse_pivot[0], coupling(node_class), coupling_rate)
    rows = coupled.shape[0]
    half = jnp.dot(
        coupled,
        lax.all_gather(prior, "col", axis=0, tiled=True),
        preferred_element_type=F32,
    ).astype(BF16)
    product = lax.dot_general(
        half,
        lax.all_gather(coupled, "col", axis=0, tiled=True),
        (((1,), (1,)), ((), ())),
        preferred_element_type=F32,
    )
    full = pivot + product
    active = step_index[0] < lengths[0]
    old = sigma_next[0]
    covariance = jnp.where(active, full.astype(BF16), old)
    first_col = lax.axis_index("col") * rows
    new_block = lax.dynamic_slice_in_dim(full, first_col, rows, 1)
    old_block = lax.dynamic_slice_in_dim(old, first_col, rows, 1)
    variances = jnp.where(active, jnp.diagonal(new_block), jnp.diagonal(old_block).astype(F32))
    return (covariance[None], variances[None])


def solution(mesh):
    local = owned if mesh.shape["col"] == 4 and mesh.shape["dom"] % 2 == 0 else gathered
    return jax.shard_map(
        local,
        mesh=mesh,
        in_specs=(
            P(("groups", "dom"), "col", None),
            P(("groups", "dom"), "col", None),
            P(("groups", "dom"), "col", None),
            P(("groups", "dom")),
            P(("groups", "dom")),
            P(("groups", "dom")),
            P("groups"),
        ),
        out_specs=(P(("groups", "dom"), "col", None), P(("groups", "dom"), "col")),
        check_vma=False,
    )
```

```python
import functools

import jax
import jax.numpy as jnp
from jax import lax
from jax.experimental import pallas as pl
from jax.experimental.pallas import tpu as pltpu
from jax.sharding import PartitionSpec as P

GX = 64
GY = 32
BF16 = jnp.bfloat16
F32 = jnp.float32
MIB = 1 << 20


def passed_along(value, axis, steps):
    count = lax.axis_size(axis)
    initial, last = (max(0, -steps), min(count, count - steps))
    return lax.ppermute(value, axis, [(source, source + steps) for source in range(initial, last)])


LIGHT = pl.CostEstimate(flops=1 << 20, bytes_accessed=1 << 16, transcendentals=0)
MEDIUM = pl.CostEstimate(flops=2000000000, bytes_accessed=1 << 16, transcendentals=0)
HEAVY = pl.CostEstimate(flops=14000000000, bytes_accessed=1 << 16, transcendentals=0)


BLOCK = 256
SPAN = 512


def window(block, nodes):
    return pl.multiple_of(jnp.clip(block * BLOCK - (SPAN - BLOCK) // 2, 0, nodes - SPAN), 128)


def weight_kernel(class_ref, out_ref):
    nodes = class_ref.shape[1]

    def fill(block, carry):
        first = pl.multiple_of(block * BLOCK, BLOCK)
        kind = class_ref[:, pl.ds(first, BLOCK)]
        across = jnp.where(
            kind == 0, 0.25, jnp.where(kind == 1, 0.375, jnp.where(kind == 2, 0.125, 0.5))
        ).astype(F32)
        along = jnp.where(
            kind == 0, 0.25, jnp.where(kind == 1, 0.125, jnp.where(kind == 2, 0.375, 0.0))
        ).astype(F32)
        column = (first + lax.broadcasted_iota(jnp.int32, (1, BLOCK), 1)) % GX
        left = jnp.where(column > 0, across, 0.0)
        right = jnp.where(column < GX - 1, across, 0.0)
        shape = (SPAN, BLOCK)
        offset = (
            lax.broadcasted_iota(jnp.int32, shape, 0)
            - lax.broadcasted_iota(jnp.int32, shape, 1)
            + (window(block, nodes) - first)
        )
        value = jnp.where(jnp.abs(offset) == GX, along, 0.0)
        value = jnp.where(offset == -1, left, value)
        value = jnp.where(offset == 1, right, value)
        value = jnp.where(offset == 0, 1.0, value)
        out_ref[block] = value.astype(BF16)
        return carry

    lax.fori_loop(0, nodes // BLOCK, fill, 0)


def coupling(node_class):
    nodes = node_class.shape[0]
    vmem = pl.BlockSpec(memory_space=pltpu.VMEM)
    return pl.pallas_call(
        weight_kernel,
        out_shape=jax.ShapeDtypeStruct((nodes // BLOCK, SPAN, BLOCK), BF16),
        in_specs=[vmem],
        out_specs=vmem,
        compiler_params=pltpu.CompilerParams(vmem_limit_bytes=6 * MIB),
        cost_estimate=LIGHT,
        name="coupling",
    )(node_class.reshape(1, nodes))


def couple_kernel(first, rate_ref, weight_ref, pivot_ref, out_ref):
    rows, nodes = out_ref.shape

    def block_of(block, carry):
        source = pl.ds(window(block, nodes), SPAN)
        target = pl.ds(pl.multiple_of(block * BLOCK, BLOCK), BLOCK)
        value = jnp.dot(
            pivot_ref[first : first + rows, source], weight_ref[block], preferred_element_type=F32
        )
        out_ref[:, target] = (rate_ref[0] * value).astype(BF16)
        return carry

    lax.fori_loop(0, nodes // BLOCK, block_of, 0)


def couple(pivot, weights, rate, part=0, parts=1):
    rows, nodes = pivot.shape[0] // parts, pivot.shape[1]
    vmem = pl.BlockSpec(memory_space=pltpu.VMEM)
    return pl.pallas_call(
        functools.partial(couple_kernel, part * rows),
        out_shape=jax.ShapeDtypeStruct((rows, nodes), BF16),
        in_specs=[pl.BlockSpec(memory_space=pltpu.SMEM), vmem, vmem],
        out_specs=vmem,
        compiler_params=pltpu.CompilerParams(vmem_limit_bytes=8 * MIB),
        cost_estimate=LIGHT,
        name="couple",
    )(rate, weights, pivot)


def turned(block, odd):
    return block + odd * (3 - 2 * block)


def route(source, target, doms):
    pairs = []
    for dom in range(doms):
        odd = dom % 2
        pairs.append((dom * 4 + turned(source, odd), dom * 4 + turned(target, odd)))
    return pairs


def moved(value, source, target):
    return lax.ppermute(value, ("dom", "col"), route(source, target, lax.axis_size("dom")))


def couple_here(place, pivot, weights, rate):
    def kernel(place_ref, *refs):
        @pl.when(place_ref[1] == 1)
        def _():
            couple_kernel(0, *refs)

    scalars, vmem = pl.BlockSpec(memory_space=pltpu.SMEM), pl.BlockSpec(memory_space=pltpu.VMEM)
    return pl.pallas_call(
        kernel,
        out_shape=jax.ShapeDtypeStruct(pivot.shape, BF16),
        in_specs=[scalars, scalars, vmem, vmem],
        out_specs=vmem,
        compiler_params=pltpu.CompilerParams(vmem_limit_bytes=8 * MIB),
        cost_estimate=LIGHT,
        name="couple_here",
    )(place, rate, weights, pivot)


def turn_kernel(place_ref, coupled_ref, *refs):
    @pl.when(place_ref[1] == 1)
    def _():
        refs[-1][...] = coupled_ref[...].T


def turn(place, panel, part, coupled, across):
    rows, nodes = coupled.shape
    chunk = 128
    steps = rows // chunk
    ratio = nodes // 4 // chunk
    return pl.pallas_call(
        turn_kernel,
        out_shape=jax.ShapeDtypeStruct((nodes, nodes), BF16),
        grid_spec=pltpu.PrefetchScalarGridSpec(
            num_scalar_prefetch=1,
            grid=(steps,),
            in_specs=[pl.BlockSpec((chunk, nodes), lambda i, place: (i, 0))]
            + ([] if across is None else [pl.BlockSpec(memory_space=pl.ANY)]),
            out_specs=pl.BlockSpec(
                (nodes, chunk),
                lambda i, place: (0, turned(panel, place[0]) * ratio + part * steps + i),
            ),
        ),
        input_output_aliases={} if across is None else {2: 0},
        compiler_params=pltpu.CompilerParams(vmem_limit_bytes=4 * MIB),
        cost_estimate=LIGHT,
        name="turn",
    )(place, coupled, *(() if across is None else (across,)))


def multiply_kernel(first, count, lefts, place_ref, *refs):
    left_refs, right_ref, out_ref = refs[:lefts], refs[lefts], refs[-1]
    width = right_ref.shape[0] // 4

    @pl.when(place_ref[1] == 1)
    def _():
        def block(step, carry):
            source = pl.multiple_of((first(place_ref[0]) + step) * width, 128)
            target = pl.multiple_of(step * width, 128)
            row = 0
            for left_ref in left_refs:
                rows = left_ref.shape[0]
                out_ref[row : row + rows, pl.ds(target, width)] = jnp.dot(
                    left_ref[...], right_ref[:, pl.ds(source, width)], preferred_element_type=F32
                ).astype(BF16)
                row += rows
            return carry

        lax.fori_loop(0, count, block, 0)


def multiply(place, lefts, right, first=lambda odd: 0, count=4):
    rows = sum(left.shape[0] for left in lefts)
    width = right.shape[0] // 4
    vmem = pl.BlockSpec(memory_space=pltpu.VMEM)
    return pl.pallas_call(
        functools.partial(multiply_kernel, first, count, len(lefts)),
        out_shape=jax.ShapeDtypeStruct((rows, count * width), BF16),
        in_specs=[pl.BlockSpec(memory_space=pltpu.SMEM)] + [vmem] * (len(lefts) + 1),
        out_specs=vmem,
        compiler_params=pltpu.CompilerParams(vmem_limit_bytes=6 * MIB),
        cost_estimate=LIGHT,
        name="multiply",
    )(place, *lefts, right)


def pack(value, out_ref, column):
    quarter = value.shape[1] // 4
    for part in range(4):
        rows = pl.ds(part * quarter, quarter)
        pack_rows(part, value[part * quarter : (part + 1) * quarter], out_ref.at[rows], column)


def two_kernel(place_ref, left_ref, right_ref, zero_ref, out_ref):
    odd = place_ref[0]
    width = right_ref.shape[0] // 4

    def product(block):
        columns = pl.ds(pl.multiple_of(block * width, 128), width)
        value = jnp.dot(left_ref[...], right_ref[:, columns], preferred_element_type=F32)
        return value.astype(BF16)

    @pl.when(place_ref[1] == 1)
    def _():
        out_ref[:, :width] = product(1 + odd)
        zero = pl.ds(pl.multiple_of((2 - 2 * odd) * width, 128), width)
        out_ref[:, width : 2 * width] = zero_ref[:, zero]
        pack(product(2 - odd), out_ref, 2 * width)


def product_two(place, half, across, zero):
    rows = half.shape[0]
    width = across.shape[0] // 4
    vmem = pl.BlockSpec(memory_space=pltpu.VMEM)
    return pl.pallas_call(
        two_kernel,
        out_shape=jax.ShapeDtypeStruct((rows, 11 * width // 4), BF16),
        in_specs=[pl.BlockSpec(memory_space=pltpu.SMEM)] + [vmem] * 3,
        out_specs=vmem,
        compiler_params=pltpu.CompilerParams(vmem_limit_bytes=6 * MIB),
        cost_estimate=LIGHT,
        name="product_two",
    )(place, half, across, zero)


def half_kernel(place_ref, left_ref, right_ref, one_ref, out_ref):
    width = one_ref.shape[1]

    @pl.when(place_ref[1] == 1)
    def _():
        def block(step, carry):
            which = turned(step + (step > 0).astype(jnp.int32), place_ref[0])
            columns = pl.ds(pl.multiple_of(which * width, 128), width)
            out_ref[:, columns] = jnp.dot(
                left_ref[...], right_ref[:, columns], preferred_element_type=F32
            ).astype(BF16)
            return carry

        lax.fori_loop(0, 3, block, 0)
        columns = pl.ds(pl.multiple_of(turned(1, place_ref[0]) * width, 128), width)
        out_ref[:, columns] = one_ref[...]


def half_product(place, left, right, one):
    vmem = pl.BlockSpec(memory_space=pltpu.VMEM)
    return pl.pallas_call(
        half_kernel,
        out_shape=jax.ShapeDtypeStruct(left.shape, BF16),
        in_specs=[pl.BlockSpec(memory_space=pltpu.SMEM)] + [vmem] * 3,
        out_specs=vmem,
        compiler_params=pltpu.CompilerParams(vmem_limit_bytes=6 * MIB),
        cost_estimate=LIGHT,
        name="half_product",
    )(place, left, right, one)


def column_kernel(place_ref, near_ref, other_ref, first_ref, second_ref, *refs):
    column_ref, out_refs = refs[0], refs[1:]

    @pl.when(place_ref[1] == 1)
    def _():
        odd = place_ref[0]
        width = near_ref.shape[0]
        for half, half_ref in ((1 - odd, near_ref), (odd, other_ref)):
            for block in range(2):
                rows = pl.ds(pl.multiple_of((2 * half + block) * width, 128), width)
                column_ref[rows, :] = half_ref[:, block * width : (block + 1) * width].T
        for left_ref, out_ref in zip((first_ref, second_ref), out_refs):
            out_ref[...] = jnp.dot(
                left_ref[...], column_ref[...], preferred_element_type=F32
            ).astype(BF16)


def own_column(place, near, other, first, second):
    rows, nodes = first.shape
    vmem = pl.BlockSpec(memory_space=pltpu.VMEM)
    return pl.pallas_call(
        column_kernel,
        out_shape=(
            jax.ShapeDtypeStruct((nodes, rows), BF16),
            jax.ShapeDtypeStruct((rows, rows), BF16),
            jax.ShapeDtypeStruct((rows, rows), BF16),
        ),
        in_specs=[pl.BlockSpec(memory_space=pltpu.SMEM)] + [vmem] * 4,
        out_specs=(vmem, vmem, vmem),
        compiler_params=pltpu.CompilerParams(vmem_limit_bytes=6 * MIB),
        cost_estimate=LIGHT,
        name="own_column",
    )(place, near, other, first, second)


def rest_kernel(place_ref, left_ref, right_ref, zero_ref, out_ref, last_ref):
    odd = place_ref[0]
    width = zero_ref.shape[1]
    half = width // 2

    def product(rows, block):
        columns = pl.ds(pl.multiple_of(block * width, 128), width)
        value = jnp.dot(left_ref[rows, :], right_ref[:, columns], preferred_element_type=F32)
        return value.astype(BF16)

    @pl.when(place_ref[1] == 1)
    def _():
        out_ref[:, pl.ds(pl.multiple_of(odd * width, 128), width)] = zero_ref[...].T
        other = pl.ds(pl.multiple_of((1 - odd) * width, 128), width)
        out_ref[:, other] = product(pl.ds(0, width), 1 + odd)
        value = product(pl.ds(0, width), 3 - 3 * odd)
        for part in range(4):
            rows = pl.ds(part * half // 2, half // 2)
            pack_rows(part, value[part * half // 2 : (part + 1) * half // 2], last_ref.at[rows], 0)


def product_rest(place, left, across, zero):
    rows, width = zero.shape
    vmem = pl.BlockSpec(memory_space=pltpu.VMEM)
    return pl.pallas_call(
        rest_kernel,
        out_shape=(
            jax.ShapeDtypeStruct((rows, 2 * width), BF16),
            jax.ShapeDtypeStruct((rows, 3 * width // 4), BF16),
        ),
        in_specs=[pl.BlockSpec(memory_space=pltpu.SMEM)] + [vmem] * 3,
        out_specs=(vmem, vmem),
        compiler_params=pltpu.CompilerParams(vmem_limit_bytes=6 * MIB),
        cost_estimate=LIGHT,
        name="product_rest",
    )(place, left, across, zero)


def pack_rows(part, value, out_ref, column):
    quarter, width = value.shape
    half = width // 2
    beside = (2, 3, 1, 0)[part] * quarter
    out_ref[:, column : column + half] = value[:, part // 2 * half : (part // 2 + 1) * half]
    out_ref[:, column + half : column + half + quarter] = value[:, beside : beside + quarter]


def unpacked_rows(part, packed_ref, column):
    quarter = packed_ref.shape[0] // 4
    half = 2 * quarter

    def beside(which):
        rows = slice(which * quarter, (which + 1) * quarter)
        return packed_ref[rows, column + half : column + half + quarter]

    rows = slice(part * quarter, (part + 1) * quarter)
    diagonal = packed_ref[rows, column : column + half]
    if part == 0:
        return diagonal, jnp.concatenate([beside(0), beside(3).T], axis=1)
    if part == 1:
        return diagonal, jnp.concatenate([beside(2).T, beside(1)], axis=1)
    if part == 2:
        return jnp.concatenate([beside(0).T, beside(2)], axis=1), diagonal
    return jnp.concatenate([beside(3), beside(1).T], axis=1), diagonal


def prior_kernel(place_ref, shifted_ref, sigma_ref, out_ref):
    @pl.when(place_ref[3] == 0)
    def _():
        out_ref[...] = shifted_ref[...]

    @pl.when(place_ref[3] != 0)
    def _():
        out_ref[...] = sigma_ref[...]


def halves_kernel(place_ref, first_ref, second_ref, near_ref, other_ref):
    near_ref[...] = first_ref[...]
    other_ref[...] = second_ref[...]


def halves(place, separator):
    rows, nodes = separator.shape
    chunk = rows // 4
    half = lambda side: pl.BlockSpec((chunk, nodes // 2), lambda i, place: (i, side(place[0])))
    out = jax.ShapeDtypeStruct((rows, nodes // 2), BF16)
    return pl.pallas_call(
        halves_kernel,
        out_shape=(out, out),
        grid_spec=pltpu.PrefetchScalarGridSpec(
            num_scalar_prefetch=1,
            grid=(4,),
            in_specs=[half(lambda odd: odd), half(lambda odd: 1 - odd)],
            out_specs=(half(lambda odd: 0), half(lambda odd: 0)),
        ),
        compiler_params=pltpu.CompilerParams(vmem_limit_bytes=6 * MIB),
        cost_estimate=LIGHT,
        name="halves",
    )(place, separator, separator)


def near_kernel(place_ref, shifted_ref, sigma_ref, row_ref, near_ref, last_ref):
    odd = place_ref[0]
    width = row_ref.shape[1] // 2
    prior_kernel(place_ref, shifted_ref, sigma_ref, row_ref)
    two = pl.ds(pl.multiple_of(odd * width, 128), width)
    three = pl.ds(pl.multiple_of((1 - odd) * width, 128), width)
    near_ref[:, :width] = row_ref[:, three]
    for part in range(4):

        @pl.when(pl.program_id(0) == part)
        def _():
            pack_rows(part, row_ref[:, two], near_ref, width)
            pack_rows(part, row_ref[:, three], last_ref, 0)


def other_half_kernel(place_ref, shifted_ref, sigma_ref, row_ref, far_ref):
    width = row_ref.shape[1] // 2
    prior_kernel(place_ref, shifted_ref, sigma_ref, row_ref)
    zero = pl.ds(pl.multiple_of(place_ref[0] * width, 128), width)
    for part in range(4):

        @pl.when(pl.program_id(0) == part)
        def _():
            pack_rows(part, row_ref[:, zero], far_ref, 0)


def prior_half(kernel, side, sent, place, shifted, sigma):
    rows, nodes = sigma.shape
    chunk = rows // 4
    quarters = (8,) + sent
    out = lambda count: jax.ShapeDtypeStruct((rows, count * nodes // 16), BF16)
    spec = lambda count: pl.BlockSpec((chunk, count * nodes // 16), lambda i, place: (i, 0))
    return pl.pallas_call(
        kernel,
        out_shape=tuple(out(count) for count in quarters),
        grid_spec=pltpu.PrefetchScalarGridSpec(
            num_scalar_prefetch=1,
            grid=(4,),
            in_specs=[
                pl.BlockSpec(
                    (chunk, nodes // 2), lambda i, place: (jnp.where(place[3] == 0, i, 0), 0)
                ),
                pl.BlockSpec(
                    (chunk, nodes // 2),
                    lambda i, place: (jnp.where(place[3] == 0, 0, i), side(place[0])),
                ),
            ],
            out_specs=tuple(spec(count) for count in quarters),
        ),
        compiler_params=pltpu.CompilerParams(vmem_limit_bytes=6 * MIB),
        cost_estimate=LIGHT,
        name="prior_half",
    )(place, shifted, sigma)


def assemble_kernel(place_ref, near, other, column, near_two, last_three, near_zero, far_zero, out_ref):
    @pl.when(place_ref[1] == 1)
    def _():
        odd = place_ref[0]
        width = near.shape[0]
        half, quarter = width // 2, width // 4

        def at(block, count=1):
            return pl.ds(pl.multiple_of(block * width, 128), count * width)

        first = 2 * (1 - odd)
        row = [turned(block, odd) for block in range(4)]
        out_ref[at(row[1]), at(first, 2)] = near[...]
        out_ref[at(row[1]), at(2 * odd, 2)] = other[...]
        out_ref[at(row[2]), at(row[3])] = near_two[:, :width]
        out_ref[at(row[3]), at(row[2])] = near_two[:, :width].T
        out_ref[at(row[0]), at(first, 2)] = near_zero[...]
        for step in range(2):
            out_ref[at(first + step), at(row[0])] = near_zero[:, step * width : (1 + step) * width].T
        for block in (0, 2, 3):
            out_ref[at(row[block]), at(row[1])] = column[at(row[block]), :]
        packed = ((0, far_zero, 0), (2, near_two, width), (3, last_three, 0))
        for block, packed_ref, start in packed:
            for part in range(4):
                rows = pl.ds(pl.multiple_of(row[block] * width + part * quarter, 128), quarter)
                for side, value in enumerate(unpacked_rows(part, packed_ref, start)):
                    columns = pl.ds(pl.multiple_of(row[block] * width + side * half, 128), half)
                    out_ref[rows, columns] = value


def assemble(place, *parts):
    nodes = 2 * parts[0].shape[1]
    vmem = pl.BlockSpec(memory_space=pltpu.VMEM)
    return pl.pallas_call(
        assemble_kernel,
        out_shape=jax.ShapeDtypeStruct((nodes, nodes), BF16),
        in_specs=[pl.BlockSpec(memory_space=pltpu.SMEM)] + [vmem] * 7,
        out_specs=vmem,
        compiler_params=pltpu.CompilerParams(vmem_limit_bytes=6 * MIB),
        cost_estimate=LIGHT,
        name="assemble",
    )(place, *parts)


def tick(place, *values, cost=HEAVY):
    def kernel(place_ref, *refs):
        for which in range(place.shape[0]):
            refs[-1][which] = place_ref[which]

    scalars = pl.BlockSpec(memory_space=pltpu.SMEM)
    return pl.pallas_call(
        kernel,
        out_shape=jax.ShapeDtypeStruct(place.shape, place.dtype),
        in_specs=[scalars] + [pl.BlockSpec(memory_space=pl.ANY)] * len(values),
        out_specs=scalars,
        compiler_params=pltpu.CompilerParams(vmem_limit_bytes=MIB),
        cost_estimate=cost,
        name="tick",
    )(place, *values)


def finish_kernel(
    place_ref, pivot_ref, sigma_ref,
    q0, q0_last, q2, q3_two,
    q01, q11, q21, q31,
    out_ref, var_ref,
):
    rows, nodes = pivot_ref.shape
    width = nodes // 4
    odd, place = place_ref[0], place_ref[1]
    here = pl.multiple_of(pl.program_id(0) * rows, 128)
    diagonal = diagonal_of(rows)

    def at(block, count=1):
        return pl.ds(pl.multiple_of(block * width, 128), count * width)

    def own(block):
        return pl.ds(pl.multiple_of(block * width + here, 128), rows)

    def add(columns, product):
        out_ref[:, columns] = (pivot_ref[:, columns].astype(F32) + product.astype(F32)).astype(BF16)

    def trace(product):
        var_ref[...] = diagonal(
            pivot_ref[:, own(place_ref[2])].astype(F32) + product.astype(F32)
        )

    active = place_ref[4] != 0

    @pl.when(active & (place == 0))
    def _():
        add(at(odd, 3), q0[...])
        add(at(turned(3, odd)), q0_last[...])
        trace(q0[:, own(2 * odd)])

    @pl.when(active & (place == 1))
    def _():
        add(at(turned(0, odd)), q01[...].T)
        add(at(turned(1, odd)), q11[...])
        add(at(turned(2, odd)), q21[...].T)
        add(at(turned(3, odd)), q31[...].T)
        trace(q11[:, pl.ds(here, rows)])

    @pl.when(active & (place == 2))
    def _():
        add(at(turned(0, odd)), q2[pl.ds(0, width), pl.ds(pl.multiple_of(width + here, 128), rows)].T)
        add(at(turned(1, odd)), q2[pl.ds(here, rows), pl.ds(0, width)])
        start = pl.program_id(0) % 2 * rows + 2 * width
        trace(q2[pl.ds(here, rows), pl.ds(pl.multiple_of(start, 128), rows)])
        for part in range(4):

            @pl.when(pl.program_id(0) == part)
            def _():
                for side, value in enumerate(unpacked_rows(part, q2, 2 * width)):
                    start = turned(2, odd) * width + side * width // 2
                    add(pl.ds(pl.multiple_of(start, 128), width // 2), value)

    @pl.when(active & (place == 3))
    def _():
        add(at(turned(2, odd)), q3_two[...])

    @pl.when(place_ref[4] == 0)
    def _():
        out_ref[...] = sigma_ref[...]
        var_ref[...] = diagonal(sigma_ref[:, own(place_ref[2])].astype(F32))


def finish(place, pivot, sigma, received, kept):
    rows, nodes = pivot.shape
    chunk = 128
    width = nodes // 4

    def picked(which, blocks):
        return pl.BlockSpec(
            (chunk, blocks * width), lambda i, place: (jnp.where(place[1] == which, i, 0), 0)
        )

    def turned_block(start):
        return pl.BlockSpec(
            (rows, chunk),
            lambda i, place: (
                0,
                jnp.where(place[1] == 1, start(place[0]) * (width // chunk) + i, 0),
            ),
        )

    return pl.pallas_call(
        finish_kernel,
        out_shape=(
            jax.ShapeDtypeStruct((rows, nodes), BF16),
            jax.ShapeDtypeStruct((1, rows), F32),
        ),
        grid_spec=pltpu.PrefetchScalarGridSpec(
            num_scalar_prefetch=1,
            grid=(rows // chunk,),
            in_specs=[
                pl.BlockSpec((chunk, nodes), lambda i, place: (i, 0)),
                pl.BlockSpec(
                    (chunk, nodes), lambda i, place: (jnp.where(place[4] == 0, i, 0), 0)
                ),
                picked(0, 3),
                picked(0, 1),
                pl.BlockSpec((rows, 11 * width // 4), lambda i, place: (0, 0)),
                picked(3, 1),
                turned_block(lambda odd: 1),
                picked(1, 1),
                turned_block(lambda odd: 0),
                turned_block(lambda odd: 1 - odd),
            ],
            out_specs=(
                pl.BlockSpec((chunk, nodes), lambda i, place: (i, 0)),
                pl.BlockSpec((1, chunk), lambda i, place: (0, i)),
            ),
        ),
        compiler_params=pltpu.CompilerParams(vmem_limit_bytes=12 * MIB),
        cost_estimate=HEAVY,
        name="finish",
    )(place, pivot, sigma, *received, *kept)


def add_in_place(pivot_ref, out_ref, sum_ref, sems, column, product):
    chunk = pivot_ref.shape[0] // 4
    copies = []
    for part in range(4):
        here = pl.ds(part * chunk, chunk)
        value = pivot_ref[here, :].astype(F32) + product(part, here).astype(F32)
        sum_ref[here, :] = value.astype(BF16)
        copies.append(
            pltpu.make_async_copy(sum_ref.at[here], out_ref.at[here, column], sems.at[part])
        )
        copies[-1].start()
    return copies


def other_kernel(place_ref, pivot_ref, q3_other, old_ref, out_ref, sum_ref, sems):
    both = pivot_ref.shape[1]
    column = pl.ds(pl.multiple_of(place_ref[0] * both, 128), both)

    @pl.when((place_ref[4] != 0) & (place_ref[1] == 3))
    def _():
        product = lambda part, here: q3_other[here, :]
        for copy in add_in_place(pivot_ref, out_ref, sum_ref, sems, column, product):
            copy.wait()


def last_kernel(
    place_ref, pivot_ref, q2_last, q3_last, old_ref, old_var_ref, out_ref, var_ref, sum_ref, sems
):
    rows, width = pivot_ref.shape
    chunk = rows // 4
    active = place_ref[4] != 0
    column = pl.ds(pl.multiple_of(turned(3, place_ref[0]) * width, 128), width)
    add = functools.partial(add_in_place, pivot_ref, out_ref, sum_ref, sems, column)
    var_ref[...] = old_var_ref[...]

    @pl.when(active & (place_ref[1] == 2))
    def _():
        for copy in add(lambda part, here: q2_last[:, here].T):
            copy.wait()

    @pl.when(active & (place_ref[1] == 3))
    def _():
        copies = add(lambda part, here: jnp.concatenate(unpacked_rows(part, q3_last, 0), axis=1))
        for start in range(0, rows, chunk):
            here = pl.ds(start, chunk)
            value = pivot_ref[here, here].astype(F32)
            value = value + q3_last[here, pl.ds(start % (2 * chunk), chunk)].astype(F32)
            var_ref[:, here] = diagonal_of(chunk)(value)
        for copy in copies:
            copy.wait()


def diagonal_of(rows):
    square = (rows, rows)
    on_diagonal = lax.broadcasted_iota(jnp.int32, square, 0) == lax.broadcasted_iota(
        jnp.int32, square, 1
    )
    return lambda value: jnp.sum(jnp.where(on_diagonal, value, 0.0), axis=0, keepdims=True)


def finish_other(place, pivot, q3_other, covariance):
    rows, nodes = pivot.shape
    vmem = pl.BlockSpec(memory_space=pltpu.VMEM)
    anywhere = pl.BlockSpec(memory_space=pl.ANY)
    return pl.pallas_call(
        other_kernel,
        out_shape=jax.ShapeDtypeStruct((rows, nodes), BF16),
        grid_spec=pltpu.PrefetchScalarGridSpec(
            num_scalar_prefetch=1,
            grid=(1,),
            in_specs=[
                pl.BlockSpec((rows, nodes // 2), lambda i, place: (0, place[0])),
                vmem,
                anywhere,
            ],
            out_specs=anywhere,
            scratch_shapes=[pltpu.VMEM((rows, nodes // 2), BF16), pltpu.SemaphoreType.DMA((4,))],
        ),
        input_output_aliases={3: 0},
        compiler_params=pltpu.CompilerParams(vmem_limit_bytes=8 * MIB),
        cost_estimate=LIGHT,
        name="finish_other",
    )(place, pivot, q3_other, covariance)


def finish_last(place, pivot, q2_last, q3_last, covariance, variances):
    rows, nodes = pivot.shape
    vmem = pl.BlockSpec(memory_space=pltpu.VMEM)
    anywhere = pl.BlockSpec(memory_space=pl.ANY)
    return pl.pallas_call(
        last_kernel,
        out_shape=(
            jax.ShapeDtypeStruct((rows, nodes), BF16),
            jax.ShapeDtypeStruct((1, rows), F32),
        ),
        grid_spec=pltpu.PrefetchScalarGridSpec(
            num_scalar_prefetch=1,
            grid=(1,),
            in_specs=[
                pl.BlockSpec((rows, nodes // 4), lambda i, place: (0, turned(3, place[0]))),
                vmem,
                vmem,
                anywhere,
                vmem,
            ],
            out_specs=(anywhere, vmem),
            scratch_shapes=[pltpu.VMEM((rows, nodes // 4), BF16), pltpu.SemaphoreType.DMA((4,))],
        ),
        input_output_aliases={4: 0},
        compiler_params=pltpu.CompilerParams(vmem_limit_bytes=8 * MIB),
        cost_estimate=LIGHT,
        name="finish_last",
    )(place, pivot, q2_last, q3_last, covariance, variances)


def owned(sigma_next, separator, inverse_pivot, coupling_rate, lengths, step_index, node_class):
    sigma, pivot = sigma_next[0], inverse_pivot[0]
    odd = lax.axis_index("dom") % 2
    col = lax.axis_index("col")
    step = step_index[0]
    place = jnp.stack([odd, turned(col, odd), col, step, step < lengths[0]]).astype(jnp.int32)
    after = lambda value, *others: lax.optimization_barrier((value, *others))[0]

    p2 = moved(pivot, 2, 1)
    p0 = moved(pivot, 0, 1)
    weights = coupling(node_class)
    c1 = [couple(pivot, weights, coupling_rate, part, 2) for part in range(2)]
    across = turn(place, 1, 0, c1[0], None)
    across = turn(place, 1, 1, c1[1], across)

    near, other = halves(place, separator[0])
    near, other = passed_along(near, "dom", -1), passed_along(other, "dom", -1)
    sides = (lambda odd: 1 - odd, lambda odd: odd)
    row_near, near, last = prior_half(
        near_kernel, sides[0], (7, 3), place, after(near, across), sigma
    )
    near_zero, near_two = moved(row_near, 0, 1), moved(near, 2, 1)
    last_three = moved(last, 3, 1)
    c2 = couple_here(place, after(p2, last), weights, coupling_rate)
    across = turn(place, 2, 0, c2, across)
    row_other, far = prior_half(
        other_half_kernel, sides[1], (3,), place, after(other, across), sigma
    )
    far_zero = moved(far, 0, 1)
    c0 = couple_here(place, after(p0, across, far), weights, coupling_rate)
    across = turn(place, 0, 0, c0, across)
    column, h0_one, h2_one = own_column(place, row_near, row_other, c0, c2)
    c3 = [
        moved(after(c1[0], last_three, near_two, near_zero, h2_one, across), 3, 1),
        moved(after(c1[1], far_zero, h2_one), 3, 1),
    ]
    prior = assemble(place, row_near, row_other, column, near_two, last_three, near_zero, far_zero)

    h0 = half_product(place, c0, prior, h0_one)
    q0_own = multiply(place, [h0], across, lambda odd: odd, 3)
    q0 = moved(q0_own, 1, 0)
    h2 = half_product(place, after(c2, q0_own), prior, h2_one)
    q2_own = product_two(place, h2, across, q0_own)
    q2 = moved(q2_own, 1, 2)

    across = turn(place, 3, 0, c3[0], after(across, q2_own))
    across = turn(place, 3, 1, c3[1], across)
    q03 = multiply(place, [h0], across, lambda odd: 3 - 3 * odd, 1)
    q0_last = moved(q03, 1, 0)
    h3 = multiply(place, [after(c3[0], q03), c3[1]], prior)
    q32 = multiply(place, [h3], across, lambda odd: 2 - odd, 1)
    q3_two = moved(q32, 1, 3)
    q3_own, q33 = product_rest(place, h3, across, after(q03, q32))
    q3_other, q3_last = moved(q3_own, 1, 3), moved(q33, 1, 3)
    h1 = multiply(place, [after(c1[0], q3_own), c1[1]], prior)
    q11 = multiply(place, [h1], across, lambda odd: 1 + odd, 1)
    received = (q0, q0_last, q2, q3_two)
    kept = (q0_own, q11, q2_own, q3_own)
    place_then = tick(tick(place, q0, cost=LIGHT), q0_last, cost=MEDIUM)
    q2_last = moved(after(q3_two, place_then), 3, 2)
    covariance, variances = finish(place_then, pivot, sigma, received, kept)
    covariance = finish_other(place, pivot, q3_other, covariance)
    covariance, variances = finish_last(place, pivot, q2_last, q3_last, covariance, variances)
    return (covariance[None], variances)


def gathered(sigma_next, separator, inverse_pivot, coupling_rate, lengths, step_index, node_class):
    shifted = passed_along(separator, "dom", -1)
    prior = jnp.where(step_index[0] == 0, shifted[0], sigma_next[0])
    pivot = inverse_pivot[0].astype(F32)
    coupled = couple(inverse_pivot[0], coupling(node_class), coupling_rate)
    rows = coupled.shape[0]
    half = jnp.dot(
        coupled,
        lax.all_gather(prior, "col", axis=0, tiled=True),
        preferred_element_type=F32,
    ).astype(BF16)
    product = lax.dot_general(
        half,
        lax.all_gather(coupled, "col", axis=0, tiled=True),
        (((1,), (1,)), ((), ())),
        preferred_element_type=F32,
    )
    full = pivot + product
    active = step_index[0] < lengths[0]
    old = sigma_next[0]
    covariance = jnp.where(active, full.astype(BF16), old)
    first_col = lax.axis_index("col") * rows
    new_block = lax.dynamic_slice_in_dim(full, first_col, rows, 1)
    old_block = lax.dynamic_slice_in_dim(old, first_col, rows, 1)
    variances = jnp.where(active, jnp.diagonal(new_block), jnp.diagonal(old_block).astype(F32))
    return (covariance[None], variances[None])


def solution(mesh):
    local = owned if mesh.shape["col"] == 4 and mesh.shape["dom"] % 2 == 0 else gathered
    return jax.shard_map(
        local,
        mesh=mesh,
        in_specs=(
            P(("groups", "dom"), "col", None),
            P(("groups", "dom"), "col", None),
            P(("groups", "dom"), "col", None),
            P(("groups", "dom")),
            P(("groups", "dom")),
            P(("groups", "dom")),
            P("groups"),
        ),
        out_specs=(P(("groups", "dom"), "col", None), P(("groups", "dom"), "col")),
        check_vma=False,
    )
```

```python
import functools

import jax
import jax.numpy as jnp
from jax import lax
from jax.experimental import pallas as pl
from jax.experimental.pallas import tpu as pltpu
from jax.sharding import PartitionSpec as P

GX = 64
GY = 32
BF16 = jnp.bfloat16
F32 = jnp.float32
MIB = 1 << 20


def passed_along(value, axis, steps):
    count = lax.axis_size(axis)
    initial, last = (max(0, -steps), min(count, count - steps))
    return lax.ppermute(value, axis, [(source, source + steps) for source in range(initial, last)])


LIGHT = pl.CostEstimate(flops=1 << 20, bytes_accessed=1 << 16, transcendentals=0)
MEDIUM = pl.CostEstimate(flops=2000000000, bytes_accessed=1 << 16, transcendentals=0)
HEAVY = pl.CostEstimate(flops=14000000000, bytes_accessed=1 << 16, transcendentals=0)


BLOCK = 256
SPAN = 512


def window(block, nodes):
    return pl.multiple_of(jnp.clip(block * BLOCK - (SPAN - BLOCK) // 2, 0, nodes - SPAN), 128)


def weight_kernel(class_ref, out_ref):
    nodes = class_ref.shape[1]

    def fill(block, carry):
        first = pl.multiple_of(block * BLOCK, BLOCK)
        kind = class_ref[:, pl.ds(first, BLOCK)]
        across = jnp.where(
            kind == 0, 0.25, jnp.where(kind == 1, 0.375, jnp.where(kind == 2, 0.125, 0.5))
        ).astype(F32)
        along = jnp.where(
            kind == 0, 0.25, jnp.where(kind == 1, 0.125, jnp.where(kind == 2, 0.375, 0.0))
        ).astype(F32)
        column = (first + lax.broadcasted_iota(jnp.int32, (1, BLOCK), 1)) % GX
        left = jnp.where(column > 0, across, 0.0)
        right = jnp.where(column < GX - 1, across, 0.0)
        shape = (SPAN, BLOCK)
        offset = (
            lax.broadcasted_iota(jnp.int32, shape, 0)
            - lax.broadcasted_iota(jnp.int32, shape, 1)
            + (window(block, nodes) - first)
        )
        value = jnp.where(jnp.abs(offset) == GX, along, 0.0)
        value = jnp.where(offset == -1, left, value)
        value = jnp.where(offset == 1, right, value)
        value = jnp.where(offset == 0, 1.0, value)
        out_ref[block] = value.astype(BF16)
        return carry

    lax.fori_loop(0, nodes // BLOCK, fill, 0)


def coupling(node_class):
    nodes = node_class.shape[0]
    vmem = pl.BlockSpec(memory_space=pltpu.VMEM)
    return pl.pallas_call(
        weight_kernel,
        out_shape=jax.ShapeDtypeStruct((nodes // BLOCK, SPAN, BLOCK), BF16),
        in_specs=[vmem],
        out_specs=vmem,
        compiler_params=pltpu.CompilerParams(vmem_limit_bytes=6 * MIB),
        cost_estimate=LIGHT,
        name="coupling",
    )(node_class.reshape(1, nodes))


def couple_kernel(first, rate_ref, weight_ref, pivot_ref, out_ref):
    rows, nodes = out_ref.shape

    def block_of(block, carry):
        source = pl.ds(window(block, nodes), SPAN)
        target = pl.ds(pl.multiple_of(block * BLOCK, BLOCK), BLOCK)
        value = jnp.dot(
            pivot_ref[first : first + rows, source], weight_ref[block], preferred_element_type=F32
        )
        out_ref[:, target] = (rate_ref[0] * value).astype(BF16)
        return carry

    lax.fori_loop(0, nodes // BLOCK, block_of, 0)


def couple(pivot, weights, rate, part=0, parts=1):
    rows, nodes = pivot.shape[0] // parts, pivot.shape[1]
    vmem = pl.BlockSpec(memory_space=pltpu.VMEM)
    return pl.pallas_call(
        functools.partial(couple_kernel, part * rows),
        out_shape=jax.ShapeDtypeStruct((rows, nodes), BF16),
        in_specs=[pl.BlockSpec(memory_space=pltpu.SMEM), vmem, vmem],
        out_specs=vmem,
        compiler_params=pltpu.CompilerParams(vmem_limit_bytes=8 * MIB),
        cost_estimate=LIGHT,
        name="couple",
    )(rate, weights, pivot)


def turned(block, odd):
    return block + odd * (3 - 2 * block)


def route(source, target, doms):
    pairs = []
    for dom in range(doms):
        odd = dom % 2
        pairs.append((dom * 4 + turned(source, odd), dom * 4 + turned(target, odd)))
    return pairs


def moved(value, source, target):
    return lax.ppermute(value, ("dom", "col"), route(source, target, lax.axis_size("dom")))


def couple_here(place, pivot, weights, rate):
    def kernel(place_ref, *refs):
        @pl.when(place_ref[1] == 1)
        def _():
            couple_kernel(0, *refs)

    scalars, vmem = pl.BlockSpec(memory_space=pltpu.SMEM), pl.BlockSpec(memory_space=pltpu.VMEM)
    return pl.pallas_call(
        kernel,
        out_shape=jax.ShapeDtypeStruct(pivot.shape, BF16),
        in_specs=[scalars, scalars, vmem, vmem],
        out_specs=vmem,
        compiler_params=pltpu.CompilerParams(vmem_limit_bytes=8 * MIB),
        cost_estimate=LIGHT,
        name="couple_here",
    )(place, rate, weights, pivot)


def turn_kernel(place_ref, coupled_ref, *refs):
    @pl.when(place_ref[1] == 1)
    def _():
        refs[-1][...] = coupled_ref[...].T


def turn(place, panel, part, coupled, across):
    rows, nodes = coupled.shape
    chunk = 128
    steps = rows // chunk
    ratio = nodes // 4 // chunk
    return pl.pallas_call(
        turn_kernel,
        out_shape=jax.ShapeDtypeStruct((nodes, nodes), BF16),
        grid_spec=pltpu.PrefetchScalarGridSpec(
            num_scalar_prefetch=1,
            grid=(steps,),
            in_specs=[pl.BlockSpec((chunk, nodes), lambda i, place: (i, 0))]
            + ([] if across is None else [pl.BlockSpec(memory_space=pl.ANY)]),
            out_specs=pl.BlockSpec(
                (nodes, chunk),
                lambda i, place: (0, turned(panel, place[0]) * ratio + part * steps + i),
            ),
        ),
        input_output_aliases={} if across is None else {2: 0},
        compiler_params=pltpu.CompilerParams(vmem_limit_bytes=4 * MIB),
        cost_estimate=LIGHT,
        name="turn",
    )(place, coupled, *(() if across is None else (across,)))


def multiply_kernel(first, count, lefts, place_ref, *refs):
    left_refs, right_ref, out_ref = refs[:lefts], refs[lefts], refs[-1]
    width = right_ref.shape[0] // 4

    @pl.when(place_ref[1] == 1)
    def _():
        def block(step, carry):
            source = pl.multiple_of((first(place_ref[0]) + step) * width, 128)
            target = pl.multiple_of(step * width, 128)
            row = 0
            for left_ref in left_refs:
                rows = left_ref.shape[0]
                out_ref[row : row + rows, pl.ds(target, width)] = jnp.dot(
                    left_ref[...], right_ref[:, pl.ds(source, width)], preferred_element_type=F32
                ).astype(BF16)
                row += rows
            return carry

        lax.fori_loop(0, count, block, 0)


def multiply(place, lefts, right, first=lambda odd: 0, count=4):
    rows = sum(left.shape[0] for left in lefts)
    width = right.shape[0] // 4
    vmem = pl.BlockSpec(memory_space=pltpu.VMEM)
    return pl.pallas_call(
        functools.partial(multiply_kernel, first, count, len(lefts)),
        out_shape=jax.ShapeDtypeStruct((rows, count * width), BF16),
        in_specs=[pl.BlockSpec(memory_space=pltpu.SMEM)] + [vmem] * (len(lefts) + 1),
        out_specs=vmem,
        compiler_params=pltpu.CompilerParams(vmem_limit_bytes=6 * MIB),
        cost_estimate=LIGHT,
        name="multiply",
    )(place, *lefts, right)


def pack(value, out_ref, column):
    quarter = value.shape[1] // 4
    for part in range(4):
        rows = pl.ds(part * quarter, quarter)
        pack_rows(part, value[part * quarter : (part + 1) * quarter], out_ref.at[rows], column)


def two_kernel(place_ref, left_ref, right_ref, zero_ref, out_ref):
    odd = place_ref[0]
    width = right_ref.shape[0] // 4

    def product(block):
        columns = pl.ds(pl.multiple_of(block * width, 128), width)
        value = jnp.dot(left_ref[...], right_ref[:, columns], preferred_element_type=F32)
        return value.astype(BF16)

    @pl.when(place_ref[1] == 1)
    def _():
        out_ref[:, :width] = product(1 + odd)
        zero = pl.ds(pl.multiple_of((2 - 2 * odd) * width, 128), width)
        out_ref[:, width : 2 * width] = zero_ref[:, zero]
        pack(product(2 - odd), out_ref, 2 * width)


def product_two(place, half, across, zero):
    rows = half.shape[0]
    width = across.shape[0] // 4
    vmem = pl.BlockSpec(memory_space=pltpu.VMEM)
    return pl.pallas_call(
        two_kernel,
        out_shape=jax.ShapeDtypeStruct((rows, 11 * width // 4), BF16),
        in_specs=[pl.BlockSpec(memory_space=pltpu.SMEM)] + [vmem] * 3,
        out_specs=vmem,
        compiler_params=pltpu.CompilerParams(vmem_limit_bytes=6 * MIB),
        cost_estimate=LIGHT,
        name="product_two",
    )(place, half, across, zero)


def half_kernel(place_ref, left_ref, right_ref, one_ref, out_ref):
    width = one_ref.shape[1]

    @pl.when(place_ref[1] == 1)
    def _():
        def block(step, carry):
            which = turned(step + (step > 0).astype(jnp.int32), place_ref[0])
            columns = pl.ds(pl.multiple_of(which * width, 128), width)
            out_ref[:, columns] = jnp.dot(
                left_ref[...], right_ref[:, columns], preferred_element_type=F32
            ).astype(BF16)
            return carry

        lax.fori_loop(0, 3, block, 0)
        columns = pl.ds(pl.multiple_of(turned(1, place_ref[0]) * width, 128), width)
        out_ref[:, columns] = one_ref[...]


def half_product(place, left, right, one):
    vmem = pl.BlockSpec(memory_space=pltpu.VMEM)
    return pl.pallas_call(
        half_kernel,
        out_shape=jax.ShapeDtypeStruct(left.shape, BF16),
        in_specs=[pl.BlockSpec(memory_space=pltpu.SMEM)] + [vmem] * 3,
        out_specs=vmem,
        compiler_params=pltpu.CompilerParams(vmem_limit_bytes=6 * MIB),
        cost_estimate=LIGHT,
        name="half_product",
    )(place, left, right, one)


def column_kernel(place_ref, near_ref, other_ref, first_ref, second_ref, *refs):
    column_ref, out_refs = refs[0], refs[1:]

    @pl.when(place_ref[1] == 1)
    def _():
        odd = place_ref[0]
        width = near_ref.shape[0]
        for half, half_ref in ((1 - odd, near_ref), (odd, other_ref)):
            for block in range(2):
                rows = pl.ds(pl.multiple_of((2 * half + block) * width, 128), width)
                column_ref[rows, :] = half_ref[:, block * width : (block + 1) * width].T
        for left_ref, out_ref in zip((first_ref, second_ref), out_refs):
            out_ref[...] = jnp.dot(
                left_ref[...], column_ref[...], preferred_element_type=F32
            ).astype(BF16)


def own_column(place, near, other, first, second):
    rows, nodes = first.shape
    vmem = pl.BlockSpec(memory_space=pltpu.VMEM)
    return pl.pallas_call(
        column_kernel,
        out_shape=(
            jax.ShapeDtypeStruct((nodes, rows), BF16),
            jax.ShapeDtypeStruct((rows, rows), BF16),
            jax.ShapeDtypeStruct((rows, rows), BF16),
        ),
        in_specs=[pl.BlockSpec(memory_space=pltpu.SMEM)] + [vmem] * 4,
        out_specs=(vmem, vmem, vmem),
        compiler_params=pltpu.CompilerParams(vmem_limit_bytes=6 * MIB),
        cost_estimate=LIGHT,
        name="own_column",
    )(place, near, other, first, second)


def rest_kernel(place_ref, left_ref, right_ref, zero_ref, out_ref, last_ref):
    odd = place_ref[0]
    width = zero_ref.shape[1]
    half = width // 2

    def product(rows, block):
        columns = pl.ds(pl.multiple_of(block * width, 128), width)
        value = jnp.dot(left_ref[rows, :], right_ref[:, columns], preferred_element_type=F32)
        return value.astype(BF16)

    @pl.when(place_ref[1] == 1)
    def _():
        out_ref[:, pl.ds(pl.multiple_of(odd * width, 128), width)] = zero_ref[...].T
        other = pl.ds(pl.multiple_of((1 - odd) * width, 128), width)
        out_ref[:, other] = product(pl.ds(0, width), 1 + odd)
        value = product(pl.ds(0, width), 3 - 3 * odd)
        for part in range(4):
            rows = pl.ds(part * half // 2, half // 2)
            pack_rows(part, value[part * half // 2 : (part + 1) * half // 2], last_ref.at[rows], 0)


def product_rest(place, left, across, zero):
    rows, width = zero.shape
    vmem = pl.BlockSpec(memory_space=pltpu.VMEM)
    return pl.pallas_call(
        rest_kernel,
        out_shape=(
            jax.ShapeDtypeStruct((rows, 2 * width), BF16),
            jax.ShapeDtypeStruct((rows, 3 * width // 4), BF16),
        ),
        in_specs=[pl.BlockSpec(memory_space=pltpu.SMEM)] + [vmem] * 3,
        out_specs=(vmem, vmem),
        compiler_params=pltpu.CompilerParams(vmem_limit_bytes=6 * MIB),
        cost_estimate=LIGHT,
        name="product_rest",
    )(place, left, across, zero)


def pack_rows(part, value, out_ref, column):
    quarter, width = value.shape
    half = width // 2
    beside = (2, 3, 1, 0)[part] * quarter
    out_ref[:, column : column + half] = value[:, part // 2 * half : (part // 2 + 1) * half]
    out_ref[:, column + half : column + half + quarter] = value[:, beside : beside + quarter]


def unpacked_rows(part, packed_ref, column):
    quarter = packed_ref.shape[0] // 4
    half = 2 * quarter

    def beside(which):
        rows = slice(which * quarter, (which + 1) * quarter)
        return packed_ref[rows, column + half : column + half + quarter]

    rows = slice(part * quarter, (part + 1) * quarter)
    diagonal = packed_ref[rows, column : column + half]
    if part == 0:
        return diagonal, jnp.concatenate([beside(0), beside(3).T], axis=1)
    if part == 1:
        return diagonal, jnp.concatenate([beside(2).T, beside(1)], axis=1)
    if part == 2:
        return jnp.concatenate([beside(0).T, beside(2)], axis=1), diagonal
    return jnp.concatenate([beside(3), beside(1).T], axis=1), diagonal


def prior_kernel(place_ref, shifted_ref, sigma_ref, out_ref):
    @pl.when(place_ref[3] == 0)
    def _():
        out_ref[...] = shifted_ref[...]

    @pl.when(place_ref[3] != 0)
    def _():
        out_ref[...] = sigma_ref[...]


def halves_kernel(place_ref, separator_ref, near_ref, other_ref, sems):
    half = near_ref.shape[1]
    copies = []
    for which, (side, out_ref) in enumerate(((place_ref[0], near_ref), (1 - place_ref[0], other_ref))):
        source = separator_ref.at[:, pl.ds(pl.multiple_of(side * half, 128), half)]
        copies.append(pltpu.make_async_copy(source, out_ref, sems.at[which]))
        copies[-1].start()
    for copy in copies:
        copy.wait()


def halves(place, separator):
    rows, nodes = separator.shape
    vmem = pl.BlockSpec(memory_space=pltpu.VMEM)
    return pl.pallas_call(
        halves_kernel,
        out_shape=(jax.ShapeDtypeStruct((rows, nodes // 2), BF16),) * 2,
        in_specs=[pl.BlockSpec(memory_space=pltpu.SMEM), pl.BlockSpec(memory_space=pltpu.HBM)],
        out_specs=(vmem, vmem),
        scratch_shapes=[pltpu.SemaphoreType.DMA((2,))],
        compiler_params=pltpu.CompilerParams(vmem_limit_bytes=6 * MIB),
        cost_estimate=LIGHT,
        name="halves",
    )(place, separator)


def near_kernel(place_ref, shifted_ref, sigma_ref, row_ref, near_ref, last_ref):
    odd = place_ref[0]
    width = row_ref.shape[1] // 2
    prior_kernel(place_ref, shifted_ref, sigma_ref, row_ref)
    two = pl.ds(pl.multiple_of(odd * width, 128), width)
    three = pl.ds(pl.multiple_of((1 - odd) * width, 128), width)
    near_ref[:, :width] = row_ref[:, three]
    for part in range(4):

        @pl.when(pl.program_id(0) == part)
        def _():
            pack_rows(part, row_ref[:, two], near_ref, width)
            pack_rows(part, row_ref[:, three], last_ref, 0)


def other_half_kernel(place_ref, shifted_ref, sigma_ref, row_ref, far_ref):
    width = row_ref.shape[1] // 2
    prior_kernel(place_ref, shifted_ref, sigma_ref, row_ref)
    zero = pl.ds(pl.multiple_of(place_ref[0] * width, 128), width)
    for part in range(4):

        @pl.when(pl.program_id(0) == part)
        def _():
            pack_rows(part, row_ref[:, zero], far_ref, 0)


def prior_half(kernel, side, sent, place, shifted, sigma):
    rows, nodes = sigma.shape
    chunk = rows // 4
    quarters = (8,) + sent
    out = lambda count: jax.ShapeDtypeStruct((rows, count * nodes // 16), BF16)
    spec = lambda count: pl.BlockSpec((chunk, count * nodes // 16), lambda i, place: (i, 0))
    return pl.pallas_call(
        kernel,
        out_shape=tuple(out(count) for count in quarters),
        grid_spec=pltpu.PrefetchScalarGridSpec(
            num_scalar_prefetch=1,
            grid=(4,),
            in_specs=[
                pl.BlockSpec(
                    (chunk, nodes // 2), lambda i, place: (jnp.where(place[3] == 0, i, 0), 0)
                ),
                pl.BlockSpec(
                    (chunk, nodes // 2),
                    lambda i, place: (jnp.where(place[3] == 0, 0, i), side(place[0])),
                ),
            ],
            out_specs=tuple(spec(count) for count in quarters),
        ),
        compiler_params=pltpu.CompilerParams(vmem_limit_bytes=6 * MIB),
        cost_estimate=LIGHT,
        name="prior_half",
    )(place, shifted, sigma)


def assemble_kernel(place_ref, near, other, column, near_two, last_three, near_zero, far_zero, out_ref):
    @pl.when(place_ref[1] == 1)
    def _():
        odd = place_ref[0]
        width = near.shape[0]
        half, quarter = width // 2, width // 4

        def at(block, count=1):
            return pl.ds(pl.multiple_of(block * width, 128), count * width)

        first = 2 * (1 - odd)
        row = [turned(block, odd) for block in range(4)]
        out_ref[at(row[1]), at(first, 2)] = near[...]
        out_ref[at(row[1]), at(2 * odd, 2)] = other[...]
        out_ref[at(row[2]), at(row[3])] = near_two[:, :width]
        out_ref[at(row[3]), at(row[2])] = near_two[:, :width].T
        out_ref[at(row[0]), at(first, 2)] = near_zero[...]
        for step in range(2):
            out_ref[at(first + step), at(row[0])] = near_zero[:, step * width : (1 + step) * width].T
        for block in (0, 2, 3):
            out_ref[at(row[block]), at(row[1])] = column[at(row[block]), :]
        packed = ((0, far_zero, 0), (2, near_two, width), (3, last_three, 0))
        for block, packed_ref, start in packed:
            for part in range(4):
                rows = pl.ds(pl.multiple_of(row[block] * width + part * quarter, 128), quarter)
                for side, value in enumerate(unpacked_rows(part, packed_ref, start)):
                    columns = pl.ds(pl.multiple_of(row[block] * width + side * half, 128), half)
                    out_ref[rows, columns] = value


def assemble(place, *parts):
    nodes = 2 * parts[0].shape[1]
    vmem = pl.BlockSpec(memory_space=pltpu.VMEM)
    return pl.pallas_call(
        assemble_kernel,
        out_shape=jax.ShapeDtypeStruct((nodes, nodes), BF16),
        in_specs=[pl.BlockSpec(memory_space=pltpu.SMEM)] + [vmem] * 7,
        out_specs=vmem,
        compiler_params=pltpu.CompilerParams(vmem_limit_bytes=6 * MIB),
        cost_estimate=LIGHT,
        name="assemble",
    )(place, *parts)


def tick(place, *values, cost=HEAVY):
    def kernel(place_ref, *refs):
        for which in range(place.shape[0]):
            refs[-1][which] = place_ref[which]

    scalars = pl.BlockSpec(memory_space=pltpu.SMEM)
    return pl.pallas_call(
        kernel,
        out_shape=jax.ShapeDtypeStruct(place.shape, place.dtype),
        in_specs=[scalars] + [pl.BlockSpec(memory_space=pl.ANY)] * len(values),
        out_specs=scalars,
        compiler_params=pltpu.CompilerParams(vmem_limit_bytes=MIB),
        cost_estimate=cost,
        name="tick",
    )(place, *values)


def finish_kernel(
    place_ref, pivot_ref, sigma_ref,
    q0, q0_last, q2, q3_two,
    q01, q11, q21, q31,
    out_ref, var_ref,
):
    rows, nodes = pivot_ref.shape
    width = nodes // 4
    odd, place = place_ref[0], place_ref[1]
    here = pl.multiple_of(pl.program_id(0) * rows, 128)
    diagonal = diagonal_of(rows)

    def at(block, count=1):
        return pl.ds(pl.multiple_of(block * width, 128), count * width)

    def own(block):
        return pl.ds(pl.multiple_of(block * width + here, 128), rows)

    def add(columns, product):
        out_ref[:, columns] = (pivot_ref[:, columns].astype(F32) + product.astype(F32)).astype(BF16)

    def trace(product):
        var_ref[...] = diagonal(
            pivot_ref[:, own(place_ref[2])].astype(F32) + product.astype(F32)
        )

    active = place_ref[4] != 0

    @pl.when(active & (place == 0))
    def _():
        add(at(odd, 3), q0[...])
        add(at(turned(3, odd)), q0_last[...])
        trace(q0[:, own(2 * odd)])

    @pl.when(active & (place == 1))
    def _():
        add(at(turned(0, odd)), q01[...].T)
        add(at(turned(1, odd)), q11[...])
        add(at(turned(2, odd)), q21[...].T)
        add(at(turned(3, odd)), q31[...].T)
        trace(q11[:, pl.ds(here, rows)])

    @pl.when(active & (place == 2))
    def _():
        add(at(turned(0, odd)), q2[pl.ds(0, width), pl.ds(pl.multiple_of(width + here, 128), rows)].T)
        add(at(turned(1, odd)), q2[pl.ds(here, rows), pl.ds(0, width)])
        start = pl.program_id(0) % 2 * rows + 2 * width
        trace(q2[pl.ds(here, rows), pl.ds(pl.multiple_of(start, 128), rows)])
        for part in range(4):

            @pl.when(pl.program_id(0) == part)
            def _():
                for side, value in enumerate(unpacked_rows(part, q2, 2 * width)):
                    start = turned(2, odd) * width + side * width // 2
                    add(pl.ds(pl.multiple_of(start, 128), width // 2), value)

    @pl.when(active & (place == 3))
    def _():
        add(at(turned(2, odd)), q3_two[...])

    @pl.when(place_ref[4] == 0)
    def _():
        out_ref[...] = sigma_ref[...]
        var_ref[...] = diagonal(sigma_ref[:, own(place_ref[2])].astype(F32))


def finish(place, pivot, sigma, received, kept):
    rows, nodes = pivot.shape
    chunk = 128
    width = nodes // 4

    def picked(which, blocks):
        return pl.BlockSpec(
            (chunk, blocks * width), lambda i, place: (jnp.where(place[1] == which, i, 0), 0)
        )

    def turned_block(start):
        return pl.BlockSpec(
            (rows, chunk),
            lambda i, place: (
                0,
                jnp.where(place[1] == 1, start(place[0]) * (width // chunk) + i, 0),
            ),
        )

    return pl.pallas_call(
        finish_kernel,
        out_shape=(
            jax.ShapeDtypeStruct((rows, nodes), BF16),
            jax.ShapeDtypeStruct((1, rows), F32),
        ),
        grid_spec=pltpu.PrefetchScalarGridSpec(
            num_scalar_prefetch=1,
            grid=(rows // chunk,),
            in_specs=[
                pl.BlockSpec((chunk, nodes), lambda i, place: (i, 0)),
                pl.BlockSpec(
                    (chunk, nodes), lambda i, place: (jnp.where(place[4] == 0, i, 0), 0)
                ),
                picked(0, 3),
                picked(0, 1),
                pl.BlockSpec((rows, 11 * width // 4), lambda i, place: (0, 0)),
                picked(3, 1),
                turned_block(lambda odd: 1),
                picked(1, 1),
                turned_block(lambda odd: 0),
                turned_block(lambda odd: 1 - odd),
            ],
            out_specs=(
                pl.BlockSpec((chunk, nodes), lambda i, place: (i, 0)),
                pl.BlockSpec((1, chunk), lambda i, place: (0, i)),
            ),
        ),
        compiler_params=pltpu.CompilerParams(vmem_limit_bytes=12 * MIB),
        cost_estimate=HEAVY,
        name="finish",
    )(place, pivot, sigma, *received, *kept)


def add_in_place(pivot_ref, out_ref, sum_ref, sems, column, product):
    chunk = pivot_ref.shape[0] // 4
    copies = []
    for part in range(4):
        here = pl.ds(part * chunk, chunk)
        value = pivot_ref[here, :].astype(F32) + product(part, here).astype(F32)
        sum_ref[here, :] = value.astype(BF16)
        copies.append(
            pltpu.make_async_copy(sum_ref.at[here], out_ref.at[here, column], sems.at[part])
        )
        copies[-1].start()
    return copies


def other_kernel(place_ref, pivot_ref, q3_other, old_ref, out_ref, sum_ref, sems):
    both = pivot_ref.shape[1]
    column = pl.ds(pl.multiple_of(place_ref[0] * both, 128), both)

    @pl.when((place_ref[4] != 0) & (place_ref[1] == 3))
    def _():
        product = lambda part, here: q3_other[here, :]
        for copy in add_in_place(pivot_ref, out_ref, sum_ref, sems, column, product):
            copy.wait()


def last_kernel(
    place_ref, pivot_ref, q2_last, q3_last, old_ref, old_var_ref, out_ref, var_ref, sum_ref, sems
):
    rows, width = pivot_ref.shape
    chunk = rows // 4
    active = place_ref[4] != 0
    column = pl.ds(pl.multiple_of(turned(3, place_ref[0]) * width, 128), width)
    add = functools.partial(add_in_place, pivot_ref, out_ref, sum_ref, sems, column)
    var_ref[...] = old_var_ref[...]

    @pl.when(active & (place_ref[1] == 2))
    def _():
        for copy in add(lambda part, here: q2_last[:, here].T):
            copy.wait()

    @pl.when(active & (place_ref[1] == 3))
    def _():
        copies = add(lambda part, here: jnp.concatenate(unpacked_rows(part, q3_last, 0), axis=1))
        for start in range(0, rows, chunk):
            here = pl.ds(start, chunk)
            value = pivot_ref[here, here].astype(F32)
            value = value + q3_last[here, pl.ds(start % (2 * chunk), chunk)].astype(F32)
            var_ref[:, here] = diagonal_of(chunk)(value)
        for copy in copies:
            copy.wait()


def diagonal_of(rows):
    square = (rows, rows)
    on_diagonal = lax.broadcasted_iota(jnp.int32, square, 0) == lax.broadcasted_iota(
        jnp.int32, square, 1
    )
    return lambda value: jnp.sum(jnp.where(on_diagonal, value, 0.0), axis=0, keepdims=True)


def finish_other(place, pivot, q3_other, covariance):
    rows, nodes = pivot.shape
    vmem = pl.BlockSpec(memory_space=pltpu.VMEM)
    anywhere = pl.BlockSpec(memory_space=pl.ANY)
    return pl.pallas_call(
        other_kernel,
        out_shape=jax.ShapeDtypeStruct((rows, nodes), BF16),
        grid_spec=pltpu.PrefetchScalarGridSpec(
            num_scalar_prefetch=1,
            grid=(1,),
            in_specs=[
                pl.BlockSpec((rows, nodes // 2), lambda i, place: (0, place[0])),
                vmem,
                anywhere,
            ],
            out_specs=anywhere,
            scratch_shapes=[pltpu.VMEM((rows, nodes // 2), BF16), pltpu.SemaphoreType.DMA((4,))],
        ),
        input_output_aliases={3: 0},
        compiler_params=pltpu.CompilerParams(vmem_limit_bytes=8 * MIB),
        cost_estimate=LIGHT,
        name="finish_other",
    )(place, pivot, q3_other, covariance)


def finish_last(place, pivot, q2_last, q3_last, covariance, variances):
    rows, nodes = pivot.shape
    vmem = pl.BlockSpec(memory_space=pltpu.VMEM)
    anywhere = pl.BlockSpec(memory_space=pl.ANY)
    return pl.pallas_call(
        last_kernel,
        out_shape=(
            jax.ShapeDtypeStruct((rows, nodes), BF16),
            jax.ShapeDtypeStruct((1, rows), F32),
        ),
        grid_spec=pltpu.PrefetchScalarGridSpec(
            num_scalar_prefetch=1,
            grid=(1,),
            in_specs=[
                pl.BlockSpec((rows, nodes // 4), lambda i, place: (0, turned(3, place[0]))),
                vmem,
                vmem,
                anywhere,
                vmem,
            ],
            out_specs=(anywhere, vmem),
            scratch_shapes=[pltpu.VMEM((rows, nodes // 4), BF16), pltpu.SemaphoreType.DMA((4,))],
        ),
        input_output_aliases={4: 0},
        compiler_params=pltpu.CompilerParams(vmem_limit_bytes=8 * MIB),
        cost_estimate=LIGHT,
        name="finish_last",
    )(place, pivot, q2_last, q3_last, covariance, variances)


def owned(sigma_next, separator, inverse_pivot, coupling_rate, lengths, step_index, node_class):
    sigma, pivot = sigma_next[0], inverse_pivot[0]
    odd = lax.axis_index("dom") % 2
    col = lax.axis_index("col")
    step = step_index[0]
    place = jnp.stack([odd, turned(col, odd), col, step, step < lengths[0]]).astype(jnp.int32)
    after = lambda value, *others: lax.optimization_barrier((value, *others))[0]

    p2 = moved(pivot, 2, 1)
    p0 = moved(pivot, 0, 1)
    weights = coupling(node_class)
    c1 = [couple(pivot, weights, coupling_rate, part, 2) for part in range(2)]
    across = turn(place, 1, 0, c1[0], None)
    across = turn(place, 1, 1, c1[1], across)

    near, other = halves(place, separator[0])
    near, other = passed_along(near, "dom", -1), passed_along(other, "dom", -1)
    sides = (lambda odd: 1 - odd, lambda odd: odd)
    row_near, near, last = prior_half(
        near_kernel, sides[0], (7, 3), place, after(near, across), sigma
    )
    near_zero, near_two = moved(row_near, 0, 1), moved(near, 2, 1)
    last_three = moved(last, 3, 1)
    c2 = couple_here(place, after(p2, last), weights, coupling_rate)
    across = turn(place, 2, 0, c2, across)
    row_other, far = prior_half(
        other_half_kernel, sides[1], (3,), place, after(other, across), sigma
    )
    far_zero = moved(far, 0, 1)
    c0 = couple_here(place, after(p0, across, far), weights, coupling_rate)
    across = turn(place, 0, 0, c0, across)
    column, h0_one, h2_one = own_column(place, row_near, row_other, c0, c2)
    c3 = [
        moved(after(c1[0], last_three, near_two, near_zero, across), 3, 1),
        moved(after(c1[1], far_zero, h2_one), 3, 1),
    ]
    prior = assemble(place, row_near, row_other, column, near_two, last_three, near_zero, far_zero)

    h0 = half_product(place, c0, prior, h0_one)
    q0_own = multiply(place, [h0], across, lambda odd: odd, 3)
    q0 = moved(q0_own, 1, 0)
    h2 = half_product(place, after(c2, q0_own), prior, h2_one)
    q2_own = product_two(place, h2, across, q0_own)
    q2 = moved(q2_own, 1, 2)

    across = turn(place, 3, 0, c3[0], after(across, q2_own))
    across = turn(place, 3, 1, c3[1], across)
    q03 = multiply(place, [h0], across, lambda odd: 3 - 3 * odd, 1)
    q0_last = moved(q03, 1, 0)
    h3 = multiply(place, [after(c3[0], q03), c3[1]], prior)
    q32 = multiply(place, [h3], across, lambda odd: 2 - odd, 1)
    q3_two = moved(q32, 1, 3)
    q3_own, q33 = product_rest(place, h3, across, after(q03, q32))
    q3_other, q3_last = moved(q3_own, 1, 3), moved(q33, 1, 3)
    h1 = multiply(place, [after(c1[0], q3_own), c1[1]], prior)
    q11 = multiply(place, [h1], across, lambda odd: 1 + odd, 1)
    received = (q0, q0_last, q2, q3_two)
    kept = (q0_own, q11, q2_own, q3_own)
    place_then = tick(tick(place, q0, cost=LIGHT), q0_last, cost=MEDIUM)
    q2_last = moved(after(q3_two, place_then), 3, 2)
    covariance, variances = finish(place_then, pivot, sigma, received, kept)
    covariance = finish_other(place, pivot, q3_other, covariance)
    covariance, variances = finish_last(place, pivot, q2_last, q3_last, covariance, variances)
    return (covariance[None], variances)


def gathered(sigma_next, separator, inverse_pivot, coupling_rate, lengths, step_index, node_class):
    shifted = passed_along(separator, "dom", -1)
    prior = jnp.where(step_index[0] == 0, shifted[0], sigma_next[0])
    pivot = inverse_pivot[0].astype(F32)
    coupled = couple(inverse_pivot[0], coupling(node_class), coupling_rate)
    rows = coupled.shape[0]
    half = jnp.dot(
        coupled,
        lax.all_gather(prior, "col", axis=0, tiled=True),
        preferred_element_type=F32,
    ).astype(BF16)
    product = lax.dot_general(
        half,
        lax.all_gather(coupled, "col", axis=0, tiled=True),
        (((1,), (1,)), ((), ())),
        preferred_element_type=F32,
    )
    full = pivot + product
    active = step_index[0] < lengths[0]
    old = sigma_next[0]
    covariance = jnp.where(active, full.astype(BF16), old)
    first_col = lax.axis_index("col") * rows
    new_block = lax.dynamic_slice_in_dim(full, first_col, rows, 1)
    old_block = lax.dynamic_slice_in_dim(old, first_col, rows, 1)
    variances = jnp.where(active, jnp.diagonal(new_block), jnp.diagonal(old_block).astype(F32))
    return (covariance[None], variances[None])


def solution(mesh):
    local = owned if mesh.shape["col"] == 4 and mesh.shape["dom"] % 2 == 0 else gathered
    return jax.shard_map(
        local,
        mesh=mesh,
        in_specs=(
            P(("groups", "dom"), "col", None),
            P(("groups", "dom"), "col", None),
            P(("groups", "dom"), "col", None),
            P(("groups", "dom")),
            P(("groups", "dom")),
            P(("groups", "dom")),
            P("groups"),
        ),
        out_specs=(P(("groups", "dom"), "col", None), P(("groups", "dom"), "col")),
        check_vma=False,
    )
```

```python
import functools

import jax
import jax.numpy as jnp
from jax import lax
from jax.experimental import pallas as pl
from jax.experimental.pallas import tpu as pltpu
from jax.sharding import PartitionSpec as P

GX = 64
GY = 32
BF16 = jnp.bfloat16
F32 = jnp.float32
MIB = 1 << 20


def passed_along(value, axis, steps):
    count = lax.axis_size(axis)
    initial, last = (max(0, -steps), min(count, count - steps))
    return lax.ppermute(value, axis, [(source, source + steps) for source in range(initial, last)])


LIGHT = pl.CostEstimate(flops=1 << 20, bytes_accessed=1 << 16, transcendentals=0)
MEDIUM = pl.CostEstimate(flops=2000000000, bytes_accessed=1 << 16, transcendentals=0)
HEAVY = pl.CostEstimate(flops=14000000000, bytes_accessed=1 << 16, transcendentals=0)


BLOCK = 256
SPAN = 512


def window(block, nodes):
    return pl.multiple_of(jnp.clip(block * BLOCK - (SPAN - BLOCK) // 2, 0, nodes - SPAN), 128)


def weight_kernel(class_ref, out_ref):
    nodes = class_ref.shape[1]

    def fill(block, carry):
        first = pl.multiple_of(block * BLOCK, BLOCK)
        kind = class_ref[:, pl.ds(first, BLOCK)]
        across = jnp.where(
            kind == 0, 0.25, jnp.where(kind == 1, 0.375, jnp.where(kind == 2, 0.125, 0.5))
        ).astype(F32)
        along = jnp.where(
            kind == 0, 0.25, jnp.where(kind == 1, 0.125, jnp.where(kind == 2, 0.375, 0.0))
        ).astype(F32)
        column = (first + lax.broadcasted_iota(jnp.int32, (1, BLOCK), 1)) % GX
        left = jnp.where(column > 0, across, 0.0)
        right = jnp.where(column < GX - 1, across, 0.0)
        shape = (SPAN, BLOCK)
        offset = (
            lax.broadcasted_iota(jnp.int32, shape, 0)
            - lax.broadcasted_iota(jnp.int32, shape, 1)
            + (window(block, nodes) - first)
        )
        value = jnp.where(jnp.abs(offset) == GX, along, 0.0)
        value = jnp.where(offset == -1, left, value)
        value = jnp.where(offset == 1, right, value)
        value = jnp.where(offset == 0, 1.0, value)
        out_ref[block] = value.astype(BF16)
        return carry

    lax.fori_loop(0, nodes // BLOCK, fill, 0)


def coupling(node_class):
    nodes = node_class.shape[0]
    vmem = pl.BlockSpec(memory_space=pltpu.VMEM)
    return pl.pallas_call(
        weight_kernel,
        out_shape=jax.ShapeDtypeStruct((nodes // BLOCK, SPAN, BLOCK), BF16),
        in_specs=[vmem],
        out_specs=vmem,
        compiler_params=pltpu.CompilerParams(vmem_limit_bytes=6 * MIB),
        cost_estimate=LIGHT,
        name="coupling",
    )(node_class.reshape(1, nodes))


def couple_kernel(first, rate_ref, weight_ref, pivot_ref, out_ref):
    rows, nodes = out_ref.shape

    def block_of(block, carry):
        source = pl.ds(window(block, nodes), SPAN)
        target = pl.ds(pl.multiple_of(block * BLOCK, BLOCK), BLOCK)
        value = jnp.dot(
            pivot_ref[first : first + rows, source], weight_ref[block], preferred_element_type=F32
        )
        out_ref[:, target] = (rate_ref[0] * value).astype(BF16)
        return carry

    lax.fori_loop(0, nodes // BLOCK, block_of, 0)


def couple(pivot, weights, rate, part=0, parts=1):
    rows, nodes = pivot.shape[0] // parts, pivot.shape[1]
    vmem = pl.BlockSpec(memory_space=pltpu.VMEM)
    return pl.pallas_call(
        functools.partial(couple_kernel, part * rows),
        out_shape=jax.ShapeDtypeStruct((rows, nodes), BF16),
        in_specs=[pl.BlockSpec(memory_space=pltpu.SMEM), vmem, vmem],
        out_specs=vmem,
        compiler_params=pltpu.CompilerParams(vmem_limit_bytes=8 * MIB),
        cost_estimate=LIGHT,
        name="couple",
    )(rate, weights, pivot)


def turned(block, odd):
    return block + odd * (3 - 2 * block)


def route(source, target, doms):
    pairs = []
    for dom in range(doms):
        odd = dom % 2
        pairs.append((dom * 4 + turned(source, odd), dom * 4 + turned(target, odd)))
    return pairs


def moved(value, source, target):
    return lax.ppermute(value, ("dom", "col"), route(source, target, lax.axis_size("dom")))


def couple_here(place, pivot, weights, rate):
    def kernel(place_ref, *refs):
        @pl.when(place_ref[1] == 1)
        def _():
            couple_kernel(0, *refs)

    scalars, vmem = pl.BlockSpec(memory_space=pltpu.SMEM), pl.BlockSpec(memory_space=pltpu.VMEM)
    return pl.pallas_call(
        kernel,
        out_shape=jax.ShapeDtypeStruct(pivot.shape, BF16),
        in_specs=[scalars, scalars, vmem, vmem],
        out_specs=vmem,
        compiler_params=pltpu.CompilerParams(vmem_limit_bytes=8 * MIB),
        cost_estimate=LIGHT,
        name="couple_here",
    )(place, rate, weights, pivot)


def turn_kernel(place_ref, coupled_ref, *refs):
    @pl.when(place_ref[1] == 1)
    def _():
        refs[-1][...] = coupled_ref[...].T


def turn(place, panel, part, coupled, across):
    rows, nodes = coupled.shape
    chunk = 128
    steps = rows // chunk
    ratio = nodes // 4 // chunk
    return pl.pallas_call(
        turn_kernel,
        out_shape=jax.ShapeDtypeStruct((nodes, nodes), BF16),
        grid_spec=pltpu.PrefetchScalarGridSpec(
            num_scalar_prefetch=1,
            grid=(steps,),
            in_specs=[pl.BlockSpec((chunk, nodes), lambda i, place: (i, 0))]
            + ([] if across is None else [pl.BlockSpec(memory_space=pl.ANY)]),
            out_specs=pl.BlockSpec(
                (nodes, chunk),
                lambda i, place: (0, turned(panel, place[0]) * ratio + part * steps + i),
            ),
        ),
        input_output_aliases={} if across is None else {2: 0},
        compiler_params=pltpu.CompilerParams(vmem_limit_bytes=4 * MIB),
        cost_estimate=LIGHT,
        name="turn",
    )(place, coupled, *(() if across is None else (across,)))


def multiply_kernel(first, count, lefts, place_ref, *refs):
    left_refs, right_ref, out_ref = refs[:lefts], refs[lefts], refs[-1]
    width = right_ref.shape[0] // 4

    @pl.when(place_ref[1] == 1)
    def _():
        def block(step, carry):
            source = pl.multiple_of((first(place_ref[0]) + step) * width, 128)
            target = pl.multiple_of(step * width, 128)
            row = 0
            for left_ref in left_refs:
                rows = left_ref.shape[0]
                out_ref[row : row + rows, pl.ds(target, width)] = jnp.dot(
                    left_ref[...], right_ref[:, pl.ds(source, width)], preferred_element_type=F32
                ).astype(BF16)
                row += rows
            return carry

        lax.fori_loop(0, count, block, 0)


def multiply(place, lefts, right, first=lambda odd: 0, count=4):
    rows = sum(left.shape[0] for left in lefts)
    width = right.shape[0] // 4
    vmem = pl.BlockSpec(memory_space=pltpu.VMEM)
    return pl.pallas_call(
        functools.partial(multiply_kernel, first, count, len(lefts)),
        out_shape=jax.ShapeDtypeStruct((rows, count * width), BF16),
        in_specs=[pl.BlockSpec(memory_space=pltpu.SMEM)] + [vmem] * (len(lefts) + 1),
        out_specs=vmem,
        compiler_params=pltpu.CompilerParams(vmem_limit_bytes=6 * MIB),
        cost_estimate=LIGHT,
        name="multiply",
    )(place, *lefts, right)


def pack(value, out_ref, column):
    quarter = value.shape[1] // 4
    for part in range(4):
        rows = pl.ds(part * quarter, quarter)
        pack_rows(part, value[part * quarter : (part + 1) * quarter], out_ref.at[rows], column)


def two_kernel(place_ref, left_ref, right_ref, zero_ref, out_ref):
    odd = place_ref[0]
    width = right_ref.shape[0] // 4

    def product(block):
        columns = pl.ds(pl.multiple_of(block * width, 128), width)
        value = jnp.dot(left_ref[...], right_ref[:, columns], preferred_element_type=F32)
        return value.astype(BF16)

    @pl.when(place_ref[1] == 1)
    def _():
        out_ref[:, :width] = product(1 + odd)
        zero = pl.ds(pl.multiple_of((2 - 2 * odd) * width, 128), width)
        out_ref[:, width : 2 * width] = zero_ref[:, zero]
        pack(product(2 - odd), out_ref, 2 * width)


def product_two(place, half, across, zero):
    rows = half.shape[0]
    width = across.shape[0] // 4
    vmem = pl.BlockSpec(memory_space=pltpu.VMEM)
    return pl.pallas_call(
        two_kernel,
        out_shape=jax.ShapeDtypeStruct((rows, 11 * width // 4), BF16),
        in_specs=[pl.BlockSpec(memory_space=pltpu.SMEM)] + [vmem] * 3,
        out_specs=vmem,
        compiler_params=pltpu.CompilerParams(vmem_limit_bytes=6 * MIB),
        cost_estimate=LIGHT,
        name="product_two",
    )(place, half, across, zero)


def half_kernel(place_ref, left_ref, right_ref, one_ref, out_ref):
    width = one_ref.shape[1]

    @pl.when(place_ref[1] == 1)
    def _():
        def block(step, carry):
            which = turned(step + (step > 0).astype(jnp.int32), place_ref[0])
            columns = pl.ds(pl.multiple_of(which * width, 128), width)
            out_ref[:, columns] = jnp.dot(
                left_ref[...], right_ref[:, columns], preferred_element_type=F32
            ).astype(BF16)
            return carry

        lax.fori_loop(0, 3, block, 0)
        columns = pl.ds(pl.multiple_of(turned(1, place_ref[0]) * width, 128), width)
        out_ref[:, columns] = one_ref[...]


def half_product(place, left, right, one):
    vmem = pl.BlockSpec(memory_space=pltpu.VMEM)
    return pl.pallas_call(
        half_kernel,
        out_shape=jax.ShapeDtypeStruct(left.shape, BF16),
        in_specs=[pl.BlockSpec(memory_space=pltpu.SMEM)] + [vmem] * 3,
        out_specs=vmem,
        compiler_params=pltpu.CompilerParams(vmem_limit_bytes=6 * MIB),
        cost_estimate=LIGHT,
        name="half_product",
    )(place, left, right, one)


def column_kernel(place_ref, near_ref, other_ref, first_ref, second_ref, *refs):
    column_ref, out_refs = refs[0], refs[1:]

    @pl.when(place_ref[1] == 1)
    def _():
        odd = place_ref[0]
        width = near_ref.shape[0]
        for half, half_ref in ((1 - odd, near_ref), (odd, other_ref)):
            for block in range(2):
                rows = pl.ds(pl.multiple_of((2 * half + block) * width, 128), width)
                column_ref[rows, :] = half_ref[:, block * width : (block + 1) * width].T
        for left_ref, out_ref in zip((first_ref, second_ref), out_refs):
            out_ref[...] = jnp.dot(
                left_ref[...], column_ref[...], preferred_element_type=F32
            ).astype(BF16)


def own_column(place, near, other, first, second):
    rows, nodes = first.shape
    vmem = pl.BlockSpec(memory_space=pltpu.VMEM)
    return pl.pallas_call(
        column_kernel,
        out_shape=(
            jax.ShapeDtypeStruct((nodes, rows), BF16),
            jax.ShapeDtypeStruct((rows, rows), BF16),
            jax.ShapeDtypeStruct((rows, rows), BF16),
        ),
        in_specs=[pl.BlockSpec(memory_space=pltpu.SMEM)] + [vmem] * 4,
        out_specs=(vmem, vmem, vmem),
        compiler_params=pltpu.CompilerParams(vmem_limit_bytes=6 * MIB),
        cost_estimate=LIGHT,
        name="own_column",
    )(place, near, other, first, second)


def rest_kernel(place_ref, left_ref, right_ref, zero_ref, out_ref, last_ref):
    odd = place_ref[0]
    width = zero_ref.shape[1]
    half = width // 2

    def product(rows, block):
        columns = pl.ds(pl.multiple_of(block * width, 128), width)
        value = jnp.dot(left_ref[rows, :], right_ref[:, columns], preferred_element_type=F32)
        return value.astype(BF16)

    @pl.when(place_ref[1] == 1)
    def _():
        out_ref[:, pl.ds(pl.multiple_of(odd * width, 128), width)] = zero_ref[...].T
        other = pl.ds(pl.multiple_of((1 - odd) * width, 128), width)
        out_ref[:, other] = product(pl.ds(0, width), 1 + odd)
        value = product(pl.ds(0, width), 3 - 3 * odd)
        for part in range(4):
            rows = pl.ds(part * half // 2, half // 2)
            pack_rows(part, value[part * half // 2 : (part + 1) * half // 2], last_ref.at[rows], 0)


def product_rest(place, left, across, zero):
    rows, width = zero.shape
    vmem = pl.BlockSpec(memory_space=pltpu.VMEM)
    return pl.pallas_call(
        rest_kernel,
        out_shape=(
            jax.ShapeDtypeStruct((rows, 2 * width), BF16),
            jax.ShapeDtypeStruct((rows, 3 * width // 4), BF16),
        ),
        in_specs=[pl.BlockSpec(memory_space=pltpu.SMEM)] + [vmem] * 3,
        out_specs=(vmem, vmem),
        compiler_params=pltpu.CompilerParams(vmem_limit_bytes=6 * MIB),
        cost_estimate=LIGHT,
        name="product_rest",
    )(place, left, across, zero)


def pack_rows(part, value, out_ref, column):
    quarter, width = value.shape
    half = width // 2
    beside = (2, 3, 1, 0)[part] * quarter
    out_ref[:, column : column + half] = value[:, part // 2 * half : (part // 2 + 1) * half]
    out_ref[:, column + half : column + half + quarter] = value[:, beside : beside + quarter]


def unpacked_rows(part, packed_ref, column):
    quarter = packed_ref.shape[0] // 4
    half = 2 * quarter

    def beside(which):
        rows = slice(which * quarter, (which + 1) * quarter)
        return packed_ref[rows, column + half : column + half + quarter]

    rows = slice(part * quarter, (part + 1) * quarter)
    diagonal = packed_ref[rows, column : column + half]
    if part == 0:
        return diagonal, jnp.concatenate([beside(0), beside(3).T], axis=1)
    if part == 1:
        return diagonal, jnp.concatenate([beside(2).T, beside(1)], axis=1)
    if part == 2:
        return jnp.concatenate([beside(0).T, beside(2)], axis=1), diagonal
    return jnp.concatenate([beside(3), beside(1).T], axis=1), diagonal


def prior_kernel(place_ref, shifted_ref, sigma_ref, out_ref):
    @pl.when(place_ref[3] == 0)
    def _():
        out_ref[...] = shifted_ref[...]

    @pl.when(place_ref[3] != 0)
    def _():
        out_ref[...] = sigma_ref[...]


def halves_kernel(place_ref, separator_ref, near_ref, other_ref, sems):
    half = near_ref.shape[1]
    copies = []
    for which, (side, out_ref) in enumerate(((place_ref[0], near_ref), (1 - place_ref[0], other_ref))):
        source = separator_ref.at[:, pl.ds(pl.multiple_of(side * half, 128), half)]
        copies.append(pltpu.make_async_copy(source, out_ref, sems.at[which]))
        copies[-1].start()
    for copy in copies:
        copy.wait()


def halves(place, separator):
    rows, nodes = separator.shape
    vmem = pl.BlockSpec(memory_space=pltpu.VMEM)
    return pl.pallas_call(
        halves_kernel,
        out_shape=(jax.ShapeDtypeStruct((rows, nodes // 2), BF16),) * 2,
        in_specs=[pl.BlockSpec(memory_space=pltpu.SMEM), pl.BlockSpec(memory_space=pltpu.HBM)],
        out_specs=(vmem, vmem),
        scratch_shapes=[pltpu.SemaphoreType.DMA((2,))],
        compiler_params=pltpu.CompilerParams(vmem_limit_bytes=6 * MIB),
        cost_estimate=LIGHT,
        name="halves",
    )(place, separator)


def near_kernel(place_ref, shifted_ref, sigma_ref, row_ref, near_ref, last_ref):
    odd = place_ref[0]
    width = row_ref.shape[1] // 2
    prior_kernel(place_ref, shifted_ref, sigma_ref, row_ref)
    two = pl.ds(pl.multiple_of(odd * width, 128), width)
    three = pl.ds(pl.multiple_of((1 - odd) * width, 128), width)
    near_ref[:, :width] = row_ref[:, three]
    for part in range(4):

        @pl.when(pl.program_id(0) == part)
        def _():
            pack_rows(part, row_ref[:, two], near_ref, width)
            pack_rows(part, row_ref[:, three], last_ref, 0)


def other_half_kernel(place_ref, shifted_ref, sigma_ref, row_ref, far_ref):
    width = row_ref.shape[1] // 2
    prior_kernel(place_ref, shifted_ref, sigma_ref, row_ref)
    zero = pl.ds(pl.multiple_of(place_ref[0] * width, 128), width)
    for part in range(4):

        @pl.when(pl.program_id(0) == part)
        def _():
            pack_rows(part, row_ref[:, zero], far_ref, 0)


def prior_half(kernel, side, sent, place, shifted, sigma):
    rows, nodes = sigma.shape
    chunk = rows // 4
    quarters = (8,) + sent
    out = lambda count: jax.ShapeDtypeStruct((rows, count * nodes // 16), BF16)
    spec = lambda count: pl.BlockSpec((chunk, count * nodes // 16), lambda i, place: (i, 0))
    return pl.pallas_call(
        kernel,
        out_shape=tuple(out(count) for count in quarters),
        grid_spec=pltpu.PrefetchScalarGridSpec(
            num_scalar_prefetch=1,
            grid=(4,),
            in_specs=[
                pl.BlockSpec(
                    (chunk, nodes // 2), lambda i, place: (jnp.where(place[3] == 0, i, 0), 0)
                ),
                pl.BlockSpec(
                    (chunk, nodes // 2),
                    lambda i, place: (jnp.where(place[3] == 0, 0, i), side(place[0])),
                ),
            ],
            out_specs=tuple(spec(count) for count in quarters),
        ),
        compiler_params=pltpu.CompilerParams(vmem_limit_bytes=6 * MIB),
        cost_estimate=LIGHT,
        name="prior_half",
    )(place, shifted, sigma)


def assemble_kernel(place_ref, near, other, column, near_two, last_three, near_zero, far_zero, out_ref):
    @pl.when(place_ref[1] == 1)
    def _():
        odd = place_ref[0]
        width = near.shape[0]
        half, quarter = width // 2, width // 4

        def at(block, count=1):
            return pl.ds(pl.multiple_of(block * width, 128), count * width)

        first = 2 * (1 - odd)
        row = [turned(block, odd) for block in range(4)]
        out_ref[at(row[1]), at(first, 2)] = near[...]
        out_ref[at(row[1]), at(2 * odd, 2)] = other[...]
        out_ref[at(row[2]), at(row[3])] = near_two[:, :width]
        out_ref[at(row[3]), at(row[2])] = near_two[:, :width].T
        out_ref[at(row[0]), at(first, 2)] = near_zero[...]
        for step in range(2):
            out_ref[at(first + step), at(row[0])] = near_zero[:, step * width : (1 + step) * width].T
        for block in (0, 2, 3):
            out_ref[at(row[block]), at(row[1])] = column[at(row[block]), :]
        packed = ((0, far_zero, 0), (2, near_two, width), (3, last_three, 0))
        for block, packed_ref, start in packed:
            for part in range(4):
                rows = pl.ds(pl.multiple_of(row[block] * width + part * quarter, 128), quarter)
                for side, value in enumerate(unpacked_rows(part, packed_ref, start)):
                    columns = pl.ds(pl.multiple_of(row[block] * width + side * half, 128), half)
                    out_ref[rows, columns] = value


def assemble(place, *parts):
    nodes = 2 * parts[0].shape[1]
    vmem = pl.BlockSpec(memory_space=pltpu.VMEM)
    return pl.pallas_call(
        assemble_kernel,
        out_shape=jax.ShapeDtypeStruct((nodes, nodes), BF16),
        in_specs=[pl.BlockSpec(memory_space=pltpu.SMEM)] + [vmem] * 7,
        out_specs=vmem,
        compiler_params=pltpu.CompilerParams(vmem_limit_bytes=6 * MIB),
        cost_estimate=LIGHT,
        name="assemble",
    )(place, *parts)


def tick(place, *values, cost=HEAVY):
    def kernel(place_ref, *refs):
        for which in range(place.shape[0]):
            refs[-1][which] = place_ref[which]

    scalars = pl.BlockSpec(memory_space=pltpu.SMEM)
    return pl.pallas_call(
        kernel,
        out_shape=jax.ShapeDtypeStruct(place.shape, place.dtype),
        in_specs=[scalars] + [pl.BlockSpec(memory_space=pl.ANY)] * len(values),
        out_specs=scalars,
        compiler_params=pltpu.CompilerParams(vmem_limit_bytes=MIB),
        cost_estimate=cost,
        name="tick",
    )(place, *values)


def finish_kernel(
    place_ref, pivot_ref, sigma_ref,
    q0, q0_last, q2, q3_two,
    q01, q11, q21, q31,
    out_ref, var_ref,
):
    rows, nodes = pivot_ref.shape
    width = nodes // 4
    odd, place = place_ref[0], place_ref[1]
    here = pl.multiple_of(pl.program_id(0) * rows, 128)
    diagonal = diagonal_of(rows)

    def at(block, count=1):
        return pl.ds(pl.multiple_of(block * width, 128), count * width)

    def own(block):
        return pl.ds(pl.multiple_of(block * width + here, 128), rows)

    def add(columns, product):
        out_ref[:, columns] = (pivot_ref[:, columns].astype(F32) + product.astype(F32)).astype(BF16)

    def trace(product):
        var_ref[...] = diagonal(
            pivot_ref[:, own(place_ref[2])].astype(F32) + product.astype(F32)
        )

    active = place_ref[4] != 0

    @pl.when(active & (place == 0))
    def _():
        add(at(odd, 3), q0[...])
        add(at(turned(3, odd)), q0_last[...])
        trace(q0[:, own(2 * odd)])

    @pl.when(active & (place == 1))
    def _():
        add(at(turned(0, odd)), q01[...].T)
        add(at(turned(1, odd)), q11[...])
        add(at(turned(2, odd)), q21[...].T)
        add(at(turned(3, odd)), q31[...].T)
        trace(q11[:, pl.ds(here, rows)])

    @pl.when(active & (place == 2))
    def _():
        add(at(turned(0, odd)), q2[pl.ds(0, width), pl.ds(pl.multiple_of(width + here, 128), rows)].T)
        add(at(turned(1, odd)), q2[pl.ds(here, rows), pl.ds(0, width)])
        start = pl.program_id(0) % 2 * rows + 2 * width
        trace(q2[pl.ds(here, rows), pl.ds(pl.multiple_of(start, 128), rows)])
        for part in range(4):

            @pl.when(pl.program_id(0) == part)
            def _():
                for side, value in enumerate(unpacked_rows(part, q2, 2 * width)):
                    start = turned(2, odd) * width + side * width // 2
                    add(pl.ds(pl.multiple_of(start, 128), width // 2), value)

    @pl.when(active & (place == 3))
    def _():
        add(at(turned(2, odd)), q3_two[...])

    @pl.when(place_ref[4] == 0)
    def _():
        out_ref[...] = sigma_ref[...]
        var_ref[...] = diagonal(sigma_ref[:, own(place_ref[2])].astype(F32))


def finish(place, pivot, sigma, received, kept):
    rows, nodes = pivot.shape
    chunk = 128
    width = nodes // 4

    def picked(which, blocks):
        return pl.BlockSpec(
            (chunk, blocks * width), lambda i, place: (jnp.where(place[1] == which, i, 0), 0)
        )

    def turned_block(start):
        return pl.BlockSpec(
            (rows, chunk),
            lambda i, place: (
                0,
                jnp.where(place[1] == 1, start(place[0]) * (width // chunk) + i, 0),
            ),
        )

    return pl.pallas_call(
        finish_kernel,
        out_shape=(
            jax.ShapeDtypeStruct((rows, nodes), BF16),
            jax.ShapeDtypeStruct((1, rows), F32),
        ),
        grid_spec=pltpu.PrefetchScalarGridSpec(
            num_scalar_prefetch=1,
            grid=(rows // chunk,),
            in_specs=[
                pl.BlockSpec((chunk, nodes), lambda i, place: (i, 0)),
                pl.BlockSpec(
                    (chunk, nodes), lambda i, place: (jnp.where(place[4] == 0, i, 0), 0)
                ),
                picked(0, 3),
                picked(0, 1),
                pl.BlockSpec((rows, 11 * width // 4), lambda i, place: (0, 0)),
                picked(3, 1),
                turned_block(lambda odd: 1),
                picked(1, 1),
                turned_block(lambda odd: 0),
                turned_block(lambda odd: 1 - odd),
            ],
            out_specs=(
                pl.BlockSpec((chunk, nodes), lambda i, place: (i, 0)),
                pl.BlockSpec((1, chunk), lambda i, place: (0, i)),
            ),
        ),
        compiler_params=pltpu.CompilerParams(vmem_limit_bytes=12 * MIB),
        cost_estimate=HEAVY,
        name="finish",
    )(place, pivot, sigma, *received, *kept)


def add_in_place(pivot_ref, out_ref, sum_ref, sems, column, product):
    chunk = pivot_ref.shape[0] // 4
    copies = []
    for part in range(4):
        here = pl.ds(part * chunk, chunk)
        value = pivot_ref[here, :].astype(F32) + product(part, here).astype(F32)
        sum_ref[here, :] = value.astype(BF16)
        copies.append(
            pltpu.make_async_copy(sum_ref.at[here], out_ref.at[here, column], sems.at[part])
        )
        copies[-1].start()
    return copies


def other_kernel(place_ref, pivot_ref, q3_other, old_ref, out_ref, sum_ref, sems):
    both = pivot_ref.shape[1]
    column = pl.ds(pl.multiple_of(place_ref[0] * both, 128), both)

    @pl.when((place_ref[4] != 0) & (place_ref[1] == 3))
    def _():
        product = lambda part, here: q3_other[here, :]
        for copy in add_in_place(pivot_ref, out_ref, sum_ref, sems, column, product):
            copy.wait()


def last_kernel(
    place_ref, pivot_ref, q2_last, q3_last, old_ref, old_var_ref, out_ref, var_ref, sum_ref, sems
):
    rows, width = pivot_ref.shape
    chunk = rows // 4
    active = place_ref[4] != 0
    column = pl.ds(pl.multiple_of(turned(3, place_ref[0]) * width, 128), width)
    add = functools.partial(add_in_place, pivot_ref, out_ref, sum_ref, sems, column)
    var_ref[...] = old_var_ref[...]

    @pl.when(active & (place_ref[1] == 2))
    def _():
        for copy in add(lambda part, here: q2_last[:, here].T):
            copy.wait()

    @pl.when(active & (place_ref[1] == 3))
    def _():
        copies = add(lambda part, here: jnp.concatenate(unpacked_rows(part, q3_last, 0), axis=1))
        for start in range(0, rows, chunk):
            here = pl.ds(start, chunk)
            value = pivot_ref[here, here].astype(F32)
            value = value + q3_last[here, pl.ds(start % (2 * chunk), chunk)].astype(F32)
            var_ref[:, here] = diagonal_of(chunk)(value)
        for copy in copies:
            copy.wait()


def diagonal_of(rows):
    square = (rows, rows)
    on_diagonal = lax.broadcasted_iota(jnp.int32, square, 0) == lax.broadcasted_iota(
        jnp.int32, square, 1
    )
    return lambda value: jnp.sum(jnp.where(on_diagonal, value, 0.0), axis=0, keepdims=True)


def finish_other(place, pivot, q3_other, covariance):
    rows, nodes = pivot.shape
    vmem = pl.BlockSpec(memory_space=pltpu.VMEM)
    anywhere = pl.BlockSpec(memory_space=pl.ANY)
    return pl.pallas_call(
        other_kernel,
        out_shape=jax.ShapeDtypeStruct((rows, nodes), BF16),
        grid_spec=pltpu.PrefetchScalarGridSpec(
            num_scalar_prefetch=1,
            grid=(1,),
            in_specs=[
                pl.BlockSpec((rows, nodes // 2), lambda i, place: (0, place[0])),
                vmem,
                anywhere,
            ],
            out_specs=anywhere,
            scratch_shapes=[pltpu.VMEM((rows, nodes // 2), BF16), pltpu.SemaphoreType.DMA((4,))],
        ),
        input_output_aliases={3: 0},
        compiler_params=pltpu.CompilerParams(vmem_limit_bytes=8 * MIB),
        cost_estimate=LIGHT,
        name="finish_other",
    )(place, pivot, q3_other, covariance)


def finish_last(place, pivot, q2_last, q3_last, covariance, variances):
    rows, nodes = pivot.shape
    vmem = pl.BlockSpec(memory_space=pltpu.VMEM)
    anywhere = pl.BlockSpec(memory_space=pl.ANY)
    return pl.pallas_call(
        last_kernel,
        out_shape=(
            jax.ShapeDtypeStruct((rows, nodes), BF16),
            jax.ShapeDtypeStruct((1, rows), F32),
        ),
        grid_spec=pltpu.PrefetchScalarGridSpec(
            num_scalar_prefetch=1,
            grid=(1,),
            in_specs=[
                pl.BlockSpec((rows, nodes // 4), lambda i, place: (0, turned(3, place[0]))),
                vmem,
                vmem,
                anywhere,
                vmem,
            ],
            out_specs=(anywhere, vmem),
            scratch_shapes=[pltpu.VMEM((rows, nodes // 4), BF16), pltpu.SemaphoreType.DMA((4,))],
        ),
        input_output_aliases={4: 0},
        compiler_params=pltpu.CompilerParams(vmem_limit_bytes=8 * MIB),
        cost_estimate=LIGHT,
        name="finish_last",
    )(place, pivot, q2_last, q3_last, covariance, variances)


def owned(sigma_next, separator, inverse_pivot, coupling_rate, lengths, step_index, node_class):
    sigma, pivot = sigma_next[0], inverse_pivot[0]
    odd = lax.axis_index("dom") % 2
    col = lax.axis_index("col")
    step = step_index[0]
    place = jnp.stack([odd, turned(col, odd), col, step, step < lengths[0]]).astype(jnp.int32)
    after = lambda value, *others: lax.optimization_barrier((value, *others))[0]

    p2 = moved(pivot, 2, 1)
    p0 = moved(pivot, 0, 1)
    weights = coupling(node_class)
    c1 = couple(pivot, weights, coupling_rate)
    across = turn(place, 1, 0, c1, None)

    near, other = halves(place, separator[0])
    near, other = passed_along(near, "dom", -1), passed_along(other, "dom", -1)
    sides = (lambda odd: 1 - odd, lambda odd: odd)
    row_near, near, last = prior_half(
        near_kernel, sides[0], (7, 3), place, after(near, across), sigma
    )
    near_zero, near_two = moved(row_near, 0, 1), moved(near, 2, 1)
    last_three = moved(last, 3, 1)
    c2 = couple_here(place, after(p2, last), weights, coupling_rate)
    across = turn(place, 2, 0, c2, across)
    row_other, far = prior_half(
        other_half_kernel, sides[1], (3,), place, after(other, across), sigma
    )
    far_zero = moved(far, 0, 1)
    c0 = couple_here(place, after(p0, across, far), weights, coupling_rate)
    across = turn(place, 0, 0, c0, across)
    column, h0_one, h2_one = own_column(place, row_near, row_other, c0, c2)
    c3 = moved(after(c1, last_three, near_two, near_zero, far_zero, across), 3, 1)
    prior = assemble(place, row_near, row_other, column, near_two, last_three, near_zero, far_zero)

    h0 = half_product(place, c0, prior, h0_one)
    q0_own = multiply(place, [h0], across, lambda odd: odd, 3)
    q0 = moved(q0_own, 1, 0)
    h2 = half_product(place, after(c2, q0_own), prior, h2_one)
    q2_own = product_two(place, h2, across, q0_own)
    q2 = moved(q2_own, 1, 2)

    across = turn(place, 3, 0, c3, after(across, q2_own))
    q03 = multiply(place, [h0], across, lambda odd: 3 - 3 * odd, 1)
    q0_last = moved(q03, 1, 0)
    h3 = multiply(place, [after(c3, q03)], prior)
    q32 = multiply(place, [h3], across, lambda odd: 2 - odd, 1)
    q3_two = moved(q32, 1, 3)
    q3_own, q33 = product_rest(place, h3, across, after(q03, q32))
    q3_other, q3_last = moved(q3_own, 1, 3), moved(q33, 1, 3)
    h1 = multiply(place, [after(c1, q3_own)], prior)
    q11 = multiply(place, [h1], across, lambda odd: 1 + odd, 1)
    received = (q0, q0_last, q2, q3_two)
    kept = (q0_own, q11, q2_own, q3_own)
    place_then = tick(tick(place, q0, cost=LIGHT), q0_last, cost=MEDIUM)
    q2_last = moved(after(q3_two, place_then), 3, 2)
    covariance, variances = finish(place_then, pivot, sigma, received, kept)
    covariance = finish_other(place, pivot, q3_other, covariance)
    covariance, variances = finish_last(place, pivot, q2_last, q3_last, covariance, variances)
    return (covariance[None], variances)


def gathered(sigma_next, separator, inverse_pivot, coupling_rate, lengths, step_index, node_class):
    shifted = passed_along(separator, "dom", -1)
    prior = jnp.where(step_index[0] == 0, shifted[0], sigma_next[0])
    pivot = inverse_pivot[0].astype(F32)
    coupled = couple(inverse_pivot[0], coupling(node_class), coupling_rate)
    rows = coupled.shape[0]
    half = jnp.dot(
        coupled,
        lax.all_gather(prior, "col", axis=0, tiled=True),
        preferred_element_type=F32,
    ).astype(BF16)
    product = lax.dot_general(
        half,
        lax.all_gather(coupled, "col", axis=0, tiled=True),
        (((1,), (1,)), ((), ())),
        preferred_element_type=F32,
    )
    full = pivot + product
    active = step_index[0] < lengths[0]
    old = sigma_next[0]
    covariance = jnp.where(active, full.astype(BF16), old)
    first_col = lax.axis_index("col") * rows
    new_block = lax.dynamic_slice_in_dim(full, first_col, rows, 1)
    old_block = lax.dynamic_slice_in_dim(old, first_col, rows, 1)
    variances = jnp.where(active, jnp.diagonal(new_block), jnp.diagonal(old_block).astype(F32))
    return (covariance[None], variances[None])


def solution(mesh):
    local = owned if mesh.shape["col"] == 4 and mesh.shape["dom"] % 2 == 0 else gathered
    return jax.shard_map(
        local,
        mesh=mesh,
        in_specs=(
            P(("groups", "dom"), "col", None),
            P(("groups", "dom"), "col", None),
            P(("groups", "dom"), "col", None),
            P(("groups", "dom")),
            P(("groups", "dom")),
            P(("groups", "dom")),
            P("groups"),
        ),
        out_specs=(P(("groups", "dom"), "col", None), P(("groups", "dom"), "col")),
        check_vma=False,
    )
```
